32 devices in a mesh: dp: 8 (over y, x, core), head: 4 (over z).
Axes of the slice: x: 2, y: 2, z: 4, core: 2. Of those that a mesh axis runs over, the one named last changes fastest.
Arguments:
- tokens: bfloat16 [16384, 1024], P(('dp', 'head')), may hold values from -6 to 6
- attn_query: bfloat16 [1024, 1024], P(None, 'head'), may hold values from -0.1875 to 0.1875
- attn_key: bfloat16 [1024, 1024], P(None, 'head'), may hold values from -0.1875 to 0.1875
- attn_value: bfloat16 [1024, 1024], P(None, 'head'), may hold values from -0.1875 to 0.1875
- attn_gate: bfloat16 [1024, 1024], P(None, 'head'), may hold values from -0.1875 to 0.1875
- attn_out: bfloat16 [1024, 1024], P('head'), may hold values from -0.1875 to 0.1875
- rotation_rates: float32 [1024], P('head'), may hold values from 0.0005 to 1
- ffn_left: bfloat16 [1024, 2816], P(None, 'head'), may hold values from -0.1875 to 0.1875
- ffn_right: bfloat16 [1024, 2816], P(None, 'head'), may hold values from -0.1875 to 0.1875
- ffn_down: bfloat16 [2816, 1024], P('head'), may hold values from -0.109375 to 0.109375
- out_grad: bfloat16 [16384, 1024], P(('dp', 'head')), may hold values from -6 to 6
Outputs:
- block_out: bfloat16 [16384, 1024], P(('dp', 'head'))
- input_grad: float32 [16384, 1024], P(('dp', 'head'))
- query_grad: float32 [1024, 1024], P(None, 'head')
- key_grad: float32 [1024, 1024], P(None, 'head')
- value_grad: float32 [1024, 1024], P(None, 'head')
- gate_grad: float32 [1024, 1024], P(None, 'head')
- out_proj_grad: float32 [1024, 1024], P('head')
- rates_grad: float32 [1024], P('head')
- left_grad: float32 [1024, 2816], P(None, 'head')
- right_grad: float32 [1024, 2816], P(None, 'head')
- down_grad: float32 [2816, 1024], P('head')
The draws below stay inside these ranges and needn't reach their ends.
All inputs are finite; a program needn't handle non-finite values.
Results may differ from the reference program's by a relative error of at most 0.025.
The reference program's roundings to bfloat16 on the way count: a program that leaves them out, or rounds other values in their place, can miss the bound.
Values may be sent and summed in bfloat16 or wider, within the bound.
A program may use at most 192 MiB of HBM per device.

```python
import math
import jax
import jax.numpy as jnp
from jax import lax

D = 1024
HEADS = 8
HEAD_DIM = 128
FF = 2816
SPAN = 256
SEQ_LEN = 2048
TOKENS = 16384
N_DP = 8
N_HEAD = 4


def level_of(own_key, extent, split, smallest, largest):
    def one(axis_at, shards_of):
        steps = jax.random.uniform(jax.random.fold_in(jax.random.fold_in(own_key, 6), axis_at), (shards_of,), jnp.float32, smallest / len(split), largest / len(split))
        return jnp.repeat(jnp.exp(steps), extent[axis_at] // shards_of).reshape((-1,) + (1,) * (len(extent) - axis_at - 1))

    gain = one(*split[0])
    for cut in split[1:]:
        gain = gain * one(*cut)
    return gain


def noise(stream_key, dims, width, limit, shards=(), held_as=jnp.bfloat16):
    factor_of = level_of(stream_key, dims, shards, -0.22, 0.18) if shards else 1.0
    values = jax.random.normal(stream_key, dims, jnp.float32) * width * factor_of
    return jnp.minimum(jnp.maximum(values, -limit), limit).astype(held_as)


def setup_inputs(seed: int = 0) -> dict:
    splits = jax.random.split(jax.random.key(seed), 12)
    tokens = noise(splits[0], (TOKENS, D), 1.0, 6.0, ((0, 32),))
    attn_query = noise(splits[1], (D, D), D ** -0.5, 0.1875, ((1, 4),))
    attn_key = noise(splits[2], (D, D), D ** -0.5, 0.1875, ((1, 4),))
    attn_value = noise(splits[3], (D, D), D ** -0.5, 0.1875, ((1, 4),))
    attn_gate = noise(splits[4], (D, D), D ** -0.5, 0.1875, ((1, 4),))
    attn_out = noise(splits[5], (D, D), D ** -0.5, 0.1875, ((0, 4),))
    rotation_rates = jnp.clip(jnp.exp(math.log(1.0) - 7.6009024 * jax.random.uniform(splits[6], (D,), jnp.float32) ** level_of(splits[6], (D,), ((0, 4),), -0.2, 0.2)), 0.0005, 1.0)
    ffn_left = noise(splits[7], (D, FF), D ** -0.5, 0.1875, ((1, 4),))
    ffn_right = noise(splits[8], (D, FF), D ** -0.5, 0.1875, ((1, 4),))
    ffn_down = noise(splits[9], (FF, D), FF ** -0.5, 0.109375, ((0, 4),))
    out_grad = noise(splits[10], (TOKENS, D), 1.0, 6.0, ((0, 32),))
    return {"tokens": tokens, "attn_query": attn_query, "attn_key": attn_key, "attn_value": attn_value, "attn_gate": attn_gate, "attn_out": attn_out, "rotation_rates": rotation_rates, "ffn_left": ffn_left, "ffn_right": ffn_right, "ffn_down": ffn_down, "out_grad": out_grad}


EPSILON = 1e-06
HIGHEST = lax.Precision.HIGHEST

@jax.custom_vjp
def low(v):
    return lax.optimization_barrier(v.astype(jnp.bfloat16)).astype(jnp.float32)

@jax.custom_vjp
def low_back(v):
    return v

def low_keep(v):
    return (low(v), None)

def low_pass(kept, grad):
    return (grad,)

def back_keep(v):
    return (v, None)

def back_low(kept, grad):
    return (low(grad),)
low.defvjp(low_keep, low_pass)
low_back.defvjp(back_keep, back_low)

def simple_norm(values):
    return values * lax.rsqrt(lax.optimization_barrier(jnp.mean(values * values, axis=-1, keepdims=True)) + EPSILON)

def matmul(left, right):
    return jnp.dot(left, right, precision=HIGHEST)

def head_rates():
    heads = jnp.arange(HEADS, dtype=jnp.float32)
    return jnp.exp2(-8.0 * (heads + 1.0) / HEADS)

def span_step(state, block):
    query, keys, values = block
    rates = head_rates()
    places = jnp.arange(SPAN, dtype=jnp.float32)
    offsets = places[:, None] - places[None, :]
    decay_mask = jnp.where(offsets[None] >= 0.0, jnp.exp(-rates[:, None, None] * jnp.maximum(offsets[None], 0.0)), 0.0)
    scores = low_back(jnp.einsum('ihd,jhd->hij', query, keys, precision=HIGHEST))
    weights = low(scores * decay_mask)
    inner = jnp.einsum('hij,jhe->ihe', weights, values, precision=HIGHEST)
    query_decay = jnp.exp(-rates[None, :] * (places[:, None] + 1.0))
    outer = jnp.einsum('ihd,hde->ihe', query * query_decay[:, :, None], state, precision=HIGHEST)
    key_decay = jnp.exp(-rates[None, :] * (SPAN - 1.0 - places[:, None]))
    fresh_term = jnp.einsum('jhd,jhe->hde', keys * key_decay[:, :, None], values, precision=HIGHEST)
    new_state = jnp.exp(-rates * SPAN)[:, None, None] * state + fresh_term
    return (new_state, inner + outer)

def sequence(inputs, attn_query, attn_key, attn_value, attn_gate, attn_out, rotation_rates, ffn_left, ffn_right, ffn_down):
    length = inputs.shape[0]
    head_width = D // N_HEAD
    ffn_width = FF // N_HEAD
    normed_in = low(simple_norm(inputs))
    copies = [low_back(normed_in) for group in range(N_HEAD)]

    def project(weight):
        pieces = [matmul(copies[group], weight[:, group * head_width:(group + 1) * head_width]) for group in range(N_HEAD)]
        return low_back(jnp.concatenate(pieces, axis=1))
    query_pre = project(attn_query)
    key_pre = project(attn_key)
    value_pre = project(attn_value)
    gate_pre = project(attn_gate)
    positions = jnp.arange(length, dtype=jnp.float32)
    angles = (positions[:, None] * rotation_rates[None, :]).reshape(length, HEADS, HEAD_DIM)

    def rotate(values):
        activated = jax.nn.silu(values).reshape(length, HEADS, HEAD_DIM)
        return jnp.concatenate([activated * jnp.cos(angles), activated * jnp.sin(angles)], axis=-1)
    query = low(rotate(query_pre))
    keys = low(rotate(key_pre))
    values = low(value_pre).reshape(length, HEADS, HEAD_DIM)

    def blocks(array):
        return array.reshape(length // SPAN, SPAN, HEADS, array.shape[-1])
    start_state = jnp.zeros((HEADS, 2 * HEAD_DIM, HEAD_DIM), jnp.float32)
    final_state, mixed_out = lax.scan(jax.checkpoint(span_step), start_state, (blocks(query), blocks(keys), blocks(values)))
    attn = low_back(mixed_out.reshape(length, HEADS * HEAD_DIM))
    gated = low(simple_norm(attn) * gate_pre)
    branch = jnp.zeros((length, D), jnp.float32)
    for group in range(N_HEAD):
        cut = slice(group * head_width, (group + 1) * head_width)
        branch = branch + low(matmul(gated[:, cut], attn_out[cut, :]))
    hidden = inputs + low_back(branch)
    normed_mid = low(simple_norm(hidden))
    feed = jnp.zeros((length, D), jnp.float32)
    for group in range(N_HEAD):
        cut = slice(group * ffn_width, (group + 1) * ffn_width)
        mid_copy = low_back(normed_mid)
        left = low_back(matmul(mid_copy, ffn_left[:, cut]))
        right = low_back(matmul(mid_copy, ffn_right[:, cut]))
        product = low(left * right)
        feed = feed + low(matmul(product, ffn_down[cut, :]))
    return hidden + low_back(feed)

def reference(tokens, attn_query, attn_key, attn_value, attn_gate, attn_out, rotation_rates, ffn_left, ffn_right, ffn_down, out_grad):
    floats = [array.astype(jnp.float32) for array in (tokens, attn_query, attn_key, attn_value, attn_gate, attn_out, rotation_rates, ffn_left, ffn_right, ffn_down)]

    def forward(inputs, *weights):
        per_sequence = inputs.reshape(N_DP, SEQ_LEN, D)

        def one_sequence(block_rows):
            return jax.checkpoint(sequence)(block_rows, *weights)
        outputs = lax.map(one_sequence, per_sequence)
        return outputs.reshape(inputs.shape)
    result, pull = jax.vjp(forward, *floats)
    grads = pull(out_grad.astype(jnp.float32))
    return (result.astype(jnp.bfloat16), grads[0], grads[1], grads[2], grads[3], grads[4], grads[5], grads[6], grads[7], grads[8], grads[9])
```

```python
import jax
import jax.numpy as jnp
from jax import lax
from jax.sharding import PartitionSpec as P

HEADS = 8
HEAD_DIM = 128
SPAN = 256
EPSILON = 1e-06
BF = jnp.bfloat16
F32 = jnp.float32


def norm_parts(values):
    scale = lax.rsqrt(jnp.mean(values * values, axis=-1, keepdims=True) + EPSILON)
    return (values * scale, scale)


def norm_back(normed, scale, grad):
    return scale * (grad - normed * jnp.mean(grad * normed, axis=-1, keepdims=True))


def plain_dot(left, right):
    return jnp.dot(left, right, preferred_element_type=F32)


def first_dot(left, right):
    return lax.dot_general(left, right, (((0,), (0,)), ((), ())), preferred_element_type=F32)


def second_dot(left, right):
    return lax.dot_general(left, right, (((1,), (1,)), ((), ())), preferred_element_type=F32)


def make(n_dp, n_head):
    def swap(array, bit):
        return lax.ppermute(array, "dp", [(i, i ^ bit) for i in range(n_dp)])

    def from_above(array, step):
        return lax.ppermute(array, "head", [((i + step) % n_head, i) for i in range(n_head)])

    def to_above(array, step):
        return lax.ppermute(array, "head", [(i, (i + step) % n_head) for i in range(n_head)])

    def share(pieces, axis):
        half = pieces.shape[axis] // 2
        by_x = swap(pieces, 2)
        by_y = swap(pieces, 4)
        low = swap(lax.slice_in_dim(by_x, 0, half, axis=axis), 4)
        high = swap(lax.slice_in_dim(by_y, half, 2 * half, axis=axis), 2)
        return [pieces, by_x, by_y, jnp.concatenate([low, high], axis=axis)]

    def collect(parts, axis):
        own, for_x, for_y, for_far = parts
        half = own.shape[axis] // 2

        def cut(array, which):
            return lax.slice_in_dim(array, which * half, (which + 1) * half, axis=axis)

        def add(left, right):
            return (left.astype(F32) + right.astype(F32)).astype(BF)

        low = swap(cut(for_far, 0), 4)
        high = swap(cut(for_far, 1), 2)
        by_x = swap(jnp.concatenate([add(cut(for_x, 0), low), cut(for_x, 1)], axis=axis), 2)
        by_y = swap(jnp.concatenate([cut(for_y, 0), add(cut(for_y, 1), high)], axis=axis), 4)
        plane = (own.astype(F32) + by_x.astype(F32) + by_y.astype(F32)).astype(BF)
        total = plane[0].astype(F32)
        for step in range(1, n_head):
            total = total + to_above(plane[step], step).astype(F32)
        if n_dp > 8:
            groups = [[i + 8 * j for j in range(n_dp // 8)] for i in range(8)]
            total = lax.psum(total, "dp", axis_index_groups=groups)
        return total.astype(BF)

    def on_device(
        tokens,
        attn_query,
        attn_key,
        attn_value,
        attn_gate,
        attn_out,
        rotation_rates,
        ffn_left,
        ffn_right,
        ffn_down,
        out_grad,
    ):
        width = tokens.shape[1]
        quarter = width // 4
        rows = tokens.shape[0]
        spans = rows // SPAN
        units = ffn_left.shape[1] // 2
        dp = lax.axis_index("dp")
        place = lax.axis_index("head")
        core = dp & 1
        plane = (dp >> 1) & 3

        def relative(array, axis):
            return jnp.concatenate(
                [
                    lax.dynamic_slice_in_dim(array, (plane ^ q) * quarter, quarter, axis=axis)
                    for q in range(4)
                ],
                axis=axis,
            )

        def half_of(array, axis):
            size = array.shape[axis] // 2
            return lax.dynamic_slice_in_dim(array, core * size, size, axis=axis)

        attn_own = jnp.concatenate(
            [half_of(w, 1) for w in (attn_query, attn_key, attn_value, attn_gate)]
            + [half_of(attn_out, 0).T],
            axis=1,
        )
        attn_own = relative(attn_own, 0)
        ffn_own = jnp.stack([half_of(ffn_left, 1).T, half_of(ffn_right, 1).T, half_of(ffn_down, 0)])
        ffn_own = relative(ffn_own, 2)

        attn_piece = attn_own[:quarter]
        attn_far = jnp.stack([from_above(attn_piece, r) for r in range(1, n_head)])
        attn_weights = jnp.concatenate(share(attn_far, 1), axis=1)
        attn_weights = [attn_own] + [attn_weights[r] for r in range(n_head - 1)]
        ffn_piece = ffn_own[:, :, :quarter]
        ffn_far = jnp.stack([from_above(ffn_piece, r) for r in range(1, n_head)], axis=1)
        ffn_rest = jnp.concatenate(share(ffn_far, 2), axis=3)
        ffn_all = jnp.concatenate([ffn_own[:, None], ffn_rest], axis=1)
        ffn_all = ffn_all.reshape(3, n_head * units, width)
        left_w, right_w, down_w = ffn_all[0], ffn_all[1], ffn_all[2]

        inputs = relative(tokens, 1).astype(F32)
        normed_one, scale_one = norm_parts(inputs)
        normed_low = normed_one.astype(BF)
        gathered_in = jnp.concatenate([normed_low, swap(normed_low, 1)], axis=0)
        out_grad = relative(out_grad, 1)
        grad_rows = jnp.concatenate([out_grad, swap(out_grad, 1)], axis=0)

        rates_own = half_of(rotation_rates, 0)
        rates_all = jnp.stack(
            [rates_own] + [from_above(rates_own, r) for r in range(1, n_head)]
        )
        positions = (place * rows + jnp.arange(rows)).astype(F32)
        angles = positions[None, :, None] * rates_all[:, None, :]
        cosines = jnp.cos(angles)[:, None]
        sines = jnp.sin(angles)[:, None]

        pre = jnp.stack([plain_dot(gathered_in, w[:, : 4 * HEAD_DIM]) for w in attn_weights])
        pre = pre.reshape(n_head, 2, rows, 4 * HEAD_DIM)
        query_pre, key_pre, value_pre, gate_pre = (
            pre[..., i * HEAD_DIM : (i + 1) * HEAD_DIM] for i in range(4)
        )

        def rotate(values):
            activated = jax.nn.silu(values)
            return jnp.concatenate([activated * cosines, activated * sines], axis=-1).astype(BF)

        def blocks(array):
            return array.reshape(n_head, 2, spans, SPAN, array.shape[-1])

        query = blocks(rotate(query_pre))
        keys = blocks(rotate(key_pre))
        values = blocks(value_pre.astype(BF))
        head_ids = 2 * ((place + jnp.arange(n_head)) % n_head) + core
        decay_rates = jnp.exp2(-8.0 * (head_ids.astype(F32) + 1.0) / HEADS)
        places = jnp.arange(SPAN, dtype=F32)
        offsets = places[:, None] - places[None, :]
        decay_mask = jnp.where(
            offsets[None] >= 0.0,
            jnp.exp(-decay_rates[:, None, None] * jnp.maximum(offsets[None], 0.0)),
            0.0,
        )[:, None, None]
        query_decay = jnp.exp(-decay_rates[:, None] * (places[None] + 1.0))[:, None, None, :, None]
        key_decay = jnp.exp(-decay_rates[:, None] * (SPAN - 1.0 - places[None]))[
            :, None, None, :, None
        ]
        span_decay = jnp.exp(-decay_rates * SPAN)[:, None, None, None]
        rows_decay = jnp.exp(-decay_rates * rows)[:, None, None, None]

        def ein(spec, left, right):
            return jnp.einsum(spec, left, right, preferred_element_type=F32)

        def exact(spec, left, right):
            left, right = left.astype(F32), right.astype(F32)
            return jnp.einsum(spec, left, right, precision=lax.Precision.HIGHEST)

        def roll(array, step):
            return jnp.roll(array, step, axis=0)

        scores = ein("hsnid,hsnjd->hsnij", query, keys)
        weights = (scores * decay_mask).astype(BF)
        attn = ein("hsnij,hsnje->hsnie", weights, values)
        value_late = values.astype(F32) * key_decay
        fresh = exact("hsnjd,hsnje->hsnde", keys, value_late)
        local_state = jnp.zeros(fresh.shape[:2] + fresh.shape[3:], F32)
        for n in range(spans):
            local_state = span_decay * local_state + fresh[:, :, n]
        state = jnp.zeros_like(local_state)
        for hop in range(n_head - 1):
            message = roll((local_state + rows_decay * state).astype(BF), -1)
            state = lax.ppermute(message, "head", [(i, i + 1) for i in range(n_head - 1)]).astype(
                F32
            )
        states = []
        for n in range(spans):
            states.append(state)
            state = span_decay * state + fresh[:, :, n]
        states = jnp.stack(states, axis=2)
        attn = attn + query_decay * exact("hsnid,hsnde->hsnie", query, states)
        attn = attn.reshape(n_head, 2, rows, HEAD_DIM)

        def core_sum(array):
            return array + swap(array[::-1], 1)

        squares = core_sum(jnp.sum(attn * attn, axis=(0, 3)))
        scale_attn = lax.rsqrt(squares / width + EPSILON)[None, :, :, None]
        attn_normed = attn * scale_attn
        gated = (attn_normed * gate_pre).astype(BF).reshape(n_head, 2 * rows, HEAD_DIM)
        out_w = jnp.concatenate([w[:, 4 * HEAD_DIM :] for w in attn_weights], axis=1)
        gated = gated.transpose(1, 0, 2).reshape(2 * rows, n_head * HEAD_DIM)

        def core_scatter(array):
            return array[:rows] + swap(array[rows:].astype(BF), 1).astype(F32)

        hidden = inputs + core_scatter(second_dot(gated, out_w))
        normed_two, scale_two = norm_parts(hidden)
        normed_low = normed_two.astype(BF)
        gathered_mid = jnp.concatenate([normed_low, swap(normed_low, 1)], axis=0)
        left = second_dot(gathered_mid, left_w)
        right = second_dot(gathered_mid, right_w)
        product = (left * right).astype(BF)
        down_grad = first_dot(product, grad_rows).astype(BF)
        grad_product = second_dot(grad_rows, down_w)
        grad_left = (grad_product * right).astype(BF)
        grad_right = (grad_product * left).astype(BF)
        left_grad = first_dot(grad_left, gathered_mid).astype(BF)
        right_grad = first_dot(grad_right, gathered_mid).astype(BF)
        grad_mid = core_scatter(plain_dot(grad_left, left_w) + plain_dot(grad_right, right_w))
        grad_hidden = out_grad.astype(F32) + norm_back(normed_two, scale_two, grad_mid)

        def ffn_total(grad):
            grad = grad.reshape(n_head, units, width)
            piece = collect([grad[:, :, q * quarter : (q + 1) * quarter] for q in range(4)], 1)
            return jnp.concatenate(share(piece, 0), axis=1)

        down_grad, left_grad, right_grad = (ffn_total(g) for g in (down_grad, left_grad, right_grad))
        block_out = (hidden + core_scatter(plain_dot(product, down_w))).astype(BF)

        branch_low = grad_hidden.astype(BF)
        branch_rows = jnp.concatenate([branch_low, swap(branch_low, 1)], axis=0)
        out_grads = first_dot(branch_rows, gated)
        grad_gated = plain_dot(branch_rows, out_w)
        grad_gated = grad_gated.reshape(2, rows, n_head, HEAD_DIM).transpose(2, 0, 1, 3)
        grad_normed = grad_gated * gate_pre
        grad_gate_pre = (grad_gated * attn_normed).astype(BF)
        products = core_sum(jnp.sum(grad_normed * attn_normed, axis=(0, 3)))[None, :, :, None]
        grad_attn = (scale_attn * (grad_normed - attn_normed * (products / width))).astype(BF)
        grad_blocks = blocks(grad_attn)
        grad_scores = (ein("hsnie,hsnje->hsnij", grad_blocks, values) * decay_mask).astype(BF)
        grad_values = ein("hsnij,hsnie->hsnje", weights, grad_blocks)
        grad_query = ein("hsnij,hsnjd->hsnid", grad_scores, keys)
        grad_keys = ein("hsnij,hsnid->hsnjd", grad_scores, query)
        grad_query = grad_query + query_decay * exact("hsnie,hsnde->hsnid", grad_blocks, states)
        grad_early = grad_blocks.astype(F32) * query_decay
        grad_states = exact("hsnid,hsnie->hsnde", query, grad_early)
        local_pending = jnp.zeros(grad_states.shape[:2] + grad_states.shape[3:], F32)
        for n in reversed(range(spans)):
            local_pending = span_decay * local_pending + grad_states[:, :, n]
        pending = jnp.zeros_like(local_pending)
        for hop in range(n_head - 1):
            message = roll((local_pending + rows_decay * pending).astype(BF), 1)
            pending = lax.ppermute(message, "head", [(i + 1, i) for i in range(n_head - 1)]).astype(
                F32
            )
        later = []
        for n in reversed(range(spans)):
            later.insert(0, pending)
            pending = span_decay * pending + grad_states[:, :, n]
        later = jnp.stack(later, axis=2)
        grad_keys = grad_keys + key_decay * exact("hsnje,hsnde->hsnjd", values, later)
        grad_values = grad_values + key_decay * exact("hsnjd,hsnde->hsnje", keys, later)

        def unrotate(grad_rotated, pre_values):
            shaped = grad_rotated.reshape(n_head, 2, rows, 2 * HEAD_DIM)
            grad_cos = shaped[..., :HEAD_DIM]
            grad_sin = shaped[..., HEAD_DIM:]
            grad_act = grad_cos * cosines + grad_sin * sines
            sigmoid_pre = jax.nn.sigmoid(pre_values)
            activated = pre_values * sigmoid_pre
            grad_angle = activated * (grad_sin * cosines - grad_cos * sines)
            grad_pre = grad_act * sigmoid_pre * (1.0 + pre_values * (1.0 - sigmoid_pre))
            return (grad_pre.astype(BF), grad_angle)

        grad_query_pre, angle_query = unrotate(grad_query, query_pre)
        grad_key_pre, angle_key = unrotate(grad_keys, key_pre)
        grad_value_pre = grad_values.reshape(n_head, 2, rows, HEAD_DIM).astype(BF)
        rates_grad = jnp.sum(
            positions[None, None, :, None] * (angle_query + angle_key), axis=(1, 2)
        )
        grad_pre = jnp.concatenate(
            [grad_query_pre, grad_key_pre, grad_value_pre, grad_gate_pre], axis=-1
        ).reshape(n_head, 2 * rows, 4 * HEAD_DIM)
        attn_grads = []
        grad_in = None
        for r in range(n_head):
            main = first_dot(gathered_in, grad_pre[r]).astype(BF)
            outs = out_grads[:, r * HEAD_DIM : (r + 1) * HEAD_DIM].astype(BF)
            attn_grads.append(jnp.concatenate([main, outs], axis=1))
            term = second_dot(grad_pre[r], attn_weights[r][:, : 4 * HEAD_DIM])
            grad_in = term if grad_in is None else grad_in + term
        grad_in = core_scatter(grad_in)
        input_grad = grad_hidden + norm_back(normed_one, scale_one, grad_in)

        attn_grads = jnp.stack(attn_grads).reshape(n_head, 4, quarter, 5 * HEAD_DIM)
        piece = collect([attn_grads[:, q] for q in range(4)], 1)
        attn_total = jnp.concatenate(share(piece, 0), axis=0)
        rates_piece = rates_grad[0]
        for step in range(1, n_head):
            rates_piece = rates_piece + to_above(rates_grad[step], step)
        groups = [list(range(0, n_dp, 2)), list(range(1, n_dp, 2))]
        rates_piece = lax.psum(rates_piece, "dp", axis_index_groups=groups)

        def both(array, axis):
            other = swap(array, 1)
            first = jnp.where(core == 0, array, other)
            second = jnp.where(core == 0, other, array)
            return first, second

        first, second = both(relative(attn_total, 0), 0)
        matrices = []
        for i in range(5):
            pair = [part[:, i * HEAD_DIM : (i + 1) * HEAD_DIM] for part in (first, second)]
            matrices.append(jnp.concatenate(pair, axis=1).astype(F32))
        query_grad, key_grad, value_grad, gate_grad, out_proj_grad = matrices
        out_proj_grad = out_proj_grad.T
        rates_grad = jnp.concatenate(both(rates_piece, 0), axis=0)
        ffn_grads = jnp.stack([relative(g, 1) for g in (left_grad, right_grad, down_grad)])
        ffn_grads = jnp.concatenate(both(ffn_grads, 1), axis=1).astype(F32)
        return (
            relative(block_out, 1),
            relative(input_grad, 1),
            query_grad,
            key_grad,
            value_grad,
            gate_grad,
            out_proj_grad,
            rates_grad,
            ffn_grads[0].T,
            ffn_grads[1].T,
            ffn_grads[2],
        )

    return on_device


def solution(mesh):
    weights = (P(None, "head"),) * 4 + (P("head", None), P("head")) + (P(None, "head"),) * 2
    weights = weights + (P("head", None),)
    rows = P(("dp", "head"), None)
    return jax.shard_map(
        make(mesh.shape["dp"], mesh.shape["head"]),
        mesh=mesh,
        in_specs=(rows,) + weights + (rows,),
        out_specs=(rows, rows) + weights,
        check_vma=False,
    )
```

```python
import functools

import jax
import jax.numpy as jnp
from jax import lax
from jax.experimental import pallas as pl
from jax.experimental.pallas import tpu as pltpu
from jax.sharding import PartitionSpec as P

HEADS = 8
HEAD_DIM = 128
SPAN = 256
EPSILON = 1e-06
BF = jnp.bfloat16
F32 = jnp.float32


def norm_parts(values):
    scale = lax.rsqrt(jnp.mean(values * values, axis=-1, keepdims=True) + EPSILON)
    return (values * scale, scale)


def norm_back(normed, scale, grad):
    return scale * (grad - normed * jnp.mean(grad * normed, axis=-1, keepdims=True))


def plain_dot(left, right):
    return jnp.dot(left, right, preferred_element_type=F32)


def first_dot(left, right):
    return lax.dot_general(left, right, (((0,), (0,)), ((), ())), preferred_element_type=F32)


def second_dot(left, right):
    return lax.dot_general(left, right, (((1,), (1,)), ((), ())), preferred_element_type=F32)


MESH = pl.DeviceIdType.MESH
ANY = pl.BlockSpec(memory_space=pl.ANY)
IN_VMEM = pl.BlockSpec(memory_space=pltpu.VMEM)


def split(value):
    high = value.astype(BF)
    return high, (value - high.astype(F32)).astype(BF)


class Place:
    def __init__(self, n_head):
        self.n_head = n_head
        dp = lax.axis_index("dp")
        self.z = lax.axis_index("head")
        self.core = lax.rem(dp, 2)
        x = lax.rem(lax.div(dp, 2), 2)
        y = lax.rem(lax.div(dp, 4), 2)
        self.plane = x + 2 * y
        self.at = [self.plane, self.plane + 1 - 2 * x, self.plane + 2 - 4 * y, 3 - self.plane]
        self.across = {"dp": dp + 1 - 2 * self.core}
        self.by_x = {"dp": dp + 2 - 4 * x}
        self.by_y = {"dp": dp + 4 - 8 * y}
        self.up = {"head": lax.rem(self.z + 1, n_head)}
        self.down = {"head": lax.rem(self.z + n_head - 1, n_head)}

    def below(self, step):
        return {"head": lax.rem(self.z + self.n_head - step, self.n_head)}

    def greet(self):
        barrier = pltpu.get_barrier_semaphore()
        others = [self.across, self.by_x, self.by_y]
        others += [self.below(step) for step in range(1, self.n_head)]
        for other in others:
            pl.semaphore_signal(barrier, inc=1, device_id=other, device_id_type=MESH)
        pl.semaphore_wait(barrier, len(others))


class Copies:
    def __init__(self, sends, receives, locals_):
        self.sends, self.receives, self.locals = sends, receives, locals_
        self.pending = []
        self.n_local = 0

    def send(self, src, dst, out, into, device, when=None):
        copy = pltpu.make_async_remote_copy(
            src_ref=src,
            dst_ref=dst,
            send_sem=self.sends.at[out],
            recv_sem=self.receives.at[into],
            device_id=device,
            device_id_type=MESH,
        )
        if when is None:
            copy.start()
            self.pending.append(copy.wait_send)
        else:
            pl.when(when)(copy.start)
            self.pending.append(lambda: pl.when(when)(copy.wait_send))

    def receive(self, dst, into, device):
        pltpu.make_async_remote_copy(
            src_ref=dst,
            dst_ref=dst,
            send_sem=self.sends.at[0],
            recv_sem=self.receives.at[into],
            device_id=device,
            device_id_type=MESH,
        ).wait_recv()

    def move(self, src, dst, later=False):
        copy = pltpu.make_async_copy(src, dst, self.locals.at[self.n_local])
        self.n_local += 1
        copy.start()
        if later:
            self.pending.append(copy.wait)
        return copy

    def finish(self):
        for wait in self.pending:
            wait()


class Gather:
    def __init__(self, place, copies, view, base):
        self.place, self.copies, self.view, self.base = place, copies, view, base

    def begin(self):
        place, z = self.place, self.place.z
        own = self.view(0, 0, None)
        last = place.n_head - 1
        self.copies.send(
            own, self.view(last, 0, None), self.base, self.base + last, place.up, when=z < last
        )
        self.copies.send(own, self.view(1, 0, None), self.base + 1, self.base + 1, place.down, when=z > 0)

    def arrived(self, slot):
        place, copies, z, base = self.place, self.copies, self.place.z, self.base
        last = place.n_head - 1
        copies.receive(self.view(slot, 0, None), base + slot, place.up)
        from_up = z + slot <= last
        piece = self.view(slot, 0, None)
        down = jnp.logical_and(from_up, z > 0)
        up = jnp.logical_and(jnp.logical_not(from_up), z < last)
        after = jnp.minimum(slot + 1, last)
        before = jnp.maximum(slot - 1, 1)
        copies.send(piece, self.view(after, 0, None), base + 1 + slot, base + after, place.down, when=down)
        copies.send(piece, self.view(before, 0, None), base + 1 + slot, base + before, place.up, when=up)
        at = base + 4 * slot + 4
        copies.send(piece, self.view(slot, 1, None), at, at, place.by_x)
        copies.send(piece, self.view(slot, 2, None), at + 1, at + 1, place.by_y)

    def spread(self, slot):
        place, copies = self.place, self.copies
        at = self.base + 4 * slot + 4
        copies.receive(self.view(slot, 1, None), at, place.by_x)
        copies.send(self.view(slot, 1, 0), self.view(slot, 3, 0), at + 2, at + 2, place.by_y)
        copies.receive(self.view(slot, 2, None), at + 1, place.by_y)
        copies.send(self.view(slot, 2, 1), self.view(slot, 3, 1), at + 3, at + 3, place.by_x)

    def complete(self, slot):
        place, copies = self.place, self.copies
        at = self.base + 4 * slot + 4
        copies.receive(self.view(slot, 3, 0), at + 2, place.by_y)
        copies.receive(self.view(slot, 3, 1), at + 3, place.by_x)


PER_GATHER = 24


def forward_kernel(
    n_head,
    tokens,
    wq,
    wk,
    wv,
    wg,
    wo,
    ffn,
    rates,
    wa_out,
    wo_out,
    wf_out,
    nin_out,
    pre_out,
    q_out,
    k_out,
    v_out,
    attn_out,
    cos_out,
    sin_out,
    fresh_out,
    carry_out,
    scale_out,
    gated_out,
    hidden_out,
    nm_out,
    wa_ref,
    wo_ref,
    wf_ref,
    x_ref,
    nin_ref,
    pre_ref,
    q_ref,
    k_ref,
    v_ref,
    attn_ref,
    cos_ref,
    sin_ref,
    fresh_ref,
    carry_ref,
    message_ref,
    squares_ref,
    other_squares_ref,
    gated_ref,
    branch_ref,
    other_branch_ref,
    hidden_ref,
    nm_ref,
    rates_ref,
    sends,
    receives,
    locals_,
):
    rows, width = tokens.shape
    quarter = width // 4
    units = ffn.shape[1] // 2
    tiles = 2 * rows // SPAN
    place = Place(n_head)
    z, core = place.z, place.core
    copies = Copies(sends, receives, locals_)

    def columns(start, size):
        return pl.ds(pl.multiple_of(start, size), size)

    own_loads = []
    for q in range(4):
        far = columns(place.at[q] * quarter, quarter)
        near = pl.ds(q * quarter, quarter)
        loads = []
        for i, w in enumerate((wq, wk, wv, wg)):
            src = w.at[far, columns(core * HEAD_DIM, HEAD_DIM)]
            loads.append(copies.move(src, wa_ref.at[0, near, pl.ds(i * HEAD_DIM, HEAD_DIM)]))
        src = wo.at[columns(core * HEAD_DIM, HEAD_DIM), far]
        loads.append(copies.move(src, wo_ref.at[pl.ds(0, HEAD_DIM), near]))
        src = ffn.at[:, pl.ds(pl.multiple_of(core * units, 16), units), far]
        loads.append(copies.move(src, wf_ref.at[:, pl.ds(0, units), near]))
        own_loads.append(loads)
    token_loads = [
        copies.move(
            tokens.at[:, columns(place.at[q] * quarter, quarter)],
            x_ref.at[:, pl.ds(q * quarter, quarter)],
        )
        for q in range(4)
    ]
    place.greet()

    def half_rows(half, size):
        return pl.ds(0, size) if half is None else pl.ds(half * (size // 2), size // 2)

    def wa_view(slot, q, half):
        at = half_rows(half, quarter)
        return wa_ref.at[slot, pl.ds(q * quarter + at.start, at.size), :]

    def wo_view(slot, q, half):
        at = half_rows(half, HEAD_DIM)
        return wo_ref.at[
            pl.ds(pl.multiple_of(slot * HEAD_DIM + at.start, HEAD_DIM // 2), at.size),
            pl.ds(q * quarter, quarter),
        ]

    def wf_view(slot, q, half):
        at = half_rows(half, units)
        return wf_ref.at[
            :,
            pl.ds(pl.multiple_of(slot * units + at.start, 16), at.size),
            pl.ds(q * quarter, quarter),
        ]

    attn_in = Gather(place, copies, wa_view, 0)
    attn_down = Gather(place, copies, wo_view, PER_GATHER)
    feed = Gather(place, copies, wf_view, 2 * PER_GATHER)
    base = 3 * PER_GATHER
    for load in own_loads[0][:4]:
        load.wait()
    attn_in.begin()
    own_loads[0][4].wait()
    attn_down.begin()
    for step in range(1, n_head):
        copies.send(rates, rates_ref.at[step], base + step, base + step, place.below(step))
    rates_ref[0] = rates[...]

    for load in token_loads:
        load.wait()

    def norm_rows(values):
        mean = jnp.mean(values * values, axis=-1, keepdims=True)
        return values * lax.rsqrt(mean + EPSILON)

    @pl.loop(0, rows // 128)
    def _(i):
        at = pl.ds(pl.multiple_of(i * 128, 128), 128)
        nin_ref[at, :] = norm_rows(x_ref[at, :].astype(F32)).astype(BF)

    base += 4
    nin_other = nin_ref.at[pl.ds(rows, rows)]
    copies.send(nin_ref.at[pl.ds(0, rows)], nin_other, base, base, place.across)
    own_loads[0][5].wait()
    feed.begin()
    for loads in own_loads[1:]:
        for load in loads:
            load.wait()
    for step in range(1, n_head):
        copies.receive(rates_ref.at[step], base - 4 + step, place.up)
    copies.receive(nin_other, base, place.across)
    copies.move(nin_ref, nin_out, later=True)

    def decay_of(head):
        exponent = jnp.full((1, 1), -8.0 / HEADS, F32) * (head + 1).astype(F32)
        return jnp.exp2(exponent)

    def tile(i):
        return pl.ds(pl.multiple_of(i * SPAN, SPAN), SPAN)

    def iota(shape, axis):
        return lax.broadcasted_iota(jnp.int32, shape, axis).astype(F32)

    def dot(left, right):
        return jnp.dot(left, right, preferred_element_type=F32)

    def slot_compute(slot):
        head = 2 * lax.rem(z + slot, n_head) + core
        decay = decay_of(head)
        rate = rates_ref[slot, pl.ds(core, 1), :]
        coarse = (z * rows).astype(F32) + 32.0 * iota((rows // 32, HEAD_DIM), 0)
        coarse = coarse * rate
        fine = iota((32, HEAD_DIM), 0) * rate
        cos_a, sin_a = jnp.cos(coarse), jnp.sin(coarse)
        cos_b, sin_b = jnp.cos(fine), jnp.sin(fine)
        for a in range(rows // 32):
            cos_row, sin_row = cos_a[a : a + 1], sin_a[a : a + 1]
            cos_ref[slot, pl.ds(a * 32, 32), :] = cos_row * cos_b - sin_row * sin_b
            sin_ref[slot, pl.ds(a * 32, 32), :] = sin_row * cos_b + cos_row * sin_b
        offsets = iota((SPAN, SPAN), 0) - iota((SPAN, SPAN), 1)
        mask = jnp.where(offsets >= 0.0, jnp.exp(-decay * jnp.maximum(offsets, 0.0)), 0.0)
        late = jnp.exp(-decay * (SPAN - 1.0 - iota((SPAN, HEAD_DIM), 0)))

        @pl.loop(0, tiles)
        def _(i):
            at = tile(i)
            pre = dot(nin_ref[at, :], wa_ref[slot])
            pre_ref[slot, at, :] = pre
            here = tile(lax.rem(i, rows // SPAN))
            cosines, sines = cos_ref[slot, here, :], sin_ref[slot, here, :]

            def rotate(values):
                activated = values / (1.0 + jnp.exp(-values))
                turned = jnp.concatenate([activated * cosines, activated * sines], axis=1)
                return turned.astype(BF)

            query = rotate(pre[:, :HEAD_DIM])
            keys = rotate(pre[:, HEAD_DIM : 2 * HEAD_DIM])
            value = pre[:, 2 * HEAD_DIM : 3 * HEAD_DIM].astype(BF)
            q_ref[slot, at, :] = query
            k_ref[slot, at, :] = keys
            v_ref[slot, at, :] = value
            scores = lax.dot_general(
                query, keys, (((1,), (1,)), ((), ())), preferred_element_type=F32
            )
            weights = (scores * mask).astype(BF)
            attn_ref[slot, at, :] = dot(weights, value)
            high, low = split(value.astype(F32) * late)
            both = lax.dot_general(
                keys,
                jnp.concatenate([high, low], axis=1),
                (((0,), (0,)), ((), ())),
                preferred_element_type=F32,
            )
            fresh_ref[slot, i] = both[:, :HEAD_DIM] + both[:, HEAD_DIM:]

        for ref, out in (
            (wa_ref, wa_out),
            (pre_ref, pre_out),
            (q_ref, q_out),
            (k_ref, k_out),
            (v_ref, v_out),
            (cos_ref, cos_out),
            (sin_ref, sin_out),
            (fresh_ref, fresh_out),
        ):
            copies.move(ref.at[slot], out.at[slot], later=True)

    last = n_head - 1
    first = 1 + 2 * lax.div(z, last)
    second = 2 + lax.rem(lax.div(z + 1, 2), 2)
    third = 6 - first - second

    attn_in.arrived(first)
    attn_down.arrived(first)
    slot_compute(0)
    attn_in.arrived(second)
    attn_down.arrived(second)
    attn_in.spread(first)
    attn_down.spread(first)
    attn_in.arrived(third)
    attn_down.arrived(third)
    attn_in.spread(second)
    attn_down.spread(second)
    attn_in.complete(first)
    slot_compute(first)
    feed.arrived(first)
    attn_in.spread(third)
    attn_down.spread(third)
    attn_in.complete(second)
    slot_compute(second)
    feed.arrived(second)
    feed.spread(first)
    attn_in.complete(third)
    slot_compute(third)
    feed.arrived(third)
    feed.spread(second)

    base += 1
    chain_base = base
    n_chain = 2 * n_head

    def chain_at(index):
        group, seq = lax.div(index, 2), lax.rem(index, 2)
        return lax.rem(group - z + n_head, n_head), seq, decay_of(2 * group + core)

    def chain_copy(index, slot, seq):
        after = lax.rem(slot + n_head - 1, n_head)
        return pltpu.make_async_remote_copy(
            src_ref=message_ref.at[slot, seq],
            dst_ref=carry_ref.at[after, seq],
            send_sem=sends.at[chain_base + index],
            recv_sem=receives.at[chain_base + index],
            device_id=place.up,
            device_id_type=MESH,
        )

    @pl.loop(0, n_chain)
    def _(index):
        slot, seq, decay = chain_at(index)

        @pl.when(z > 0)
        def _():
            copies.receive(carry_ref.at[slot, seq], chain_base + index, place.down)

        @pl.when(z == 0)
        def _():
            carry_ref[slot, seq] = jnp.zeros(carry_ref.shape[2:], BF)

        @pl.when(z < last)
        def _():
            total = jnp.exp(-decay * rows) * carry_ref[slot, seq].astype(F32)
            for n in range(rows // SPAN):
                left = rows - (n + 1) * SPAN
                total += jnp.exp(-decay * left) * fresh_ref[slot, seq * (rows // SPAN) + n]
            message_ref[slot, seq] = total.astype(BF)
            chain_copy(index, slot, seq).start()

    copies.move(carry_ref, carry_out, later=True)

    squares_ref[...] = jnp.zeros_like(squares_ref)

    @pl.loop(0, n_head)
    def _(slot):
        decay = decay_of(2 * lax.rem(z + slot, n_head) + core)
        early = jnp.exp(-decay * (iota((SPAN, HEAD_DIM), 0) + 1.0))

        @pl.loop(0, 2)
        def _(seq):
            state = carry_ref[slot, seq].astype(F32)
            for n in range(rows // SPAN):
                i = seq * (rows // SPAN) + n
                at = tile(i)
                both = dot(q_ref[slot, at, :], jnp.concatenate(split(state), axis=1))
                attn = attn_ref[slot, at, :]
                attn += early * (both[:, :HEAD_DIM] + both[:, HEAD_DIM:])
                attn_ref[slot, at, :] = attn
                squares_ref[at, :] += jnp.sum(attn * attn, axis=-1, keepdims=True)
                if n + 1 < rows // SPAN:
                    state = jnp.exp(-decay * SPAN) * state + fresh_ref[slot, i]

    copies.move(attn_ref, attn_out, later=True)
    base += n_chain
    own, other = pl.ds(0, rows), pl.ds(rows, rows)
    copies.send(squares_ref.at[own], other_squares_ref.at[other], base, base, place.across)
    copies.send(squares_ref.at[other], other_squares_ref.at[own], base + 1, base + 1, place.across)
    feed.spread(third)
    for slot in (first, second, third):
        attn_down.complete(slot)
    copies.receive(other_squares_ref.at[other], base, place.across)
    copies.receive(other_squares_ref.at[own], base + 1, place.across)

    @pl.loop(0, tiles)
    def _(i):
        at = tile(i)
        total = squares_ref[at, :] + other_squares_ref[at, :]
        scale = lax.rsqrt(total / width + EPSILON)
        other_squares_ref[at, :] = scale
        for slot in range(n_head):
            gate = pre_ref[slot, at, pl.ds(3 * HEAD_DIM, HEAD_DIM)]
            gated = (attn_ref[slot, at, :] * scale * gate).astype(BF)
            gated_ref[at, pl.ds(slot * HEAD_DIM, HEAD_DIM)] = gated

    copies.move(other_squares_ref, scale_out, later=True)
    copies.move(gated_ref, gated_out, later=True)
    copies.move(wo_ref, wo_out, later=True)
    base += 2

    @pl.loop(0, rows // SPAN)
    def _(i):
        gated = gated_ref[pl.ds(pl.multiple_of(rows + i * SPAN, SPAN), SPAN), :]
        branch_ref[tile(i), :] = dot(gated, wo_ref[...]).astype(BF)

    copies.send(branch_ref, other_branch_ref, base, base, place.across)

    @pl.loop(0, rows // SPAN)
    def _(i):
        at = tile(i)
        hidden_ref[at, :] = x_ref[at, :].astype(F32) + dot(gated_ref[at, :], wo_ref[...])

    copies.receive(other_branch_ref, base, place.across)

    @pl.loop(0, rows // 128)
    def _(i):
        at = pl.ds(pl.multiple_of(i * 128, 128), 128)
        hidden = hidden_ref[at, :] + other_branch_ref[at, :].astype(F32)
        hidden_ref[at, :] = hidden
        nm_ref[at, :] = norm_rows(hidden).astype(BF)

    copies.send(nm_ref.at[own], nm_ref.at[other], base + 1, base + 1, place.across)
    copies.move(hidden_ref, hidden_out, later=True)
    for slot in (first, second, third):
        feed.complete(slot)
    copies.move(wf_ref, wf_out, later=True)
    copies.receive(nm_ref.at[other], base + 1, place.across)
    copies.move(nm_ref, nm_out, later=True)

    @pl.when(z < last)
    def _():
        @pl.loop(0, n_chain)
        def _(index):
            slot, seq, _ = chain_at(index)
            chain_copy(index, slot, seq).wait_send()

    copies.finish()


def forward(n_head, tokens, wq, wk, wv, wg, wo, ffn, rates):
    rows, width = tokens.shape
    units = ffn.shape[1] // 2
    tall = 2 * rows
    buffers = [
        ((n_head, width, 4 * HEAD_DIM), BF),
        ((n_head * HEAD_DIM, width), BF),
        ((3, n_head * units, width), BF),
        ((rows, width), BF),
        ((tall, width), BF),
        ((n_head, tall, 4 * HEAD_DIM), F32),
        ((n_head, tall, 2 * HEAD_DIM), BF),
        ((n_head, tall, 2 * HEAD_DIM), BF),
        ((n_head, tall, HEAD_DIM), BF),
        ((n_head, tall, HEAD_DIM), F32),
        ((n_head, rows, HEAD_DIM), F32),
        ((n_head, rows, HEAD_DIM), F32),
        ((n_head, tall // SPAN, 2 * HEAD_DIM, HEAD_DIM), F32),
        ((n_head, 2, 2 * HEAD_DIM, HEAD_DIM), BF),
        ((n_head, 2, 2 * HEAD_DIM, HEAD_DIM), BF),
        ((tall, HEAD_DIM), F32),
        ((tall, HEAD_DIM), F32),
        ((tall, n_head * HEAD_DIM), BF),
        ((rows, width), BF),
        ((rows, width), BF),
        ((rows, width), F32),
        ((tall, width), BF),
        ((n_head, 8, HEAD_DIM), F32),
    ]
    out_of = [0, 1, 2, 4, 5, 6, 7, 8, 9, 10, 11, 12, 13, 16, 17, 20, 21]
    n_sems = 3 * PER_GATHER + 4 + 1 + 2 * n_head + 2 + 2
    return pl.pallas_call(
        functools.partial(forward_kernel, n_head),
        out_shape=[jax.ShapeDtypeStruct(*buffers[i]) for i in out_of],
        in_specs=[ANY] * 7 + [IN_VMEM],
        out_specs=[ANY] * len(out_of),
        scratch_shapes=[pltpu.VMEM(*b) for b in buffers]
        + [
            pltpu.SemaphoreType.DMA((n_sems,)),
            pltpu.SemaphoreType.DMA((n_sems,)),
            pltpu.SemaphoreType.DMA((80,)),
        ],
        compiler_params=pltpu.CompilerParams(
            collective_id=0, has_side_effects=True, vmem_limit_bytes=62 << 20
        ),
        name="forward",
    )(tokens, wq, wk, wv, wg, wo, ffn, rates)


def make(n_dp, n_head):
    def swap(array, bit):
        return lax.ppermute(array, "dp", [(i, i ^ bit) for i in range(n_dp)])

    def from_above(array, step):
        return lax.ppermute(array, "head", [((i + step) % n_head, i) for i in range(n_head)])

    def to_above(array, step):
        return lax.ppermute(array, "head", [(i, (i + step) % n_head) for i in range(n_head)])

    def share(pieces, axis):
        half = pieces.shape[axis] // 2
        by_x = swap(pieces, 2)
        by_y = swap(pieces, 4)
        low = swap(lax.slice_in_dim(by_x, 0, half, axis=axis), 4)
        high = swap(lax.slice_in_dim(by_y, half, 2 * half, axis=axis), 2)
        return [pieces, by_x, by_y, jnp.concatenate([low, high], axis=axis)]

    def collect(parts, axis):
        own, for_x, for_y, for_far = parts
        half = own.shape[axis] // 2

        def cut(array, which):
            return lax.slice_in_dim(array, which * half, (which + 1) * half, axis=axis)

        def add(left, right):
            return (left.astype(F32) + right.astype(F32)).astype(BF)

        low = swap(cut(for_far, 0), 4)
        high = swap(cut(for_far, 1), 2)
        by_x = swap(jnp.concatenate([add(cut(for_x, 0), low), cut(for_x, 1)], axis=axis), 2)
        by_y = swap(jnp.concatenate([cut(for_y, 0), add(cut(for_y, 1), high)], axis=axis), 4)
        plane = (own.astype(F32) + by_x.astype(F32) + by_y.astype(F32)).astype(BF)
        total = plane[0].astype(F32)
        for step in range(1, n_head):
            total = total + to_above(plane[step], step).astype(F32)
        if n_dp > 8:
            groups = [[i + 8 * j for j in range(n_dp // 8)] for i in range(8)]
            total = lax.psum(total, "dp", axis_index_groups=groups)
        return total.astype(BF)

    def on_device(
        tokens,
        attn_query,
        attn_key,
        attn_value,
        attn_gate,
        attn_out,
        rotation_rates,
        ffn_left,
        ffn_right,
        ffn_down,
        out_grad,
    ):
        width = tokens.shape[1]
        quarter = width // 4
        rows = tokens.shape[0]
        spans = rows // SPAN
        units = ffn_left.shape[1] // 2
        dp = lax.axis_index("dp")
        place = lax.axis_index("head")
        core = dp & 1
        plane = (dp >> 1) & 3

        def relative(array, axis):
            return jnp.concatenate(
                [
                    lax.dynamic_slice_in_dim(array, (plane ^ q) * quarter, quarter, axis=axis)
                    for q in range(4)
                ],
                axis=axis,
            )

        def half_of(array, axis):
            size = array.shape[axis] // 2
            return lax.dynamic_slice_in_dim(array, core * size, size, axis=axis)

        ffn = jnp.stack([ffn_left.T, ffn_right.T, ffn_down])
        rates_in = jnp.pad(rotation_rates.reshape(2, HEAD_DIM), ((0, 6), (0, 0)))
        (
            attn_weights,
            out_w,
            ffn_all,
            gathered_in,
            pre,
            query,
            keys,
            values,
            attn,
            cosines,
            sines,
            fresh,
            carry,
            scale_attn,
            gated,
            hidden,
            gathered_mid,
        ) = forward(
            n_head,
            tokens,
            attn_query,
            attn_key,
            attn_value,
            attn_gate,
            attn_out,
            ffn,
            rates_in,
        )
        left_w, right_w, down_w = ffn_all[0], ffn_all[1], ffn_all[2]
        out_w = out_w.T

        inputs = relative(tokens, 1).astype(F32)
        normed_one, scale_one = norm_parts(inputs)
        out_grad = relative(out_grad, 1)
        grad_rows = jnp.concatenate([out_grad, swap(out_grad, 1)], axis=0)
        positions = (place * rows + jnp.arange(rows)).astype(F32)
        cosines, sines = cosines[:, None], sines[:, None]
        pre = pre.reshape(n_head, 2, rows, 4 * HEAD_DIM)
        query_pre, key_pre, value_pre, gate_pre = (
            pre[..., i * HEAD_DIM : (i + 1) * HEAD_DIM] for i in range(4)
        )

        def blocks(array):
            return array.reshape(n_head, 2, spans, SPAN, array.shape[-1])

        query, keys, values = blocks(query), blocks(keys), blocks(values)
        head_ids = 2 * ((place + jnp.arange(n_head)) % n_head) + core
        decay_rates = jnp.exp2(-8.0 * (head_ids.astype(F32) + 1.0) / HEADS)
        places = jnp.arange(SPAN, dtype=F32)
        offsets = places[:, None] - places[None, :]
        decay_mask = jnp.where(
            offsets[None] >= 0.0,
            jnp.exp(-decay_rates[:, None, None] * jnp.maximum(offsets[None], 0.0)),
            0.0,
        )[:, None, None]
        query_decay = jnp.exp(-decay_rates[:, None] * (places[None] + 1.0))[:, None, None, :, None]
        key_decay = jnp.exp(-decay_rates[:, None] * (SPAN - 1.0 - places[None]))[
            :, None, None, :, None
        ]
        span_decay = jnp.exp(-decay_rates * SPAN)[:, None, None, None]
        rows_decay = jnp.exp(-decay_rates * rows)[:, None, None, None]

        def ein(spec, left, right):
            return jnp.einsum(spec, left, right, preferred_element_type=F32)

        def exact(spec, left, right):
            left, right = left.astype(F32), right.astype(F32)
            return jnp.einsum(spec, left, right, precision=lax.Precision.HIGHEST)

        def roll(array, step):
            return jnp.roll(array, step, axis=0)

        scores = ein("hsnid,hsnjd->hsnij", query, keys)
        weights = (scores * decay_mask).astype(BF)
        fresh = fresh.reshape(n_head, 2, spans, 2 * HEAD_DIM, HEAD_DIM)
        state = carry.astype(F32)
        states = []
        for n in range(spans):
            states.append(state)
            state = span_decay * state + fresh[:, :, n]
        states = jnp.stack(states, axis=2)
        attn = attn.reshape(n_head, 2, rows, HEAD_DIM)
        scale_attn = scale_attn[:, :1].reshape(1, 2, rows, 1)
        attn_normed = attn * scale_attn

        def core_sum(array):
            return array + swap(array[::-1], 1)

        def core_scatter(array):
            return array[:rows] + swap(array[rows:].astype(BF), 1).astype(F32)

        normed_two, scale_two = norm_parts(hidden)
        left = second_dot(gathered_mid, left_w)
        right = second_dot(gathered_mid, right_w)
        product = (left * right).astype(BF)
        down_grad = first_dot(product, grad_rows).astype(BF)
        grad_product = second_dot(grad_rows, down_w)
        grad_left = (grad_product * right).astype(BF)
        grad_right = (grad_product * left).astype(BF)
        left_grad = first_dot(grad_left, gathered_mid).astype(BF)
        right_grad = first_dot(grad_right, gathered_mid).astype(BF)
        grad_mid = core_scatter(plain_dot(grad_left, left_w) + plain_dot(grad_right, right_w))
        grad_hidden = out_grad.astype(F32) + norm_back(normed_two, scale_two, grad_mid)

        def ffn_total(grad):
            grad = grad.reshape(n_head, units, width)
            piece = collect([grad[:, :, q * quarter : (q + 1) * quarter] for q in range(4)], 1)
            return jnp.concatenate(share(piece, 0), axis=1)

        down_grad, left_grad, right_grad = (ffn_total(g) for g in (down_grad, left_grad, right_grad))
        block_out = (hidden + core_scatter(plain_dot(product, down_w))).astype(BF)

        branch_low = grad_hidden.astype(BF)
        branch_rows = jnp.concatenate([branch_low, swap(branch_low, 1)], axis=0)
        out_grads = first_dot(branch_rows, gated)
        grad_gated = plain_dot(branch_rows, out_w)
        grad_gated = grad_gated.reshape(2, rows, n_head, HEAD_DIM).transpose(2, 0, 1, 3)
        grad_normed = grad_gated * gate_pre
        grad_gate_pre = (grad_gated * attn_normed).astype(BF)
        products = core_sum(jnp.sum(grad_normed * attn_normed, axis=(0, 3)))[None, :, :, None]
        grad_attn = (scale_attn * (grad_normed - attn_normed * (products / width))).astype(BF)
        grad_blocks = blocks(grad_attn)
        grad_scores = (ein("hsnie,hsnje->hsnij", grad_blocks, values) * decay_mask).astype(BF)
        grad_values = ein("hsnij,hsnie->hsnje", weights, grad_blocks)
        grad_query = ein("hsnij,hsnjd->hsnid", grad_scores, keys)
        grad_keys = ein("hsnij,hsnid->hsnjd", grad_scores, query)
        grad_query = grad_query + query_decay * exact("hsnie,hsnde->hsnid", grad_blocks, states)
        grad_early = grad_blocks.astype(F32) * query_decay
        grad_states = exact("hsnid,hsnie->hsnde", query, grad_early)
        local_pending = jnp.zeros(grad_states.shape[:2] + grad_states.shape[3:], F32)
        for n in reversed(range(spans)):
            local_pending = span_decay * local_pending + grad_states[:, :, n]
        pending = jnp.zeros_like(local_pending)
        for hop in range(n_head - 1):
            message = roll((local_pending + rows_decay * pending).astype(BF), 1)
            pending = lax.ppermute(message, "head", [(i + 1, i) for i in range(n_head - 1)]).astype(
                F32
            )
        later = []
        for n in reversed(range(spans)):
            later.insert(0, pending)
            pending = span_decay * pending + grad_states[:, :, n]
        later = jnp.stack(later, axis=2)
        grad_keys = grad_keys + key_decay * exact("hsnje,hsnde->hsnjd", values, later)
        grad_values = grad_values + key_decay * exact("hsnjd,hsnde->hsnje", keys, later)

        def unrotate(grad_rotated, pre_values):
            shaped = grad_rotated.reshape(n_head, 2, rows, 2 * HEAD_DIM)
            grad_cos = shaped[..., :HEAD_DIM]
            grad_sin = shaped[..., HEAD_DIM:]
            grad_act = grad_cos * cosines + grad_sin * sines
            sigmoid_pre = jax.nn.sigmoid(pre_values)
            activated = pre_values * sigmoid_pre
            grad_angle = activated * (grad_sin * cosines - grad_cos * sines)
            grad_pre = grad_act * sigmoid_pre * (1.0 + pre_values * (1.0 - sigmoid_pre))
            return (grad_pre.astype(BF), grad_angle)

        grad_query_pre, angle_query = unrotate(grad_query, query_pre)
        grad_key_pre, angle_key = unrotate(grad_keys, key_pre)
        grad_value_pre = grad_values.reshape(n_head, 2, rows, HEAD_DIM).astype(BF)
        rates_grad = jnp.sum(
            positions[None, None, :, None] * (angle_query + angle_key), axis=(1, 2)
        )
        grad_pre = jnp.concatenate(
            [grad_query_pre, grad_key_pre, grad_value_pre, grad_gate_pre], axis=-1
        ).reshape(n_head, 2 * rows, 4 * HEAD_DIM)
        attn_grads = []
        grad_in = None
        for r in range(n_head):
            main = first_dot(gathered_in, grad_pre[r]).astype(BF)
            outs = out_grads[:, r * HEAD_DIM : (r + 1) * HEAD_DIM].astype(BF)
            attn_grads.append(jnp.concatenate([main, outs], axis=1))
            term = second_dot(grad_pre[r], attn_weights[r])
            grad_in = term if grad_in is None else grad_in + term
        grad_in = core_scatter(grad_in)
        input_grad = grad_hidden + norm_back(normed_one, scale_one, grad_in)

        attn_grads = jnp.stack(attn_grads).reshape(n_head, 4, quarter, 5 * HEAD_DIM)
        piece = collect([attn_grads[:, q] for q in range(4)], 1)
        attn_total = jnp.concatenate(share(piece, 0), axis=0)
        rates_piece = rates_grad[0]
        for step in range(1, n_head):
            rates_piece = rates_piece + to_above(rates_grad[step], step)
        groups = [list(range(0, n_dp, 2)), list(range(1, n_dp, 2))]
        rates_piece = lax.psum(rates_piece, "dp", axis_index_groups=groups)

        def both(array, axis):
            other = swap(array, 1)
            first = jnp.where(core == 0, array, other)
            second = jnp.where(core == 0, other, array)
            return first, second

        first, second = both(relative(attn_total, 0), 0)
        matrices = []
        for i in range(5):
            pair = [part[:, i * HEAD_DIM : (i + 1) * HEAD_DIM] for part in (first, second)]
            matrices.append(jnp.concatenate(pair, axis=1).astype(F32))
        query_grad, key_grad, value_grad, gate_grad, out_proj_grad = matrices
        out_proj_grad = out_proj_grad.T
        rates_grad = jnp.concatenate(both(rates_piece, 0), axis=0)
        ffn_grads = jnp.stack([relative(g, 1) for g in (left_grad, right_grad, down_grad)])
        ffn_grads = jnp.concatenate(both(ffn_grads, 1), axis=1).astype(F32)
        return (
            relative(block_out, 1),
            relative(input_grad, 1),
            query_grad,
            key_grad,
            value_grad,
            gate_grad,
            out_proj_grad,
            rates_grad,
            ffn_grads[0].T,
            ffn_grads[1].T,
            ffn_grads[2],
        )

    return on_device


def solution(mesh):
    weights = (P(None, "head"),) * 4 + (P("head", None), P("head")) + (P(None, "head"),) * 2
    weights = weights + (P("head", None),)
    rows = P(("dp", "head"), None)
    return jax.shard_map(
        make(mesh.shape["dp"], mesh.shape["head"]),
        mesh=mesh,
        in_specs=(rows,) + weights + (rows,),
        out_specs=(rows, rows) + weights,
        check_vma=False,
    )
```

```python
import functools

import jax
import jax.numpy as jnp
from jax import lax
from jax.experimental import pallas as pl
from jax.experimental.pallas import tpu as pltpu
from jax.sharding import PartitionSpec as P

HEADS = 8
HEAD_DIM = 128
SPAN = 256
EPSILON = 1e-06
BF = jnp.bfloat16
F32 = jnp.float32


def norm_parts(values):
    scale = lax.rsqrt(jnp.mean(values * values, axis=-1, keepdims=True) + EPSILON)
    return (values * scale, scale)


def norm_back(normed, scale, grad):
    return scale * (grad - normed * jnp.mean(grad * normed, axis=-1, keepdims=True))


def plain_dot(left, right):
    return jnp.dot(left, right, preferred_element_type=F32)


def first_dot(left, right):
    return lax.dot_general(left, right, (((0,), (0,)), ((), ())), preferred_element_type=F32)


def second_dot(left, right):
    return lax.dot_general(left, right, (((1,), (1,)), ((), ())), preferred_element_type=F32)


MESH = pl.DeviceIdType.MESH
ANY = pl.BlockSpec(memory_space=pl.ANY)
IN_VMEM = pl.BlockSpec(memory_space=pltpu.VMEM)


def split(value):
    high = value.astype(BF)
    return high, (value - high.astype(F32)).astype(BF)


class Place:
    def __init__(self, n_head):
        self.n_head = n_head
        dp = lax.axis_index("dp")
        self.z = lax.axis_index("head")
        self.core = lax.rem(dp, 2)
        x = lax.rem(lax.div(dp, 2), 2)
        y = lax.rem(lax.div(dp, 4), 2)
        self.plane = x + 2 * y
        self.at = [self.plane, self.plane + 1 - 2 * x, self.plane + 2 - 4 * y, 3 - self.plane]
        self.across = {"dp": dp + 1 - 2 * self.core}
        self.by_x = {"dp": dp + 2 - 4 * x}
        self.by_y = {"dp": dp + 4 - 8 * y}
        self.up = {"head": lax.rem(self.z + 1, n_head)}
        self.down = {"head": lax.rem(self.z + n_head - 1, n_head)}

    def above(self, step):
        return {"head": lax.rem(self.z + step, self.n_head)}

    def below(self, step):
        return {"head": lax.rem(self.z + self.n_head - step, self.n_head)}

    def greet(self):
        barrier = pltpu.get_barrier_semaphore()
        others = [self.across, self.by_x, self.by_y]
        others += [self.below(step) for step in range(1, self.n_head)]
        for other in others:
            pl.semaphore_signal(barrier, inc=1, device_id=other, device_id_type=MESH)
        pl.semaphore_wait(barrier, len(others))


class Copies:
    def __init__(self, sends, receives, locals_):
        self.sends, self.receives, self.locals = sends, receives, locals_
        self.pending = []
        self.started = {}
        self.n_local = 0

    def send(self, src, dst, out, into, device, when=None):
        copy = pltpu.make_async_remote_copy(
            src_ref=src,
            dst_ref=dst,
            send_sem=self.sends.at[out],
            recv_sem=self.receives.at[into],
            device_id=device,
            device_id_type=MESH,
        )
        if when is None:
            copy.start()
            self.pending.append(copy.wait_send)
            if isinstance(out, int):
                self.started[out] = copy.wait_send
        else:
            pl.when(when)(copy.start)
            self.pending.append(lambda: pl.when(when)(copy.wait_send))

    def receive(self, dst, into, device):
        pltpu.make_async_remote_copy(
            src_ref=dst,
            dst_ref=dst,
            send_sem=self.sends.at[0],
            recv_sem=self.receives.at[into],
            device_id=device,
            device_id_type=MESH,
        ).wait_recv()

    def move(self, src, dst, later=False):
        copy = pltpu.make_async_copy(src, dst, self.locals.at[self.n_local])
        self.n_local += 1
        copy.start()
        if later:
            self.pending.append(copy.wait)
        return copy

    def sent(self, out):
        wait = self.started.pop(out)
        self.pending.remove(wait)
        wait()

    def finish(self):
        for wait in self.pending:
            wait()


class Gather:
    def __init__(self, place, copies, view, base):
        self.place, self.copies, self.view, self.base = place, copies, view, base

    def begin(self):
        place, z = self.place, self.place.z
        own = self.view(0, 0, None)
        last = place.n_head - 1
        self.copies.send(
            own, self.view(last, 0, None), self.base, self.base + last, place.up, when=z < last
        )
        self.copies.send(own, self.view(1, 0, None), self.base + 1, self.base + 1, place.down, when=z > 0)

    def arrived(self, slot):
        place, copies, z, base = self.place, self.copies, self.place.z, self.base
        last = place.n_head - 1
        copies.receive(self.view(slot, 0, None), base + slot, place.up)
        from_up = z + slot <= last
        piece = self.view(slot, 0, None)
        down = jnp.logical_and(from_up, z > 0)
        up = jnp.logical_and(jnp.logical_not(from_up), z < last)
        after = jnp.minimum(slot + 1, last)
        before = jnp.maximum(slot - 1, 1)
        copies.send(piece, self.view(after, 0, None), base + 1 + slot, base + after, place.down, when=down)
        copies.send(piece, self.view(before, 0, None), base + 1 + slot, base + before, place.up, when=up)
        at = base + 4 * slot + 4
        copies.send(piece, self.view(slot, 1, None), at, at, place.by_x)
        copies.send(piece, self.view(slot, 2, None), at + 1, at + 1, place.by_y)

    def spread(self, slot):
        place, copies = self.place, self.copies
        at = self.base + 4 * slot + 4
        copies.receive(self.view(slot, 1, None), at, place.by_x)
        copies.send(self.view(slot, 1, 0), self.view(slot, 3, 0), at + 2, at + 2, place.by_y)
        copies.receive(self.view(slot, 2, None), at + 1, place.by_y)
        copies.send(self.view(slot, 2, 1), self.view(slot, 3, 1), at + 3, at + 3, place.by_x)

    def complete(self, slot):
        place, copies = self.place, self.copies
        at = self.base + 4 * slot + 4
        copies.receive(self.view(slot, 3, 0), at + 2, place.by_y)
        copies.receive(self.view(slot, 3, 1), at + 3, place.by_x)


PER_GATHER = 24


def forward_kernel(
    n_head,
    tokens,
    out_grad,
    wq,
    wk,
    wv,
    wg,
    wo,
    ffn,
    rates,
    wa_out,
    wo_out,
    wf_out,
    nin_out,
    pre_out,
    q_out,
    k_out,
    v_out,
    attn_out,
    cos_out,
    sin_out,
    fresh_out,
    carry_out,
    scale_out,
    gated_out,
    hidden_out,
    nm_out,
    og_out,
    wa_ref,
    wo_ref,
    wf_ref,
    x_ref,
    nin_ref,
    pre_ref,
    q_ref,
    k_ref,
    v_ref,
    attn_ref,
    cos_ref,
    sin_ref,
    fresh_ref,
    carry_ref,
    message_ref,
    squares_ref,
    other_squares_ref,
    gated_ref,
    branch_ref,
    other_branch_ref,
    hidden_ref,
    nm_ref,
    rates_ref,
    og_ref,
    sends,
    receives,
    locals_,
):
    rows, width = tokens.shape
    quarter = width // 4
    units = ffn.shape[1] // 2
    tiles = 2 * rows // SPAN
    place = Place(n_head)
    z, core = place.z, place.core
    copies = Copies(sends, receives, locals_)

    def columns(start, size):
        return pl.ds(pl.multiple_of(start, size), size)

    own_loads = []
    for q in range(4):
        far = columns(place.at[q] * quarter, quarter)
        near = pl.ds(q * quarter, quarter)
        loads = []
        for i, w in enumerate((wq, wk, wv, wg)):
            src = w.at[far, columns(core * HEAD_DIM, HEAD_DIM)]
            loads.append(copies.move(src, wa_ref.at[0, near, pl.ds(i * HEAD_DIM, HEAD_DIM)]))
        src = wo.at[columns(core * HEAD_DIM, HEAD_DIM), far]
        loads.append(copies.move(src, wo_ref.at[pl.ds(0, HEAD_DIM), near]))
        src = ffn.at[:, pl.ds(pl.multiple_of(core * units, 16), units), far]
        loads.append(copies.move(src, wf_ref.at[:, pl.ds(0, units), near]))
        own_loads.append(loads)
    token_loads = [
        copies.move(
            tokens.at[:, columns(place.at[q] * quarter, quarter)],
            x_ref.at[:, pl.ds(q * quarter, quarter)],
        )
        for q in range(4)
    ]
    grad_loads = [
        copies.move(
            out_grad.at[:, columns(place.at[q] * quarter, quarter)],
            og_ref.at[pl.ds(0, rows), pl.ds(q * quarter, quarter)],
        )
        for q in range(4)
    ]
    place.greet()

    def half_rows(half, size):
        return pl.ds(0, size) if half is None else pl.ds(half * (size // 2), size // 2)

    def wa_view(slot, q, half):
        at = half_rows(half, quarter)
        return wa_ref.at[slot, pl.ds(q * quarter + at.start, at.size), :]

    def wo_view(slot, q, half):
        at = half_rows(half, HEAD_DIM)
        return wo_ref.at[
            pl.ds(pl.multiple_of(slot * HEAD_DIM + at.start, HEAD_DIM // 2), at.size),
            pl.ds(q * quarter, quarter),
        ]

    def wf_view(slot, q, half):
        at = half_rows(half, units)
        return wf_ref.at[
            :,
            pl.ds(pl.multiple_of(slot * units + at.start, 16), at.size),
            pl.ds(q * quarter, quarter),
        ]

    attn_in = Gather(place, copies, wa_view, 0)
    attn_down = Gather(place, copies, wo_view, PER_GATHER)
    feed = Gather(place, copies, wf_view, 2 * PER_GATHER)
    base = 3 * PER_GATHER
    for load in own_loads[0][:4]:
        load.wait()
    attn_in.begin()
    own_loads[0][4].wait()
    attn_down.begin()
    for step in range(1, n_head):
        copies.send(rates, rates_ref.at[step], base + step, base + step, place.below(step))
    rates_ref[0] = rates[...]

    for load in token_loads:
        load.wait()

    def norm_rows(values):
        mean = jnp.mean(values * values, axis=-1, keepdims=True)
        return values * lax.rsqrt(mean + EPSILON)

    @pl.loop(0, rows // 128)
    def _(i):
        at = pl.ds(pl.multiple_of(i * 128, 128), 128)
        nin_ref[at, :] = norm_rows(x_ref[at, :].astype(F32)).astype(BF)

    base += 4
    for load in grad_loads:
        load.wait()
    og_other = og_ref.at[pl.ds(rows, rows)]
    copies.send(og_ref.at[pl.ds(0, rows)], og_other, base, base, place.across)
    base += 1
    nin_other = nin_ref.at[pl.ds(rows, rows)]
    copies.send(nin_ref.at[pl.ds(0, rows)], nin_other, base, base, place.across)
    own_loads[0][5].wait()
    feed.begin()
    for loads in own_loads[1:]:
        for load in loads:
            load.wait()
    for step in range(1, n_head):
        copies.receive(rates_ref.at[step], base - 5 + step, place.up)
    copies.receive(nin_other, base, place.across)
    copies.move(nin_ref, nin_out, later=True)
    copies.receive(og_other, base - 1, place.across)
    copies.move(og_ref, og_out, later=True)

    def decay_of(head):
        exponent = jnp.full((1, 1), -8.0 / HEADS, F32) * (head + 1).astype(F32)
        return jnp.exp2(exponent)

    def tile(i):
        return pl.ds(pl.multiple_of(i * SPAN, SPAN), SPAN)

    def iota(shape, axis):
        return lax.broadcasted_iota(jnp.int32, shape, axis).astype(F32)

    def dot(left, right):
        return jnp.dot(left, right, preferred_element_type=F32)

    def slot_compute(slot):
        head = 2 * lax.rem(z + slot, n_head) + core
        decay = decay_of(head)
        rate = rates_ref[slot, pl.ds(core, 1), :]
        coarse = (z * rows).astype(F32) + 32.0 * iota((rows // 32, HEAD_DIM), 0)
        coarse = coarse * rate
        fine = iota((32, HEAD_DIM), 0) * rate
        cos_a, sin_a = jnp.cos(coarse), jnp.sin(coarse)
        cos_b, sin_b = jnp.cos(fine), jnp.sin(fine)
        for a in range(rows // 32):
            cos_row, sin_row = cos_a[a : a + 1], sin_a[a : a + 1]
            cos_ref[slot, pl.ds(a * 32, 32), :] = cos_row * cos_b - sin_row * sin_b
            sin_ref[slot, pl.ds(a * 32, 32), :] = sin_row * cos_b + cos_row * sin_b
        offsets = iota((SPAN, SPAN), 0) - iota((SPAN, SPAN), 1)
        mask = jnp.where(offsets >= 0.0, jnp.exp(-decay * jnp.maximum(offsets, 0.0)), 0.0)
        late = jnp.exp(-decay * (SPAN - 1.0 - iota((SPAN, HEAD_DIM), 0)))

        @pl.loop(0, tiles)
        def _(i):
            at = tile(i)
            pre = dot(nin_ref[at, :], wa_ref[slot])
            pre_ref[slot, at, :] = pre
            here = tile(lax.rem(i, rows // SPAN))
            cosines, sines = cos_ref[slot, here, :], sin_ref[slot, here, :]

            def rotate(values):
                activated = values / (1.0 + jnp.exp(-values))
                turned = jnp.concatenate([activated * cosines, activated * sines], axis=1)
                return turned.astype(BF)

            query = rotate(pre[:, :HEAD_DIM])
            keys = rotate(pre[:, HEAD_DIM : 2 * HEAD_DIM])
            value = pre[:, 2 * HEAD_DIM : 3 * HEAD_DIM].astype(BF)
            q_ref[slot, at, :] = query
            k_ref[slot, at, :] = keys
            v_ref[slot, at, :] = value
            scores = lax.dot_general(
                query, keys, (((1,), (1,)), ((), ())), preferred_element_type=F32
            )
            weights = (scores * mask).astype(BF)
            attn_ref[slot, at, :] = dot(weights, value)
            high, low = split(value.astype(F32) * late)
            both = lax.dot_general(
                keys,
                jnp.concatenate([high, low], axis=1),
                (((0,), (0,)), ((), ())),
                preferred_element_type=F32,
            )
            fresh_ref[slot, i] = both[:, :HEAD_DIM] + both[:, HEAD_DIM:]

        for ref, out in (
            (wa_ref, wa_out),
            (pre_ref, pre_out),
            (q_ref, q_out),
            (k_ref, k_out),
            (v_ref, v_out),
            (cos_ref, cos_out),
            (sin_ref, sin_out),
            (fresh_ref, fresh_out),
        ):
            copies.move(ref.at[slot], out.at[slot], later=True)

    last = n_head - 1
    first = 1 + 2 * lax.div(z, last)
    second = 2 + lax.rem(lax.div(z + 1, 2), 2)
    third = 6 - first - second

    attn_in.arrived(first)
    attn_down.arrived(first)
    slot_compute(0)
    attn_in.arrived(second)
    attn_down.arrived(second)
    attn_in.spread(first)
    attn_down.spread(first)
    attn_in.arrived(third)
    attn_down.arrived(third)
    attn_in.spread(second)
    attn_down.spread(second)
    attn_in.complete(first)
    slot_compute(first)
    feed.arrived(first)
    attn_in.spread(third)
    attn_down.spread(third)
    attn_in.complete(second)
    slot_compute(second)
    feed.arrived(second)
    feed.spread(first)
    attn_in.complete(third)
    slot_compute(third)
    feed.arrived(third)
    feed.spread(second)

    base += 1
    chain_base = base
    n_chain = 2 * n_head

    def chain_at(index):
        group, seq = lax.div(index, 2), lax.rem(index, 2)
        return lax.rem(group - z + n_head, n_head), seq, decay_of(2 * group + core)

    def chain_copy(index, slot, seq):
        after = lax.rem(slot + n_head - 1, n_head)
        return pltpu.make_async_remote_copy(
            src_ref=message_ref.at[slot, seq],
            dst_ref=carry_ref.at[after, seq],
            send_sem=sends.at[chain_base + index],
            recv_sem=receives.at[chain_base + index],
            device_id=place.up,
            device_id_type=MESH,
        )

    @pl.loop(0, n_chain)
    def _(index):
        slot, seq, decay = chain_at(index)

        @pl.when(z > 0)
        def _():
            copies.receive(carry_ref.at[slot, seq], chain_base + index, place.down)

        @pl.when(z == 0)
        def _():
            carry_ref[slot, seq] = jnp.zeros(carry_ref.shape[2:], BF)

        @pl.when(z < last)
        def _():
            total = jnp.exp(-decay * rows) * carry_ref[slot, seq].astype(F32)
            for n in range(rows // SPAN):
                left = rows - (n + 1) * SPAN
                total += jnp.exp(-decay * left) * fresh_ref[slot, seq * (rows // SPAN) + n]
            message_ref[slot, seq] = total.astype(BF)
            chain_copy(index, slot, seq).start()

    copies.move(carry_ref, carry_out, later=True)

    squares_ref[...] = jnp.zeros_like(squares_ref)

    @pl.loop(0, n_head)
    def _(slot):
        decay = decay_of(2 * lax.rem(z + slot, n_head) + core)
        early = jnp.exp(-decay * (iota((SPAN, HEAD_DIM), 0) + 1.0))

        @pl.loop(0, 2)
        def _(seq):
            state = carry_ref[slot, seq].astype(F32)
            for n in range(rows // SPAN):
                i = seq * (rows // SPAN) + n
                at = tile(i)
                both = dot(q_ref[slot, at, :], jnp.concatenate(split(state), axis=1))
                attn = attn_ref[slot, at, :]
                attn += early * (both[:, :HEAD_DIM] + both[:, HEAD_DIM:])
                attn_ref[slot, at, :] = attn
                squares_ref[at, :] += jnp.sum(attn * attn, axis=-1, keepdims=True)
                if n + 1 < rows // SPAN:
                    state = jnp.exp(-decay * SPAN) * state + fresh_ref[slot, i]

    copies.move(attn_ref, attn_out, later=True)
    base += n_chain
    own, other = pl.ds(0, rows), pl.ds(rows, rows)
    copies.send(squares_ref.at[own], other_squares_ref.at[other], base, base, place.across)
    copies.send(squares_ref.at[other], other_squares_ref.at[own], base + 1, base + 1, place.across)
    feed.spread(third)
    for slot in (first, second, third):
        attn_down.complete(slot)
    copies.receive(other_squares_ref.at[other], base, place.across)
    copies.receive(other_squares_ref.at[own], base + 1, place.across)

    @pl.loop(0, tiles)
    def _(i):
        at = tile(i)
        total = squares_ref[at, :] + other_squares_ref[at, :]
        scale = lax.rsqrt(total / width + EPSILON)
        other_squares_ref[at, :] = scale
        for slot in range(n_head):
            gate = pre_ref[slot, at, pl.ds(3 * HEAD_DIM, HEAD_DIM)]
            gated = (attn_ref[slot, at, :] * scale * gate).astype(BF)
            gated_ref[at, pl.ds(slot * HEAD_DIM, HEAD_DIM)] = gated

    copies.move(other_squares_ref, scale_out, later=True)
    copies.move(gated_ref, gated_out, later=True)
    copies.move(wo_ref, wo_out, later=True)
    base += 2

    @pl.loop(0, rows // SPAN)
    def _(i):
        gated = gated_ref[pl.ds(pl.multiple_of(rows + i * SPAN, SPAN), SPAN), :]
        branch_ref[tile(i), :] = dot(gated, wo_ref[...]).astype(BF)

    copies.send(branch_ref, other_branch_ref, base, base, place.across)

    @pl.loop(0, rows // SPAN)
    def _(i):
        at = tile(i)
        hidden_ref[at, :] = x_ref[at, :].astype(F32) + dot(gated_ref[at, :], wo_ref[...])

    copies.receive(other_branch_ref, base, place.across)

    @pl.loop(0, rows // 128)
    def _(i):
        at = pl.ds(pl.multiple_of(i * 128, 128), 128)
        hidden = hidden_ref[at, :] + other_branch_ref[at, :].astype(F32)
        hidden_ref[at, :] = hidden
        nm_ref[at, :] = norm_rows(hidden).astype(BF)

    copies.send(nm_ref.at[own], nm_ref.at[other], base + 1, base + 1, place.across)
    copies.move(hidden_ref, hidden_out, later=True)
    for slot in (first, second, third):
        feed.complete(slot)
    copies.move(wf_ref, wf_out, later=True)
    copies.receive(nm_ref.at[other], base + 1, place.across)
    copies.move(nm_ref, nm_out, later=True)

    @pl.when(z < last)
    def _():
        @pl.loop(0, n_chain)
        def _(index):
            slot, seq, _ = chain_at(index)
            chain_copy(index, slot, seq).wait_send()

    copies.finish()


def forward(n_head, tokens, out_grad, wq, wk, wv, wg, wo, ffn, rates):
    rows, width = tokens.shape
    units = ffn.shape[1] // 2
    tall = 2 * rows
    buffers = [
        ((n_head, width, 4 * HEAD_DIM), BF),
        ((n_head * HEAD_DIM, width), BF),
        ((3, n_head * units, width), BF),
        ((rows, width), BF),
        ((tall, width), BF),
        ((n_head, tall, 4 * HEAD_DIM), F32),
        ((n_head, tall, 2 * HEAD_DIM), BF),
        ((n_head, tall, 2 * HEAD_DIM), BF),
        ((n_head, tall, HEAD_DIM), BF),
        ((n_head, tall, HEAD_DIM), F32),
        ((n_head, rows, HEAD_DIM), F32),
        ((n_head, rows, HEAD_DIM), F32),
        ((n_head, tall // SPAN, 2 * HEAD_DIM, HEAD_DIM), F32),
        ((n_head, 2, 2 * HEAD_DIM, HEAD_DIM), BF),
        ((n_head, 2, 2 * HEAD_DIM, HEAD_DIM), BF),
        ((tall, HEAD_DIM), F32),
        ((tall, HEAD_DIM), F32),
        ((tall, n_head * HEAD_DIM), BF),
        ((rows, width), BF),
        ((rows, width), BF),
        ((rows, width), F32),
        ((tall, width), BF),
        ((n_head, 8, HEAD_DIM), F32),
        ((tall, width), BF),
    ]
    out_of = [0, 1, 2, 4, 5, 6, 7, 8, 9, 10, 11, 12, 13, 16, 17, 20, 21, 23]
    n_sems = 3 * PER_GATHER + 4 + 1 + 1 + 2 * n_head + 2 + 2
    return pl.pallas_call(
        functools.partial(forward_kernel, n_head),
        out_shape=[jax.ShapeDtypeStruct(*buffers[i]) for i in out_of],
        in_specs=[ANY] * 8 + [IN_VMEM],
        out_specs=[ANY] * len(out_of),
        scratch_shapes=[pltpu.VMEM(*b) for b in buffers]
        + [
            pltpu.SemaphoreType.DMA((n_sems,)),
            pltpu.SemaphoreType.DMA((n_sems,)),
            pltpu.SemaphoreType.DMA((80,)),
        ],
        compiler_params=pltpu.CompilerParams(
            collective_id=0, has_side_effects=True, vmem_limit_bytes=62 << 20
        ),
        name="forward",
    )(tokens, out_grad, wq, wk, wv, wg, wo, ffn, rates)


class Scatter:
    def __init__(self, place, copies, view, far_x, far_y, near_x, near_y, high, base):
        self.place, self.copies, self.view, self.base = place, copies, view, base
        self.far_x, self.far_y, self.near_x, self.near_y, self.high = far_x, far_y, near_x, near_y, high

    def begin(self, slot):
        place, at = self.place, self.base + 4 * slot
        self.copies.send(self.view(slot, 3, 0), self.far_y.at[slot], at, at, place.by_y)
        self.copies.send(self.view(slot, 3, 1), self.far_x.at[slot], at + 1, at + 1, place.by_x)

    def middle(self, slot):
        place, copies, at = self.place, self.copies, self.base + 4 * slot
        copies.receive(self.far_y.at[slot], at, place.by_y)
        add_to(self.view(slot, 1, 0), self.far_y.at[slot])
        copies.send(self.view(slot, 1, None), self.near_x.at[slot], at + 2, at + 2, place.by_x)
        copies.receive(self.far_x.at[slot], at + 1, place.by_x)
        add_to(self.view(slot, 2, 1), self.far_x.at[slot])
        copies.send(self.view(slot, 2, None), self.near_y.at[slot], at + 3, at + 3, place.by_y)

    def end(self, slot):
        place, copies, at = self.place, self.copies, self.base + 4 * slot
        copies.receive(self.near_x.at[slot], at + 2, place.by_x)
        copies.receive(self.near_y.at[slot], at + 3, place.by_y)
        add_to(self.view(slot, 0, None), self.near_x.at[slot], self.near_y.at[slot])
        if slot:
            at = self.base + 4 * place.n_head + slot
            into = self.high.at[slot - 1]
            copies.send(self.view(slot, 0, None), into, at, at, place.above(slot))

    def total(self):
        place = self.place
        high = [self.high.at[slot - 1] for slot in range(1, place.n_head)]
        for slot, part in enumerate(high, 1):
            self.copies.receive(part, self.base + 4 * place.n_head + slot, place.up)
        add_to(self.view(0, 0, None), *high)


PER_SCATTER = 20


def add_to(ref, *others):
    def add(*refs):
        total = refs[0][...].astype(F32)
        for other in refs[1:]:
            total += other[...].astype(F32)
        refs[0][...] = total.astype(BF)

    if len(ref.shape) == 2:
        add(ref, *others)
    else:
        for i in range(ref.shape[0]):
            add(ref.at[i], *(other.at[i] for other in others))


def dot(left, right):
    return jnp.dot(left, right, preferred_element_type=F32)


def iota(shape, axis):
    return lax.broadcasted_iota(jnp.int32, shape, axis).astype(F32)


def decay_of(head):
    exponent = jnp.full((1, 1), -8.0 / HEADS, F32) * (head + 1).astype(F32)
    return jnp.exp2(exponent)


def middle_kernel(
    n_head,
    wf,
    nm,
    og,
    hidden,
    wo,
    pre,
    query,
    keys,
    values,
    attn,
    cosines,
    sines,
    fresh,
    carry,
    scale,
    feed_out,
    block_out,
    hidden_grad_out,
    branch_out,
    pre_out,
    rates_out,
    wf_ref,
    t_ref,
    g_ref,
    far_x,
    far_y,
    near_x,
    near_y,
    high,
    nm_ref,
    og_ref,
    hidden_ref,
    mid_ref,
    send_ref,
    got_ref,
    block_ref,
    wo_ref,
    gate_ref,
    attn_ref,
    ga_ref,
    qk_pre_ref,
    cos_ref,
    sin_ref,
    fresh_ref,
    carry_ref,
    late_ref,
    pending_ref,
    message_ref,
    scale_ref,
    sum_ref,
    other_sum_ref,
    rates_ref,
    sends,
    receives,
    locals_,
):
    rows, width = hidden.shape
    quarter = width // 4
    units = wf.shape[1] // n_head
    spans = rows // SPAN
    tiles = 2 * spans
    last = n_head - 1
    place = Place(n_head)
    z, core = place.z, place.core
    copies = Copies(sends, receives, locals_)
    own, other = pl.ds(0, rows), pl.ds(rows, rows)

    order = (2, 1, 3, 0)
    load_nm = copies.move(nm, nm_ref)
    load_og = copies.move(og, og_ref)
    load_wf = {}
    for slot in order:
        at = pl.ds(slot * units, units)
        load_wf[slot] = copies.move(wf.at[:, at, :], wf_ref.at[:, at, :])
    early_loads = [
        copies.move(hidden, hidden_ref),
        copies.move(wo, wo_ref),
        copies.move(scale, scale_ref),
        copies.move(attn, attn_ref),
        copies.move(pre.at[:, :, pl.ds(3 * HEAD_DIM, HEAD_DIM)], gate_ref),
        copies.move(carry, carry_ref),
    ]
    for seq in range(2):
        for slot in range(n_head):
            early_loads.append(copies.move(fresh.at[slot, seq * spans], fresh_ref.at[slot, seq]))
    place.greet()

    def tile(i):
        return pl.ds(pl.multiple_of(i * SPAN, SPAN), SPAN)

    def dot_last(left, right):
        return lax.dot_general(left, right, (((1,), (1,)), ((), ())), preferred_element_type=F32)

    def dot_first(left, right):
        return lax.dot_general(left, right, (((0,), (0,)), ((), ())), preferred_element_type=F32)

    def g_view(slot, q, half):
        size = units if half is None else units // 2
        start = slot * units + (half or 0) * size
        return g_ref.at[:, pl.ds(start, size), pl.ds(q * quarter, quarter)]

    feed = Scatter(place, copies, g_view, far_x, far_y, near_x, near_y, high, 0)
    base = PER_SCATTER

    def feed_slot(slot):
        at = pl.ds(slot * units, units)

        @pl.loop(0, tiles)
        def _(i):
            rows_at = tile(i)
            left = dot_last(wf_ref[0, at, :], nm_ref[rows_at, :])
            right = dot_last(wf_ref[1, at, :], nm_ref[rows_at, :])
            grad = dot_last(wf_ref[2, at, :], og_ref[rows_at, :])
            t_ref[0, at, rows_at] = (grad * right).astype(BF)
            t_ref[1, at, rows_at] = (grad * left).astype(BF)
            t_ref[2, at, rows_at] = (left * right).astype(BF)

        @pl.loop(0, width // SPAN)
        def _(i):
            columns = tile(i)
            for m, right in enumerate((nm_ref, nm_ref, og_ref)):
                g_ref[m, at, columns] = dot(t_ref[m, at, :], right[:, columns]).astype(BF)

    load_nm.wait()
    load_og.wait()
    for i, slot in enumerate(order):
        load_wf[slot].wait()
        feed_slot(slot)
        feed.begin(slot)
        if i == 2:
            feed.middle(order[0])
    feed.middle(order[1])
    for load in early_loads:
        load.wait()

    @pl.loop(0, spans)
    def _(i):
        at = tile(spans + i)
        total = dot_first(t_ref[0, :, at], wf_ref[0]) + dot_first(t_ref[1, :, at], wf_ref[1])
        send_ref[tile(i), :] = total.astype(BF)

    copies.send(send_ref, got_ref, base, base, place.across)

    @pl.loop(0, spans)
    def _(i):
        at = tile(i)
        total = dot_first(t_ref[0, :, at], wf_ref[0]) + dot_first(t_ref[1, :, at], wf_ref[1])
        mid_ref[at, :] = total

    feed.end(order[0])
    copies.receive(got_ref, base, place.across)

    @pl.loop(0, rows // 128)
    def _(i):
        at = pl.ds(pl.multiple_of(i * 128, 128), 128)
        grad = mid_ref[at, :] + got_ref[at, :].astype(F32)
        values = hidden_ref[at, :]
        norm = lax.rsqrt(jnp.mean(values * values, axis=-1, keepdims=True) + EPSILON)
        normed = values * norm
        mean = jnp.mean(grad * normed, axis=-1, keepdims=True)
        grad = og_ref[at, :].astype(F32) + norm * (grad - normed * mean)
        mid_ref[at, :] = grad
        nm_ref[at, :] = grad.astype(BF)

    copies.send(nm_ref.at[own], nm_ref.at[other], base + 1, base + 1, place.across)
    copies.move(mid_ref, hidden_grad_out, later=True)
    copies.sent(base)

    @pl.loop(0, spans)
    def _(i):
        send_ref[tile(i), :] = dot_first(t_ref[2, :, tile(spans + i)], wf_ref[2]).astype(BF)

    copies.receive(nm_ref.at[other], base + 1, place.across)
    copies.move(nm_ref, branch_out, later=True)
    copies.send(send_ref, got_ref, base + 2, base + 2, place.across)

    @pl.loop(0, spans)
    def _(i):
        at = tile(i)
        hidden_ref[at, :] += dot_first(t_ref[2, :, at], wf_ref[2])

    loads = []
    for slot in range(n_head):
        lanes = pl.ds(slot * 2 * HEAD_DIM, 2 * HEAD_DIM)
        loads.append(copies.move(query.at[slot], t_ref.at[0, pl.ds(0, 2 * rows), lanes]))
        loads.append(copies.move(keys.at[slot], t_ref.at[1, pl.ds(0, 2 * rows), lanes]))
        lanes = pl.ds(slot * HEAD_DIM, HEAD_DIM)
        loads.append(copies.move(values.at[slot], wf_ref.at[1, pl.ds(0, 2 * rows), lanes]))

    def late_loads(slot):
        turn = slot % 2
        return [
            copies.move(pre.at[slot, :, pl.ds(0, 2 * HEAD_DIM)], qk_pre_ref.at[turn]),
            copies.move(cosines.at[slot], cos_ref.at[turn]),
            copies.move(sines.at[slot], sin_ref.at[turn]),
        ]

    slot_loads = {slot: late_loads(slot) for slot in range(2)}

    def q_at(slot, at):
        return t_ref[0, at, pl.ds(slot * 2 * HEAD_DIM, 2 * HEAD_DIM)]

    def k_at(slot, at):
        return t_ref[1, at, pl.ds(slot * 2 * HEAD_DIM, 2 * HEAD_DIM)]

    def v_at(slot, at):
        return wf_ref[1, at, pl.ds(slot * HEAD_DIM, HEAD_DIM)]

    def pre_at(slot, at, part):
        start = (slot % 2) * 4 * HEAD_DIM + part * HEAD_DIM
        holder = t_ref.at[2] if slot < 2 else wf_ref.at[0]
        return holder.at[at, pl.ds(start, HEAD_DIM)]

    @pl.loop(0, tiles)
    def _(i):
        at = tile(i)
        grad = dot_last(nm_ref[at, :], wo_ref[...])
        norm = scale_ref[at, :]
        total = jnp.zeros((SPAN, 1), F32)
        for slot in range(n_head):
            part = grad[:, slot * HEAD_DIM : (slot + 1) * HEAD_DIM]
            normed = attn_ref[slot, at, :] * norm
            pre_at(slot, at, 3)[...] = (part * normed).astype(BF)
            part = part * gate_ref[slot, at, :]
            gate_ref[slot, at, :] = part
            total += jnp.sum(part * normed, axis=-1, keepdims=True)
        sum_ref[at, :] = jnp.broadcast_to(total, (SPAN, HEAD_DIM))

    base += 3
    copies.send(sum_ref.at[own], other_sum_ref.at[other], base, base, place.across)
    copies.send(sum_ref.at[other], other_sum_ref.at[own], base + 1, base + 1, place.across)
    feed.middle(order[2])
    copies.receive(got_ref, base - 1, place.across)

    @pl.loop(0, rows // 128)
    def _(i):
        at = pl.ds(pl.multiple_of(i * 128, 128), 128)
        block_ref[at, :] = (hidden_ref[at, :] + got_ref[at, :].astype(F32)).astype(BF)

    for q in range(4):
        far = pl.ds(pl.multiple_of(place.at[q] * quarter, quarter), quarter)
        src = block_ref.at[:, pl.ds(q * quarter, quarter)]
        copies.move(src, block_out.at[:, far], later=True)
    copies.receive(other_sum_ref.at[other], base, place.across)
    copies.receive(other_sum_ref.at[own], base + 1, place.across)
    base += 2
    for load in loads:
        load.wait()

    def slot_decay(slot):
        return decay_of(2 * lax.rem(z + slot, n_head) + core)

    for slot in range(n_head):
        decay = slot_decay(slot)
        early = jnp.exp(-decay * (iota((SPAN, HEAD_DIM), 0) + 1.0))

        @pl.loop(0, tiles)
        def _(i):
            at = tile(i)
            norm = scale_ref[at, :]
            mean = (sum_ref[at, :] + other_sum_ref[at, :]) / width
            grad = norm * (gate_ref[slot, at, :] - attn_ref[slot, at, :] * norm * mean)
            grad = grad.astype(BF)
            ga_ref[slot, at, :] = grad
            both = dot_first(
                q_at(slot, at), jnp.concatenate(split(grad.astype(F32) * early), axis=1)
            )
            late_ref[slot, i] = both[:, :HEAD_DIM] + both[:, HEAD_DIM:]

    n_chain = 2 * n_head
    chain_base = base

    def chain_at(index):
        group, seq = lax.div(index, 2), lax.rem(index, 2)
        return lax.rem(group - z + n_head, n_head), seq, decay_of(2 * group + core)

    def chain_copy(index, slot, seq):
        return pltpu.make_async_remote_copy(
            src_ref=message_ref.at[slot, seq],
            dst_ref=pending_ref.at[lax.rem(slot + 1, n_head), seq],
            send_sem=sends.at[chain_base + index],
            recv_sem=receives.at[chain_base + index],
            device_id=place.down,
            device_id_type=MESH,
        )

    @pl.loop(0, n_chain)
    def _(index):
        slot, seq, decay = chain_at(index)

        @pl.when(z < last)
        def _():
            copies.receive(pending_ref.at[slot, seq], chain_base + index, place.up)

        @pl.when(z == last)
        def _():
            pending_ref[slot, seq] = jnp.zeros(pending_ref.shape[2:], BF)

        @pl.when(z > 0)
        def _():
            total = jnp.exp(-decay * rows) * pending_ref[slot, seq].astype(F32)
            for n in range(spans):
                total += jnp.exp(-decay * (n * SPAN)) * late_ref[slot, seq * spans + n]
            message_ref[slot, seq] = total.astype(BF)
            chain_copy(index, slot, seq).start()

    feed.end(order[1])
    feed.middle(order[3])

    offsets = iota((SPAN, SPAN), 0) - iota((SPAN, SPAN), 1)

    def back_slot(slot):
        turn = slot % 2
        decay = slot_decay(slot)
        mask = jnp.where(offsets >= 0.0, jnp.exp(-decay * jnp.maximum(offsets, 0.0)), 0.0)
        places = iota((SPAN, 1), 0)
        early = jnp.exp(-decay * (places + 1.0))
        late = jnp.exp(-decay * (SPAN - 1.0 - places))
        span_decay = jnp.exp(-decay * SPAN)
        rates_ref[slot] = jnp.zeros((8, HEAD_DIM), F32)

        @pl.loop(0, 2)
        def _(seq):
            for n in range(spans):
                i = seq * spans + n
                at, here = tile(i), pl.ds(n * SPAN, SPAN)
                state = carry_ref[slot, seq].astype(F32)
                if n == 1:
                    state = span_decay * state + fresh_ref[slot, seq]
                later = pending_ref[slot, seq].astype(F32)
                if n == 0:
                    later = span_decay * later + late_ref[slot, seq * spans + 1]
                q, k, v, grad = q_at(slot, at), k_at(slot, at), v_at(slot, at), ga_ref[slot, at, :]
                weights = (dot_last(q, k) * mask).astype(BF)
                scores = (dot_last(grad, v) * mask).astype(BF)
                state_high, state_low = split(state)
                grad_query = dot(scores, k)
                grad_query += early * (dot_last(grad, state_high) + dot_last(grad, state_low))
                later_high, later_low = split(later)
                grad_keys = dot_first(scores, q)
                grad_keys += late * (dot_last(v, later_high) + dot_last(v, later_low))
                both = dot(k, jnp.concatenate([later_high, later_low], axis=1))
                grad_values = dot_first(weights, grad)
                grad_values += late * (both[:, :HEAD_DIM] + both[:, HEAD_DIM:])
                pre_at(slot, at, 2)[...] = grad_values.astype(BF)
                cosine, sine = cos_ref[turn, here, :], sin_ref[turn, here, :]
                angles = jnp.zeros((SPAN, HEAD_DIM), F32)
                for part, turned in enumerate((grad_query, grad_keys)):
                    value = qk_pre_ref[turn, at, pl.ds(part * HEAD_DIM, HEAD_DIM)]
                    by_cos, by_sin = turned[:, :HEAD_DIM], turned[:, HEAD_DIM:]
                    gate = 1.0 / (1.0 + jnp.exp(-value))
                    act = by_cos * cosine + by_sin * sine
                    angles += value * gate * (by_sin * cosine - by_cos * sine)
                    act = act * gate * (1.0 + value * (1.0 - gate))
                    pre_at(slot, at, part)[...] = act.astype(BF)
                steps = (z * rows + n * SPAN).astype(F32) + places
                rates_ref[slot, pl.ds(0, 1), :] += jnp.sum(steps * angles, axis=0, keepdims=True)

    for slot in range(n_head):
        for load in slot_loads[slot]:
            load.wait()
        back_slot(slot)
        if slot + 2 < n_head:
            slot_loads[slot + 2] = late_loads(slot + 2)
        lanes = pl.ds((slot % 2) * 4 * HEAD_DIM, 4 * HEAD_DIM)
        holder = t_ref.at[2] if slot < 2 else wf_ref.at[0]
        copies.move(holder.at[pl.ds(0, 2 * rows), lanes], pre_out.at[slot], later=True)
        if slot == 1:
            feed.end(order[2])
    feed.end(order[3])
    feed.total()
    copies.move(g_view(0, 0, None), feed_out, later=True)
    copies.move(rates_ref, rates_out, later=True)

    @pl.when(z > 0)
    def _():
        @pl.loop(0, n_chain)
        def _(index):
            slot, seq, _ = chain_at(index)
            chain_copy(index, slot, seq).wait_send()

    copies.finish()


def middle(n_head, wf, nm, og, hidden, wo, pre, query, keys, values, attn, cos, sin, fresh, carry, scale):
    rows, width = hidden.shape
    units = wf.shape[1] // n_head
    quarter = width // 4
    tall = 2 * rows
    halves = (n_head, 3, units // 2, quarter)
    wholes = (n_head, 3, units, quarter)
    buffers = [
        (wf.shape, BF),
        (wf.shape, BF),
        (wf.shape, BF),
        (halves, BF),
        (halves, BF),
        (wholes, BF),
        (wholes, BF),
        ((n_head - 1,) + wholes[1:], BF),
        ((tall, width), BF),
        ((tall, width), BF),
        ((rows, width), F32),
        ((rows, width), F32),
        ((rows, width), BF),
        ((rows, width), BF),
        ((rows, width), BF),
        (wo.shape, BF),
        ((n_head, tall, HEAD_DIM), F32),
        ((n_head, tall, HEAD_DIM), F32),
        ((n_head, tall, HEAD_DIM), BF),
        ((2, tall, 2 * HEAD_DIM), F32),
        ((2, rows, HEAD_DIM), F32),
        ((2, rows, HEAD_DIM), F32),
        ((n_head, 2, 2 * HEAD_DIM, HEAD_DIM), F32),
        ((n_head, 2, 2 * HEAD_DIM, HEAD_DIM), BF),
        ((n_head, tall // SPAN, 2 * HEAD_DIM, HEAD_DIM), F32),
        ((n_head, 2, 2 * HEAD_DIM, HEAD_DIM), BF),
        ((n_head, 2, 2 * HEAD_DIM, HEAD_DIM), BF),
        ((tall, HEAD_DIM), F32),
        ((tall, HEAD_DIM), F32),
        ((tall, HEAD_DIM), F32),
        ((n_head, 8, HEAD_DIM), F32),
    ]
    outs = [
        (wholes[1:], BF),
        ((rows, width), BF),
        ((rows, width), F32),
        ((tall, width), BF),
        ((n_head, tall, 4 * HEAD_DIM), BF),
        ((n_head, 8, HEAD_DIM), F32),
    ]
    n_sems = PER_SCATTER + 3 + 2 + 2 * n_head
    return pl.pallas_call(
        functools.partial(middle_kernel, n_head),
        out_shape=[jax.ShapeDtypeStruct(*out) for out in outs],
        in_specs=[ANY] * 15,
        out_specs=[ANY] * len(outs),
        scratch_shapes=[pltpu.VMEM(*b) for b in buffers]
        + [
            pltpu.SemaphoreType.DMA((n_sems,)),
            pltpu.SemaphoreType.DMA((n_sems,)),
            pltpu.SemaphoreType.DMA((64,)),
        ],
        compiler_params=pltpu.CompilerParams(
            collective_id=1, has_side_effects=True, vmem_limit_bytes=63 << 20
        ),
        name="middle",
    )(wf, nm, og, hidden, wo, pre, query, keys, values, attn, cos, sin, fresh, carry, scale)


def make(n_dp, n_head):
    def swap(array, bit):
        return lax.ppermute(array, "dp", [(i, i ^ bit) for i in range(n_dp)])

    def from_above(array, step):
        return lax.ppermute(array, "head", [((i + step) % n_head, i) for i in range(n_head)])

    def to_above(array, step):
        return lax.ppermute(array, "head", [(i, (i + step) % n_head) for i in range(n_head)])

    def share(pieces, axis):
        half = pieces.shape[axis] // 2
        by_x = swap(pieces, 2)
        by_y = swap(pieces, 4)
        low = swap(lax.slice_in_dim(by_x, 0, half, axis=axis), 4)
        high = swap(lax.slice_in_dim(by_y, half, 2 * half, axis=axis), 2)
        return [pieces, by_x, by_y, jnp.concatenate([low, high], axis=axis)]

    def collect(parts, axis):
        own, for_x, for_y, for_far = parts
        half = own.shape[axis] // 2

        def cut(array, which):
            return lax.slice_in_dim(array, which * half, (which + 1) * half, axis=axis)

        def add(left, right):
            return (left.astype(F32) + right.astype(F32)).astype(BF)

        low = swap(cut(for_far, 0), 4)
        high = swap(cut(for_far, 1), 2)
        by_x = swap(jnp.concatenate([add(cut(for_x, 0), low), cut(for_x, 1)], axis=axis), 2)
        by_y = swap(jnp.concatenate([cut(for_y, 0), add(cut(for_y, 1), high)], axis=axis), 4)
        plane = (own.astype(F32) + by_x.astype(F32) + by_y.astype(F32)).astype(BF)
        total = plane[0].astype(F32)
        for step in range(1, n_head):
            total = total + to_above(plane[step], step).astype(F32)
        if n_dp > 8:
            groups = [[i + 8 * j for j in range(n_dp // 8)] for i in range(8)]
            total = lax.psum(total, "dp", axis_index_groups=groups)
        return total.astype(BF)

    def on_device(
        tokens,
        attn_query,
        attn_key,
        attn_value,
        attn_gate,
        attn_out,
        rotation_rates,
        ffn_left,
        ffn_right,
        ffn_down,
        out_grad,
    ):
        width = tokens.shape[1]
        quarter = width // 4
        rows = tokens.shape[0]
        spans = rows // SPAN
        units = ffn_left.shape[1] // 2
        dp = lax.axis_index("dp")
        place = lax.axis_index("head")
        core = dp & 1
        plane = (dp >> 1) & 3

        def relative(array, axis):
            return jnp.concatenate(
                [
                    lax.dynamic_slice_in_dim(array, (plane ^ q) * quarter, quarter, axis=axis)
                    for q in range(4)
                ],
                axis=axis,
            )

        def half_of(array, axis):
            size = array.shape[axis] // 2
            return lax.dynamic_slice_in_dim(array, core * size, size, axis=axis)

        ffn = jnp.stack([ffn_left.T, ffn_right.T, ffn_down])
        rates_in = jnp.pad(rotation_rates.reshape(2, HEAD_DIM), ((0, 6), (0, 0)))
        (
            attn_weights,
            out_w,
            ffn_all,
            gathered_in,
            pre,
            query,
            keys,
            values,
            attn,
            cosines,
            sines,
            fresh,
            carry,
            scale_attn,
            gated,
            hidden,
            gathered_mid,
            grad_rows,
        ) = forward(
            n_head,
            tokens,
            out_grad,
            attn_query,
            attn_key,
            attn_value,
            attn_gate,
            attn_out,
            ffn,
            rates_in,
        )
        feed_piece, block_out, grad_hidden, branch_rows, grad_pre, rates_grad = middle(
            n_head,
            ffn_all,
            gathered_mid,
            grad_rows,
            hidden,
            out_w,
            pre,
            query,
            keys,
            values,
            attn,
            cosines,
            sines,
            fresh,
            carry,
            scale_attn,
        )
        rates_grad = rates_grad[:, 0]
        left_grad, right_grad, down_grad = jnp.concatenate(share(feed_piece, 1), axis=2)
        inputs = relative(tokens, 1).astype(F32)
        normed_one, scale_one = norm_parts(inputs)
        out_grads = first_dot(branch_rows, gated)

        def core_scatter(array):
            return array[:rows] + swap(array[rows:].astype(BF), 1).astype(F32)

        attn_grads = []
        grad_in = None
        for r in range(n_head):
            main = first_dot(gathered_in, grad_pre[r]).astype(BF)
            outs = out_grads[:, r * HEAD_DIM : (r + 1) * HEAD_DIM].astype(BF)
            attn_grads.append(jnp.concatenate([main, outs], axis=1))
            term = second_dot(grad_pre[r], attn_weights[r])
            grad_in = term if grad_in is None else grad_in + term
        grad_in = core_scatter(grad_in)
        input_grad = grad_hidden + norm_back(normed_one, scale_one, grad_in)

        attn_grads = jnp.stack(attn_grads).reshape(n_head, 4, quarter, 5 * HEAD_DIM)
        piece = collect([attn_grads[:, q] for q in range(4)], 1)
        attn_total = jnp.concatenate(share(piece, 0), axis=0)
        rates_piece = rates_grad[0]
        for step in range(1, n_head):
            rates_piece = rates_piece + to_above(rates_grad[step], step)
        groups = [list(range(0, n_dp, 2)), list(range(1, n_dp, 2))]
        rates_piece = lax.psum(rates_piece, "dp", axis_index_groups=groups)

        def both(array, axis):
            other = swap(array, 1)
            first = jnp.where(core == 0, array, other)
            second = jnp.where(core == 0, other, array)
            return first, second

        first, second = both(relative(attn_total, 0), 0)
        matrices = []
        for i in range(5):
            pair = [part[:, i * HEAD_DIM : (i + 1) * HEAD_DIM] for part in (first, second)]
            matrices.append(jnp.concatenate(pair, axis=1).astype(F32))
        query_grad, key_grad, value_grad, gate_grad, out_proj_grad = matrices
        out_proj_grad = out_proj_grad.T
        rates_grad = jnp.concatenate(both(rates_piece, 0), axis=0)
        ffn_grads = jnp.stack([relative(g, 1) for g in (left_grad, right_grad, down_grad)])
        ffn_grads = jnp.concatenate(both(ffn_grads, 1), axis=1).astype(F32)
        return (
            block_out,
            relative(input_grad, 1),
            query_grad,
            key_grad,
            value_grad,
            gate_grad,
            out_proj_grad,
            rates_grad,
            ffn_grads[0].T,
            ffn_grads[1].T,
            ffn_grads[2],
        )

    return on_device


def solution(mesh):
    weights = (P(None, "head"),) * 4 + (P("head", None), P("head")) + (P(None, "head"),) * 2
    weights = weights + (P("head", None),)
    rows = P(("dp", "head"), None)
    return jax.shard_map(
        make(mesh.shape["dp"], mesh.shape["head"]),
        mesh=mesh,
        in_specs=(rows,) + weights + (rows,),
        out_specs=(rows, rows) + weights,
        check_vma=False,
    )
```

```python
import functools

import jax
import jax.numpy as jnp
from jax import lax
from jax.experimental import pallas as pl
from jax.experimental.pallas import tpu as pltpu
from jax.sharding import PartitionSpec as P

HEADS = 8
HEAD_DIM = 128
SPAN = 256
EPSILON = 1e-06
BF = jnp.bfloat16
F32 = jnp.float32


MESH = pl.DeviceIdType.MESH
ANY = pl.BlockSpec(memory_space=pl.ANY)
IN_VMEM = pl.BlockSpec(memory_space=pltpu.VMEM)


def split(value):
    high = value.astype(BF)
    return high, (value - high.astype(F32)).astype(BF)


class Place:
    def __init__(self, n_head):
        self.n_head = n_head
        dp = lax.axis_index("dp")
        self.z = lax.axis_index("head")
        self.core = lax.rem(dp, 2)
        x = lax.rem(lax.div(dp, 2), 2)
        y = lax.rem(lax.div(dp, 4), 2)
        self.plane = x + 2 * y
        self.at = [self.plane, self.plane + 1 - 2 * x, self.plane + 2 - 4 * y, 3 - self.plane]
        self.across = {"dp": dp + 1 - 2 * self.core}
        self.by_x = {"dp": dp + 2 - 4 * x}
        self.by_y = {"dp": dp + 4 - 8 * y}
        self.up = {"head": lax.rem(self.z + 1, n_head)}
        self.down = {"head": lax.rem(self.z + n_head - 1, n_head)}

    def above(self, step):
        return {"head": lax.rem(self.z + step, self.n_head)}

    def below(self, step):
        return {"head": lax.rem(self.z + self.n_head - step, self.n_head)}

    def greet(self):
        barrier = pltpu.get_barrier_semaphore()
        others = [self.across, self.by_x, self.by_y]
        others += [self.below(step) for step in range(1, self.n_head)]
        for other in others:
            pl.semaphore_signal(barrier, inc=1, device_id=other, device_id_type=MESH)
        pl.semaphore_wait(barrier, len(others))


class Copies:
    def __init__(self, sends, receives, locals_):
        self.sends, self.receives, self.locals = sends, receives, locals_
        self.pending = []
        self.started = {}
        self.n_local = 0

    def send(self, src, dst, out, into, device, when=None):
        copy = pltpu.make_async_remote_copy(
            src_ref=src,
            dst_ref=dst,
            send_sem=self.sends.at[out],
            recv_sem=self.receives.at[into],
            device_id=device,
            device_id_type=MESH,
        )
        if when is None:
            copy.start()
            self.pending.append(copy.wait_send)
            if isinstance(out, int):
                self.started[out] = copy.wait_send
        else:
            pl.when(when)(copy.start)
            self.pending.append(lambda: pl.when(when)(copy.wait_send))

    def receive(self, dst, into, device):
        pltpu.make_async_remote_copy(
            src_ref=dst,
            dst_ref=dst,
            send_sem=self.sends.at[0],
            recv_sem=self.receives.at[into],
            device_id=device,
            device_id_type=MESH,
        ).wait_recv()

    def move(self, src, dst, later=False):
        copy = pltpu.make_async_copy(src, dst, self.locals.at[self.n_local])
        self.n_local += 1
        copy.start()
        if later:
            self.pending.append(copy.wait)
        return copy

    def sent(self, out):
        wait = self.started.pop(out)
        self.pending.remove(wait)
        wait()

    def finish(self):
        for wait in self.pending:
            wait()


class Gather:
    def __init__(self, place, copies, view, base):
        self.place, self.copies, self.view, self.base = place, copies, view, base

    def begin(self):
        place, z = self.place, self.place.z
        own = self.view(0, 0, None)
        last = place.n_head - 1
        self.copies.send(
            own, self.view(last, 0, None), self.base, self.base + last, place.up, when=z < last
        )
        self.copies.send(own, self.view(1, 0, None), self.base + 1, self.base + 1, place.down, when=z > 0)

    def arrived(self, slot):
        place, copies, z, base = self.place, self.copies, self.place.z, self.base
        last = place.n_head - 1
        copies.receive(self.view(slot, 0, None), base + slot, place.up)
        from_up = z + slot <= last
        piece = self.view(slot, 0, None)
        down = jnp.logical_and(from_up, z > 0)
        up = jnp.logical_and(jnp.logical_not(from_up), z < last)
        after = jnp.minimum(slot + 1, last)
        before = jnp.maximum(slot - 1, 1)
        copies.send(piece, self.view(after, 0, None), base + 1 + slot, base + after, place.down, when=down)
        copies.send(piece, self.view(before, 0, None), base + 1 + slot, base + before, place.up, when=up)
        at = base + 4 * slot + 4
        copies.send(piece, self.view(slot, 1, None), at, at, place.by_x)
        copies.send(piece, self.view(slot, 2, None), at + 1, at + 1, place.by_y)

    def spread(self, slot):
        place, copies = self.place, self.copies
        at = self.base + 4 * slot + 4
        copies.receive(self.view(slot, 1, None), at, place.by_x)
        copies.send(self.view(slot, 1, 0), self.view(slot, 3, 0), at + 2, at + 2, place.by_y)
        copies.receive(self.view(slot, 2, None), at + 1, place.by_y)
        copies.send(self.view(slot, 2, 1), self.view(slot, 3, 1), at + 3, at + 3, place.by_x)

    def complete(self, slot):
        place, copies = self.place, self.copies
        at = self.base + 4 * slot + 4
        copies.receive(self.view(slot, 3, 0), at + 2, place.by_y)
        copies.receive(self.view(slot, 3, 1), at + 3, place.by_x)


PER_GATHER = 24


def forward_kernel(
    n_head,
    tokens,
    out_grad,
    wq,
    wk,
    wv,
    wg,
    wo,
    ffn,
    rates,
    wa_out,
    wo_out,
    wf_out,
    nin_out,
    pre_out,
    q_out,
    k_out,
    v_out,
    attn_out,
    cos_out,
    sin_out,
    fresh_out,
    carry_out,
    scale_out,
    gated_out,
    hidden_out,
    nm_out,
    og_out,
    wa_ref,
    wo_ref,
    wf_ref,
    x_ref,
    nin_ref,
    pre_ref,
    q_ref,
    k_ref,
    v_ref,
    attn_ref,
    cos_ref,
    sin_ref,
    fresh_ref,
    carry_ref,
    message_ref,
    squares_ref,
    other_squares_ref,
    gated_ref,
    branch_ref,
    other_branch_ref,
    hidden_ref,
    nm_ref,
    rates_ref,
    og_ref,
    sends,
    receives,
    locals_,
):
    rows, width = tokens.shape
    quarter = width // 4
    units = ffn.shape[1] // 2
    tiles = 2 * rows // SPAN
    place = Place(n_head)
    z, core = place.z, place.core
    copies = Copies(sends, receives, locals_)

    def columns(start, size):
        return pl.ds(pl.multiple_of(start, size), size)

    own_loads = []
    for q in range(4):
        far = columns(place.at[q] * quarter, quarter)
        near = pl.ds(q * quarter, quarter)
        loads = []
        for i, w in enumerate((wq, wk, wv, wg)):
            src = w.at[far, columns(core * HEAD_DIM, HEAD_DIM)]
            loads.append(copies.move(src, wa_ref.at[0, near, pl.ds(i * HEAD_DIM, HEAD_DIM)]))
        src = wo.at[columns(core * HEAD_DIM, HEAD_DIM), far]
        loads.append(copies.move(src, wo_ref.at[pl.ds(0, HEAD_DIM), near]))
        src = ffn.at[:, pl.ds(pl.multiple_of(core * units, 16), units), far]
        loads.append(copies.move(src, wf_ref.at[:, pl.ds(0, units), near]))
        own_loads.append(loads)
    token_loads = [
        copies.move(
            tokens.at[:, columns(place.at[q] * quarter, quarter)],
            x_ref.at[:, pl.ds(q * quarter, quarter)],
        )
        for q in range(4)
    ]
    grad_loads = [
        copies.move(
            out_grad.at[:, columns(place.at[q] * quarter, quarter)],
            og_ref.at[pl.ds(0, rows), pl.ds(q * quarter, quarter)],
        )
        for q in range(4)
    ]
    place.greet()

    def half_rows(half, size):
        return pl.ds(0, size) if half is None else pl.ds(half * (size // 2), size // 2)

    def wa_view(slot, q, half):
        at = half_rows(half, quarter)
        return wa_ref.at[slot, pl.ds(q * quarter + at.start, at.size), :]

    def wo_view(slot, q, half):
        at = half_rows(half, HEAD_DIM)
        return wo_ref.at[
            pl.ds(pl.multiple_of(slot * HEAD_DIM + at.start, HEAD_DIM // 2), at.size),
            pl.ds(q * quarter, quarter),
        ]

    def wf_view(slot, q, half):
        at = half_rows(half, units)
        return wf_ref.at[
            :,
            pl.ds(pl.multiple_of(slot * units + at.start, 16), at.size),
            pl.ds(q * quarter, quarter),
        ]

    attn_in = Gather(place, copies, wa_view, 0)
    attn_down = Gather(place, copies, wo_view, PER_GATHER)
    feed = Gather(place, copies, wf_view, 2 * PER_GATHER)
    base = 3 * PER_GATHER
    for load in own_loads[0][:4]:
        load.wait()
    attn_in.begin()
    own_loads[0][4].wait()
    attn_down.begin()
    for step in range(1, n_head):
        copies.send(rates, rates_ref.at[step], base + step, base + step, place.below(step))
    rates_ref[0] = rates[...]

    for load in token_loads:
        load.wait()

    def norm_rows(values):
        mean = jnp.mean(values * values, axis=-1, keepdims=True)
        return values * lax.rsqrt(mean + EPSILON)

    @pl.loop(0, rows // 128)
    def _(i):
        at = pl.ds(pl.multiple_of(i * 128, 128), 128)
        nin_ref[at, :] = norm_rows(x_ref[at, :].astype(F32)).astype(BF)

    base += 4
    for load in grad_loads:
        load.wait()
    og_other = og_ref.at[pl.ds(rows, rows)]
    copies.send(og_ref.at[pl.ds(0, rows)], og_other, base, base, place.across)
    base += 1
    nin_other = nin_ref.at[pl.ds(rows, rows)]
    copies.send(nin_ref.at[pl.ds(0, rows)], nin_other, base, base, place.across)
    own_loads[0][5].wait()
    feed.begin()
    for loads in own_loads[1:]:
        for load in loads:
            load.wait()
    for step in range(1, n_head):
        copies.receive(rates_ref.at[step], base - 5 + step, place.up)
    copies.receive(nin_other, base, place.across)
    copies.move(nin_ref, nin_out, later=True)
    copies.receive(og_other, base - 1, place.across)
    copies.move(og_ref, og_out, later=True)

    def decay_of(head):
        exponent = jnp.full((1, 1), -8.0 / HEADS, F32) * (head + 1).astype(F32)
        return jnp.exp2(exponent)

    def tile(i):
        return pl.ds(pl.multiple_of(i * SPAN, SPAN), SPAN)

    def iota(shape, axis):
        return lax.broadcasted_iota(jnp.int32, shape, axis).astype(F32)

    def dot(left, right):
        return jnp.dot(left, right, preferred_element_type=F32)

    def slot_compute(slot):
        head = 2 * lax.rem(z + slot, n_head) + core
        decay = decay_of(head)
        rate = rates_ref[slot, pl.ds(core, 1), :]
        coarse = (z * rows).astype(F32) + 32.0 * iota((rows // 32, HEAD_DIM), 0)
        coarse = coarse * rate
        fine = iota((32, HEAD_DIM), 0) * rate
        cos_a, sin_a = jnp.cos(coarse), jnp.sin(coarse)
        cos_b, sin_b = jnp.cos(fine), jnp.sin(fine)
        for a in range(rows // 32):
            cos_row, sin_row = cos_a[a : a + 1], sin_a[a : a + 1]
            cos_ref[slot, pl.ds(a * 32, 32), :] = cos_row * cos_b - sin_row * sin_b
            sin_ref[slot, pl.ds(a * 32, 32), :] = sin_row * cos_b + cos_row * sin_b
        offsets = iota((SPAN, SPAN), 0) - iota((SPAN, SPAN), 1)
        mask = jnp.where(offsets >= 0.0, jnp.exp(-decay * jnp.maximum(offsets, 0.0)), 0.0)
        late = jnp.exp(-decay * (SPAN - 1.0 - iota((SPAN, HEAD_DIM), 0)))

        @pl.loop(0, tiles)
        def _(i):
            at = tile(i)
            pre = dot(nin_ref[at, :], wa_ref[slot])
            pre_ref[slot, at, :] = pre
            here = tile(lax.rem(i, rows // SPAN))
            cosines, sines = cos_ref[slot, here, :], sin_ref[slot, here, :]

            def rotate(values):
                activated = values / (1.0 + jnp.exp(-values))
                turned = jnp.concatenate([activated * cosines, activated * sines], axis=1)
                return turned.astype(BF)

            query = rotate(pre[:, :HEAD_DIM])
            keys = rotate(pre[:, HEAD_DIM : 2 * HEAD_DIM])
            value = pre[:, 2 * HEAD_DIM : 3 * HEAD_DIM].astype(BF)
            q_ref[slot, at, :] = query
            k_ref[slot, at, :] = keys
            v_ref[slot, at, :] = value
            scores = lax.dot_general(
                query, keys, (((1,), (1,)), ((), ())), preferred_element_type=F32
            )
            weights = (scores * mask).astype(BF)
            attn_ref[slot, at, :] = dot(weights, value)
            high, low = split(value.astype(F32) * late)
            both = lax.dot_general(
                keys,
                jnp.concatenate([high, low], axis=1),
                (((0,), (0,)), ((), ())),
                preferred_element_type=F32,
            )
            fresh_ref[slot, i] = both[:, :HEAD_DIM] + both[:, HEAD_DIM:]

        for ref, out in (
            (wa_ref, wa_out),
            (pre_ref, pre_out),
            (q_ref, q_out),
            (k_ref, k_out),
            (v_ref, v_out),
            (cos_ref, cos_out),
            (sin_ref, sin_out),
            (fresh_ref, fresh_out),
        ):
            copies.move(ref.at[slot], out.at[slot], later=True)

    last = n_head - 1
    first = 1 + 2 * lax.div(z, last)
    second = 2 + lax.rem(lax.div(z + 1, 2), 2)
    third = 6 - first - second

    attn_in.arrived(first)
    attn_down.arrived(first)
    slot_compute(0)
    attn_in.arrived(second)
    attn_down.arrived(second)
    attn_in.spread(first)
    attn_down.spread(first)
    attn_in.arrived(third)
    attn_down.arrived(third)
    attn_in.spread(second)
    attn_down.spread(second)
    attn_in.complete(first)
    slot_compute(first)
    feed.arrived(first)
    attn_in.spread(third)
    attn_down.spread(third)
    attn_in.complete(second)
    slot_compute(second)
    feed.arrived(second)
    feed.spread(first)
    attn_in.complete(third)
    slot_compute(third)
    feed.arrived(third)
    feed.spread(second)

    base += 1
    chain_base = base
    n_chain = 2 * n_head

    def chain_at(index):
        group, seq = lax.div(index, 2), lax.rem(index, 2)
        return lax.rem(group - z + n_head, n_head), seq, decay_of(2 * group + core)

    def chain_copy(index, slot, seq):
        after = lax.rem(slot + n_head - 1, n_head)
        return pltpu.make_async_remote_copy(
            src_ref=message_ref.at[slot, seq],
            dst_ref=carry_ref.at[after, seq],
            send_sem=sends.at[chain_base + index],
            recv_sem=receives.at[chain_base + index],
            device_id=place.up,
            device_id_type=MESH,
        )

    @pl.loop(0, n_chain)
    def _(index):
        slot, seq, decay = chain_at(index)

        @pl.when(z > 0)
        def _():
            copies.receive(carry_ref.at[slot, seq], chain_base + index, place.down)

        @pl.when(z == 0)
        def _():
            carry_ref[slot, seq] = jnp.zeros(carry_ref.shape[2:], BF)

        @pl.when(z < last)
        def _():
            total = jnp.exp(-decay * rows) * carry_ref[slot, seq].astype(F32)
            for n in range(rows // SPAN):
                left = rows - (n + 1) * SPAN
                total += jnp.exp(-decay * left) * fresh_ref[slot, seq * (rows // SPAN) + n]
            message_ref[slot, seq] = total.astype(BF)
            chain_copy(index, slot, seq).start()

    copies.move(carry_ref, carry_out, later=True)

    squares_ref[...] = jnp.zeros_like(squares_ref)

    @pl.loop(0, n_head)
    def _(slot):
        decay = decay_of(2 * lax.rem(z + slot, n_head) + core)
        early = jnp.exp(-decay * (iota((SPAN, HEAD_DIM), 0) + 1.0))

        @pl.loop(0, 2)
        def _(seq):
            state = carry_ref[slot, seq].astype(F32)
            for n in range(rows // SPAN):
                i = seq * (rows // SPAN) + n
                at = tile(i)
                both = dot(q_ref[slot, at, :], jnp.concatenate(split(state), axis=1))
                attn = attn_ref[slot, at, :]
                attn += early * (both[:, :HEAD_DIM] + both[:, HEAD_DIM:])
                attn_ref[slot, at, :] = attn
                squares_ref[at, :] += jnp.sum(attn * attn, axis=-1, keepdims=True)
                if n + 1 < rows // SPAN:
                    state = jnp.exp(-decay * SPAN) * state + fresh_ref[slot, i]

    copies.move(attn_ref, attn_out, later=True)
    base += n_chain
    own, other = pl.ds(0, rows), pl.ds(rows, rows)
    copies.send(squares_ref.at[own], other_squares_ref.at[other], base, base, place.across)
    copies.send(squares_ref.at[other], other_squares_ref.at[own], base + 1, base + 1, place.across)
    feed.spread(third)
    for slot in (first, second, third):
        attn_down.complete(slot)
    copies.receive(other_squares_ref.at[other], base, place.across)
    copies.receive(other_squares_ref.at[own], base + 1, place.across)

    @pl.loop(0, tiles)
    def _(i):
        at = tile(i)
        total = squares_ref[at, :] + other_squares_ref[at, :]
        scale = lax.rsqrt(total / width + EPSILON)
        other_squares_ref[at, :] = scale
        for slot in range(n_head):
            gate = pre_ref[slot, at, pl.ds(3 * HEAD_DIM, HEAD_DIM)]
            gated = (attn_ref[slot, at, :] * scale * gate).astype(BF)
            gated_ref[at, pl.ds(slot * HEAD_DIM, HEAD_DIM)] = gated

    copies.move(other_squares_ref, scale_out, later=True)
    copies.move(gated_ref, gated_out, later=True)
    copies.move(wo_ref, wo_out, later=True)
    base += 2

    @pl.loop(0, rows // SPAN)
    def _(i):
        gated = gated_ref[pl.ds(pl.multiple_of(rows + i * SPAN, SPAN), SPAN), :]
        branch_ref[tile(i), :] = dot(gated, wo_ref[...]).astype(BF)

    copies.send(branch_ref, other_branch_ref, base, base, place.across)

    @pl.loop(0, rows // SPAN)
    def _(i):
        at = tile(i)
        hidden_ref[at, :] = x_ref[at, :].astype(F32) + dot(gated_ref[at, :], wo_ref[...])

    copies.receive(other_branch_ref, base, place.across)

    @pl.loop(0, rows // 128)
    def _(i):
        at = pl.ds(pl.multiple_of(i * 128, 128), 128)
        hidden = hidden_ref[at, :] + other_branch_ref[at, :].astype(F32)
        hidden_ref[at, :] = hidden
        nm_ref[at, :] = norm_rows(hidden).astype(BF)

    copies.send(nm_ref.at[own], nm_ref.at[other], base + 1, base + 1, place.across)
    copies.move(hidden_ref, hidden_out, later=True)
    for slot in (first, second, third):
        feed.complete(slot)
    copies.move(wf_ref, wf_out, later=True)
    copies.receive(nm_ref.at[other], base + 1, place.across)
    copies.move(nm_ref, nm_out, later=True)

    @pl.when(z < last)
    def _():
        @pl.loop(0, n_chain)
        def _(index):
            slot, seq, _ = chain_at(index)
            chain_copy(index, slot, seq).wait_send()

    copies.finish()


def forward(n_head, tokens, out_grad, wq, wk, wv, wg, wo, ffn, rates):
    rows, width = tokens.shape
    units = ffn.shape[1] // 2
    tall = 2 * rows
    buffers = [
        ((n_head, width, 4 * HEAD_DIM), BF),
        ((n_head * HEAD_DIM, width), BF),
        ((3, n_head * units, width), BF),
        ((rows, width), BF),
        ((tall, width), BF),
        ((n_head, tall, 4 * HEAD_DIM), F32),
        ((n_head, tall, 2 * HEAD_DIM), BF),
        ((n_head, tall, 2 * HEAD_DIM), BF),
        ((n_head, tall, HEAD_DIM), BF),
        ((n_head, tall, HEAD_DIM), F32),
        ((n_head, rows, HEAD_DIM), F32),
        ((n_head, rows, HEAD_DIM), F32),
        ((n_head, tall // SPAN, 2 * HEAD_DIM, HEAD_DIM), F32),
        ((n_head, 2, 2 * HEAD_DIM, HEAD_DIM), BF),
        ((n_head, 2, 2 * HEAD_DIM, HEAD_DIM), BF),
        ((tall, HEAD_DIM), F32),
        ((tall, HEAD_DIM), F32),
        ((tall, n_head * HEAD_DIM), BF),
        ((rows, width), BF),
        ((rows, width), BF),
        ((rows, width), F32),
        ((tall, width), BF),
        ((n_head, 8, HEAD_DIM), F32),
        ((tall, width), BF),
    ]
    out_of = [0, 1, 2, 4, 5, 6, 7, 8, 9, 10, 11, 12, 13, 16, 17, 20, 21, 23]
    n_sems = 3 * PER_GATHER + 4 + 1 + 1 + 2 * n_head + 2 + 2
    return pl.pallas_call(
        functools.partial(forward_kernel, n_head),
        out_shape=[jax.ShapeDtypeStruct(*buffers[i]) for i in out_of],
        in_specs=[ANY] * 8 + [IN_VMEM],
        out_specs=[ANY] * len(out_of),
        scratch_shapes=[pltpu.VMEM(*b) for b in buffers]
        + [
            pltpu.SemaphoreType.DMA((n_sems,)),
            pltpu.SemaphoreType.DMA((n_sems,)),
            pltpu.SemaphoreType.DMA((80,)),
        ],
        compiler_params=pltpu.CompilerParams(
            collective_id=0, has_side_effects=True, vmem_limit_bytes=62 << 20
        ),
        name="forward",
    )(tokens, out_grad, wq, wk, wv, wg, wo, ffn, rates)


class Scatter:
    def __init__(self, place, copies, view, far_x, far_y, near_x, near_y, high, base):
        self.place, self.copies, self.view, self.base = place, copies, view, base
        self.far_x, self.far_y, self.near_x, self.near_y, self.high = far_x, far_y, near_x, near_y, high

    def begin(self, slot):
        place, at = self.place, self.base + 4 * slot
        self.copies.send(self.view(slot, 3, 0), self.far_y.at[slot], at, at, place.by_y)
        self.copies.send(self.view(slot, 3, 1), self.far_x.at[slot], at + 1, at + 1, place.by_x)

    def middle(self, slot):
        place, copies, at = self.place, self.copies, self.base + 4 * slot
        copies.receive(self.far_y.at[slot], at, place.by_y)
        add_to(self.view(slot, 1, 0), self.far_y.at[slot])
        copies.send(self.view(slot, 1, None), self.near_x.at[slot], at + 2, at + 2, place.by_x)
        copies.receive(self.far_x.at[slot], at + 1, place.by_x)
        add_to(self.view(slot, 2, 1), self.far_x.at[slot])
        copies.send(self.view(slot, 2, None), self.near_y.at[slot], at + 3, at + 3, place.by_y)

    def end(self, slot):
        place, copies, at = self.place, self.copies, self.base + 4 * slot
        copies.receive(self.near_x.at[slot], at + 2, place.by_x)
        copies.receive(self.near_y.at[slot], at + 3, place.by_y)
        add_to(self.view(slot, 0, None), self.near_x.at[slot], self.near_y.at[slot])
        if slot:
            at = self.base + 4 * place.n_head + slot
            into = self.high.at[slot - 1]
            copies.send(self.view(slot, 0, None), into, at, at, place.above(slot))

    def total(self, into=None):
        place = self.place
        high = [self.high.at[slot - 1] for slot in range(1, place.n_head)]
        for slot, part in enumerate(high, 1):
            self.copies.receive(part, self.base + 4 * place.n_head + slot, place.up)
        add_to(self.view(0, 0, None), *high, into=into)


PER_SCATTER = 20


def add_to(ref, *others, into=None):
    def add(into, *refs):
        total = refs[0][...].astype(F32)
        for other in refs[1:]:
            total += other[...].astype(F32)
        into[...] = total.astype(BF)

    refs = (ref if into is None else into, ref) + others
    if len(ref.shape) == 2:
        add(*refs)
    else:
        for i in range(ref.shape[0]):
            add(*(one.at[i] for one in refs))


def dot(left, right):
    return jnp.dot(left, right, preferred_element_type=F32)


def iota(shape, axis):
    return lax.broadcasted_iota(jnp.int32, shape, axis).astype(F32)


def decay_of(head):
    exponent = jnp.full((1, 1), -8.0 / HEADS, F32) * (head + 1).astype(F32)
    return jnp.exp2(exponent)


def middle_kernel(
    n_head,
    wf,
    nm,
    og,
    hidden,
    wo,
    pre,
    query,
    keys,
    values,
    attn,
    cosines,
    sines,
    fresh,
    carry,
    scale,
    feed_out,
    block_out,
    hidden_grad_out,
    branch_out,
    pre_out,
    rates_out,
    wf_ref,
    t_ref,
    g_ref,
    far_x,
    far_y,
    near_x,
    near_y,
    high,
    nm_ref,
    og_ref,
    hidden_ref,
    mid_ref,
    send_ref,
    got_ref,
    block_ref,
    wo_ref,
    gate_ref,
    attn_ref,
    ga_ref,
    qk_pre_ref,
    cos_ref,
    sin_ref,
    fresh_ref,
    carry_ref,
    late_ref,
    pending_ref,
    message_ref,
    scale_ref,
    sum_ref,
    other_sum_ref,
    rates_ref,
    sends,
    receives,
    locals_,
):
    rows, width = hidden.shape
    quarter = width // 4
    units = wf.shape[1] // n_head
    spans = rows // SPAN
    tiles = 2 * spans
    last = n_head - 1
    place = Place(n_head)
    z, core = place.z, place.core
    copies = Copies(sends, receives, locals_)
    own, other = pl.ds(0, rows), pl.ds(rows, rows)

    order = (2, 1, 3, 0)
    load_nm = copies.move(nm, nm_ref)
    load_og = copies.move(og, og_ref)
    load_wf = {}
    for slot in order:
        at = pl.ds(slot * units, units)
        load_wf[slot] = copies.move(wf.at[:, at, :], wf_ref.at[:, at, :])
    early_loads = [
        copies.move(hidden, hidden_ref),
        copies.move(wo, wo_ref),
        copies.move(scale, scale_ref),
        copies.move(attn, attn_ref),
        copies.move(pre.at[:, :, pl.ds(3 * HEAD_DIM, HEAD_DIM)], gate_ref),
        copies.move(carry, carry_ref),
    ]
    for seq in range(2):
        for slot in range(n_head):
            early_loads.append(copies.move(fresh.at[slot, seq * spans], fresh_ref.at[slot, seq]))
    place.greet()

    def tile(i):
        return pl.ds(pl.multiple_of(i * SPAN, SPAN), SPAN)

    def dot_last(left, right):
        return lax.dot_general(left, right, (((1,), (1,)), ((), ())), preferred_element_type=F32)

    def dot_first(left, right):
        return lax.dot_general(left, right, (((0,), (0,)), ((), ())), preferred_element_type=F32)

    def g_view(slot, q, half):
        size = units if half is None else units // 2
        start = slot * units + (half or 0) * size
        return g_ref.at[:, pl.ds(start, size), pl.ds(q * quarter, quarter)]

    feed = Scatter(place, copies, g_view, far_x, far_y, near_x, near_y, high, 0)
    base = PER_SCATTER

    def feed_slot(slot):
        at = pl.ds(slot * units, units)

        @pl.loop(0, tiles)
        def _(i):
            rows_at = tile(i)
            left = dot_last(wf_ref[0, at, :], nm_ref[rows_at, :])
            right = dot_last(wf_ref[1, at, :], nm_ref[rows_at, :])
            grad = dot_last(wf_ref[2, at, :], og_ref[rows_at, :])
            t_ref[0, at, rows_at] = (grad * right).astype(BF)
            t_ref[1, at, rows_at] = (grad * left).astype(BF)
            t_ref[2, at, rows_at] = (left * right).astype(BF)

        @pl.loop(0, width // SPAN)
        def _(i):
            columns = tile(i)
            for m, right in enumerate((nm_ref, nm_ref, og_ref)):
                g_ref[m, at, columns] = dot(t_ref[m, at, :], right[:, columns]).astype(BF)

    load_nm.wait()
    load_og.wait()
    for i, slot in enumerate(order):
        load_wf[slot].wait()
        feed_slot(slot)
        feed.begin(slot)
        if i == 2:
            feed.middle(order[0])
    feed.middle(order[1])
    for load in early_loads:
        load.wait()

    @pl.loop(0, spans)
    def _(i):
        at = tile(spans + i)
        total = dot_first(t_ref[0, :, at], wf_ref[0]) + dot_first(t_ref[1, :, at], wf_ref[1])
        send_ref[tile(i), :] = total.astype(BF)

    copies.send(send_ref, got_ref, base, base, place.across)

    @pl.loop(0, spans)
    def _(i):
        at = tile(i)
        total = dot_first(t_ref[0, :, at], wf_ref[0]) + dot_first(t_ref[1, :, at], wf_ref[1])
        mid_ref[at, :] = total

    feed.end(order[0])
    copies.receive(got_ref, base, place.across)

    @pl.loop(0, rows // 128)
    def _(i):
        at = pl.ds(pl.multiple_of(i * 128, 128), 128)
        grad = mid_ref[at, :] + got_ref[at, :].astype(F32)
        values = hidden_ref[at, :]
        norm = lax.rsqrt(jnp.mean(values * values, axis=-1, keepdims=True) + EPSILON)
        normed = values * norm
        mean = jnp.mean(grad * normed, axis=-1, keepdims=True)
        grad = og_ref[at, :].astype(F32) + norm * (grad - normed * mean)
        mid_ref[at, :] = grad
        nm_ref[at, :] = grad.astype(BF)

    copies.send(nm_ref.at[own], nm_ref.at[other], base + 1, base + 1, place.across)
    copies.move(mid_ref, hidden_grad_out, later=True)
    copies.sent(base)

    @pl.loop(0, spans)
    def _(i):
        send_ref[tile(i), :] = dot_first(t_ref[2, :, tile(spans + i)], wf_ref[2]).astype(BF)

    copies.receive(nm_ref.at[other], base + 1, place.across)
    copies.move(nm_ref, branch_out, later=True)
    copies.send(send_ref, got_ref, base + 2, base + 2, place.across)

    @pl.loop(0, spans)
    def _(i):
        at = tile(i)
        hidden_ref[at, :] += dot_first(t_ref[2, :, at], wf_ref[2])

    loads = []
    for slot in range(n_head):
        lanes = pl.ds(slot * 2 * HEAD_DIM, 2 * HEAD_DIM)
        loads.append(copies.move(query.at[slot], t_ref.at[0, pl.ds(0, 2 * rows), lanes]))
        loads.append(copies.move(keys.at[slot], t_ref.at[1, pl.ds(0, 2 * rows), lanes]))
        lanes = pl.ds(slot * HEAD_DIM, HEAD_DIM)
        loads.append(copies.move(values.at[slot], wf_ref.at[1, pl.ds(0, 2 * rows), lanes]))

    def late_loads(slot):
        turn = slot % 2
        return [
            copies.move(pre.at[slot, :, pl.ds(0, 2 * HEAD_DIM)], qk_pre_ref.at[turn]),
            copies.move(cosines.at[slot], cos_ref.at[turn]),
            copies.move(sines.at[slot], sin_ref.at[turn]),
        ]

    slot_loads = {slot: late_loads(slot) for slot in range(2)}

    def q_at(slot, at):
        return t_ref[0, at, pl.ds(slot * 2 * HEAD_DIM, 2 * HEAD_DIM)]

    def k_at(slot, at):
        return t_ref[1, at, pl.ds(slot * 2 * HEAD_DIM, 2 * HEAD_DIM)]

    def v_at(slot, at):
        return wf_ref[1, at, pl.ds(slot * HEAD_DIM, HEAD_DIM)]

    def pre_at(slot, at, part):
        start = (slot % 2) * 4 * HEAD_DIM + part * HEAD_DIM
        holder = t_ref.at[2] if slot < 2 else wf_ref.at[0]
        return holder.at[at, pl.ds(start, HEAD_DIM)]

    @pl.loop(0, tiles)
    def _(i):
        at = tile(i)
        grad = dot_last(nm_ref[at, :], wo_ref[...])
        norm = scale_ref[at, :]
        total = jnp.zeros((SPAN, 1), F32)
        for slot in range(n_head):
            part = grad[:, slot * HEAD_DIM : (slot + 1) * HEAD_DIM]
            normed = attn_ref[slot, at, :] * norm
            pre_at(slot, at, 3)[...] = (part * normed).astype(BF)
            part = part * gate_ref[slot, at, :]
            gate_ref[slot, at, :] = part
            total += jnp.sum(part * normed, axis=-1, keepdims=True)
        sum_ref[at, :] = jnp.broadcast_to(total, (SPAN, HEAD_DIM))

    base += 3
    copies.send(sum_ref.at[own], other_sum_ref.at[other], base, base, place.across)
    copies.send(sum_ref.at[other], other_sum_ref.at[own], base + 1, base + 1, place.across)
    feed.middle(order[2])
    copies.receive(got_ref, base - 1, place.across)

    @pl.loop(0, rows // 128)
    def _(i):
        at = pl.ds(pl.multiple_of(i * 128, 128), 128)
        block_ref[at, :] = (hidden_ref[at, :] + got_ref[at, :].astype(F32)).astype(BF)

    for q in range(4):
        far = pl.ds(pl.multiple_of(place.at[q] * quarter, quarter), quarter)
        src = block_ref.at[:, pl.ds(q * quarter, quarter)]
        copies.move(src, block_out.at[:, far], later=True)
    copies.receive(other_sum_ref.at[other], base, place.across)
    copies.receive(other_sum_ref.at[own], base + 1, place.across)
    base += 2
    for load in loads:
        load.wait()

    def slot_decay(slot):
        return decay_of(2 * lax.rem(z + slot, n_head) + core)

    for slot in range(n_head):
        decay = slot_decay(slot)
        early = jnp.exp(-decay * (iota((SPAN, HEAD_DIM), 0) + 1.0))

        @pl.loop(0, tiles)
        def _(i):
            at = tile(i)
            norm = scale_ref[at, :]
            mean = (sum_ref[at, :] + other_sum_ref[at, :]) / width
            grad = norm * (gate_ref[slot, at, :] - attn_ref[slot, at, :] * norm * mean)
            grad = grad.astype(BF)
            ga_ref[slot, at, :] = grad
            both = dot_first(
                q_at(slot, at), jnp.concatenate(split(grad.astype(F32) * early), axis=1)
            )
            late_ref[slot, i] = both[:, :HEAD_DIM] + both[:, HEAD_DIM:]

    n_chain = 2 * n_head
    chain_base = base

    def chain_at(index):
        group, seq = lax.div(index, 2), lax.rem(index, 2)
        return lax.rem(group - z + n_head, n_head), seq, decay_of(2 * group + core)

    def chain_copy(index, slot, seq):
        return pltpu.make_async_remote_copy(
            src_ref=message_ref.at[slot, seq],
            dst_ref=pending_ref.at[lax.rem(slot + 1, n_head), seq],
            send_sem=sends.at[chain_base + index],
            recv_sem=receives.at[chain_base + index],
            device_id=place.down,
            device_id_type=MESH,
        )

    @pl.loop(0, n_chain)
    def _(index):
        slot, seq, decay = chain_at(index)

        @pl.when(z < last)
        def _():
            copies.receive(pending_ref.at[slot, seq], chain_base + index, place.up)

        @pl.when(z == last)
        def _():
            pending_ref[slot, seq] = jnp.zeros(pending_ref.shape[2:], BF)

        @pl.when(z > 0)
        def _():
            total = jnp.exp(-decay * rows) * pending_ref[slot, seq].astype(F32)
            for n in range(spans):
                total += jnp.exp(-decay * (n * SPAN)) * late_ref[slot, seq * spans + n]
            message_ref[slot, seq] = total.astype(BF)
            chain_copy(index, slot, seq).start()

    feed.end(order[1])
    feed.middle(order[3])

    offsets = iota((SPAN, SPAN), 0) - iota((SPAN, SPAN), 1)

    def back_slot(slot):
        turn = slot % 2
        decay = slot_decay(slot)
        mask = jnp.where(offsets >= 0.0, jnp.exp(-decay * jnp.maximum(offsets, 0.0)), 0.0)
        places = iota((SPAN, 1), 0)
        early = jnp.exp(-decay * (places + 1.0))
        late = jnp.exp(-decay * (SPAN - 1.0 - places))
        span_decay = jnp.exp(-decay * SPAN)
        rates_ref[slot] = jnp.zeros((8, HEAD_DIM), F32)

        @pl.loop(0, 2)
        def _(seq):
            for n in range(spans):
                i = seq * spans + n
                at, here = tile(i), pl.ds(n * SPAN, SPAN)
                state = carry_ref[slot, seq].astype(F32)
                if n == 1:
                    state = span_decay * state + fresh_ref[slot, seq]
                later = pending_ref[slot, seq].astype(F32)
                if n == 0:
                    later = span_decay * later + late_ref[slot, seq * spans + 1]
                q, k, v, grad = q_at(slot, at), k_at(slot, at), v_at(slot, at), ga_ref[slot, at, :]
                weights = (dot_last(q, k) * mask).astype(BF)
                scores = (dot_last(grad, v) * mask).astype(BF)
                state_high, state_low = split(state)
                grad_query = dot(scores, k)
                grad_query += early * (dot_last(grad, state_high) + dot_last(grad, state_low))
                later_high, later_low = split(later)
                grad_keys = dot_first(scores, q)
                grad_keys += late * (dot_last(v, later_high) + dot_last(v, later_low))
                both = dot(k, jnp.concatenate([later_high, later_low], axis=1))
                grad_values = dot_first(weights, grad)
                grad_values += late * (both[:, :HEAD_DIM] + both[:, HEAD_DIM:])
                pre_at(slot, at, 2)[...] = grad_values.astype(BF)
                cosine, sine = cos_ref[turn, here, :], sin_ref[turn, here, :]
                angles = jnp.zeros((SPAN, HEAD_DIM), F32)
                for part, turned in enumerate((grad_query, grad_keys)):
                    value = qk_pre_ref[turn, at, pl.ds(part * HEAD_DIM, HEAD_DIM)]
                    by_cos, by_sin = turned[:, :HEAD_DIM], turned[:, HEAD_DIM:]
                    gate = 1.0 / (1.0 + jnp.exp(-value))
                    act = by_cos * cosine + by_sin * sine
                    angles += value * gate * (by_sin * cosine - by_cos * sine)
                    act = act * gate * (1.0 + value * (1.0 - gate))
                    pre_at(slot, at, part)[...] = act.astype(BF)
                steps = (z * rows + n * SPAN).astype(F32) + places
                rates_ref[slot, pl.ds(0, 1), :] += jnp.sum(steps * angles, axis=0, keepdims=True)

    for slot in range(n_head):
        for load in slot_loads[slot]:
            load.wait()
        back_slot(slot)
        if slot + 2 < n_head:
            slot_loads[slot + 2] = late_loads(slot + 2)
        lanes = pl.ds((slot % 2) * 4 * HEAD_DIM, 4 * HEAD_DIM)
        holder = t_ref.at[2] if slot < 2 else wf_ref.at[0]
        copies.move(holder.at[pl.ds(0, 2 * rows), lanes], pre_out.at[slot], later=True)
        if slot == 1:
            feed.end(order[2])
    feed.end(order[3])
    feed.total()
    copies.move(g_view(0, 0, None), feed_out, later=True)
    copies.move(rates_ref, rates_out, later=True)

    @pl.when(z > 0)
    def _():
        @pl.loop(0, n_chain)
        def _(index):
            slot, seq, _ = chain_at(index)
            chain_copy(index, slot, seq).wait_send()

    copies.finish()


def middle(n_head, wf, nm, og, hidden, wo, pre, query, keys, values, attn, cos, sin, fresh, carry, scale):
    rows, width = hidden.shape
    units = wf.shape[1] // n_head
    quarter = width // 4
    tall = 2 * rows
    halves = (n_head, 3, units // 2, quarter)
    wholes = (n_head, 3, units, quarter)
    buffers = [
        (wf.shape, BF),
        (wf.shape, BF),
        (wf.shape, BF),
        (halves, BF),
        (halves, BF),
        (wholes, BF),
        (wholes, BF),
        ((n_head - 1,) + wholes[1:], BF),
        ((tall, width), BF),
        ((tall, width), BF),
        ((rows, width), F32),
        ((rows, width), F32),
        ((rows, width), BF),
        ((rows, width), BF),
        ((rows, width), BF),
        (wo.shape, BF),
        ((n_head, tall, HEAD_DIM), F32),
        ((n_head, tall, HEAD_DIM), F32),
        ((n_head, tall, HEAD_DIM), BF),
        ((2, tall, 2 * HEAD_DIM), F32),
        ((2, rows, HEAD_DIM), F32),
        ((2, rows, HEAD_DIM), F32),
        ((n_head, 2, 2 * HEAD_DIM, HEAD_DIM), F32),
        ((n_head, 2, 2 * HEAD_DIM, HEAD_DIM), BF),
        ((n_head, tall // SPAN, 2 * HEAD_DIM, HEAD_DIM), F32),
        ((n_head, 2, 2 * HEAD_DIM, HEAD_DIM), BF),
        ((n_head, 2, 2 * HEAD_DIM, HEAD_DIM), BF),
        ((tall, HEAD_DIM), F32),
        ((tall, HEAD_DIM), F32),
        ((tall, HEAD_DIM), F32),
        ((n_head, 8, HEAD_DIM), F32),
    ]
    outs = [
        (wholes[1:], BF),
        ((rows, width), BF),
        ((rows, width), F32),
        ((tall, width), BF),
        ((n_head, tall, 4 * HEAD_DIM), BF),
        ((n_head, 8, HEAD_DIM), F32),
    ]
    n_sems = PER_SCATTER + 3 + 2 + 2 * n_head
    return pl.pallas_call(
        functools.partial(middle_kernel, n_head),
        out_shape=[jax.ShapeDtypeStruct(*out) for out in outs],
        in_specs=[ANY] * 15,
        out_specs=[ANY] * len(outs),
        scratch_shapes=[pltpu.VMEM(*b) for b in buffers]
        + [
            pltpu.SemaphoreType.DMA((n_sems,)),
            pltpu.SemaphoreType.DMA((n_sems,)),
            pltpu.SemaphoreType.DMA((64,)),
        ],
        compiler_params=pltpu.CompilerParams(
            collective_id=1, has_side_effects=True, vmem_limit_bytes=63 << 20
        ),
        name="middle",
    )(wf, nm, og, hidden, wo, pre, query, keys, values, attn, cos, sin, fresh, carry, scale)


class Share:
    def __init__(self, place, copies, view, base):
        self.place, self.copies, self.view, self.base = place, copies, view, base

    def hand_over(self, q):
        at = self.base + 4 + q
        self.copies.send(self.view(0, q, None), self.view(1, q, None), at, at, self.place.across)

    def begin(self):
        place, copies, at = self.place, self.copies, self.base
        copies.send(self.view(0, 0, None), self.view(0, 1, None), at, at, place.by_x)
        copies.send(self.view(0, 0, None), self.view(0, 2, None), at + 1, at + 1, place.by_y)
        self.hand_over(0)

    def spread(self):
        place, copies, at = self.place, self.copies, self.base
        copies.receive(self.view(0, 1, None), at, place.by_x)
        copies.send(self.view(0, 1, 0), self.view(0, 3, 0), at + 2, at + 2, place.by_y)
        copies.receive(self.view(0, 2, None), at + 1, place.by_y)
        copies.send(self.view(0, 2, 1), self.view(0, 3, 1), at + 3, at + 3, place.by_x)
        self.hand_over(1)
        self.hand_over(2)

    def complete(self):
        place, copies, at = self.place, self.copies, self.base
        copies.receive(self.view(0, 3, 0), at + 2, place.by_y)
        copies.receive(self.view(0, 3, 1), at + 3, place.by_x)
        self.hand_over(3)

    def other_side(self):
        for q in range(4):
            self.copies.receive(self.view(1, q, None), self.base + 4 + q, self.place.across)


PER_SHARE = 8


def last_kernel(
    n_head,
    feed_piece,
    tokens,
    nin,
    branch,
    gated,
    pre,
    wa,
    hidden_grad,
    rates,
    input_out,
    feed_out,
    attn_out,
    down_out,
    rates_out,
    feed_ref,
    attn_ref,
    down_ref,
    ga_ref,
    a_far_x,
    a_far_y,
    a_near_x,
    a_near_y,
    a_high,
    gd_ref,
    d_far_x,
    d_far_y,
    d_near_x,
    d_near_y,
    d_high,
    nin_ref,
    branch_ref,
    gated_ref,
    pre_ref,
    wa_ref,
    x_ref,
    grad_ref,
    send_ref,
    got_ref,
    rates_high,
    rates_sum,
    rates_got,
    rates_both,
    sends,
    receives,
    locals_,
):
    rows, width = tokens.shape
    quarter = width // 4
    units = feed_piece.shape[1]
    spans = rows // SPAN
    place = Place(n_head)
    copies = Copies(sends, receives, locals_)
    order = (2, 1, 3, 0)

    load_feed = copies.move(feed_piece, feed_ref.at[0, :, :, pl.ds(0, quarter)])
    load_nin = copies.move(nin, nin_ref)
    load_pre = {slot: copies.move(pre.at[slot], pre_ref.at[slot]) for slot in order}
    load_gated = copies.move(gated, gated_ref)
    load_branch = copies.move(branch, branch_ref)
    late_loads = [copies.move(wa, wa_ref), copies.move(hidden_grad, grad_ref)]
    for q in range(4):
        far = pl.ds(pl.multiple_of(place.at[q] * quarter, quarter), quarter)
        late_loads.append(copies.move(tokens.at[:, far], x_ref.at[:, pl.ds(q * quarter, quarter)]))
    place.greet()

    def tile(i):
        return pl.ds(pl.multiple_of(i * SPAN, SPAN), SPAN)

    def dot_last(left, right):
        return lax.dot_general(left, right, (((1,), (1,)), ((), ())), preferred_element_type=F32)

    def dot_first(left, right):
        return lax.dot_general(left, right, (((0,), (0,)), ((), ())), preferred_element_type=F32)

    def part(start, half, size):
        if half is None:
            return pl.ds(start, size)
        return pl.ds(start + half * (size // 2), size // 2)

    def feed_view(side, q, half):
        return feed_ref.at[side, :, part(0, half, units), pl.ds(q * quarter, quarter)]

    def attn_view(side, q, half):
        return attn_ref.at[side, part(q * quarter, half, quarter), :]

    def down_view(side, q, half):
        return down_ref.at[side, part(0, half, HEAD_DIM), pl.ds(q * quarter, quarter)]

    def ga_view(slot, q, half):
        return ga_ref.at[slot, part(q * quarter, half, quarter), :]

    def gd_view(slot, q, half):
        return gd_ref.at[slot, part(0, half, HEAD_DIM), pl.ds(q * quarter, quarter)]

    attn = Scatter(place, copies, ga_view, a_far_x, a_far_y, a_near_x, a_near_y, a_high, 0)
    down = Scatter(place, copies, gd_view, d_far_x, d_far_y, d_near_x, d_near_y, d_high, PER_SCATTER)
    base = 2 * PER_SCATTER
    feed_share = Share(place, copies, feed_view, base)
    attn_share = Share(place, copies, attn_view, base + PER_SHARE)
    down_share = Share(place, copies, down_view, base + 2 * PER_SHARE)
    base += 3 * PER_SHARE

    load_feed.wait()
    feed_share.begin()
    for slot in range(1, n_head):
        into = rates_high.at[slot - 1]
        copies.send(rates.at[slot], into, base + slot, base + slot, place.above(slot))
    load_nin.wait()

    def slot_grads(slot):
        load_pre[slot].wait()

        @pl.loop(0, 4)
        def _(i):
            at = tile(3 - i)
            ga_ref[slot, at, :] = dot_first(nin_ref[:, at], pre_ref[slot]).astype(BF)

        lanes = pl.ds(slot * HEAD_DIM, HEAD_DIM)
        gd_ref[slot] = dot_first(gated_ref[:, lanes], branch_ref[...]).astype(BF)

    def begin(slot):
        attn.begin(slot)
        down.begin(slot)

    def middle_step(slot):
        attn.middle(slot)
        down.middle(slot)

    def end(slot):
        attn.end(slot)
        down.end(slot)

    load_gated.wait()
    load_branch.wait()
    slot_grads(order[0])
    begin(order[0])
    slot_grads(order[1])
    begin(order[1])
    slot_grads(order[2])
    begin(order[2])
    middle_step(order[0])
    slot_grads(order[3])
    begin(order[3])
    for load in late_loads:
        load.wait()

    def grad_in(at):
        total = dot_last(pre_ref[0, at, :], wa_ref[0])
        for slot in range(1, n_head):
            total += dot_last(pre_ref[slot, at, :], wa_ref[slot])
        return total

    @pl.loop(0, spans)
    def _(i):
        send_ref[tile(i), :] = grad_in(tile(spans + i)).astype(BF)

    copies.send(send_ref, got_ref, base, base, place.across)
    middle_step(order[1])

    total = rates[0]
    for slot in range(1, n_head):
        copies.receive(rates_high.at[slot - 1], base + slot, place.up)
        total += rates_high[slot - 1]
    base += n_head
    rates_sum[0] = total
    copies.send(rates_sum.at[0], rates_got.at[0], base, base, place.by_x)

    end(order[0])
    middle_step(order[2])
    copies.receive(rates_got.at[0], base, place.by_x)
    rates_sum[1] = total + rates_got[0]
    copies.send(rates_sum.at[1], rates_got.at[1], base + 1, base + 1, place.by_y)

    copies.receive(got_ref, base - n_head, place.across)

    @pl.loop(0, spans)
    def _(i):
        at = tile(i)
        values = x_ref[at, :].astype(F32)
        norm = lax.rsqrt(jnp.mean(values * values, axis=-1, keepdims=True) + EPSILON)
        normed = values * norm
        grad = grad_in(at) + got_ref[at, :].astype(F32)
        mean = jnp.mean(grad * normed, axis=-1, keepdims=True)
        grad_ref[at, :] += norm * (grad - normed * mean)

    for q in range(4):
        far = pl.ds(pl.multiple_of(place.at[q] * quarter, quarter), quarter)
        src = grad_ref.at[:, pl.ds(q * quarter, quarter)]
        copies.move(src, input_out.at[:, far], later=True)
    end(order[1])
    middle_step(order[3])
    copies.receive(rates_got.at[1], base + 1, place.by_y)
    rates_both[0] = rates_sum[1] + rates_got[1]
    copies.send(rates_both.at[0], rates_both.at[1], base + 2, base + 2, place.across)
    feed_share.spread()
    end(order[2])
    end(order[3])
    attn.total(attn_view(0, 0, None))
    attn_share.begin()
    down.total(down_view(0, 0, None))
    down_share.begin()
    copies.receive(rates_both.at[1], base + 2, place.across)
    sides = (place.core, 1 - place.core)
    for side in range(2):
        copies.move(rates_both.at[side], rates_out.at[sides[side]], later=True)

    def write(ref, out, side, q):
        far = pl.ds(pl.multiple_of(place.at[q] * quarter, quarter), quarter)
        near = pl.ds(q * quarter, quarter)
        if ref is attn_ref:
            src, dst = ref.at[side, near], out.at[sides[side], far]
        elif ref is down_ref:
            src, dst = ref.at[side, :, near], out.at[sides[side], :, far]
        else:
            src, dst = ref.at[side, :, :, near], out.at[sides[side], :, :, far]
        copies.move(src, dst, later=True)

    feed_share.complete()
    for q in range(4):
        write(feed_ref, feed_out, 0, q)
    feed_share.other_side()
    for q in range(4):
        write(feed_ref, feed_out, 1, q)
    attn_share.spread()
    down_share.spread()
    for q in range(3):
        write(attn_ref, attn_out, 0, q)
        write(down_ref, down_out, 0, q)
    attn_share.complete()
    down_share.complete()
    write(attn_ref, attn_out, 0, 3)
    write(down_ref, down_out, 0, 3)
    attn_share.other_side()
    down_share.other_side()
    for q in range(4):
        write(attn_ref, attn_out, 1, q)
        write(down_ref, down_out, 1, q)
    copies.finish()


def last(n_head, feed_piece, tokens, nin, branch, gated, pre, wa, hidden_grad, rates):
    rows, width = tokens.shape
    _, units, quarter = feed_piece.shape
    tall = 2 * rows

    def scatter_buffers(shape, halved):
        half = tuple(n // 2 if i == halved else n for i, n in enumerate(shape))
        return [
            ((n_head,) + half, BF),
            ((n_head,) + half, BF),
            ((n_head,) + shape, BF),
            ((n_head,) + shape, BF),
            ((n_head - 1,) + shape, BF),
        ]

    outs = [
        ((rows, width), F32),
        ((2, 3, units, width), BF),
        ((2, width, 4 * HEAD_DIM), BF),
        ((2, HEAD_DIM, width), BF),
        ((2, 8, HEAD_DIM), F32),
    ]
    buffers = [
        outs[1],
        outs[2],
        outs[3],
        ((n_head, width, 4 * HEAD_DIM), BF),
        *scatter_buffers((quarter, 4 * HEAD_DIM), 0),
        ((n_head, HEAD_DIM, width), BF),
        *scatter_buffers((HEAD_DIM, quarter), 0),
        ((tall, width), BF),
        ((tall, width), BF),
        (gated.shape, BF),
        (pre.shape, BF),
        (wa.shape, BF),
        ((rows, width), BF),
        ((rows, width), F32),
        ((rows, width), BF),
        ((rows, width), BF),
        ((n_head - 1, 8, HEAD_DIM), F32),
        ((2, 8, HEAD_DIM), F32),
        ((2, 8, HEAD_DIM), F32),
        ((2, 8, HEAD_DIM), F32),
    ]
    n_sems = 2 * PER_SCATTER + 3 * PER_SHARE + n_head + 3
    return pl.pallas_call(
        functools.partial(last_kernel, n_head),
        out_shape=[jax.ShapeDtypeStruct(*out) for out in outs],
        in_specs=[ANY] * 8 + [IN_VMEM],
        out_specs=[ANY] * len(outs),
        scratch_shapes=[pltpu.VMEM(*b) for b in buffers]
        + [
            pltpu.SemaphoreType.DMA((n_sems,)),
            pltpu.SemaphoreType.DMA((n_sems,)),
            pltpu.SemaphoreType.DMA((64,)),
        ],
        compiler_params=pltpu.CompilerParams(
            collective_id=2, has_side_effects=True, vmem_limit_bytes=60 << 20
        ),
        name="last",
    )(feed_piece, tokens, nin, branch, gated, pre, wa, hidden_grad, rates)


def make(n_dp, n_head):
    def on_device(
        tokens,
        attn_query,
        attn_key,
        attn_value,
        attn_gate,
        attn_out,
        rotation_rates,
        ffn_left,
        ffn_right,
        ffn_down,
        out_grad,
    ):
        ffn = jnp.stack([ffn_left.T, ffn_right.T, ffn_down])
        rates_in = jnp.pad(rotation_rates.reshape(2, HEAD_DIM), ((0, 6), (0, 0)))
        (
            attn_weights,
            out_w,
            ffn_all,
            gathered_in,
            pre,
            query,
            keys,
            values,
            attn,
            cosines,
            sines,
            fresh,
            carry,
            scale_attn,
            gated,
            hidden,
            gathered_mid,
            grad_rows,
        ) = forward(
            n_head,
            tokens,
            out_grad,
            attn_query,
            attn_key,
            attn_value,
            attn_gate,
            attn_out,
            ffn,
            rates_in,
        )
        feed_piece, block_out, grad_hidden, branch_rows, grad_pre, rates_grad = middle(
            n_head,
            ffn_all,
            gathered_mid,
            grad_rows,
            hidden,
            out_w,
            pre,
            query,
            keys,
            values,
            attn,
            cosines,
            sines,
            fresh,
            carry,
            scale_attn,
        )
        input_grad, feed_grads, attn_grads, down_grads, rates_grad = last(
            n_head,
            feed_piece,
            tokens,
            gathered_in,
            branch_rows,
            gated,
            grad_pre,
            attn_weights,
            grad_hidden,
            rates_grad,
        )

        def over_rest(grad):
            if n_dp == 8:
                return grad
            groups = [[i + 8 * j for j in range(n_dp // 8)] for i in range(8)]
            return lax.psum(grad, "dp", axis_index_groups=groups)

        def projection(i):
            halves = attn_grads[:, :, i * HEAD_DIM : (i + 1) * HEAD_DIM].astype(F32)
            return over_rest(jnp.concatenate([halves[0], halves[1]], axis=1))

        def feed(i):
            return feed_grads[:, i].astype(F32).reshape(-1, tokens.shape[1])

        return (
            block_out,
            input_grad,
            projection(0),
            projection(1),
            projection(2),
            projection(3),
            over_rest(down_grads.astype(F32).reshape(-1, tokens.shape[1])),
            over_rest(rates_grad[:, 0].reshape(-1)),
            over_rest(feed(0).T),
            over_rest(feed(1).T),
            over_rest(feed(2)),
        )

    return on_device


def solution(mesh):
    weights = (P(None, "head"),) * 4 + (P("head", None), P("head")) + (P(None, "head"),) * 2
    weights = weights + (P("head", None),)
    rows = P(("dp", "head"), None)
    return jax.shard_map(
        make(mesh.shape["dp"], mesh.shape["head"]),
        mesh=mesh,
        in_specs=(rows,) + weights + (rows,),
        out_specs=(rows, rows) + weights,
        check_vma=False,
    )
```

```python
import functools

import jax
import jax.numpy as jnp
from jax import lax
from jax.experimental import pallas as pl
from jax.experimental.pallas import tpu as pltpu
from jax.sharding import PartitionSpec as P

HEADS = 8
HEAD_DIM = 128
SPAN = 256
EPSILON = 1e-06
BF = jnp.bfloat16
F32 = jnp.float32


MESH = pl.DeviceIdType.MESH
ANY = pl.BlockSpec(memory_space=pl.ANY)
IN_VMEM = pl.BlockSpec(memory_space=pltpu.VMEM)


def split(value):
    high = value.astype(BF)
    return high, (value - high.astype(F32)).astype(BF)


class Place:
    def __init__(self, n_head):
        self.n_head = n_head
        dp = lax.axis_index("dp")
        self.z = lax.axis_index("head")
        self.core = lax.rem(dp, 2)
        x = lax.rem(lax.div(dp, 2), 2)
        y = lax.rem(lax.div(dp, 4), 2)
        self.plane = x + 2 * y
        self.at = [self.plane, self.plane + 1 - 2 * x, self.plane + 2 - 4 * y, 3 - self.plane]
        self.across = {"dp": dp + 1 - 2 * self.core}
        self.by_x = {"dp": dp + 2 - 4 * x}
        self.by_y = {"dp": dp + 4 - 8 * y}
        self.up = {"head": lax.rem(self.z + 1, n_head)}
        self.down = {"head": lax.rem(self.z + n_head - 1, n_head)}

    def above(self, step):
        return {"head": lax.rem(self.z + step, self.n_head)}

    def below(self, step):
        return {"head": lax.rem(self.z + self.n_head - step, self.n_head)}

    def greet(self):
        barrier = pltpu.get_barrier_semaphore()
        others = [self.across, self.by_x, self.by_y]
        others += [self.below(step) for step in range(1, self.n_head)]
        for other in others:
            pl.semaphore_signal(barrier, inc=1, device_id=other, device_id_type=MESH)
        pl.semaphore_wait(barrier, len(others))


class Copies:
    def __init__(self, sends, receives, locals_):
        self.sends, self.receives, self.locals = sends, receives, locals_
        self.pending = []
        self.started = {}
        self.n_local = 0

    def send(self, src, dst, out, into, device, when=None):
        copy = pltpu.make_async_remote_copy(
            src_ref=src,
            dst_ref=dst,
            send_sem=self.sends.at[out],
            recv_sem=self.receives.at[into],
            device_id=device,
            device_id_type=MESH,
        )
        if when is None:
            copy.start()
            self.pending.append(copy.wait_send)
            if isinstance(out, int):
                self.started[out] = copy.wait_send
        else:
            pl.when(when)(copy.start)
            self.pending.append(lambda: pl.when(when)(copy.wait_send))

    def receive(self, dst, into, device):
        pltpu.make_async_remote_copy(
            src_ref=dst,
            dst_ref=dst,
            send_sem=self.sends.at[0],
            recv_sem=self.receives.at[into],
            device_id=device,
            device_id_type=MESH,
        ).wait_recv()

    def move(self, src, dst, later=False):
        copy = pltpu.make_async_copy(src, dst, self.locals.at[self.n_local])
        self.n_local += 1
        copy.start()
        if later:
            self.pending.append(copy.wait)
        return copy

    def sent(self, out):
        wait = self.started.pop(out)
        self.pending.remove(wait)
        wait()

    def finish(self):
        for wait in self.pending:
            wait()


class Gather:
    def __init__(self, place, copies, view, base):
        self.place, self.copies, self.view, self.base = place, copies, view, base

    def begin(self):
        place, z = self.place, self.place.z
        own = self.view(0, 0, None)
        last = place.n_head - 1
        self.copies.send(
            own, self.view(last, 0, None), self.base, self.base + last, place.up, when=z < last
        )
        self.copies.send(own, self.view(1, 0, None), self.base + 1, self.base + 1, place.down, when=z > 0)

    def arrived(self, slot, when=True):
        place, copies, z, base = self.place, self.copies, self.place.z, self.base
        last = place.n_head - 1
        if when is True:
            copies.receive(self.view(slot, 0, None), base + slot, place.up)
        else:
            pl.when(when)(lambda: copies.receive(self.view(slot, 0, None), base + slot, place.up))
        from_up = z + slot <= last
        piece = self.view(slot, 0, None)
        down = jnp.logical_and(jnp.logical_and(from_up, z > 0), when)
        up = jnp.logical_and(jnp.logical_not(from_up), z < last)
        up = jnp.logical_and(up, when)
        always = None if when is True else when
        after = jnp.minimum(slot + 1, last)
        before = jnp.maximum(slot - 1, 1)
        copies.send(piece, self.view(after, 0, None), base + 1 + slot, base + after, place.down, when=down)
        copies.send(piece, self.view(before, 0, None), base + 1 + slot, base + before, place.up, when=up)
        at = base + 4 * slot + 4
        copies.send(piece, self.view(slot, 1, None), at, at, place.by_x, when=always)
        copies.send(piece, self.view(slot, 2, None), at + 1, at + 1, place.by_y, when=always)

    def spread(self, slot):
        place, copies = self.place, self.copies
        at = self.base + 4 * slot + 4
        copies.receive(self.view(slot, 1, None), at, place.by_x)
        copies.send(self.view(slot, 1, 0), self.view(slot, 3, 0), at + 2, at + 2, place.by_y)
        copies.receive(self.view(slot, 2, None), at + 1, place.by_y)
        copies.send(self.view(slot, 2, 1), self.view(slot, 3, 1), at + 3, at + 3, place.by_x)

    def complete(self, slot):
        place, copies = self.place, self.copies
        at = self.base + 4 * slot + 4
        copies.receive(self.view(slot, 3, 0), at + 2, place.by_y)
        copies.receive(self.view(slot, 3, 1), at + 3, place.by_x)


PER_GATHER = 24


def forward_kernel(
    n_head,
    tokens,
    out_grad,
    wq,
    wk,
    wv,
    wg,
    wo,
    ffn_left,
    ffn_right,
    ffn_down,
    rates,
    wa_out,
    wo_out,
    wf_out,
    nin_out,
    pre_out,
    q_out,
    k_out,
    v_out,
    attn_out,
    cos_out,
    sin_out,
    fresh_out,
    carry_out,
    scale_out,
    gated_out,
    hidden_out,
    nm_out,
    og_out,
    wa_ref,
    wo_ref,
    wf_ref,
    x_ref,
    nin_ref,
    pre_ref,
    q_ref,
    k_ref,
    v_ref,
    attn_ref,
    cos_ref,
    sin_ref,
    fresh_ref,
    carry_ref,
    message_ref,
    squares_ref,
    other_squares_ref,
    gated_ref,
    branch_ref,
    other_branch_ref,
    hidden_ref,
    nm_ref,
    rates_ref,
    og_ref,
    sends,
    receives,
    locals_,
):
    rows, width = tokens.shape
    quarter = width // 4
    units = ffn_down.shape[0] // 2
    tiles = 2 * rows // SPAN
    place = Place(n_head)
    z, core = place.z, place.core
    copies = Copies(sends, receives, locals_)

    def columns(start, size):
        return pl.ds(pl.multiple_of(start, size), size)

    own_loads = []
    for q in range(4):
        far = columns(place.at[q] * quarter, quarter)
        near = pl.ds(q * quarter, quarter)
        loads = []
        for i, w in enumerate((wq, wk, wv, wg)):
            src = w.at[far, columns(core * HEAD_DIM, HEAD_DIM)]
            loads.append(copies.move(src, wa_ref.at[0, near, pl.ds(i * HEAD_DIM, HEAD_DIM)]))
        src = wo.at[columns(core * HEAD_DIM, HEAD_DIM), far]
        loads.append(copies.move(src, wo_ref.at[pl.ds(0, HEAD_DIM), near]))
        for i, w in enumerate((ffn_left, ffn_right, ffn_down)):
            src = w.at[pl.ds(pl.multiple_of(core * units, 16), units), far]
            loads.append(copies.move(src, wf_ref.at[i, pl.ds(0, units), near]))
        own_loads.append(loads)
    token_loads = [
        copies.move(
            tokens.at[:, columns(place.at[q] * quarter, quarter)],
            x_ref.at[:, pl.ds(q * quarter, quarter)],
        )
        for q in range(4)
    ]
    grad_loads = [
        copies.move(
            out_grad.at[:, columns(place.at[q] * quarter, quarter)],
            og_ref.at[pl.ds(0, rows), pl.ds(q * quarter, quarter)],
        )
        for q in range(4)
    ]
    place.greet()

    def half_rows(half, size):
        return pl.ds(0, size) if half is None else pl.ds(half * (size // 2), size // 2)

    def wa_view(slot, q, half):
        at = half_rows(half, quarter)
        return wa_ref.at[slot, pl.ds(q * quarter + at.start, at.size), :]

    def wo_view(slot, q, half):
        at = half_rows(half, HEAD_DIM)
        return wo_ref.at[
            pl.ds(pl.multiple_of(slot * HEAD_DIM + at.start, HEAD_DIM // 2), at.size),
            pl.ds(q * quarter, quarter),
        ]

    def wf_view(slot, q, half):
        at = half_rows(half, units)
        return wf_ref.at[
            :,
            pl.ds(pl.multiple_of(slot * units + at.start, 16), at.size),
            pl.ds(q * quarter, quarter),
        ]

    attn_in = Gather(place, copies, wa_view, 0)
    attn_down = Gather(place, copies, wo_view, PER_GATHER)
    feed = Gather(place, copies, wf_view, 2 * PER_GATHER)
    base = 3 * PER_GATHER
    for load in own_loads[0][:4]:
        load.wait()
    attn_in.begin()
    own_loads[0][4].wait()
    attn_down.begin()
    for step in range(1, n_head):
        copies.send(rates, rates_ref.at[step], base + step, base + step, place.below(step))
    rates_ref[0] = rates[...]

    for load in token_loads:
        load.wait()

    def norm_rows(values):
        mean = jnp.mean(values * values, axis=-1, keepdims=True)
        return values * lax.rsqrt(mean + EPSILON)

    @pl.loop(0, rows // 128)
    def _(i):
        at = pl.ds(pl.multiple_of(i * 128, 128), 128)
        nin_ref[at, :] = norm_rows(x_ref[at, :].astype(F32)).astype(BF)

    base += 4
    for load in grad_loads:
        load.wait()
    og_other = og_ref.at[pl.ds(rows, rows)]
    copies.send(og_ref.at[pl.ds(0, rows)], og_other, base, base, place.across)
    base += 1
    nin_other = nin_ref.at[pl.ds(rows, rows)]
    copies.send(nin_ref.at[pl.ds(0, rows)], nin_other, base, base, place.across)
    for q, loads in enumerate(own_loads):
        for load in loads[5:] if q == 0 else loads:
            load.wait()
    for step in range(1, n_head):
        copies.receive(rates_ref.at[step], base - 5 + step, place.up)
    copies.receive(nin_other, base, place.across)
    copies.move(nin_ref, nin_out, later=True)
    copies.receive(og_other, base - 1, place.across)
    copies.move(og_ref, og_out, later=True)

    def decay_of(head):
        exponent = jnp.full((1, 1), -8.0 / HEADS, F32) * (head + 1).astype(F32)
        return jnp.exp2(exponent)

    def tile(i):
        return pl.ds(pl.multiple_of(i * SPAN, SPAN), SPAN)

    def iota(shape, axis):
        return lax.broadcasted_iota(jnp.int32, shape, axis).astype(F32)

    def dot(left, right):
        return jnp.dot(left, right, preferred_element_type=F32)

    def slot_compute(slot):
        head = 2 * lax.rem(z + slot, n_head) + core
        decay = decay_of(head)
        rate = rates_ref[slot, :, columns(core * HEAD_DIM, HEAD_DIM)]
        coarse = (z * rows).astype(F32) + 32.0 * iota((rows // 32, HEAD_DIM), 0)
        coarse = coarse * rate
        fine = iota((32, HEAD_DIM), 0) * rate
        cos_a, sin_a = jnp.cos(coarse), jnp.sin(coarse)
        cos_b, sin_b = jnp.cos(fine), jnp.sin(fine)
        for a in range(rows // 32):
            cos_row, sin_row = cos_a[a : a + 1], sin_a[a : a + 1]
            cos_ref[slot, pl.ds(a * 32, 32), :] = cos_row * cos_b - sin_row * sin_b
            sin_ref[slot, pl.ds(a * 32, 32), :] = sin_row * cos_b + cos_row * sin_b
        offsets = iota((SPAN, SPAN), 0) - iota((SPAN, SPAN), 1)
        mask = jnp.where(offsets >= 0.0, jnp.exp(-decay * jnp.maximum(offsets, 0.0)), 0.0)
        late = jnp.exp(-decay * (SPAN - 1.0 - iota((SPAN, HEAD_DIM), 0)))

        @pl.loop(0, tiles)
        def _(i):
            at = tile(i)
            pre = dot(nin_ref[at, :], wa_ref[slot])
            pre_ref[slot, at, :] = pre
            here = tile(lax.rem(i, rows // SPAN))
            cosines, sines = cos_ref[slot, here, :], sin_ref[slot, here, :]

            def rotate(values):
                activated = values / (1.0 + jnp.exp(-values))
                turned = jnp.concatenate([activated * cosines, activated * sines], axis=1)
                return turned.astype(BF)

            query = rotate(pre[:, :HEAD_DIM])
            keys = rotate(pre[:, HEAD_DIM : 2 * HEAD_DIM])
            value = pre[:, 2 * HEAD_DIM : 3 * HEAD_DIM].astype(BF)
            q_ref[slot, at, :] = query
            k_ref[slot, at, :] = keys
            v_ref[slot, at, :] = value
            scores = lax.dot_general(
                query, keys, (((1,), (1,)), ((), ())), preferred_element_type=F32
            )
            weights = (scores * mask).astype(BF)
            attn_ref[slot, at, :] = dot(weights, value)
            high, low = split(value.astype(F32) * late)
            both = lax.dot_general(
                keys,
                jnp.concatenate([high, low], axis=1),
                (((0,), (0,)), ((), ())),
                preferred_element_type=F32,
            )
            fresh_ref[slot, i] = both[:, :HEAD_DIM] + both[:, HEAD_DIM:]

        for ref, out in (
            (wa_ref, wa_out),
            (pre_ref, pre_out),
            (q_ref, q_out),
            (k_ref, k_out),
            (v_ref, v_out),
            (cos_ref, cos_out),
            (sin_ref, sin_out),
            (fresh_ref, fresh_out),
        ):
            copies.move(ref.at[slot], out.at[slot], later=True)

    last = n_head - 1
    first = 1 + 2 * lax.div(z, last)
    second = 2 + lax.rem(lax.div(z + 1, 2), 2)
    third = 6 - first - second

    attn_in.arrived(first)
    attn_down.arrived(first)
    slot_compute(0)
    attn_in.arrived(second)
    attn_down.arrived(second)
    attn_in.spread(first)
    attn_down.spread(first)
    attn_in.arrived(third)
    attn_down.arrived(third)
    feed.begin()
    attn_in.spread(second)
    attn_down.spread(second)
    attn_in.complete(first)
    slot_compute(first)
    attn_in.spread(third)
    attn_down.spread(third)
    feed.arrived(first)
    attn_in.complete(second)
    slot_compute(second)
    inner = jnp.logical_and(z > 0, z < last)
    feed.arrived(second, inner)
    attn_in.complete(third)
    slot_compute(third)
    base += 1
    chain_base = base
    n_chain = 2 * n_head

    def chain_at(index):
        group, seq = lax.div(index, 2), lax.rem(index, 2)
        return lax.rem(group - z + n_head, n_head), seq, decay_of(2 * group + core)

    def chain_copy(index, slot, seq):
        after = lax.rem(slot + n_head - 1, n_head)
        return pltpu.make_async_remote_copy(
            src_ref=message_ref.at[slot, seq],
            dst_ref=carry_ref.at[after, seq],
            send_sem=sends.at[chain_base + index],
            recv_sem=receives.at[chain_base + index],
            device_id=place.up,
            device_id_type=MESH,
        )

    def hand_on(index, slot, seq, decay):
        total = jnp.exp(-decay * rows) * carry_ref[slot, seq].astype(F32)
        for n in range(rows // SPAN):
            left = rows - (n + 1) * SPAN
            total += jnp.exp(-decay * left) * fresh_ref[slot, seq * (rows // SPAN) + n]
        message_ref[slot, seq] = total.astype(BF)
        chain_copy(index, slot, seq).start()

    @pl.when(z == 0)
    def _():
        @pl.loop(0, n_chain)
        def _(index):
            slot, seq, decay = chain_at(index)
            carry_ref[slot, seq] = jnp.zeros(carry_ref.shape[2:], BF)
            hand_on(index, slot, seq, decay)

    feed.arrived(second, jnp.logical_not(inner))
    feed.spread(first)
    feed.arrived(third)

    @pl.when(z > 0)
    def _():
        @pl.loop(0, n_chain)
        def _(index):
            slot, seq, decay = chain_at(index)
            copies.receive(carry_ref.at[slot, seq], chain_base + index, place.down)
            pl.when(z < last)(lambda: hand_on(index, slot, seq, decay))

    copies.move(carry_ref, carry_out, later=True)
    feed.spread(second)

    def apply(seq):
        mine = pl.ds(seq * rows, rows)
        squares_ref[mine, :] = jnp.zeros((rows, HEAD_DIM), F32)

        @pl.loop(0, n_head)
        def _(slot):
            decay = decay_of(2 * lax.rem(z + slot, n_head) + core)
            early = jnp.exp(-decay * (iota((SPAN, HEAD_DIM), 0) + 1.0))
            state = carry_ref[slot, seq].astype(F32)
            for n in range(rows // SPAN):
                i = seq * (rows // SPAN) + n
                at = pl.ds(i * SPAN, SPAN)
                both = dot(q_ref[slot, at, :], jnp.concatenate(split(state), axis=1))
                attn = attn_ref[slot, at, :]
                attn += early * (both[:, :HEAD_DIM] + both[:, HEAD_DIM:])
                attn_ref[slot, at, :] = attn
                squares_ref[at, :] += jnp.sum(attn * attn, axis=-1, keepdims=True)
                if n + 1 < rows // SPAN:
                    state = jnp.exp(-decay * SPAN) * state + fresh_ref[slot, i]

    def gating(seq):
        for n in range(rows // SPAN):
            at = pl.ds(seq * rows + n * SPAN, SPAN)
            total = squares_ref[at, :] + other_squares_ref[at, :]
            scale = lax.rsqrt(total / width + EPSILON)
            other_squares_ref[at, :] = scale
            for slot in range(n_head):
                gate = pre_ref[slot, at, pl.ds(3 * HEAD_DIM, HEAD_DIM)]
                gated = (attn_ref[slot, at, :] * scale * gate).astype(BF)
                gated_ref[at, pl.ds(slot * HEAD_DIM, HEAD_DIM)] = gated

    base += n_chain
    own, other = pl.ds(0, rows), pl.ds(rows, rows)
    apply(1)
    copies.send(squares_ref.at[other], other_squares_ref.at[own], base, base, place.across)
    apply(0)
    copies.send(squares_ref.at[own], other_squares_ref.at[other], base + 1, base + 1, place.across)
    copies.move(attn_ref, attn_out, later=True)
    for slot in (first, second, third):
        attn_down.complete(slot)
    copies.receive(other_squares_ref.at[other], base + 1, place.across)
    gating(1)
    base += 2
    for n in range(rows // SPAN):
        gated = gated_ref[pl.ds(rows + n * SPAN, SPAN), :]
        branch_ref[pl.ds(n * SPAN, SPAN), :] = dot(gated, wo_ref[...]).astype(BF)
    copies.send(branch_ref, other_branch_ref, base, base, place.across)
    copies.receive(other_squares_ref.at[own], base - 2, place.across)
    gating(0)
    copies.move(other_squares_ref, scale_out, later=True)
    copies.move(gated_ref, gated_out, later=True)
    copies.move(wo_ref, wo_out, later=True)
    feed.spread(third)

    @pl.loop(0, rows // SPAN)
    def _(i):
        at = tile(i)
        hidden_ref[at, :] = x_ref[at, :].astype(F32) + dot(gated_ref[at, :], wo_ref[...])

    copies.receive(other_branch_ref, base, place.across)

    @pl.loop(0, rows // 128)
    def _(i):
        at = pl.ds(pl.multiple_of(i * 128, 128), 128)
        hidden = hidden_ref[at, :] + other_branch_ref[at, :].astype(F32)
        hidden_ref[at, :] = hidden
        nm_ref[at, :] = norm_rows(hidden).astype(BF)

    copies.send(nm_ref.at[own], nm_ref.at[other], base + 1, base + 1, place.across)
    copies.move(hidden_ref, hidden_out, later=True)
    for slot in (first, second, third):
        feed.complete(slot)
    copies.move(wf_ref, wf_out, later=True)
    copies.receive(nm_ref.at[other], base + 1, place.across)
    copies.move(nm_ref, nm_out, later=True)

    @pl.when(z < last)
    def _():
        @pl.loop(0, n_chain)
        def _(index):
            slot, seq, _ = chain_at(index)
            chain_copy(index, slot, seq).wait_send()

    copies.finish()


def forward(n_head, tokens, out_grad, wq, wk, wv, wg, wo, ffn_left, ffn_right, ffn_down, rates):
    rows, width = tokens.shape
    units = ffn_down.shape[0] // 2
    tall = 2 * rows
    buffers = [
        ((n_head, width, 4 * HEAD_DIM), BF),
        ((n_head * HEAD_DIM, width), BF),
        ((3, n_head * units, width), BF),
        ((rows, width), BF),
        ((tall, width), BF),
        ((n_head, tall, 4 * HEAD_DIM), F32),
        ((n_head, tall, 2 * HEAD_DIM), BF),
        ((n_head, tall, 2 * HEAD_DIM), BF),
        ((n_head, tall, HEAD_DIM), BF),
        ((n_head, tall, HEAD_DIM), F32),
        ((n_head, rows, HEAD_DIM), F32),
        ((n_head, rows, HEAD_DIM), F32),
        ((n_head, tall // SPAN, 2 * HEAD_DIM, HEAD_DIM), F32),
        ((n_head, 2, 2 * HEAD_DIM, HEAD_DIM), BF),
        ((n_head, 2, 2 * HEAD_DIM, HEAD_DIM), BF),
        ((tall, HEAD_DIM), F32),
        ((tall, HEAD_DIM), F32),
        ((tall, n_head * HEAD_DIM), BF),
        ((rows, width), BF),
        ((rows, width), BF),
        ((rows, width), F32),
        ((tall, width), BF),
        ((n_head, 1, 2 * HEAD_DIM), F32),
        ((tall, width), BF),
    ]
    out_of = [0, 1, 2, 4, 5, 6, 7, 8, 9, 10, 11, 12, 13, 16, 17, 20, 21, 23]
    n_sems = 3 * PER_GATHER + 4 + 1 + 1 + 2 * n_head + 2 + 2
    return pl.pallas_call(
        functools.partial(forward_kernel, n_head),
        out_shape=[jax.ShapeDtypeStruct(*buffers[i]) for i in out_of],
        in_specs=[ANY] * 10 + [IN_VMEM],
        out_specs=[ANY] * len(out_of),
        scratch_shapes=[pltpu.VMEM(*b) for b in buffers]
        + [
            pltpu.SemaphoreType.DMA((n_sems,)),
            pltpu.SemaphoreType.DMA((n_sems,)),
            pltpu.SemaphoreType.DMA((96,)),
        ],
        compiler_params=pltpu.CompilerParams(
            collective_id=0, has_side_effects=True, vmem_limit_bytes=62 << 20
        ),
        name="forward",
    )(tokens, out_grad, wq, wk, wv, wg, wo, ffn_left, ffn_right, ffn_down, rates)


class Scatter:
    def __init__(self, place, copies, view, far_x, far_y, near_x, near_y, high, base):
        self.place, self.copies, self.view, self.base = place, copies, view, base
        self.far_x, self.far_y, self.near_x, self.near_y, self.high = far_x, far_y, near_x, near_y, high

    def begin(self, slot):
        place, at = self.place, self.base + 4 * slot
        self.copies.send(self.view(slot, 3, 0), self.far_y.at[slot], at, at, place.by_y)
        self.copies.send(self.view(slot, 3, 1), self.far_x.at[slot], at + 1, at + 1, place.by_x)

    def middle(self, slot):
        place, copies, at = self.place, self.copies, self.base + 4 * slot
        copies.receive(self.far_y.at[slot], at, place.by_y)
        add_to(self.view(slot, 1, 0), self.far_y.at[slot])
        copies.send(self.view(slot, 1, None), self.near_x.at[slot], at + 2, at + 2, place.by_x)
        copies.receive(self.far_x.at[slot], at + 1, place.by_x)
        add_to(self.view(slot, 2, 1), self.far_x.at[slot])
        copies.send(self.view(slot, 2, None), self.near_y.at[slot], at + 3, at + 3, place.by_y)

    def end(self, slot, onward=True):
        place, copies, at = self.place, self.copies, self.base + 4 * slot
        copies.receive(self.near_x.at[slot], at + 2, place.by_x)
        copies.receive(self.near_y.at[slot], at + 3, place.by_y)
        add_to(self.view(slot, 0, None), self.near_x.at[slot], self.near_y.at[slot])
        if slot and onward:
            self.go_up(slot)

    def go_up(self, slot):
        at = self.base + 4 * self.place.n_head + slot
        into = self.high.at[slot - 1]
        self.copies.send(self.view(slot, 0, None), into, at, at, self.place.above(slot))

    def total(self, into=None, slots=(1, 2, 3)):
        place = self.place
        high = [self.high.at[slot - 1] for slot in slots]
        for slot, part in zip(slots, high):
            self.copies.receive(part, self.base + 4 * place.n_head + slot, place.up)
        add_to(self.view(0, 0, None), *high, into=into)


PER_SCATTER = 20


def add_to(ref, *others, into=None):
    def add(into, *refs):
        total = refs[0][...].astype(F32)
        for other in refs[1:]:
            total += other[...].astype(F32)
        into[...] = total.astype(BF)

    refs = (ref if into is None else into, ref) + others
    if len(ref.shape) == 2:
        add(*refs)
    else:
        for i in range(ref.shape[0]):
            add(*(one.at[i] for one in refs))


def dot(left, right):
    return jnp.dot(left, right, preferred_element_type=F32)


def iota(shape, axis):
    return lax.broadcasted_iota(jnp.int32, shape, axis).astype(F32)


def decay_of(head):
    exponent = jnp.full((1, 1), -8.0 / HEADS, F32) * (head + 1).astype(F32)
    return jnp.exp2(exponent)


def middle_kernel(
    n_head,
    wf,
    nm,
    og,
    hidden,
    wo,
    pre,
    query,
    keys,
    values,
    attn,
    cosines,
    sines,
    fresh,
    carry,
    scale,
    feed_out,
    block_out,
    hidden_grad_out,
    branch_out,
    pre_out,
    rates_out,
    wf_ref,
    t_ref,
    g_ref,
    far_x,
    far_y,
    near_x,
    near_y,
    high,
    nm_ref,
    og_ref,
    hidden_ref,
    mid_ref,
    send_ref,
    got_ref,
    block_ref,
    wo_ref,
    gate_ref,
    attn_ref,
    ga_ref,
    qk_pre_ref,
    cos_ref,
    sin_ref,
    fresh_ref,
    carry_ref,
    late_ref,
    pending_ref,
    message_ref,
    scale_ref,
    sum_ref,
    other_sum_ref,
    rates_ref,
    sends,
    receives,
    locals_,
):
    rows, width = hidden.shape
    quarter = width // 4
    units = wf.shape[1] // n_head
    spans = rows // SPAN
    tiles = 2 * spans
    last = n_head - 1
    place = Place(n_head)
    z, core = place.z, place.core
    copies = Copies(sends, receives, locals_)
    own, other = pl.ds(0, rows), pl.ds(rows, rows)

    order = (2, 1, 3, 0)
    load_nm = copies.move(nm, nm_ref)
    load_og = copies.move(og, og_ref)
    load_wf = {}
    for slot in order:
        at = pl.ds(slot * units, units)
        load_wf[slot] = copies.move(wf.at[:, at, :], wf_ref.at[:, at, :])
    early_loads = [
        copies.move(hidden, hidden_ref),
        copies.move(wo, wo_ref),
        copies.move(scale, scale_ref),
        copies.move(attn, attn_ref),
        copies.move(pre.at[:, :, pl.ds(3 * HEAD_DIM, HEAD_DIM)], gate_ref),
        copies.move(carry, carry_ref),
    ]
    for seq in range(2):
        for slot in range(n_head):
            early_loads.append(copies.move(fresh.at[slot, seq * spans], fresh_ref.at[slot, seq]))
    place.greet()

    def tile(i):
        return pl.ds(pl.multiple_of(i * SPAN, SPAN), SPAN)

    def dot_last(left, right):
        return lax.dot_general(left, right, (((1,), (1,)), ((), ())), preferred_element_type=F32)

    def dot_first(left, right):
        return lax.dot_general(left, right, (((0,), (0,)), ((), ())), preferred_element_type=F32)

    def g_view(slot, q, half):
        size = units if half is None else units // 2
        start = slot * units + (half or 0) * size
        return g_ref.at[:, pl.ds(start, size), pl.ds(q * quarter, quarter)]

    feed = Scatter(place, copies, g_view, far_x, far_y, near_x, near_y, high, 0)
    base = PER_SCATTER

    def feed_slot(slot):
        at = pl.ds(slot * units, units)

        @pl.loop(0, tiles)
        def _(i):
            rows_at = tile(i)
            left = dot_last(wf_ref[0, at, :], nm_ref[rows_at, :])
            right = dot_last(wf_ref[1, at, :], nm_ref[rows_at, :])
            grad = dot_last(wf_ref[2, at, :], og_ref[rows_at, :])
            t_ref[0, at, rows_at] = (grad * right).astype(BF)
            t_ref[1, at, rows_at] = (grad * left).astype(BF)
            t_ref[2, at, rows_at] = (left * right).astype(BF)

        def gradient(columns):
            for m, right in enumerate((nm_ref, nm_ref, og_ref)):
                g_ref[m, at, columns] = dot(t_ref[m, at, :], right[:, columns]).astype(BF)

        gradient(pl.ds(3 * quarter, quarter))
        feed.begin(slot)

        @pl.loop(0, 3)
        def _(q):
            gradient(pl.ds(pl.multiple_of(q * quarter, quarter), quarter))

    load_nm.wait()
    load_og.wait()
    for i, slot in enumerate(order):
        load_wf[slot].wait()
        feed_slot(slot)
        if i == 1:
            feed.middle(order[0])
    feed.middle(order[1])
    for load in early_loads:
        load.wait()

    @pl.loop(0, spans)
    def _(i):
        at = tile(spans + i)
        total = dot_first(t_ref[0, :, at], wf_ref[0]) + dot_first(t_ref[1, :, at], wf_ref[1])
        send_ref[tile(i), :] = total.astype(BF)

    copies.send(send_ref, got_ref, base, base, place.across)
    feed.end(order[0])

    @pl.loop(0, spans)
    def _(i):
        at = tile(i)
        total = dot_first(t_ref[0, :, at], wf_ref[0]) + dot_first(t_ref[1, :, at], wf_ref[1])
        mid_ref[at, :] = total

    copies.receive(got_ref, base, place.across)

    @pl.loop(0, rows // 128)
    def _(i):
        at = pl.ds(pl.multiple_of(i * 128, 128), 128)
        grad = mid_ref[at, :] + got_ref[at, :].astype(F32)
        values = hidden_ref[at, :]
        norm = lax.rsqrt(jnp.mean(values * values, axis=-1, keepdims=True) + EPSILON)
        normed = values * norm
        mean = jnp.mean(grad * normed, axis=-1, keepdims=True)
        grad = og_ref[at, :].astype(F32) + norm * (grad - normed * mean)
        mid_ref[at, :] = grad
        nm_ref[at, :] = grad.astype(BF)

    copies.send(nm_ref.at[own], nm_ref.at[other], base + 1, base + 1, place.across)
    copies.move(mid_ref, hidden_grad_out, later=True)
    loads = []
    for slot in range(n_head):
        lanes = pl.ds(slot * 2 * HEAD_DIM, 2 * HEAD_DIM)
        loads.append(copies.move(query.at[slot], t_ref.at[0, pl.ds(0, 2 * rows), lanes]))
        loads.append(copies.move(keys.at[slot], t_ref.at[1, pl.ds(0, 2 * rows), lanes]))
        lanes = pl.ds(slot * HEAD_DIM, HEAD_DIM)
        loads.append(copies.move(values.at[slot], wf_ref.at[1, pl.ds(0, 2 * rows), lanes]))

    def late_loads(slot):
        turn = slot % 2
        return [
            copies.move(pre.at[slot, :, pl.ds(0, 2 * HEAD_DIM)], qk_pre_ref.at[turn]),
            copies.move(cosines.at[slot], cos_ref.at[turn]),
            copies.move(sines.at[slot], sin_ref.at[turn]),
        ]

    slot_loads = {slot: late_loads(slot) for slot in range(2)}

    def q_at(slot, at):
        return t_ref[0, at, pl.ds(slot * 2 * HEAD_DIM, 2 * HEAD_DIM)]

    def k_at(slot, at):
        return t_ref[1, at, pl.ds(slot * 2 * HEAD_DIM, 2 * HEAD_DIM)]

    def v_at(slot, at):
        return wf_ref[1, at, pl.ds(slot * HEAD_DIM, HEAD_DIM)]

    def pre_of(slot):
        holder, start = ((wf_ref.at[0], 0), (wf_ref.at[0], 1), (wf_ref.at[1], 1), (og_ref, 0))[slot]
        return holder, start * 4 * HEAD_DIM

    def pre_at(slot, at, part):
        holder, start = pre_of(slot)
        return holder.at[at, pl.ds(start + part * HEAD_DIM, HEAD_DIM)]

    def gate_back(seq):
        for n in range(spans):
            at = pl.ds(seq * rows + n * SPAN, SPAN)
            grad = dot_last(nm_ref[at, :], wo_ref[...])
            norm = scale_ref[at, :]
            total = jnp.zeros((SPAN, 1), F32)
            for slot in range(n_head):
                part = grad[:, slot * HEAD_DIM : (slot + 1) * HEAD_DIM]
                normed = attn_ref[slot, at, :] * norm
                pre_at(slot, at, 3)[...] = (part * normed).astype(BF)
                part = part * gate_ref[slot, at, :]
                gate_ref[slot, at, :] = part
                total += jnp.sum(part * normed, axis=-1, keepdims=True)
            sum_ref[at, :] = jnp.broadcast_to(total, (SPAN, HEAD_DIM))

    gate_back(0)
    base += 2
    copies.send(sum_ref.at[own], other_sum_ref.at[other], base, base, place.across)
    copies.receive(nm_ref.at[other], base - 1, place.across)
    copies.move(nm_ref, branch_out, later=True)
    feed.middle(order[2])
    gate_back(1)
    copies.send(sum_ref.at[other], other_sum_ref.at[own], base + 1, base + 1, place.across)
    copies.sent(base - 2)
    feed.middle(order[3])
    for load in loads:
        load.wait()
    copies.receive(other_sum_ref.at[other], base, place.across)
    copies.receive(other_sum_ref.at[own], base + 1, place.across)
    base += 2

    def slot_decay(slot):
        return decay_of(2 * lax.rem(z + slot, n_head) + core)

    for slot in range(n_head):
        decay = slot_decay(slot)
        early = jnp.exp(-decay * (iota((SPAN, HEAD_DIM), 0) + 1.0))

        @pl.loop(0, tiles)
        def _(i):
            at = tile(i)
            norm = scale_ref[at, :]
            mean = (sum_ref[at, :] + other_sum_ref[at, :]) / width
            grad = norm * (gate_ref[slot, at, :] - attn_ref[slot, at, :] * norm * mean)
            grad = grad.astype(BF)
            ga_ref[slot, at, :] = grad
            both = dot_first(
                q_at(slot, at), jnp.concatenate(split(grad.astype(F32) * early), axis=1)
            )
            late_ref[slot, i] = both[:, :HEAD_DIM] + both[:, HEAD_DIM:]

    n_chain = 2 * n_head
    chain_base = base

    def chain_at(index):
        group, seq = lax.div(index, 2), lax.rem(index, 2)
        return lax.rem(group - z + n_head, n_head), seq, decay_of(2 * group + core)

    def chain_copy(index, slot, seq):
        return pltpu.make_async_remote_copy(
            src_ref=message_ref.at[slot, seq],
            dst_ref=pending_ref.at[lax.rem(slot + 1, n_head), seq],
            send_sem=sends.at[chain_base + index],
            recv_sem=receives.at[chain_base + index],
            device_id=place.down,
            device_id_type=MESH,
        )

    def chain_step(index):
        slot, seq, decay = chain_at(index)

        @pl.when(z < last)
        def _():
            copies.receive(pending_ref.at[slot, seq], chain_base + index, place.up)

        @pl.when(z == last)
        def _():
            pending_ref[slot, seq] = jnp.zeros(pending_ref.shape[2:], BF)

        @pl.when(z > 0)
        def _():
            total = jnp.exp(-decay * rows) * pending_ref[slot, seq].astype(F32)
            for n in range(spans):
                total += jnp.exp(-decay * (n * SPAN)) * late_ref[slot, seq * spans + n]
            message_ref[slot, seq] = total.astype(BF)
            chain_copy(index, slot, seq).start()

    base += n_chain
    for i in range(n_chain):
        chain_step(i)
        if i < spans:
            at = pl.ds(rows + i * SPAN, SPAN)
            send_ref[pl.ds(i * SPAN, SPAN), :] = dot_first(t_ref[2, :, at], wf_ref[2]).astype(BF)
            if i + 1 == spans:
                copies.send(send_ref, got_ref, base, base, place.across)
        elif i < tiles:
            at = pl.ds((i - spans) * SPAN, SPAN)
            hidden_ref[at, :] += dot_first(t_ref[2, :, at], wf_ref[2])
    copies.receive(got_ref, base, place.across)

    @pl.loop(0, rows // 128)
    def _(i):
        at = pl.ds(pl.multiple_of(i * 128, 128), 128)
        block_ref[at, :] = (hidden_ref[at, :] + got_ref[at, :].astype(F32)).astype(BF)

    for q in range(4):
        far = pl.ds(pl.multiple_of(place.at[q] * quarter, quarter), quarter)
        src = block_ref.at[:, pl.ds(q * quarter, quarter)]
        copies.move(src, block_out.at[:, far], later=True)
    feed.end(order[1], False)

    offsets = iota((SPAN, SPAN), 0) - iota((SPAN, SPAN), 1)

    def back_slot(slot):
        turn = slot % 2
        decay = slot_decay(slot)
        mask = jnp.where(offsets >= 0.0, jnp.exp(-decay * jnp.maximum(offsets, 0.0)), 0.0)
        places = iota((SPAN, 1), 0)
        early = jnp.exp(-decay * (places + 1.0))
        late = jnp.exp(-decay * (SPAN - 1.0 - places))
        span_decay = jnp.exp(-decay * SPAN)
        rates_ref[slot] = jnp.zeros((8, HEAD_DIM), F32)

        @pl.loop(0, 2)
        def _(seq):
            for n in range(spans):
                i = seq * spans + n
                at, here = tile(i), pl.ds(n * SPAN, SPAN)
                state = carry_ref[slot, seq].astype(F32)
                if n == 1:
                    state = span_decay * state + fresh_ref[slot, seq]
                later = pending_ref[slot, seq].astype(F32)
                if n == 0:
                    later = span_decay * later + late_ref[slot, seq * spans + 1]
                q, k, v, grad = q_at(slot, at), k_at(slot, at), v_at(slot, at), ga_ref[slot, at, :]
                weights = (dot_last(q, k) * mask).astype(BF)
                scores = (dot_last(grad, v) * mask).astype(BF)
                state_high, state_low = split(state)
                grad_query = dot(scores, k)
                grad_query += early * (dot_last(grad, state_high) + dot_last(grad, state_low))
                later_high, later_low = split(later)
                grad_keys = dot_first(scores, q)
                grad_keys += late * (dot_last(v, later_high) + dot_last(v, later_low))
                both = dot(k, jnp.concatenate([later_high, later_low], axis=1))
                grad_values = dot_first(weights, grad)
                grad_values += late * (both[:, :HEAD_DIM] + both[:, HEAD_DIM:])
                pre_at(slot, at, 2)[...] = grad_values.astype(BF)
                cosine, sine = cos_ref[turn, here, :], sin_ref[turn, here, :]
                angles = jnp.zeros((SPAN, HEAD_DIM), F32)
                for part, turned in enumerate((grad_query, grad_keys)):
                    value = qk_pre_ref[turn, at, pl.ds(part * HEAD_DIM, HEAD_DIM)]
                    by_cos, by_sin = turned[:, :HEAD_DIM], turned[:, HEAD_DIM:]
                    gate = 1.0 / (1.0 + jnp.exp(-value))
                    act = by_cos * cosine + by_sin * sine
                    angles += value * gate * (by_sin * cosine - by_cos * sine)
                    act = act * gate * (1.0 + value * (1.0 - gate))
                    pre_at(slot, at, part)[...] = act.astype(BF)
                steps = (z * rows + n * SPAN).astype(F32) + places
                rates_ref[slot, pl.ds(0, 1), :] += jnp.sum(steps * angles, axis=0, keepdims=True)

    for slot in range(n_head):
        for load in slot_loads[slot]:
            load.wait()
        back_slot(slot)
        if slot + 2 < n_head:
            slot_loads[slot + 2] = late_loads(slot + 2)
        holder, start = pre_of(slot)
        src = holder.at[pl.ds(0, 2 * rows), pl.ds(start, 4 * HEAD_DIM)]
        copies.move(src, pre_out.at[slot], later=True)
    feed.end(order[2], False)
    for i, slot in enumerate(order[1:3], 1):
        copies.move(g_view(slot, 0, None), feed_out.at[i], later=True)
    feed.end(order[3])
    feed.total(slots=order[:1])
    copies.move(g_view(0, 0, None), feed_out.at[0], later=True)
    copies.move(rates_ref, rates_out, later=True)

    @pl.when(z > 0)
    def _():
        @pl.loop(0, n_chain)
        def _(index):
            slot, seq, _ = chain_at(index)
            chain_copy(index, slot, seq).wait_send()

    copies.finish()


def middle(n_head, wf, nm, og, hidden, wo, pre, query, keys, values, attn, cos, sin, fresh, carry, scale):
    rows, width = hidden.shape
    units = wf.shape[1] // n_head
    quarter = width // 4
    tall = 2 * rows
    halves = (n_head, 3, units // 2, quarter)
    wholes = (n_head, 3, units, quarter)
    buffers = [
        (wf.shape, BF),
        (wf.shape, BF),
        (wf.shape, BF),
        (halves, BF),
        (halves, BF),
        (wholes, BF),
        (wholes, BF),
        ((n_head - 1,) + wholes[1:], BF),
        ((tall, width), BF),
        ((tall, width), BF),
        ((rows, width), F32),
        ((rows, width), F32),
        ((rows, width), BF),
        ((rows, width), BF),
        ((rows, width), BF),
        (wo.shape, BF),
        ((n_head, tall, HEAD_DIM), F32),
        ((n_head, tall, HEAD_DIM), F32),
        ((n_head, tall, HEAD_DIM), BF),
        ((2, tall, 2 * HEAD_DIM), F32),
        ((2, rows, HEAD_DIM), F32),
        ((2, rows, HEAD_DIM), F32),
        ((n_head, 2, 2 * HEAD_DIM, HEAD_DIM), F32),
        ((n_head, 2, 2 * HEAD_DIM, HEAD_DIM), BF),
        ((n_head, tall // SPAN, 2 * HEAD_DIM, HEAD_DIM), F32),
        ((n_head, 2, 2 * HEAD_DIM, HEAD_DIM), BF),
        ((n_head, 2, 2 * HEAD_DIM, HEAD_DIM), BF),
        ((tall, HEAD_DIM), F32),
        ((tall, HEAD_DIM), F32),
        ((tall, HEAD_DIM), F32),
        ((n_head, 8, HEAD_DIM), F32),
    ]
    outs = [
        ((3,) + wholes[1:], BF),
        ((rows, width), BF),
        ((rows, width), F32),
        ((tall, width), BF),
        ((n_head, tall, 4 * HEAD_DIM), BF),
        ((n_head, 8, HEAD_DIM), F32),
    ]
    n_sems = PER_SCATTER + 2 + 2 + 2 * n_head + 1
    return pl.pallas_call(
        functools.partial(middle_kernel, n_head),
        out_shape=[jax.ShapeDtypeStruct(*out) for out in outs],
        in_specs=[ANY] * 15,
        out_specs=[ANY] * len(outs),
        scratch_shapes=[pltpu.VMEM(*b) for b in buffers]
        + [
            pltpu.SemaphoreType.DMA((n_sems,)),
            pltpu.SemaphoreType.DMA((n_sems,)),
            pltpu.SemaphoreType.DMA((64,)),
        ],
        compiler_params=pltpu.CompilerParams(
            collective_id=1, has_side_effects=True, vmem_limit_bytes=63 << 20
        ),
        name="middle",
    )(wf, nm, og, hidden, wo, pre, query, keys, values, attn, cos, sin, fresh, carry, scale)


class Share:
    def __init__(self, place, copies, view, base):
        self.place, self.copies, self.view, self.base = place, copies, view, base

    def hand_over(self, q):
        at = self.base + 4 + q
        self.copies.send(self.view(0, q, None), self.view(1, q, None), at, at, self.place.across)

    def begin(self):
        place, copies, at = self.place, self.copies, self.base
        copies.send(self.view(0, 0, None), self.view(0, 1, None), at, at, place.by_x)
        copies.send(self.view(0, 0, None), self.view(0, 2, None), at + 1, at + 1, place.by_y)
        self.hand_over(0)

    def spread(self):
        place, copies, at = self.place, self.copies, self.base
        copies.receive(self.view(0, 1, None), at, place.by_x)
        copies.send(self.view(0, 1, 0), self.view(0, 3, 0), at + 2, at + 2, place.by_y)
        copies.receive(self.view(0, 2, None), at + 1, place.by_y)
        copies.send(self.view(0, 2, 1), self.view(0, 3, 1), at + 3, at + 3, place.by_x)
        self.hand_over(1)
        self.hand_over(2)

    def complete(self):
        place, copies, at = self.place, self.copies, self.base
        copies.receive(self.view(0, 3, 0), at + 2, place.by_y)
        copies.receive(self.view(0, 3, 1), at + 3, place.by_x)
        self.hand_over(3)

    def other_side(self):
        for q in range(4):
            self.copies.receive(self.view(1, q, None), self.base + 4 + q, self.place.across)


PER_SHARE = 8


def last_kernel(
    n_head,
    feed_piece,
    tokens,
    nin,
    branch,
    gated,
    pre,
    wa,
    hidden_grad,
    rates,
    input_out,
    feed_out,
    attn_out,
    down_out,
    rates_out,
    piece_ref,
    piece_high,
    feed_ref,
    attn_ref,
    down_ref,
    ga_ref,
    a_far_x,
    a_far_y,
    a_near_x,
    a_near_y,
    a_high,
    gd_ref,
    d_far_x,
    d_far_y,
    d_near_x,
    d_near_y,
    d_high,
    nin_ref,
    branch_ref,
    gated_ref,
    pre_ref,
    wa_ref,
    x_ref,
    grad_ref,
    send_ref,
    got_ref,
    rates_high,
    rates_sum,
    rates_got,
    rates_both,
    sends,
    receives,
    locals_,
):
    rows, width = tokens.shape
    quarter = width // 4
    units = feed_piece.shape[2]
    spans = rows // SPAN
    place = Place(n_head)
    copies = Copies(sends, receives, locals_)
    order = (2, 1, 3, 0)

    load_feed = [copies.move(feed_piece.at[i], piece_ref.at[i]) for i in range(3)]
    load_nin = copies.move(nin, nin_ref)
    load_pre = {slot: copies.move(pre.at[slot], pre_ref.at[slot]) for slot in order}
    load_gated = copies.move(gated, gated_ref)
    load_branch = copies.move(branch, branch_ref)
    late_loads = [copies.move(wa, wa_ref), copies.move(hidden_grad, grad_ref)]
    for q in range(4):
        far = pl.ds(pl.multiple_of(place.at[q] * quarter, quarter), quarter)
        late_loads.append(copies.move(tokens.at[:, far], x_ref.at[:, pl.ds(q * quarter, quarter)]))
    place.greet()

    def tile(i):
        return pl.ds(pl.multiple_of(i * SPAN, SPAN), SPAN)

    def dot_last(left, right):
        return lax.dot_general(left, right, (((1,), (1,)), ((), ())), preferred_element_type=F32)

    def dot_first(left, right):
        return lax.dot_general(left, right, (((0,), (0,)), ((), ())), preferred_element_type=F32)

    def part(start, half, size):
        if half is None:
            return pl.ds(start, size)
        return pl.ds(start + half * (size // 2), size // 2)

    def feed_view(side, q, half):
        return feed_ref.at[side, :, part(0, half, units), pl.ds(q * quarter, quarter)]

    def attn_view(side, q, half):
        return attn_ref.at[side, part(q * quarter, half, quarter), :]

    def down_view(side, q, half):
        return down_ref.at[side, part(0, half, HEAD_DIM), pl.ds(q * quarter, quarter)]

    def ga_view(slot, q, half):
        return ga_ref.at[slot, part(q * quarter, half, quarter), :]

    def gd_view(slot, q, half):
        return gd_ref.at[slot, part(0, half, HEAD_DIM), pl.ds(q * quarter, quarter)]

    attn = Scatter(place, copies, ga_view, a_far_x, a_far_y, a_near_x, a_near_y, a_high, 0)
    down = Scatter(place, copies, gd_view, d_far_x, d_far_y, d_near_x, d_near_y, d_high, PER_SCATTER)
    base = 2 * PER_SCATTER
    feed_share = Share(place, copies, feed_view, base)
    attn_share = Share(place, copies, attn_view, base + PER_SHARE)
    down_share = Share(place, copies, down_view, base + 2 * PER_SHARE)
    base += 3 * PER_SHARE

    for i, slot in enumerate(order[1:3], 1):
        load_feed[i].wait()
        at = base + n_head + 3 + i - 1
        copies.send(piece_ref.at[i], piece_high.at[i - 1], at, at, place.above(slot))
    for slot in range(1, n_head):
        into = rates_high.at[slot - 1]
        copies.send(rates.at[slot], into, base + slot, base + slot, place.above(slot))
    load_nin.wait()

    def slot_grads(slot):
        load_pre[slot].wait()

        @pl.loop(0, 4)
        def _(i):
            at = tile(3 - i)
            ga_ref[slot, at, :] = dot_first(nin_ref[:, at], pre_ref[slot]).astype(BF)

        lanes = pl.ds(slot * HEAD_DIM, HEAD_DIM)
        gd_ref[slot] = dot_first(gated_ref[:, lanes], branch_ref[...]).astype(BF)

    def begin(slot):
        attn.begin(slot)
        down.begin(slot)

    def middle_step(slot):
        attn.middle(slot)
        down.middle(slot)

    def end(slot):
        attn.end(slot)
        down.end(slot)

    load_gated.wait()
    load_branch.wait()
    slot_grads(order[0])
    begin(order[0])
    slot_grads(order[1])
    begin(order[1])
    slot_grads(order[2])
    begin(order[2])
    middle_step(order[0])
    slot_grads(order[3])
    begin(order[3])
    for load in late_loads:
        load.wait()

    def grad_in(at):
        total = dot_last(pre_ref[0, at, :], wa_ref[0])
        for slot in range(1, n_head):
            total += dot_last(pre_ref[slot, at, :], wa_ref[slot])
        return total

    @pl.loop(0, spans)
    def _(i):
        send_ref[tile(i), :] = grad_in(tile(spans + i)).astype(BF)

    copies.send(send_ref, got_ref, base, base, place.across)
    middle_step(order[1])
    middle_step(order[2])
    load_feed[0].wait()
    for i in range(2):
        copies.receive(piece_high.at[i], base + n_head + 3 + i, place.up)
    add_to(piece_ref.at[0], piece_high.at[0], piece_high.at[1], into=feed_view(0, 0, None))
    feed_share.begin()

    total = rates[0]
    for slot in range(1, n_head):
        copies.receive(rates_high.at[slot - 1], base + slot, place.up)
        total += rates_high[slot - 1]
    base += n_head
    rates_sum[0] = total
    copies.send(rates_sum.at[0], rates_got.at[0], base, base, place.by_x)

    end(order[0])
    copies.receive(rates_got.at[0], base, place.by_x)
    rates_sum[1] = total + rates_got[0]
    copies.send(rates_sum.at[1], rates_got.at[1], base + 1, base + 1, place.by_y)

    copies.receive(got_ref, base - n_head, place.across)

    @pl.loop(0, spans)
    def _(i):
        at = tile(i)
        values = x_ref[at, :].astype(F32)
        norm = lax.rsqrt(jnp.mean(values * values, axis=-1, keepdims=True) + EPSILON)
        normed = values * norm
        grad = grad_in(at) + got_ref[at, :].astype(F32)
        mean = jnp.mean(grad * normed, axis=-1, keepdims=True)
        grad_ref[at, :] += norm * (grad - normed * mean)

    for q in range(4):
        far = pl.ds(pl.multiple_of(place.at[q] * quarter, quarter), quarter)
        src = grad_ref.at[:, pl.ds(q * quarter, quarter)]
        copies.move(src, input_out.at[:, far], later=True)
    end(order[1])
    middle_step(order[3])
    copies.receive(rates_got.at[1], base + 1, place.by_y)
    rates_both[0] = rates_sum[1] + rates_got[1]
    copies.send(rates_both.at[0], rates_both.at[1], base + 2, base + 2, place.across)
    feed_share.spread()
    end(order[2])
    end(order[3])
    attn.total(attn_view(0, 0, None))
    attn_share.begin()
    down.total(down_view(0, 0, None))
    down_share.begin()
    copies.receive(rates_both.at[1], base + 2, place.across)
    sides = (place.core, 1 - place.core)
    for side in range(2):
        copies.move(rates_both.at[side], rates_out.at[sides[side]], later=True)

    def write(ref, out, side, q):
        far = pl.ds(pl.multiple_of(place.at[q] * quarter, quarter), quarter)
        near = pl.ds(q * quarter, quarter)
        if ref is attn_ref:
            src, dst = ref.at[side, near], out.at[sides[side], far]
        elif ref is down_ref:
            src, dst = ref.at[side, :, near], out.at[sides[side], :, far]
        else:
            src, dst = ref.at[side, :, :, near], out.at[sides[side], :, :, far]
        copies.move(src, dst, later=True)

    feed_share.complete()
    for q in range(4):
        write(feed_ref, feed_out, 0, q)
    feed_share.other_side()
    for q in range(4):
        write(feed_ref, feed_out, 1, q)
    attn_share.spread()
    down_share.spread()
    for q in range(3):
        write(attn_ref, attn_out, 0, q)
        write(down_ref, down_out, 0, q)
    attn_share.complete()
    down_share.complete()
    write(attn_ref, attn_out, 0, 3)
    write(down_ref, down_out, 0, 3)
    attn_share.other_side()
    down_share.other_side()
    for q in range(4):
        write(attn_ref, attn_out, 1, q)
        write(down_ref, down_out, 1, q)
    copies.finish()


def last(n_head, feed_piece, tokens, nin, branch, gated, pre, wa, hidden_grad, rates):
    rows, width = tokens.shape
    _, _, units, quarter = feed_piece.shape
    tall = 2 * rows

    def scatter_buffers(shape, halved):
        half = tuple(n // 2 if i == halved else n for i, n in enumerate(shape))
        return [
            ((n_head,) + half, BF),
            ((n_head,) + half, BF),
            ((n_head,) + shape, BF),
            ((n_head,) + shape, BF),
            ((n_head - 1,) + shape, BF),
        ]

    outs = [
        ((rows, width), F32),
        ((2, 3, units, width), BF),
        ((2, width, 4 * HEAD_DIM), BF),
        ((2, HEAD_DIM, width), BF),
        ((2, 8, HEAD_DIM), F32),
    ]
    buffers = [
        (feed_piece.shape, BF),
        ((2,) + feed_piece.shape[1:], BF),
        outs[1],
        outs[2],
        outs[3],
        ((n_head, width, 4 * HEAD_DIM), BF),
        *scatter_buffers((quarter, 4 * HEAD_DIM), 0),
        ((n_head, HEAD_DIM, width), BF),
        *scatter_buffers((HEAD_DIM, quarter), 0),
        ((tall, width), BF),
        ((tall, width), BF),
        (gated.shape, BF),
        (pre.shape, BF),
        (wa.shape, BF),
        ((rows, width), BF),
        ((rows, width), F32),
        ((rows, width), BF),
        ((rows, width), BF),
        ((n_head - 1, 8, HEAD_DIM), F32),
        ((2, 8, HEAD_DIM), F32),
        ((2, 8, HEAD_DIM), F32),
        ((2, 8, HEAD_DIM), F32),
    ]
    n_sems = 2 * PER_SCATTER + 3 * PER_SHARE + n_head + 3 + 2
    return pl.pallas_call(
        functools.partial(last_kernel, n_head),
        out_shape=[jax.ShapeDtypeStruct(*out) for out in outs],
        in_specs=[ANY] * 8 + [IN_VMEM],
        out_specs=[ANY] * len(outs),
        scratch_shapes=[pltpu.VMEM(*b) for b in buffers]
        + [
            pltpu.SemaphoreType.DMA((n_sems,)),
            pltpu.SemaphoreType.DMA((n_sems,)),
            pltpu.SemaphoreType.DMA((64,)),
        ],
        compiler_params=pltpu.CompilerParams(
            collective_id=2, has_side_effects=True, vmem_limit_bytes=60 << 20
        ),
        name="last",
    )(feed_piece, tokens, nin, branch, gated, pre, wa, hidden_grad, rates)


def finish_kernel(block, grad, feed, attn, down, rates, *refs):
    outs, (block_ref, grad_ref, feed_ref, attn_ref, down_ref) = refs[:11], refs[11:16]
    results, locals_ = refs[16:-1], refs[-1]
    copies = Copies(None, None, locals_)
    (block_out, grad_out, q_out, k_out, v_out, g_out, o_out, rates_out, l_out, r_out, d_out) = outs
    units = feed.shape[2]
    loads = [
        copies.move(feed.at[side, i], feed_ref.at[side, i]) for i in range(3) for side in range(2)
    ]
    loads += [copies.move(attn, attn_ref), copies.move(down, down_ref)]
    loads += [copies.move(grad, grad_ref), copies.move(block, block_ref)]
    l_ref, r_ref, d_ref, q_ref, k_ref, v_ref, g_ref, o_ref, rates_ref = results
    for side in range(2):
        rates_ref[:, pl.ds(side * HEAD_DIM, HEAD_DIM)] = rates[side, pl.ds(0, 1), :]
    copies.move(rates_ref, rates_out, later=True)
    for i, (ref, out) in enumerate(((l_ref, l_out), (r_ref, r_out), (d_ref, d_out))):
        for side in range(2):
            at = pl.ds(side * units, units)
            loads.pop(0).wait()
            ref[at, :] = feed_ref[side, i].astype(F32)
            copies.move(ref.at[at], out.at[at], later=True)
    loads.pop(0).wait()
    for i, (ref, out) in enumerate(((q_ref, q_out), (k_ref, k_out), (v_ref, v_out), (g_ref, g_out))):
        lanes = pl.ds(i * HEAD_DIM, HEAD_DIM)
        for side in range(2):
            ref[:, pl.ds(side * HEAD_DIM, HEAD_DIM)] = attn_ref[side, :, lanes].astype(F32)
        copies.move(ref, out, later=True)
    loads.pop(0).wait()
    for side in range(2):
        o_ref[pl.ds(side * HEAD_DIM, HEAD_DIM), :] = down_ref[side].astype(F32)
    copies.move(o_ref, o_out, later=True)
    loads.pop(0).wait()
    copies.move(grad_ref, grad_out, later=True)
    loads.pop(0).wait()
    copies.move(block_ref, block_out, later=True)
    copies.finish()


def finish(block, grad, feed, attn, down, rates):
    _, _, units, width = feed.shape
    projection = ((width, 2 * HEAD_DIM), F32)
    back = ((2 * HEAD_DIM, width), F32)
    results = [((2 * units, width), F32)] * 3 + [projection] * 4 + [back]
    results.append(((1, 2 * HEAD_DIM), F32))
    outs = [(block.shape, BF), (grad.shape, F32)] + results[3:] + results[:3]
    buffers = [(block.shape, BF), (grad.shape, F32)]
    buffers += [(a.shape, BF) for a in (feed, attn, down)] + results
    return pl.pallas_call(
        finish_kernel,
        out_shape=[jax.ShapeDtypeStruct(*out) for out in outs],
        in_specs=[ANY] * 5 + [IN_VMEM],
        out_specs=[ANY] * len(outs),
        scratch_shapes=[pltpu.VMEM(*b) for b in buffers] + [pltpu.SemaphoreType.DMA((48,))],
        compiler_params=pltpu.CompilerParams(vmem_limit_bytes=62 << 20),
        name="finish",
    )(block, grad, feed, attn, down, rates)


def make(n_dp, n_head):
    def on_device(
        tokens,
        attn_query,
        attn_key,
        attn_value,
        attn_gate,
        attn_out,
        rotation_rates,
        ffn_left,
        ffn_right,
        ffn_down,
        out_grad,
    ):
        rates_in = rotation_rates.reshape(1, -1)
        (
            attn_weights,
            out_w,
            ffn_all,
            gathered_in,
            pre,
            query,
            keys,
            values,
            attn,
            cosines,
            sines,
            fresh,
            carry,
            scale_attn,
            gated,
            hidden,
            gathered_mid,
            grad_rows,
        ) = forward(
            n_head,
            tokens,
            out_grad,
            attn_query,
            attn_key,
            attn_value,
            attn_gate,
            attn_out,
            ffn_left.T,
            ffn_right.T,
            ffn_down,
            rates_in,
        )
        feed_piece, block_out, grad_hidden, branch_rows, grad_pre, rates_grad = middle(
            n_head,
            ffn_all,
            gathered_mid,
            grad_rows,
            hidden,
            out_w,
            pre,
            query,
            keys,
            values,
            attn,
            cosines,
            sines,
            fresh,
            carry,
            scale_attn,
        )
        input_grad, *grads = last(
            n_head,
            feed_piece,
            tokens,
            gathered_in,
            branch_rows,
            gated,
            grad_pre,
            attn_weights,
            grad_hidden,
            rates_grad,
        )

        results = finish(block_out, input_grad, *grads)
        rates_grad, left_grad, right_grad = results[7][0], results[8].T, results[9].T
        results = list(results[:7]) + [rates_grad, left_grad, right_grad, results[10]]
        if n_dp > 8:
            groups = [[i + 8 * j for j in range(n_dp // 8)] for i in range(8)]
            grads = [lax.psum(grad, "dp", axis_index_groups=groups) for grad in results[2:]]
            results = results[:2] + grads
        return tuple(results)

    return on_device


def solution(mesh):
    weights = (P(None, "head"),) * 4 + (P("head", None), P("head")) + (P(None, "head"),) * 2
    weights = weights + (P("head", None),)
    rows = P(("dp", "head"), None)
    return jax.shard_map(
        make(mesh.shape["dp"], mesh.shape["head"]),
        mesh=mesh,
        in_specs=(rows,) + weights + (rows,),
        out_specs=(rows, rows) + weights,
        check_vma=False,
    )
```

```python
import functools

import jax
import jax.numpy as jnp
from jax import lax
from jax.experimental import pallas as pl
from jax.experimental.pallas import tpu as pltpu
from jax.sharding import PartitionSpec as P

HEADS = 8
HEAD_DIM = 128
SPAN = 256
EPSILON = 1e-06
BF = jnp.bfloat16
F32 = jnp.float32


MESH = pl.DeviceIdType.MESH
ANY = pl.BlockSpec(memory_space=pl.ANY)
IN_VMEM = pl.BlockSpec(memory_space=pltpu.VMEM)


def split(value):
    high = value.astype(BF)
    return high, (value - high.astype(F32)).astype(BF)


class Place:
    def __init__(self, n_head):
        self.n_head = n_head
        dp = lax.axis_index("dp")
        self.z = lax.axis_index("head")
        self.core = lax.rem(dp, 2)
        x = lax.rem(lax.div(dp, 2), 2)
        y = lax.rem(lax.div(dp, 4), 2)
        self.plane = x + 2 * y
        self.at = [self.plane, self.plane + 1 - 2 * x, self.plane + 2 - 4 * y, 3 - self.plane]
        self.across = {"dp": dp + 1 - 2 * self.core}
        self.by_x = {"dp": dp + 2 - 4 * x}
        self.by_y = {"dp": dp + 4 - 8 * y}
        self.up = {"head": lax.rem(self.z + 1, n_head)}
        self.down = {"head": lax.rem(self.z + n_head - 1, n_head)}

    def above(self, step):
        return {"head": lax.rem(self.z + step, self.n_head)}

    def below(self, step):
        return {"head": lax.rem(self.z + self.n_head - step, self.n_head)}

    def greet(self):
        barrier = pltpu.get_barrier_semaphore()
        others = [self.across, self.by_x, self.by_y]
        others += [self.below(step) for step in range(1, self.n_head)]
        for other in others:
            pl.semaphore_signal(barrier, inc=1, device_id=other, device_id_type=MESH)
        pl.semaphore_wait(barrier, len(others))


class Copies:
    def __init__(self, sends, receives, locals_):
        self.sends, self.receives, self.locals = sends, receives, locals_
        self.pending = []
        self.started = {}
        self.n_local = 0

    def send(self, src, dst, out, into, device, when=None):
        copy = pltpu.make_async_remote_copy(
            src_ref=src,
            dst_ref=dst,
            send_sem=self.sends.at[out],
            recv_sem=self.receives.at[into],
            device_id=device,
            device_id_type=MESH,
        )
        if when is None:
            copy.start()
            self.pending.append(copy.wait_send)
            if isinstance(out, int):
                self.started[out] = copy.wait_send
        else:
            pl.when(when)(copy.start)
            self.pending.append(lambda: pl.when(when)(copy.wait_send))

    def receive(self, dst, into, device):
        pltpu.make_async_remote_copy(
            src_ref=dst,
            dst_ref=dst,
            send_sem=self.sends.at[0],
            recv_sem=self.receives.at[into],
            device_id=device,
            device_id_type=MESH,
        ).wait_recv()

    def move(self, src, dst, later=False):
        copy = pltpu.make_async_copy(src, dst, self.locals.at[self.n_local])
        self.n_local += 1
        copy.start()
        if later:
            self.pending.append(copy.wait)
        return copy

    def sent(self, out):
        wait = self.started.pop(out)
        self.pending.remove(wait)
        wait()

    def finish(self):
        for wait in self.pending:
            wait()


class Gather:
    def __init__(self, place, copies, view, base, late=None):
        self.place, self.copies, self.view, self.base = place, copies, view, base
        self.late = late

    def begin(self):
        place, z = self.place, self.place.z
        own = self.view(0, 0, None)
        last = place.n_head - 1
        self.copies.send(
            own, self.view(last, 0, None), self.base, self.base + last, place.up, when=z < last
        )
        self.copies.send(own, self.view(1, 0, None), self.base + 1, self.base + 1, place.down, when=z > 0)

    def arrived(self, slot, when=True):
        place, copies, z, base = self.place, self.copies, self.place.z, self.base
        last = place.n_head - 1
        if when is True:
            copies.receive(self.view(slot, 0, None), base + slot, place.up)
        else:
            pl.when(when)(lambda: copies.receive(self.view(slot, 0, None), base + slot, place.up))
        from_up = z + slot <= last
        piece = self.view(slot, 0, None)
        down = jnp.logical_and(jnp.logical_and(from_up, z > 0), when)
        up = jnp.logical_and(jnp.logical_not(from_up), z < last)
        up = jnp.logical_and(up, when)
        always = None if when is True else when
        after = jnp.minimum(slot + 1, last)
        before = jnp.maximum(slot - 1, 1)
        copies.send(piece, self.view(after, 0, None), base + 1 + slot, base + after, place.down, when=down)
        copies.send(piece, self.view(before, 0, None), base + 1 + slot, base + before, place.up, when=up)
        at = base + 4 * slot + 4
        copies.send(piece, self.view(slot, 1, None), at, at, place.by_x, when=always)
        copies.send(piece, self.view(slot, 2, None), at + 1, at + 1, place.by_y, when=always)

    def spread(self, slot):
        place, copies = self.place, self.copies
        at = self.base + 4 * slot + 4
        now = None if self.late is None else slot != self.late
        low, high = self.view(slot, 3, 0), self.view(slot, 3, 1)
        copies.receive(self.view(slot, 1, None), at, place.by_x)
        copies.send(self.view(slot, 1, 0), low, at + 2, at + 2, place.by_y, when=now)
        copies.receive(self.view(slot, 2, None), at + 1, place.by_y)
        copies.send(self.view(slot, 2, 1), high, at + 3, at + 3, place.by_x, when=now)

    def complete(self, slot):
        place, copies = self.place, self.copies
        at = self.base + 4 * slot + 4

        def receive():
            copies.receive(self.view(slot, 3, 0), at + 2, place.by_y)
            copies.receive(self.view(slot, 3, 1), at + 3, place.by_x)

        if self.late is None:
            receive()
        else:
            pl.when(slot != self.late)(receive)


PER_GATHER = 24


def forward_kernel(
    n_head,
    tokens,
    out_grad,
    wq,
    wk,
    wv,
    wg,
    wo,
    ffn_left,
    ffn_right,
    ffn_down,
    rates,
    wa_out,
    wo_out,
    wf_out,
    nin_out,
    pre_out,
    q_out,
    k_out,
    v_out,
    attn_out,
    cos_out,
    sin_out,
    fresh_out,
    carry_out,
    scale_out,
    gated_out,
    hidden_out,
    nm_out,
    og_out,
    wa_ref,
    wo_ref,
    wf_ref,
    x_ref,
    nin_ref,
    pre_ref,
    q_ref,
    k_ref,
    v_ref,
    attn_ref,
    cos_ref,
    sin_ref,
    fresh_ref,
    carry_ref,
    message_ref,
    squares_ref,
    other_squares_ref,
    gated_ref,
    branch_ref,
    other_branch_ref,
    hidden_ref,
    nm_ref,
    rates_ref,
    og_ref,
    sends,
    receives,
    locals_,
):
    rows, width = tokens.shape
    quarter = width // 4
    units = ffn_down.shape[0] // 2
    tiles = 2 * rows // SPAN
    place = Place(n_head)
    z, core = place.z, place.core
    last = n_head - 1
    copies = Copies(sends, receives, locals_)

    def columns(start, size):
        return pl.ds(pl.multiple_of(start, size), size)

    own_loads = []
    for q in range(4):
        far = columns(place.at[q] * quarter, quarter)
        near = pl.ds(q * quarter, quarter)
        loads = []
        for i, w in enumerate((wq, wk, wv, wg)):
            src = w.at[far, columns(core * HEAD_DIM, HEAD_DIM)]
            loads.append(copies.move(src, wa_ref.at[0, near, pl.ds(i * HEAD_DIM, HEAD_DIM)]))
        src = wo.at[columns(core * HEAD_DIM, HEAD_DIM), far]
        loads.append(copies.move(src, wo_ref.at[pl.ds(0, HEAD_DIM), near]))
        for i, w in enumerate((ffn_left, ffn_right, ffn_down)):
            src = w.at[pl.ds(pl.multiple_of(core * units, 16), units), far]
            loads.append(copies.move(src, wf_ref.at[i, pl.ds(0, units), near]))
        own_loads.append(loads)
    token_loads = [
        copies.move(
            tokens.at[:, columns(place.at[q] * quarter, quarter)],
            x_ref.at[:, pl.ds(q * quarter, quarter)],
        )
        for q in range(4)
    ]
    grad_loads = [
        copies.move(
            out_grad.at[:, columns(place.at[q] * quarter, quarter)],
            og_ref.at[pl.ds(0, rows), pl.ds(q * quarter, quarter)],
        )
        for q in range(4)
    ]
    place.greet()

    def half_rows(half, size):
        return pl.ds(0, size) if half is None else pl.ds(half * (size // 2), size // 2)

    def wa_view(part, slot, q, half):
        at = half_rows(half, quarter)
        lanes = pl.ds(part * 2 * HEAD_DIM, 2 * HEAD_DIM)
        return wa_ref.at[slot, pl.ds(q * quarter + at.start, at.size), lanes]

    def wo_view(slot, q, half):
        at = half_rows(half, HEAD_DIM)
        return wo_ref.at[
            pl.ds(pl.multiple_of(slot * HEAD_DIM + at.start, HEAD_DIM // 2), at.size),
            pl.ds(q * quarter, quarter),
        ]

    def wf_view(slot, q, half):
        at = half_rows(half, units)
        return wf_ref.at[
            :,
            pl.ds(pl.multiple_of(slot * units + at.start, 16), at.size),
            pl.ds(q * quarter, quarter),
        ]

    attn_all = [
        Gather(place, copies, functools.partial(wa_view, part), part * PER_GATHER)
        for part in range(2)
    ]
    attn_all.append(Gather(place, copies, wo_view, 2 * PER_GATHER))
    feed = Gather(place, copies, wf_view, 3 * PER_GATHER, late=last)
    base = 4 * PER_GATHER
    for loads, part in zip((own_loads[0][:2], own_loads[0][2:4], own_loads[0][4:5]), attn_all):
        for load in loads:
            load.wait()
        part.begin()
    for step in range(1, n_head):
        copies.send(rates, rates_ref.at[step], base + step, base + step, place.below(step))
    rates_ref[0] = rates[...]

    for load in token_loads:
        load.wait()

    def norm_rows(values):
        mean = jnp.mean(values * values, axis=-1, keepdims=True)
        return values * lax.rsqrt(mean + EPSILON)

    @pl.loop(0, rows // 128)
    def _(i):
        at = pl.ds(pl.multiple_of(i * 128, 128), 128)
        nin_ref[at, :] = norm_rows(x_ref[at, :].astype(F32)).astype(BF)

    base += 4
    for load in grad_loads:
        load.wait()
    og_other = og_ref.at[pl.ds(rows, rows)]
    copies.send(og_ref.at[pl.ds(0, rows)], og_other, base, base, place.across)
    base += 1
    nin_other = nin_ref.at[pl.ds(rows, rows)]
    copies.send(nin_ref.at[pl.ds(0, rows)], nin_other, base, base, place.across)
    for q, loads in enumerate(own_loads):
        for load in loads[5:] if q == 0 else loads:
            load.wait()
    for step in range(1, n_head):
        copies.receive(rates_ref.at[step], base - 5 + step, place.up)
    copies.receive(nin_other, base, place.across)
    copies.move(nin_ref, nin_out, later=True)
    own_rows = pl.ds(0, units)
    copies.move(wf_ref.at[:, own_rows], wf_out.at[:, own_rows], later=True)
    copies.receive(og_other, base - 1, place.across)
    copies.move(og_ref, og_out, later=True)

    def decay_of(head):
        exponent = jnp.full((1, 1), -8.0 / HEADS, F32) * (head + 1).astype(F32)
        return jnp.exp2(exponent)

    def tile(i):
        return pl.ds(pl.multiple_of(i * SPAN, SPAN), SPAN)

    def iota(shape, axis):
        return lax.broadcasted_iota(jnp.int32, shape, axis).astype(F32)

    def dot(left, right):
        return jnp.dot(left, right, preferred_element_type=F32)

    def slot_compute(slot):
        head = 2 * lax.rem(z + slot, n_head) + core
        decay = decay_of(head)
        rate = rates_ref[slot, :, columns(core * HEAD_DIM, HEAD_DIM)]
        coarse = (z * rows).astype(F32) + 32.0 * iota((rows // 32, HEAD_DIM), 0)
        coarse = coarse * rate
        fine = iota((32, HEAD_DIM), 0) * rate
        cos_a, sin_a = jnp.cos(coarse), jnp.sin(coarse)
        cos_b, sin_b = jnp.cos(fine), jnp.sin(fine)
        for a in range(rows // 32):
            cos_row, sin_row = cos_a[a : a + 1], sin_a[a : a + 1]
            cos_ref[slot, pl.ds(a * 32, 32), :] = cos_row * cos_b - sin_row * sin_b
            sin_ref[slot, pl.ds(a * 32, 32), :] = sin_row * cos_b + cos_row * sin_b
        offsets = iota((SPAN, SPAN), 0) - iota((SPAN, SPAN), 1)
        mask = jnp.where(offsets >= 0.0, jnp.exp(-decay * jnp.maximum(offsets, 0.0)), 0.0)
        late = jnp.exp(-decay * (SPAN - 1.0 - iota((SPAN, HEAD_DIM), 0)))

        @pl.loop(0, tiles)
        def _(i):
            at = tile(i)
            pre = dot(nin_ref[at, :], wa_ref[slot])
            pre_ref[slot, at, :] = pre
            here = tile(lax.rem(i, rows // SPAN))
            cosines, sines = cos_ref[slot, here, :], sin_ref[slot, here, :]

            def rotate(values):
                activated = values / (1.0 + jnp.exp(-values))
                turned = jnp.concatenate([activated * cosines, activated * sines], axis=1)
                return turned.astype(BF)

            query = rotate(pre[:, :HEAD_DIM])
            keys = rotate(pre[:, HEAD_DIM : 2 * HEAD_DIM])
            value = pre[:, 2 * HEAD_DIM : 3 * HEAD_DIM].astype(BF)
            q_ref[slot, at, :] = query
            k_ref[slot, at, :] = keys
            v_ref[slot, at, :] = value
            scores = lax.dot_general(
                query, keys, (((1,), (1,)), ((), ())), preferred_element_type=F32
            )
            weights = (scores * mask).astype(BF)
            attn_ref[slot, at, :] = dot(weights, value)
            high, low = split(value.astype(F32) * late)
            both = lax.dot_general(
                keys,
                jnp.concatenate([high, low], axis=1),
                (((0,), (0,)), ((), ())),
                preferred_element_type=F32,
            )
            fresh_ref[slot, i] = both[:, :HEAD_DIM] + both[:, HEAD_DIM:]

        for ref, out in (
            (wa_ref, wa_out),
            (pre_ref, pre_out),
            (q_ref, q_out),
            (k_ref, k_out),
            (v_ref, v_out),
            (cos_ref, cos_out),
            (sin_ref, sin_out),
            (fresh_ref, fresh_out),
        ):
            copies.move(ref.at[slot], out.at[slot], later=True)

    first = 1 + 2 * lax.div(z, last)
    second = 2 + lax.rem(lax.div(z + 1, 2), 2)
    third = 6 - first - second

    for part in attn_all:
        part.arrived(first)
    slot_compute(0)
    for part in attn_all:
        part.arrived(second)
    for part in attn_all:
        part.spread(first)
    for part in attn_all:
        part.arrived(third)
    feed.begin()
    for part in attn_all:
        part.spread(second)
    for part in attn_all[:2]:
        part.complete(first)
    slot_compute(first)
    for part in attn_all:
        part.spread(third)
    feed.arrived(first)
    for part in attn_all[:2]:
        part.complete(second)
    slot_compute(second)
    inner = jnp.logical_and(z > 0, z < last)
    feed.arrived(second, inner)
    for part in attn_all[:2]:
        part.complete(third)
    slot_compute(third)
    base += 1
    chain_base = base
    n_chain = 2 * n_head

    def chain_at(index):
        group, seq = lax.div(index, 2), lax.rem(index, 2)
        return lax.rem(group - z + n_head, n_head), seq, decay_of(2 * group + core)

    def chain_copy(index, slot, seq):
        after = lax.rem(slot + n_head - 1, n_head)
        return pltpu.make_async_remote_copy(
            src_ref=message_ref.at[slot, seq],
            dst_ref=carry_ref.at[after, seq],
            send_sem=sends.at[chain_base + index],
            recv_sem=receives.at[chain_base + index],
            device_id=place.up,
            device_id_type=MESH,
        )

    def hand_on(index, slot, seq, decay):
        total = jnp.exp(-decay * rows) * carry_ref[slot, seq].astype(F32)
        for n in range(rows // SPAN):
            left = rows - (n + 1) * SPAN
            total += jnp.exp(-decay * left) * fresh_ref[slot, seq * (rows // SPAN) + n]
        message_ref[slot, seq] = total.astype(BF)
        chain_copy(index, slot, seq).start()

    @pl.when(z == 0)
    def _():
        @pl.loop(0, n_chain)
        def _(index):
            slot, seq, decay = chain_at(index)
            carry_ref[slot, seq] = jnp.zeros(carry_ref.shape[2:], BF)
            hand_on(index, slot, seq, decay)

    feed.arrived(second, jnp.logical_not(inner))
    feed.spread(first)
    feed.arrived(third)

    @pl.when(z > 0)
    def _():
        @pl.loop(0, n_chain)
        def _(index):
            slot, seq, decay = chain_at(index)
            copies.receive(carry_ref.at[slot, seq], chain_base + index, place.down)
            pl.when(z < last)(lambda: hand_on(index, slot, seq, decay))

    copies.move(carry_ref, carry_out, later=True)
    feed.spread(second)

    def feed_done(slot):
        feed.complete(slot)
        at = pl.ds(pl.multiple_of(slot * units, 16), units)
        copies.move(wf_ref.at[:, at], wf_out.at[:, at], later=True)

    def apply(seq):
        mine = pl.ds(seq * rows, rows)
        squares_ref[mine, :] = jnp.zeros((rows, HEAD_DIM), F32)

        @pl.loop(0, n_head)
        def _(slot):
            decay = decay_of(2 * lax.rem(z + slot, n_head) + core)
            early = jnp.exp(-decay * (iota((SPAN, HEAD_DIM), 0) + 1.0))
            state = carry_ref[slot, seq].astype(F32)
            for n in range(rows // SPAN):
                i = seq * (rows // SPAN) + n
                at = pl.ds(i * SPAN, SPAN)
                both = dot(q_ref[slot, at, :], jnp.concatenate(split(state), axis=1))
                attn = attn_ref[slot, at, :]
                attn += early * (both[:, :HEAD_DIM] + both[:, HEAD_DIM:])
                attn_ref[slot, at, :] = attn
                squares_ref[at, :] += jnp.sum(attn * attn, axis=-1, keepdims=True)
                if n + 1 < rows // SPAN:
                    state = jnp.exp(-decay * SPAN) * state + fresh_ref[slot, i]

    def gating(seq):
        for n in range(rows // SPAN):
            at = pl.ds(seq * rows + n * SPAN, SPAN)
            total = squares_ref[at, :] + other_squares_ref[at, :]
            scale = lax.rsqrt(total / width + EPSILON)
            other_squares_ref[at, :] = scale
            for slot in range(n_head):
                gate = pre_ref[slot, at, pl.ds(3 * HEAD_DIM, HEAD_DIM)]
                gated = (attn_ref[slot, at, :] * scale * gate).astype(BF)
                gated_ref[at, pl.ds(slot * HEAD_DIM, HEAD_DIM)] = gated

    base += n_chain
    own, other = pl.ds(0, rows), pl.ds(rows, rows)
    apply(1)
    copies.send(squares_ref.at[other], other_squares_ref.at[own], base, base, place.across)
    apply(0)
    copies.send(squares_ref.at[own], other_squares_ref.at[other], base + 1, base + 1, place.across)
    copies.move(attn_ref, attn_out, later=True)
    for slot in (first, second, third):
        attn_all[2].complete(slot)
    copies.receive(other_squares_ref.at[other], base + 1, place.across)
    gating(1)
    feed_done(first)
    base += 2
    for n in range(rows // SPAN):
        gated = gated_ref[pl.ds(rows + n * SPAN, SPAN), :]
        branch_ref[pl.ds(n * SPAN, SPAN), :] = dot(gated, wo_ref[...]).astype(BF)
    copies.send(branch_ref, other_branch_ref, base, base, place.across)
    copies.receive(other_squares_ref.at[own], base - 2, place.across)
    gating(0)
    copies.move(other_squares_ref, scale_out, later=True)
    copies.move(gated_ref, gated_out, later=True)
    copies.move(wo_ref, wo_out, later=True)
    feed.spread(third)
    feed_done(second)

    @pl.loop(0, rows // SPAN)
    def _(i):
        at = tile(i)
        hidden_ref[at, :] = x_ref[at, :].astype(F32) + dot(gated_ref[at, :], wo_ref[...])

    copies.receive(other_branch_ref, base, place.across)

    @pl.loop(0, rows // 128)
    def _(i):
        at = pl.ds(pl.multiple_of(i * 128, 128), 128)
        hidden = hidden_ref[at, :] + other_branch_ref[at, :].astype(F32)
        hidden_ref[at, :] = hidden
        nm_ref[at, :] = norm_rows(hidden).astype(BF)

    copies.send(nm_ref.at[own], nm_ref.at[other], base + 1, base + 1, place.across)
    copies.move(hidden_ref, hidden_out, later=True)
    feed_done(third)
    copies.receive(nm_ref.at[other], base + 1, place.across)
    copies.move(nm_ref, nm_out, later=True)

    @pl.when(z < last)
    def _():
        @pl.loop(0, n_chain)
        def _(index):
            slot, seq, _ = chain_at(index)
            chain_copy(index, slot, seq).wait_send()

    copies.finish()


def forward(n_head, tokens, out_grad, wq, wk, wv, wg, wo, ffn_left, ffn_right, ffn_down, rates):
    rows, width = tokens.shape
    units = ffn_down.shape[0] // 2
    tall = 2 * rows
    buffers = [
        ((n_head, width, 4 * HEAD_DIM), BF),
        ((n_head * HEAD_DIM, width), BF),
        ((3, n_head * units, width), BF),
        ((rows, width), BF),
        ((tall, width), BF),
        ((n_head, tall, 4 * HEAD_DIM), F32),
        ((n_head, tall, 2 * HEAD_DIM), BF),
        ((n_head, tall, 2 * HEAD_DIM), BF),
        ((n_head, tall, HEAD_DIM), BF),
        ((n_head, tall, HEAD_DIM), F32),
        ((n_head, rows, HEAD_DIM), F32),
        ((n_head, rows, HEAD_DIM), F32),
        ((n_head, tall // SPAN, 2 * HEAD_DIM, HEAD_DIM), F32),
        ((n_head, 2, 2 * HEAD_DIM, HEAD_DIM), BF),
        ((n_head, 2, 2 * HEAD_DIM, HEAD_DIM), BF),
        ((tall, HEAD_DIM), F32),
        ((tall, HEAD_DIM), F32),
        ((tall, n_head * HEAD_DIM), BF),
        ((rows, width), BF),
        ((rows, width), BF),
        ((rows, width), F32),
        ((tall, width), BF),
        ((n_head, 1, 2 * HEAD_DIM), F32),
        ((tall, width), BF),
    ]
    out_of = [0, 1, 2, 4, 5, 6, 7, 8, 9, 10, 11, 12, 13, 16, 17, 20, 21, 23]
    n_sems = 4 * PER_GATHER + 4 + 1 + 1 + 2 * n_head + 2 + 2
    return pl.pallas_call(
        functools.partial(forward_kernel, n_head),
        out_shape=[jax.ShapeDtypeStruct(*buffers[i]) for i in out_of],
        in_specs=[ANY] * 10 + [IN_VMEM],
        out_specs=[ANY] * len(out_of),
        scratch_shapes=[pltpu.VMEM(*b) for b in buffers]
        + [
            pltpu.SemaphoreType.DMA((n_sems,)),
            pltpu.SemaphoreType.DMA((n_sems,)),
            pltpu.SemaphoreType.DMA((96,)),
        ],
        compiler_params=pltpu.CompilerParams(
            collective_id=0, has_side_effects=True, vmem_limit_bytes=62 << 20
        ),
        name="forward",
    )(tokens, out_grad, wq, wk, wv, wg, wo, ffn_left, ffn_right, ffn_down, rates)


class Scatter:
    def __init__(self, place, copies, view, far_x, far_y, near_x, near_y, high, base):
        self.place, self.copies, self.view, self.base = place, copies, view, base
        self.far_x, self.far_y, self.near_x, self.near_y, self.high = far_x, far_y, near_x, near_y, high

    def begin(self, slot):
        place, at = self.place, self.base + 4 * slot
        self.copies.send(self.view(slot, 3, 0), self.far_y.at[slot], at, at, place.by_y)
        self.copies.send(self.view(slot, 3, 1), self.far_x.at[slot], at + 1, at + 1, place.by_x)

    def middle(self, slot):
        place, copies, at = self.place, self.copies, self.base + 4 * slot
        copies.receive(self.far_y.at[slot], at, place.by_y)
        add_to(self.view(slot, 1, 0), self.far_y.at[slot])
        copies.send(self.view(slot, 1, None), self.near_x.at[slot], at + 2, at + 2, place.by_x)
        copies.receive(self.far_x.at[slot], at + 1, place.by_x)
        add_to(self.view(slot, 2, 1), self.far_x.at[slot])
        copies.send(self.view(slot, 2, None), self.near_y.at[slot], at + 3, at + 3, place.by_y)

    def end(self, slot, onward=True):
        place, copies, at = self.place, self.copies, self.base + 4 * slot
        copies.receive(self.near_x.at[slot], at + 2, place.by_x)
        copies.receive(self.near_y.at[slot], at + 3, place.by_y)
        add_to(self.view(slot, 0, None), self.near_x.at[slot], self.near_y.at[slot])
        if slot and onward:
            self.go_up(slot)

    def go_up(self, slot):
        at = self.base + 4 * self.place.n_head + slot
        into = self.high.at[slot - 1]
        self.copies.send(self.view(slot, 0, None), into, at, at, self.place.above(slot))

    def total(self, into=None, slots=(1, 2, 3)):
        place = self.place
        high = [self.high.at[slot - 1] for slot in slots]
        for slot, part in zip(slots, high):
            self.copies.receive(part, self.base + 4 * place.n_head + slot, place.up)
        add_to(self.view(0, 0, None), *high, into=into)


PER_SCATTER = 20


def add_to(ref, *others, into=None):
    def add(into, *refs):
        total = refs[0][...].astype(F32)
        for other in refs[1:]:
            total += other[...].astype(F32)
        into[...] = total.astype(BF)

    refs = (ref if into is None else into, ref) + others
    if len(ref.shape) == 2:
        add(*refs)
    else:
        for i in range(ref.shape[0]):
            add(*(one.at[i] for one in refs))


def dot(left, right):
    return jnp.dot(left, right, preferred_element_type=F32)


def iota(shape, axis):
    return lax.broadcasted_iota(jnp.int32, shape, axis).astype(F32)


def decay_of(head):
    exponent = jnp.full((1, 1), -8.0 / HEADS, F32) * (head + 1).astype(F32)
    return jnp.exp2(exponent)


def middle_kernel(
    n_head,
    wf,
    nm,
    og,
    hidden,
    wo,
    pre,
    query,
    keys,
    values,
    attn,
    cosines,
    sines,
    fresh,
    carry,
    scale,
    feed_out,
    block_out,
    hidden_grad_out,
    branch_out,
    pre_out,
    rates_out,
    wf_ref,
    t_ref,
    g_ref,
    far_x,
    far_y,
    near_x,
    near_y,
    high,
    nm_ref,
    og_ref,
    hidden_ref,
    mid_ref,
    send_ref,
    got_ref,
    block_ref,
    wo_ref,
    gate_ref,
    attn_ref,
    ga_ref,
    qk_pre_ref,
    cos_ref,
    sin_ref,
    fresh_ref,
    carry_ref,
    late_ref,
    pending_ref,
    message_ref,
    scale_ref,
    sum_ref,
    other_sum_ref,
    rates_ref,
    sends,
    receives,
    locals_,
):
    rows, width = hidden.shape
    quarter = width // 4
    units = wf.shape[1] // n_head
    spans = rows // SPAN
    tiles = 2 * spans
    last = n_head - 1
    place = Place(n_head)
    z, core = place.z, place.core
    copies = Copies(sends, receives, locals_)
    own, other = pl.ds(0, rows), pl.ds(rows, rows)

    order = (2, 1, 3, 0)
    load_nm = copies.move(nm, nm_ref)
    load_og = copies.move(og, og_ref)
    load_wf = {}
    for slot in order:
        at = pl.ds(slot * units, units)
        lanes = pl.ds(0, width if slot < last else width - quarter)
        load_wf[slot] = copies.move(wf.at[:, at, lanes], wf_ref.at[:, at, lanes])
    early_loads = [
        copies.move(hidden, hidden_ref),
        copies.move(wo, wo_ref),
        copies.move(scale, scale_ref),
        copies.move(attn, attn_ref),
        copies.move(pre.at[:, :, pl.ds(3 * HEAD_DIM, HEAD_DIM)], gate_ref),
        copies.move(carry, carry_ref),
    ]
    for seq in range(2):
        for slot in range(n_head):
            early_loads.append(copies.move(fresh.at[slot, seq * spans], fresh_ref.at[slot, seq]))
    place.greet()

    def tile(i):
        return pl.ds(pl.multiple_of(i * SPAN, SPAN), SPAN)

    def dot_last(left, right):
        return lax.dot_general(left, right, (((1,), (1,)), ((), ())), preferred_element_type=F32)

    def dot_first(left, right):
        return lax.dot_general(left, right, (((0,), (0,)), ((), ())), preferred_element_type=F32)

    def g_view(slot, q, half):
        size = units if half is None else units // 2
        start = slot * units + (half or 0) * size
        return g_ref.at[:, pl.ds(start, size), pl.ds(q * quarter, quarter)]

    def late_view(ref, q, half):
        rows_at = pl.ds(last * units + half * (units // 2), units // 2)
        return ref.at[:, rows_at, pl.ds(q * quarter, quarter)]

    base = PER_SCATTER
    late_low, late_high = late_view(wf_ref, 3, 0), late_view(wf_ref, 3, 1)
    copies.send(late_view(wf, 1, 0), late_low, base, base, place.by_y)
    copies.send(late_view(wf, 2, 1), late_high, base + 1, base + 1, place.by_x)
    feed = Scatter(place, copies, g_view, far_x, far_y, near_x, near_y, high, 0)

    def feed_slot(slot):
        at = pl.ds(slot * units, units)

        @pl.loop(0, tiles)
        def _(i):
            rows_at = tile(i)
            left = dot_last(wf_ref[0, at, :], nm_ref[rows_at, :])
            right = dot_last(wf_ref[1, at, :], nm_ref[rows_at, :])
            grad = dot_last(wf_ref[2, at, :], og_ref[rows_at, :])
            t_ref[0, at, rows_at] = (grad * right).astype(BF)
            t_ref[1, at, rows_at] = (grad * left).astype(BF)
            t_ref[2, at, rows_at] = (left * right).astype(BF)

        def gradient(columns):
            for m, right in enumerate((nm_ref, nm_ref, og_ref)):
                g_ref[m, at, columns] = dot(t_ref[m, at, :], right[:, columns]).astype(BF)

        gradient(pl.ds(3 * quarter, quarter))
        feed.begin(slot)

        @pl.loop(0, 3)
        def _(q):
            gradient(pl.ds(pl.multiple_of(q * quarter, quarter), quarter))

    load_nm.wait()
    load_og.wait()
    for i, slot in enumerate(order):
        load_wf[slot].wait()
        if slot == last:
            copies.receive(late_low, base, place.by_y)
            copies.receive(late_high, base + 1, place.by_x)
        feed_slot(slot)
        if i == 1:
            feed.middle(order[0])
    feed.middle(order[1])
    base += 2
    for load in early_loads:
        load.wait()

    @pl.loop(0, spans)
    def _(i):
        at = tile(spans + i)
        total = dot_first(t_ref[0, :, at], wf_ref[0]) + dot_first(t_ref[1, :, at], wf_ref[1])
        send_ref[tile(i), :] = total.astype(BF)

    copies.send(send_ref, got_ref, base, base, place.across)
    feed.end(order[0])

    @pl.loop(0, spans)
    def _(i):
        at = tile(i)
        total = dot_first(t_ref[0, :, at], wf_ref[0]) + dot_first(t_ref[1, :, at], wf_ref[1])
        mid_ref[at, :] = total

    copies.receive(got_ref, base, place.across)

    @pl.loop(0, rows // 128)
    def _(i):
        at = pl.ds(pl.multiple_of(i * 128, 128), 128)
        grad = mid_ref[at, :] + got_ref[at, :].astype(F32)
        values = hidden_ref[at, :]
        norm = lax.rsqrt(jnp.mean(values * values, axis=-1, keepdims=True) + EPSILON)
        normed = values * norm
        mean = jnp.mean(grad * normed, axis=-1, keepdims=True)
        grad = og_ref[at, :].astype(F32) + norm * (grad - normed * mean)
        mid_ref[at, :] = grad
        nm_ref[at, :] = grad.astype(BF)

    copies.send(nm_ref.at[own], nm_ref.at[other], base + 1, base + 1, place.across)
    copies.move(mid_ref, hidden_grad_out, later=True)
    loads = []
    for slot in range(n_head):
        lanes = pl.ds(slot * 2 * HEAD_DIM, 2 * HEAD_DIM)
        loads.append(copies.move(query.at[slot], t_ref.at[0, pl.ds(0, 2 * rows), lanes]))
        loads.append(copies.move(keys.at[slot], t_ref.at[1, pl.ds(0, 2 * rows), lanes]))
        lanes = pl.ds(slot * HEAD_DIM, HEAD_DIM)
        loads.append(copies.move(values.at[slot], wf_ref.at[1, pl.ds(0, 2 * rows), lanes]))

    def late_loads(slot):
        turn = slot % 2
        return [
            copies.move(pre.at[slot, :, pl.ds(0, 2 * HEAD_DIM)], qk_pre_ref.at[turn]),
            copies.move(cosines.at[slot], cos_ref.at[turn]),
            copies.move(sines.at[slot], sin_ref.at[turn]),
        ]

    slot_loads = {slot: late_loads(slot) for slot in range(2)}

    def q_at(slot, at):
        return t_ref[0, at, pl.ds(slot * 2 * HEAD_DIM, 2 * HEAD_DIM)]

    def k_at(slot, at):
        return t_ref[1, at, pl.ds(slot * 2 * HEAD_DIM, 2 * HEAD_DIM)]

    def v_at(slot, at):
        return wf_ref[1, at, pl.ds(slot * HEAD_DIM, HEAD_DIM)]

    def pre_of(slot):
        holder, start = ((wf_ref.at[0], 0), (wf_ref.at[0], 1), (wf_ref.at[1], 1), (og_ref, 0))[slot]
        return holder, start * 4 * HEAD_DIM

    def pre_at(slot, at, part):
        holder, start = pre_of(slot)
        return holder.at[at, pl.ds(start + part * HEAD_DIM, HEAD_DIM)]

    def gate_back(seq):
        for n in range(spans):
            at = pl.ds(seq * rows + n * SPAN, SPAN)
            grad = dot_last(nm_ref[at, :], wo_ref[...])
            norm = scale_ref[at, :]
            total = jnp.zeros((SPAN, 1), F32)
            for slot in range(n_head):
                part = grad[:, slot * HEAD_DIM : (slot + 1) * HEAD_DIM]
                normed = attn_ref[slot, at, :] * norm
                pre_at(slot, at, 3)[...] = (part * normed).astype(BF)
                part = part * gate_ref[slot, at, :]
                gate_ref[slot, at, :] = part
                total += jnp.sum(part * normed, axis=-1, keepdims=True)
            sum_ref[at, :] = jnp.broadcast_to(total, (SPAN, HEAD_DIM))

    gate_back(0)
    base += 2
    copies.send(sum_ref.at[own], other_sum_ref.at[other], base, base, place.across)
    copies.receive(nm_ref.at[other], base - 1, place.across)
    copies.move(nm_ref, branch_out, later=True)
    feed.middle(order[2])
    gate_back(1)
    copies.send(sum_ref.at[other], other_sum_ref.at[own], base + 1, base + 1, place.across)
    copies.sent(base - 2)
    feed.middle(order[3])
    for load in loads:
        load.wait()
    copies.receive(other_sum_ref.at[other], base, place.across)
    copies.receive(other_sum_ref.at[own], base + 1, place.across)
    base += 2

    def slot_decay(slot):
        return decay_of(2 * lax.rem(z + slot, n_head) + core)

    for slot in range(n_head):
        decay = slot_decay(slot)
        early = jnp.exp(-decay * (iota((SPAN, HEAD_DIM), 0) + 1.0))

        @pl.loop(0, tiles)
        def _(i):
            at = tile(i)
            norm = scale_ref[at, :]
            mean = (sum_ref[at, :] + other_sum_ref[at, :]) / width
            grad = norm * (gate_ref[slot, at, :] - attn_ref[slot, at, :] * norm * mean)
            grad = grad.astype(BF)
            ga_ref[slot, at, :] = grad
            both = dot_first(
                q_at(slot, at), jnp.concatenate(split(grad.astype(F32) * early), axis=1)
            )
            late_ref[slot, i] = both[:, :HEAD_DIM] + both[:, HEAD_DIM:]

    n_chain = 2 * n_head
    chain_base = base

    def chain_at(index):
        group, seq = lax.div(index, 2), lax.rem(index, 2)
        return lax.rem(group - z + n_head, n_head), seq, decay_of(2 * group + core)

    def chain_copy(index, slot, seq):
        return pltpu.make_async_remote_copy(
            src_ref=message_ref.at[slot, seq],
            dst_ref=pending_ref.at[lax.rem(slot + 1, n_head), seq],
            send_sem=sends.at[chain_base + index],
            recv_sem=receives.at[chain_base + index],
            device_id=place.down,
            device_id_type=MESH,
        )

    def chain_step(index):
        slot, seq, decay = chain_at(index)

        @pl.when(z < last)
        def _():
            copies.receive(pending_ref.at[slot, seq], chain_base + index, place.up)

        @pl.when(z == last)
        def _():
            pending_ref[slot, seq] = jnp.zeros(pending_ref.shape[2:], BF)

        @pl.when(z > 0)
        def _():
            total = jnp.exp(-decay * rows) * pending_ref[slot, seq].astype(F32)
            for n in range(spans):
                total += jnp.exp(-decay * (n * SPAN)) * late_ref[slot, seq * spans + n]
            message_ref[slot, seq] = total.astype(BF)
            chain_copy(index, slot, seq).start()

    base += n_chain
    for i in range(n_chain):
        chain_step(i)
        if i < spans:
            at = pl.ds(rows + i * SPAN, SPAN)
            send_ref[pl.ds(i * SPAN, SPAN), :] = dot_first(t_ref[2, :, at], wf_ref[2]).astype(BF)
            if i + 1 == spans:
                copies.send(send_ref, got_ref, base, base, place.across)
        elif i < tiles:
            at = pl.ds((i - spans) * SPAN, SPAN)
            hidden_ref[at, :] += dot_first(t_ref[2, :, at], wf_ref[2])
    copies.receive(got_ref, base, place.across)

    @pl.loop(0, rows // 128)
    def _(i):
        at = pl.ds(pl.multiple_of(i * 128, 128), 128)
        block_ref[at, :] = (hidden_ref[at, :] + got_ref[at, :].astype(F32)).astype(BF)

    for q in range(4):
        far = pl.ds(pl.multiple_of(place.at[q] * quarter, quarter), quarter)
        src = block_ref.at[:, pl.ds(q * quarter, quarter)]
        copies.move(src, block_out.at[:, far], later=True)
    feed.end(order[1], False)

    offsets = iota((SPAN, SPAN), 0) - iota((SPAN, SPAN), 1)

    def back_slot(slot):
        turn = slot % 2
        decay = slot_decay(slot)
        mask = jnp.where(offsets >= 0.0, jnp.exp(-decay * jnp.maximum(offsets, 0.0)), 0.0)
        places = iota((SPAN, 1), 0)
        early = jnp.exp(-decay * (places + 1.0))
        late = jnp.exp(-decay * (SPAN - 1.0 - places))
        span_decay = jnp.exp(-decay * SPAN)
        rates_ref[slot] = jnp.zeros((8, HEAD_DIM), F32)

        @pl.loop(0, 2)
        def _(seq):
            for n in range(spans):
                i = seq * spans + n
                at, here = tile(i), pl.ds(n * SPAN, SPAN)
                state = carry_ref[slot, seq].astype(F32)
                if n == 1:
                    state = span_decay * state + fresh_ref[slot, seq]
                later = pending_ref[slot, seq].astype(F32)
                if n == 0:
                    later = span_decay * later + late_ref[slot, seq * spans + 1]
                q, k, v, grad = q_at(slot, at), k_at(slot, at), v_at(slot, at), ga_ref[slot, at, :]
                weights = (dot_last(q, k) * mask).astype(BF)
                scores = (dot_last(grad, v) * mask).astype(BF)
                state_high, state_low = split(state)
                grad_query = dot(scores, k)
                grad_query += early * (dot_last(grad, state_high) + dot_last(grad, state_low))
                later_high, later_low = split(later)
                grad_keys = dot_first(scores, q)
                grad_keys += late * (dot_last(v, later_high) + dot_last(v, later_low))
                both = dot(k, jnp.concatenate([later_high, later_low], axis=1))
                grad_values = dot_first(weights, grad)
                grad_values += late * (both[:, :HEAD_DIM] + both[:, HEAD_DIM:])
                pre_at(slot, at, 2)[...] = grad_values.astype(BF)
                cosine, sine = cos_ref[turn, here, :], sin_ref[turn, here, :]
                angles = jnp.zeros((SPAN, HEAD_DIM), F32)
                for part, turned in enumerate((grad_query, grad_keys)):
                    value = qk_pre_ref[turn, at, pl.ds(part * HEAD_DIM, HEAD_DIM)]
                    by_cos, by_sin = turned[:, :HEAD_DIM], turned[:, HEAD_DIM:]
                    gate = 1.0 / (1.0 + jnp.exp(-value))
                    act = by_cos * cosine + by_sin * sine
                    angles += value * gate * (by_sin * cosine - by_cos * sine)
                    act = act * gate * (1.0 + value * (1.0 - gate))
                    pre_at(slot, at, part)[...] = act.astype(BF)
                steps = (z * rows + n * SPAN).astype(F32) + places
                rates_ref[slot, pl.ds(0, 1), :] += jnp.sum(steps * angles, axis=0, keepdims=True)

    for slot in range(n_head):
        for load in slot_loads[slot]:
            load.wait()
        back_slot(slot)
        if slot + 2 < n_head:
            slot_loads[slot + 2] = late_loads(slot + 2)
        holder, start = pre_of(slot)
        src = holder.at[pl.ds(0, 2 * rows), pl.ds(start, 4 * HEAD_DIM)]
        copies.move(src, pre_out.at[slot], later=True)
    feed.end(order[2], False)
    for i, slot in enumerate(order[1:3], 1):
        copies.move(g_view(slot, 0, None), feed_out.at[i], later=True)
    feed.end(order[3])
    feed.total(slots=order[:1])
    copies.move(g_view(0, 0, None), feed_out.at[0], later=True)
    copies.move(rates_ref, rates_out, later=True)

    @pl.when(z > 0)
    def _():
        @pl.loop(0, n_chain)
        def _(index):
            slot, seq, _ = chain_at(index)
            chain_copy(index, slot, seq).wait_send()

    copies.finish()


def middle(n_head, wf, nm, og, hidden, wo, pre, query, keys, values, attn, cos, sin, fresh, carry, scale):
    rows, width = hidden.shape
    units = wf.shape[1] // n_head
    quarter = width // 4
    tall = 2 * rows
    halves = (n_head, 3, units // 2, quarter)
    wholes = (n_head, 3, units, quarter)
    buffers = [
        (wf.shape, BF),
        (wf.shape, BF),
        (wf.shape, BF),
        (halves, BF),
        (halves, BF),
        (wholes, BF),
        (wholes, BF),
        ((n_head - 1,) + wholes[1:], BF),
        ((tall, width), BF),
        ((tall, width), BF),
        ((rows, width), F32),
        ((rows, width), F32),
        ((rows, width), BF),
        ((rows, width), BF),
        ((rows, width), BF),
        (wo.shape, BF),
        ((n_head, tall, HEAD_DIM), F32),
        ((n_head, tall, HEAD_DIM), F32),
        ((n_head, tall, HEAD_DIM), BF),
        ((2, tall, 2 * HEAD_DIM), F32),
        ((2, rows, HEAD_DIM), F32),
        ((2, rows, HEAD_DIM), F32),
        ((n_head, 2, 2 * HEAD_DIM, HEAD_DIM), F32),
        ((n_head, 2, 2 * HEAD_DIM, HEAD_DIM), BF),
        ((n_head, tall // SPAN, 2 * HEAD_DIM, HEAD_DIM), F32),
        ((n_head, 2, 2 * HEAD_DIM, HEAD_DIM), BF),
        ((n_head, 2, 2 * HEAD_DIM, HEAD_DIM), BF),
        ((tall, HEAD_DIM), F32),
        ((tall, HEAD_DIM), F32),
        ((tall, HEAD_DIM), F32),
        ((n_head, 8, HEAD_DIM), F32),
    ]
    outs = [
        ((3,) + wholes[1:], BF),
        ((rows, width), BF),
        ((rows, width), F32),
        ((tall, width), BF),
        ((n_head, tall, 4 * HEAD_DIM), BF),
        ((n_head, 8, HEAD_DIM), F32),
    ]
    n_sems = PER_SCATTER + 2 + 2 + 2 + 2 * n_head + 1
    return pl.pallas_call(
        functools.partial(middle_kernel, n_head),
        out_shape=[jax.ShapeDtypeStruct(*out) for out in outs],
        in_specs=[ANY] * 15,
        out_specs=[ANY] * len(outs),
        scratch_shapes=[pltpu.VMEM(*b) for b in buffers]
        + [
            pltpu.SemaphoreType.DMA((n_sems,)),
            pltpu.SemaphoreType.DMA((n_sems,)),
            pltpu.SemaphoreType.DMA((64,)),
        ],
        compiler_params=pltpu.CompilerParams(
            collective_id=1, has_side_effects=True, vmem_limit_bytes=63 << 20
        ),
        name="middle",
    )(wf, nm, og, hidden, wo, pre, query, keys, values, attn, cos, sin, fresh, carry, scale)


class Share:
    def __init__(self, place, copies, view, base):
        self.place, self.copies, self.view, self.base = place, copies, view, base

    def pass_on(self, q, half, at, device):
        part = self.view(0, q, half)
        self.copies.send(part, part, self.base + at, self.base + at, device)

    def begin(self):
        self.pass_on(0, None, 0, self.place.by_x)
        self.pass_on(0, None, 1, self.place.by_y)
        self.pass_on(0, None, 4, self.place.across)

    def spread(self):
        place, copies, at = self.place, self.copies, self.base
        copies.receive(self.view(0, 1, None), at, place.by_x)
        self.pass_on(1, 0, 2, place.by_y)
        copies.receive(self.view(0, 2, None), at + 1, place.by_y)
        self.pass_on(2, 1, 3, place.by_x)
        self.pass_on(1, None, 5, place.across)
        self.pass_on(2, None, 6, place.across)

    def complete(self):
        place, copies, at = self.place, self.copies, self.base
        copies.receive(self.view(0, 3, 0), at + 2, place.by_y)
        copies.receive(self.view(0, 3, 1), at + 3, place.by_x)
        self.pass_on(3, None, 7, place.across)

    def other_side(self):
        for q in range(4):
            self.copies.receive(self.view(1, q, None), self.base + 4 + q, self.place.across)


PER_SHARE = 8


def last_kernel(
    n_head,
    feed_piece,
    tokens,
    nin,
    branch,
    gated,
    pre,
    wa,
    hidden_grad,
    rates,
    block,
    input_ref,
    block_ref,
    feed_ref,
    attn_ref,
    down_ref,
    rates_both,
    piece_ref,
    piece_high,
    ga_ref,
    a_far_x,
    a_far_y,
    a_near_x,
    a_near_y,
    a_high,
    gd_ref,
    d_far_x,
    d_far_y,
    d_near_x,
    d_near_y,
    d_high,
    nin_ref,
    branch_ref,
    gated_ref,
    pre_ref,
    wa_ref,
    x_ref,
    grad_ref,
    send_ref,
    got_ref,
    rates_high,
    rates_sum,
    rates_got,
    sends,
    receives,
    locals_,
):
    rows, width = tokens.shape
    quarter = width // 4
    units = feed_piece.shape[2]
    spans = rows // SPAN
    place = Place(n_head)
    copies = Copies(sends, receives, locals_)
    order = (2, 1, 3, 0)

    load_feed = [copies.move(feed_piece.at[i], piece_ref.at[i]) for i in range(3)]
    load_nin = copies.move(nin, nin_ref)
    load_pre = {slot: copies.move(pre.at[slot], pre_ref.at[slot]) for slot in order}
    load_gated = copies.move(gated, gated_ref)
    load_branch = copies.move(branch, branch_ref)
    late_loads = [copies.move(wa, wa_ref), copies.move(hidden_grad, grad_ref)]
    late_loads.append(copies.move(block, block_ref))
    for q in range(4):
        far = pl.ds(pl.multiple_of(place.at[q] * quarter, quarter), quarter)
        late_loads.append(copies.move(tokens.at[:, far], x_ref.at[:, pl.ds(q * quarter, quarter)]))
    place.greet()

    def tile(i):
        return pl.ds(pl.multiple_of(i * SPAN, SPAN), SPAN)

    def dot_last(left, right):
        return lax.dot_general(left, right, (((1,), (1,)), ((), ())), preferred_element_type=F32)

    def dot_first(left, right):
        return lax.dot_general(left, right, (((0,), (0,)), ((), ())), preferred_element_type=F32)

    def part(start, half, size):
        if half is None:
            return pl.ds(start, size)
        return pl.ds(start + half * (size // 2), size // 2)

    sides = (place.core, 1 - place.core)

    def start_of(q):
        return pl.multiple_of(place.at[q] * quarter, quarter)

    def feed_view(side, q, half):
        return feed_ref.at[sides[side], :, part(0, half, units), pl.ds(start_of(q), quarter)]

    def attn_view(side, q, half):
        at = part(0, half, quarter)
        start = pl.multiple_of(start_of(q) + at.start, quarter // 2)
        return attn_ref.at[sides[side], pl.ds(start, at.size), :]

    def down_view(side, q, half):
        return down_ref.at[sides[side], part(0, half, HEAD_DIM), pl.ds(start_of(q), quarter)]

    def ga_view(slot, q, half):
        return ga_ref.at[slot, part(q * quarter, half, quarter), :]

    def gd_view(slot, q, half):
        return gd_ref.at[slot, part(0, half, HEAD_DIM), pl.ds(q * quarter, quarter)]

    attn = Scatter(place, copies, ga_view, a_far_x, a_far_y, a_near_x, a_near_y, a_high, 0)
    down = Scatter(place, copies, gd_view, d_far_x, d_far_y, d_near_x, d_near_y, d_high, PER_SCATTER)
    base = 2 * PER_SCATTER
    feed_share = Share(place, copies, feed_view, base)
    attn_share = Share(place, copies, attn_view, base + PER_SHARE)
    down_share = Share(place, copies, down_view, base + 2 * PER_SHARE)
    base += 3 * PER_SHARE

    for i, slot in enumerate(order[1:3], 1):
        load_feed[i].wait()
        at = base + n_head + 3 + i - 1
        copies.send(piece_ref.at[i], piece_high.at[i - 1], at, at, place.above(slot))
    for slot in range(1, n_head):
        into = rates_high.at[slot - 1]
        copies.send(rates.at[slot], into, base + slot, base + slot, place.above(slot))
    load_nin.wait()

    def slot_grads(slot):
        load_pre[slot].wait()

        def gradient(at):
            ga_ref[slot, at, :] = dot_first(nin_ref[:, at], pre_ref[slot]).astype(BF)

        gradient(pl.ds(3 * quarter, quarter))
        attn.begin(slot)
        pl.loop(0, 3)(lambda q: gradient(pl.ds(pl.multiple_of(q * quarter, quarter), quarter)))
        if slot == order[0]:
            load_gated.wait()
            load_branch.wait()
        lanes = pl.ds(slot * HEAD_DIM, HEAD_DIM)
        gd_ref[slot] = dot_first(gated_ref[:, lanes], branch_ref[...]).astype(BF)
        down.begin(slot)

    def middle_step(slot):
        attn.middle(slot)
        down.middle(slot)

    def end(slot):
        attn.end(slot)
        down.end(slot)

    slot_grads(order[0])
    slot_grads(order[1])
    middle_step(order[0])
    slot_grads(order[2])
    slot_grads(order[3])
    for load in late_loads:
        load.wait()

    def grad_in(at):
        total = dot_last(pre_ref[0, at, :], wa_ref[0])
        for slot in range(1, n_head):
            total += dot_last(pre_ref[slot, at, :], wa_ref[slot])
        return total

    @pl.loop(0, spans)
    def _(i):
        send_ref[tile(i), :] = grad_in(tile(spans + i)).astype(BF)

    copies.send(send_ref, got_ref, base, base, place.across)
    middle_step(order[1])
    middle_step(order[2])
    load_feed[0].wait()
    for i in range(2):
        copies.receive(piece_high.at[i], base + n_head + 3 + i, place.up)
    add_to(piece_ref.at[0], piece_high.at[0], piece_high.at[1], into=feed_view(0, 0, None))
    feed_share.begin()

    total = rates[0]
    for slot in range(1, n_head):
        copies.receive(rates_high.at[slot - 1], base + slot, place.up)
        total += rates_high[slot - 1]
    base += n_head
    rates_sum[0] = total
    copies.send(rates_sum.at[0], rates_got.at[0], base, base, place.by_x)

    end(order[0])
    copies.receive(rates_got.at[0], base, place.by_x)
    rates_sum[1] = total + rates_got[0]
    copies.send(rates_sum.at[1], rates_got.at[1], base + 1, base + 1, place.by_y)

    copies.receive(got_ref, base - n_head, place.across)

    @pl.loop(0, spans)
    def _(i):
        at = tile(i)
        values = x_ref[at, :].astype(F32)
        norm = lax.rsqrt(jnp.mean(values * values, axis=-1, keepdims=True) + EPSILON)
        normed = values * norm
        grad = grad_in(at) + got_ref[at, :].astype(F32)
        mean = jnp.mean(grad * normed, axis=-1, keepdims=True)
        grad_ref[at, :] += norm * (grad - normed * mean)

    for q in range(4):
        far = pl.ds(pl.multiple_of(place.at[q] * quarter, quarter), quarter)
        src = grad_ref.at[:, pl.ds(q * quarter, quarter)]
        copies.move(src, input_ref.at[:, far], later=True)
    end(order[1])
    middle_step(order[3])
    copies.receive(rates_got.at[1], base + 1, place.by_y)
    rates_both[sides[0]] = rates_sum[1] + rates_got[1]
    mine = rates_both.at[sides[0]]
    copies.send(mine, mine, base + 2, base + 2, place.across)
    feed_share.spread()
    end(order[2])
    end(order[3])
    attn.total(attn_view(0, 0, None))
    attn_share.begin()
    down.total(down_view(0, 0, None))
    down_share.begin()
    copies.receive(rates_both.at[sides[1]], base + 2, place.across)
    feed_share.complete()
    attn_share.spread()
    down_share.spread()
    feed_share.other_side()
    attn_share.complete()
    down_share.complete()
    attn_share.other_side()
    down_share.other_side()
    copies.finish()


def last(n_head, feed_piece, tokens, nin, branch, gated, pre, wa, hidden_grad, rates, block):
    rows, width = tokens.shape
    _, _, units, quarter = feed_piece.shape
    tall = 2 * rows

    def scatter_buffers(shape, halved):
        half = tuple(n // 2 if i == halved else n for i, n in enumerate(shape))
        return [
            ((n_head,) + half, BF),
            ((n_head,) + half, BF),
            ((n_head,) + shape, BF),
            ((n_head,) + shape, BF),
            ((n_head - 1,) + shape, BF),
        ]

    outs = [
        ((rows, width), F32),
        ((rows, width), BF),
        ((2, 3, units, width), BF),
        ((2, width, 4 * HEAD_DIM), BF),
        ((2, HEAD_DIM, width), BF),
        ((2, 8, HEAD_DIM), F32),
    ]
    buffers = [
        (feed_piece.shape, BF),
        ((2,) + feed_piece.shape[1:], BF),
        ((n_head, width, 4 * HEAD_DIM), BF),
        *scatter_buffers((quarter, 4 * HEAD_DIM), 0),
        ((n_head, HEAD_DIM, width), BF),
        *scatter_buffers((HEAD_DIM, quarter), 0),
        ((tall, width), BF),
        ((tall, width), BF),
        (gated.shape, BF),
        (pre.shape, BF),
        (wa.shape, BF),
        ((rows, width), BF),
        ((rows, width), F32),
        ((rows, width), BF),
        ((rows, width), BF),
        ((n_head - 1, 8, HEAD_DIM), F32),
        ((2, 8, HEAD_DIM), F32),
        ((2, 8, HEAD_DIM), F32),
    ]
    n_sems = 2 * PER_SCATTER + 3 * PER_SHARE + n_head + 3 + 2
    far = [feed_piece, tokens, nin, branch, gated, pre, wa, hidden_grad]
    far = [pltpu.with_memory_space_constraint(array, pltpu.HBM) for array in far]
    block = pltpu.with_memory_space_constraint(block, pltpu.HBM)
    return pl.pallas_call(
        functools.partial(last_kernel, n_head),
        out_shape=[pltpu.VMEM(*out) for out in outs],
        in_specs=[ANY] * 8 + [IN_VMEM, ANY],
        out_specs=[IN_VMEM] * len(outs),
        scratch_shapes=[pltpu.VMEM(*b) for b in buffers]
        + [
            pltpu.SemaphoreType.DMA((n_sems,)),
            pltpu.SemaphoreType.DMA((n_sems,)),
            pltpu.SemaphoreType.DMA((64,)),
        ],
        compiler_params=pltpu.CompilerParams(
            collective_id=2, has_side_effects=True, vmem_limit_bytes=42 << 20
        ),
        name="last",
    )(*far, rates, block)


def finish_kernel(grad, block, feed, attn, down, rates, *refs):
    outs, results, locals_ = refs[:11], refs[11:-1], refs[-1]
    copies = Copies(None, None, locals_)
    (block_out, grad_out, q_out, k_out, v_out, g_out, o_out, rates_out, l_out, r_out, d_out) = outs
    units = feed.shape[2]
    copies.move(grad, grad_out, later=True)
    copies.move(block, block_out, later=True)
    l_ref, r_ref, d_ref, q_ref, k_ref, v_ref, g_ref, o_ref, rates_ref = results
    for side in range(2):
        rates_ref[:, pl.ds(side * HEAD_DIM, HEAD_DIM)] = rates[side, pl.ds(0, 1), :]
    copies.move(rates_ref, rates_out, later=True)
    for i, (ref, out) in enumerate(((l_ref, l_out), (r_ref, r_out), (d_ref, d_out))):
        for side in range(2):
            at = pl.ds(side * units, units)
            ref[at, :] = feed[side, i].astype(F32)
            copies.move(ref.at[at], out.at[at], later=True)
    for i, (ref, out) in enumerate(((q_ref, q_out), (k_ref, k_out), (v_ref, v_out), (g_ref, g_out))):
        lanes = pl.ds(i * HEAD_DIM, HEAD_DIM)
        for side in range(2):
            ref[:, pl.ds(side * HEAD_DIM, HEAD_DIM)] = attn[side, :, lanes].astype(F32)
        copies.move(ref, out, later=True)
    for side in range(2):
        o_ref[pl.ds(side * HEAD_DIM, HEAD_DIM), :] = down[side].astype(F32)
    copies.move(o_ref, o_out, later=True)
    copies.finish()


def finish(grad, block, feed, attn, down, rates):
    _, _, units, width = feed.shape
    projection = ((width, 2 * HEAD_DIM), F32)
    back = ((2 * HEAD_DIM, width), F32)
    results = [((2 * units, width), F32)] * 3 + [projection] * 4 + [back]
    results.append(((1, 2 * HEAD_DIM), F32))
    outs = [(block.shape, BF), (grad.shape, F32)] + results[3:] + results[:3]
    return pl.pallas_call(
        finish_kernel,
        out_shape=[jax.ShapeDtypeStruct(*out) for out in outs],
        in_specs=[IN_VMEM] * 6,
        out_specs=[ANY] * len(outs),
        scratch_shapes=[pltpu.VMEM(*b) for b in results] + [pltpu.SemaphoreType.DMA((48,))],
        compiler_params=pltpu.CompilerParams(vmem_limit_bytes=24 << 20),
        name="finish",
    )(grad, block, feed, attn, down, rates)


def make(n_dp, n_head):
    def on_device(
        tokens,
        attn_query,
        attn_key,
        attn_value,
        attn_gate,
        attn_out,
        rotation_rates,
        ffn_left,
        ffn_right,
        ffn_down,
        out_grad,
    ):
        rates_in = rotation_rates.reshape(1, -1)
        (
            attn_weights,
            out_w,
            ffn_all,
            gathered_in,
            pre,
            query,
            keys,
            values,
            attn,
            cosines,
            sines,
            fresh,
            carry,
            scale_attn,
            gated,
            hidden,
            gathered_mid,
            grad_rows,
        ) = forward(
            n_head,
            tokens,
            out_grad,
            attn_query,
            attn_key,
            attn_value,
            attn_gate,
            attn_out,
            ffn_left.T,
            ffn_right.T,
            ffn_down,
            rates_in,
        )
        feed_piece, block_out, grad_hidden, branch_rows, grad_pre, rates_grad = middle(
            n_head,
            ffn_all,
            gathered_mid,
            grad_rows,
            hidden,
            out_w,
            pre,
            query,
            keys,
            values,
            attn,
            cosines,
            sines,
            fresh,
            carry,
            scale_attn,
        )
        grads = last(
            n_head,
            feed_piece,
            tokens,
            gathered_in,
            branch_rows,
            gated,
            grad_pre,
            attn_weights,
            grad_hidden,
            rates_grad,
            block_out,
        )

        results = finish(*grads)
        rates_grad, left_grad, right_grad = results[7][0], results[8].T, results[9].T
        results = list(results[:7]) + [rates_grad, left_grad, right_grad, results[10]]
        if n_dp > 8:
            groups = [[i + 8 * j for j in range(n_dp // 8)] for i in range(8)]
            grads = [lax.psum(grad, "dp", axis_index_groups=groups) for grad in results[2:]]
            results = results[:2] + grads
        return tuple(results)

    return on_device


def solution(mesh):
    weights = (P(None, "head"),) * 4 + (P("head", None), P("head")) + (P(None, "head"),) * 2
    weights = weights + (P("head", None),)
    rows = P(("dp", "head"), None)
    return jax.shard_map(
        make(mesh.shape["dp"], mesh.shape["head"]),
        mesh=mesh,
        in_specs=(rows,) + weights + (rows,),
        out_specs=(rows, rows) + weights,
        check_vma=False,
    )
```

```python
import functools

import jax
import jax.numpy as jnp
from jax import lax
from jax.experimental import pallas as pl
from jax.experimental.pallas import tpu as pltpu
from jax.sharding import PartitionSpec as P

HEADS = 8
HEAD_DIM = 128
SPAN = 256
EPSILON = 1e-06
BF = jnp.bfloat16
F32 = jnp.float32


MESH = pl.DeviceIdType.MESH
ANY = pl.BlockSpec(memory_space=pl.ANY)
IN_VMEM = pl.BlockSpec(memory_space=pltpu.VMEM)


def split(value):
    high = value.astype(BF)
    return high, (value - high.astype(F32)).astype(BF)


class Place:
    def __init__(self, n_head):
        self.n_head = n_head
        dp = lax.axis_index("dp")
        self.z = lax.axis_index("head")
        self.core = lax.rem(dp, 2)
        x = lax.rem(lax.div(dp, 2), 2)
        y = lax.rem(lax.div(dp, 4), 2)
        self.plane = x + 2 * y
        self.at = [self.plane, self.plane + 1 - 2 * x, self.plane + 2 - 4 * y, 3 - self.plane]
        self.across = {"dp": dp + 1 - 2 * self.core}
        self.by_x = {"dp": dp + 2 - 4 * x}
        self.by_y = {"dp": dp + 4 - 8 * y}
        self.up = {"head": lax.rem(self.z + 1, n_head)}
        self.down = {"head": lax.rem(self.z + n_head - 1, n_head)}

    def above(self, step):
        return {"head": lax.rem(self.z + step, self.n_head)}

    def below(self, step):
        return {"head": lax.rem(self.z + self.n_head - step, self.n_head)}

    def greet(self):
        others = [self.across, self.by_x, self.by_y]
        others += [self.below(step) for step in range(1, self.n_head)]
        for other in others:
            barrier = pltpu.get_barrier_semaphore()
            pl.semaphore_signal(barrier, inc=1, device_id=other, device_id_type=MESH)

    def meet(self):
        pl.semaphore_wait(pltpu.get_barrier_semaphore(), self.n_head + 2)


class Copies:
    def __init__(self, sends, receives, locals_):
        self.sends, self.receives, self.locals = sends, receives, locals_
        self.pending = []
        self.started = {}
        self.n_local = 0

    def send(self, src, dst, out, into, device, when=None):
        copy = pltpu.make_async_remote_copy(
            src_ref=src,
            dst_ref=dst,
            send_sem=self.sends.at[out],
            recv_sem=self.receives.at[into],
            device_id=device,
            device_id_type=MESH,
        )
        if when is None:
            copy.start()
            self.pending.append(copy.wait_send)
            if isinstance(out, int):
                self.started[out] = copy.wait_send
        else:
            pl.when(when)(copy.start)
            self.pending.append(lambda: pl.when(when)(copy.wait_send))

    def receive(self, dst, into, device):
        pltpu.make_async_remote_copy(
            src_ref=dst,
            dst_ref=dst,
            send_sem=self.sends.at[0],
            recv_sem=self.receives.at[into],
            device_id=device,
            device_id_type=MESH,
        ).wait_recv()

    def move(self, src, dst, later=False):
        copy = pltpu.make_async_copy(src, dst, self.locals.at[self.n_local])
        self.n_local += 1
        copy.start()
        if later:
            self.pending.append(copy.wait)
        return copy

    def sent(self, out):
        wait = self.started.pop(out)
        self.pending.remove(wait)
        wait()

    def finish(self):
        for wait in self.pending:
            wait()


class Gather:
    def __init__(self, place, copies, view, base, late=None):
        self.place, self.copies, self.view, self.base = place, copies, view, base
        self.late = late

    def begin(self):
        place, z = self.place, self.place.z
        own = self.view(0, 0, None)
        last = place.n_head - 1
        self.copies.send(
            own, self.view(last, 0, None), self.base, self.base + last, place.up, when=z < last
        )
        self.copies.send(own, self.view(1, 0, None), self.base + 1, self.base + 1, place.down, when=z > 0)

    def arrived(self, slot, when=True):
        place, copies, z, base = self.place, self.copies, self.place.z, self.base
        last = place.n_head - 1
        if when is True:
            copies.receive(self.view(slot, 0, None), base + slot, place.up)
        else:
            pl.when(when)(lambda: copies.receive(self.view(slot, 0, None), base + slot, place.up))
        from_up = z + slot <= last
        piece = self.view(slot, 0, None)
        down = jnp.logical_and(jnp.logical_and(from_up, z > 0), when)
        up = jnp.logical_and(jnp.logical_not(from_up), z < last)
        up = jnp.logical_and(up, when)
        always = None if when is True else when
        after = jnp.minimum(slot + 1, last)
        before = jnp.maximum(slot - 1, 1)
        copies.send(piece, self.view(after, 0, None), base + 1 + slot, base + after, place.down, when=down)
        copies.send(piece, self.view(before, 0, None), base + 1 + slot, base + before, place.up, when=up)
        at = base + 4 * slot + 4
        copies.send(piece, self.view(slot, 1, None), at, at, place.by_x, when=always)
        copies.send(piece, self.view(slot, 2, None), at + 1, at + 1, place.by_y, when=always)

    def spread(self, slot):
        place, copies = self.place, self.copies
        at = self.base + 4 * slot + 4
        now = None if self.late is None else slot != self.late
        low, high = self.view(slot, 3, 0), self.view(slot, 3, 1)
        copies.receive(self.view(slot, 1, None), at, place.by_x)
        copies.send(self.view(slot, 1, 0), low, at + 2, at + 2, place.by_y, when=now)
        copies.receive(self.view(slot, 2, None), at + 1, place.by_y)
        copies.send(self.view(slot, 2, 1), high, at + 3, at + 3, place.by_x, when=now)

    def complete(self, slot):
        place, copies = self.place, self.copies
        at = self.base + 4 * slot + 4

        def receive():
            copies.receive(self.view(slot, 3, 0), at + 2, place.by_y)
            copies.receive(self.view(slot, 3, 1), at + 3, place.by_x)

        if self.late is None:
            receive()
        else:
            pl.when(slot != self.late)(receive)


PER_GATHER = 24


def forward_kernel(
    n_head,
    tokens,
    out_grad,
    wq,
    wk,
    wv,
    wg,
    wo,
    ffn_left,
    ffn_right,
    ffn_down,
    rates,
    wa_out,
    wo_out,
    wf_out,
    nin_out,
    pre_out,
    q_out,
    k_out,
    v_out,
    attn_out,
    cos_out,
    sin_out,
    fresh_out,
    carry_out,
    scale_out,
    gated_out,
    hidden_out,
    nm_out,
    og_out,
    wa_ref,
    wo_ref,
    wf_ref,
    x_ref,
    nin_ref,
    pre_ref,
    q_ref,
    k_ref,
    v_ref,
    attn_ref,
    cos_ref,
    sin_ref,
    fresh_ref,
    carry_ref,
    message_ref,
    squares_ref,
    other_squares_ref,
    gated_ref,
    branch_ref,
    other_branch_ref,
    hidden_ref,
    nm_ref,
    rates_ref,
    og_ref,
    sends,
    receives,
    locals_,
):
    rows, width = tokens.shape
    quarter = width // 4
    units = ffn_down.shape[0] // 2
    tiles = 2 * rows // SPAN
    place = Place(n_head)
    z, core = place.z, place.core
    last = n_head - 1
    place.greet()
    copies = Copies(sends, receives, locals_)

    def columns(start, size):
        return pl.ds(pl.multiple_of(start, size), size)

    def own_weights(q):
        far = columns(place.at[q] * quarter, quarter)
        near = pl.ds(q * quarter, quarter)
        loads = []
        for i, w in enumerate((wq, wk, wv, wg)):
            src = w.at[far, columns(core * HEAD_DIM, HEAD_DIM)]
            loads.append(copies.move(src, wa_ref.at[0, near, pl.ds(i * HEAD_DIM, HEAD_DIM)]))
        src = wo.at[columns(core * HEAD_DIM, HEAD_DIM), far]
        loads.append(copies.move(src, wo_ref.at[pl.ds(0, HEAD_DIM), near]))
        for i, w in enumerate((ffn_left, ffn_right, ffn_down)):
            src = w.at[pl.ds(pl.multiple_of(core * units, 16), units), far]
            loads.append(copies.move(src, wf_ref.at[i, pl.ds(0, units), near]))
        return loads

    own_loads = [own_weights(0)]
    token_loads = [
        copies.move(
            tokens.at[:, columns(place.at[q] * quarter, quarter)],
            x_ref.at[:, pl.ds(q * quarter, quarter)],
        )
        for q in range(4)
    ]
    place.meet()

    def half_rows(half, size):
        return pl.ds(0, size) if half is None else pl.ds(half * (size // 2), size // 2)

    def wa_view(part, slot, q, half):
        at = half_rows(half, quarter)
        lanes = pl.ds(part * 2 * HEAD_DIM, 2 * HEAD_DIM)
        return wa_ref.at[slot, pl.ds(q * quarter + at.start, at.size), lanes]

    def wo_view(slot, q, half):
        at = half_rows(half, HEAD_DIM)
        return wo_ref.at[
            pl.ds(pl.multiple_of(slot * HEAD_DIM + at.start, HEAD_DIM // 2), at.size),
            pl.ds(q * quarter, quarter),
        ]

    def wf_view(slot, q, half):
        at = half_rows(half, units)
        return wf_ref.at[
            :,
            pl.ds(pl.multiple_of(slot * units + at.start, 16), at.size),
            pl.ds(q * quarter, quarter),
        ]

    attn_all = [
        Gather(place, copies, functools.partial(wa_view, part), part * PER_GATHER)
        for part in range(2)
    ]
    attn_all.append(Gather(place, copies, wo_view, 2 * PER_GATHER))
    feed = Gather(place, copies, wf_view, 3 * PER_GATHER, late=last)
    base = 4 * PER_GATHER
    for loads, part in zip((own_loads[0][:2], own_loads[0][2:4], own_loads[0][4:5]), attn_all):
        for load in loads:
            load.wait()
        part.begin()
    grad_loads = [
        copies.move(
            out_grad.at[:, columns(place.at[q] * quarter, quarter)],
            og_ref.at[pl.ds(0, rows), pl.ds(q * quarter, quarter)],
        )
        for q in range(4)
    ]
    own_loads += [own_weights(q) for q in range(1, 4)]
    for step in range(1, n_head):
        copies.send(rates, rates_ref.at[step], base + step, base + step, place.below(step))
    rates_ref[0] = rates[...]

    for load in token_loads:
        load.wait()

    def norm_rows(values):
        mean = jnp.mean(values * values, axis=-1, keepdims=True)
        return values * lax.rsqrt(mean + EPSILON)

    @pl.loop(0, rows // 128)
    def _(i):
        at = pl.ds(pl.multiple_of(i * 128, 128), 128)
        nin_ref[at, :] = norm_rows(x_ref[at, :].astype(F32)).astype(BF)

    base += 4
    for load in grad_loads:
        load.wait()
    og_other = og_ref.at[pl.ds(rows, rows)]
    copies.send(og_ref.at[pl.ds(0, rows)], og_other, base, base, place.across)
    base += 1
    nin_other = nin_ref.at[pl.ds(rows, rows)]
    copies.send(nin_ref.at[pl.ds(0, rows)], nin_other, base, base, place.across)
    for q, loads in enumerate(own_loads):
        for load in loads[5:] if q == 0 else loads:
            load.wait()
    for step in range(1, n_head):
        copies.receive(rates_ref.at[step], base - 5 + step, place.up)
    copies.receive(nin_other, base, place.across)
    copies.move(nin_ref, nin_out, later=True)
    own_rows = pl.ds(0, units)
    copies.move(wf_ref.at[:, own_rows], wf_out.at[:, own_rows], later=True)
    copies.receive(og_other, base - 1, place.across)
    copies.move(og_ref, og_out, later=True)

    def decay_of(head):
        exponent = jnp.full((1, 1), -8.0 / HEADS, F32) * (head + 1).astype(F32)
        return jnp.exp2(exponent)

    def tile(i):
        return pl.ds(pl.multiple_of(i * SPAN, SPAN), SPAN)

    def iota(shape, axis):
        return lax.broadcasted_iota(jnp.int32, shape, axis).astype(F32)

    def dot(left, right):
        return jnp.dot(left, right, preferred_element_type=F32)

    def slot_compute(slot):
        head = 2 * lax.rem(z + slot, n_head) + core
        decay = decay_of(head)
        rate = rates_ref[slot, :, columns(core * HEAD_DIM, HEAD_DIM)]
        coarse = (z * rows).astype(F32) + 32.0 * iota((rows // 32, HEAD_DIM), 0)
        coarse = coarse * rate
        fine = iota((32, HEAD_DIM), 0) * rate
        cos_a, sin_a = jnp.cos(coarse), jnp.sin(coarse)
        cos_b, sin_b = jnp.cos(fine), jnp.sin(fine)
        for a in range(rows // 32):
            cos_row, sin_row = cos_a[a : a + 1], sin_a[a : a + 1]
            cos_ref[slot, pl.ds(a * 32, 32), :] = cos_row * cos_b - sin_row * sin_b
            sin_ref[slot, pl.ds(a * 32, 32), :] = sin_row * cos_b + cos_row * sin_b
        offsets = iota((SPAN, SPAN), 0) - iota((SPAN, SPAN), 1)
        mask = jnp.where(offsets >= 0.0, jnp.exp(-decay * jnp.maximum(offsets, 0.0)), 0.0)
        late = jnp.exp(-decay * (SPAN - 1.0 - iota((SPAN, HEAD_DIM), 0)))

        @pl.loop(0, tiles)
        def _(i):
            at = tile(i)
            pre = dot(nin_ref[at, :], wa_ref[slot])
            pre_ref[slot, at, :] = pre
            here = tile(lax.rem(i, rows // SPAN))
            cosines, sines = cos_ref[slot, here, :], sin_ref[slot, here, :]

            def rotate(values):
                activated = values / (1.0 + jnp.exp(-values))
                turned = jnp.concatenate([activated * cosines, activated * sines], axis=1)
                return turned.astype(BF)

            query = rotate(pre[:, :HEAD_DIM])
            keys = rotate(pre[:, HEAD_DIM : 2 * HEAD_DIM])
            value = pre[:, 2 * HEAD_DIM : 3 * HEAD_DIM].astype(BF)
            q_ref[slot, at, :] = query
            k_ref[slot, at, :] = keys
            v_ref[slot, at, :] = value
            scores = lax.dot_general(
                query, keys, (((1,), (1,)), ((), ())), preferred_element_type=F32
            )
            weights = (scores * mask).astype(BF)
            attn_ref[slot, at, :] = dot(weights, value)
            high, low = split(value.astype(F32) * late)
            both = lax.dot_general(
                keys,
                jnp.concatenate([high, low], axis=1),
                (((0,), (0,)), ((), ())),
                preferred_element_type=F32,
            )
            fresh_ref[slot, i] = both[:, :HEAD_DIM] + both[:, HEAD_DIM:]

        for ref, out in (
            (wa_ref, wa_out),
            (pre_ref, pre_out),
            (q_ref, q_out),
            (k_ref, k_out),
            (v_ref, v_out),
            (cos_ref, cos_out),
            (sin_ref, sin_out),
            (fresh_ref, fresh_out),
        ):
            copies.move(ref.at[slot], out.at[slot], later=True)

    first = 1 + 2 * lax.div(z, last)
    second = 2 + lax.rem(lax.div(z + 1, 2), 2)
    third = 6 - first - second

    for part in attn_all:
        part.arrived(first)
    slot_compute(0)
    for part in attn_all:
        part.arrived(second)
    for part in attn_all:
        part.spread(first)
    for part in attn_all:
        part.arrived(third)
    feed.begin()
    for part in attn_all:
        part.spread(second)
    for part in attn_all[:2]:
        part.complete(first)
    slot_compute(first)
    for part in attn_all:
        part.spread(third)
    feed.arrived(first)
    for part in attn_all[:2]:
        part.complete(second)
    slot_compute(second)
    inner = jnp.logical_and(z > 0, z < last)
    feed.arrived(second, inner)
    for part in attn_all[:2]:
        part.complete(third)
    slot_compute(third)
    base += 1
    chain_base = base
    n_chain = 2 * n_head

    def chain_at(index):
        group, seq = lax.div(index, 2), lax.rem(index, 2)
        return lax.rem(group - z + n_head, n_head), seq, decay_of(2 * group + core)

    def chain_copy(index, slot, seq):
        after = lax.rem(slot + n_head - 1, n_head)
        return pltpu.make_async_remote_copy(
            src_ref=message_ref.at[slot, seq],
            dst_ref=carry_ref.at[after, seq],
            send_sem=sends.at[chain_base + index],
            recv_sem=receives.at[chain_base + index],
            device_id=place.up,
            device_id_type=MESH,
        )

    def hand_on(index, slot, seq, decay):
        total = jnp.exp(-decay * rows) * carry_ref[slot, seq].astype(F32)
        for n in range(rows // SPAN):
            left = rows - (n + 1) * SPAN
            total += jnp.exp(-decay * left) * fresh_ref[slot, seq * (rows // SPAN) + n]
        message_ref[slot, seq] = total.astype(BF)
        chain_copy(index, slot, seq).start()

    @pl.when(z == 0)
    def _():
        @pl.loop(0, n_chain)
        def _(index):
            slot, seq, decay = chain_at(index)
            carry_ref[slot, seq] = jnp.zeros(carry_ref.shape[2:], BF)
            hand_on(index, slot, seq, decay)

    feed.arrived(second, jnp.logical_not(inner))
    feed.spread(first)
    feed.arrived(third)

    @pl.when(z > 0)
    def _():
        @pl.loop(0, n_chain)
        def _(index):
            slot, seq, decay = chain_at(index)
            copies.receive(carry_ref.at[slot, seq], chain_base + index, place.down)
            pl.when(z < last)(lambda: hand_on(index, slot, seq, decay))

    copies.move(carry_ref, carry_out, later=True)
    feed.spread(second)

    def feed_done(slot):
        feed.complete(slot)
        at = pl.ds(pl.multiple_of(slot * units, 16), units)
        copies.move(wf_ref.at[:, at], wf_out.at[:, at], later=True)

    def apply(seq):
        mine = pl.ds(seq * rows, rows)
        squares_ref[mine, :] = jnp.zeros((rows, HEAD_DIM), F32)

        @pl.loop(0, n_head)
        def _(slot):
            decay = decay_of(2 * lax.rem(z + slot, n_head) + core)
            early = jnp.exp(-decay * (iota((SPAN, HEAD_DIM), 0) + 1.0))
            state = carry_ref[slot, seq].astype(F32)
            for n in range(rows // SPAN):
                i = seq * (rows // SPAN) + n
                at = pl.ds(i * SPAN, SPAN)
                both = dot(q_ref[slot, at, :], jnp.concatenate(split(state), axis=1))
                attn = attn_ref[slot, at, :]
                attn += early * (both[:, :HEAD_DIM] + both[:, HEAD_DIM:])
                attn_ref[slot, at, :] = attn
                squares_ref[at, :] += jnp.sum(attn * attn, axis=-1, keepdims=True)
                if n + 1 < rows // SPAN:
                    state = jnp.exp(-decay * SPAN) * state + fresh_ref[slot, i]

    def gating(seq):
        for n in range(rows // SPAN):
            at = pl.ds(seq * rows + n * SPAN, SPAN)
            total = squares_ref[at, :] + other_squares_ref[at, :]
            scale = lax.rsqrt(total / width + EPSILON)
            other_squares_ref[at, :] = scale
            for slot in range(n_head):
                gate = pre_ref[slot, at, pl.ds(3 * HEAD_DIM, HEAD_DIM)]
                gated = (attn_ref[slot, at, :] * scale * gate).astype(BF)
                gated_ref[at, pl.ds(slot * HEAD_DIM, HEAD_DIM)] = gated

    base += n_chain
    own, other = pl.ds(0, rows), pl.ds(rows, rows)
    apply(1)
    copies.send(squares_ref.at[other], other_squares_ref.at[own], base, base, place.across)
    apply(0)
    copies.send(squares_ref.at[own], other_squares_ref.at[other], base + 1, base + 1, place.across)
    copies.move(attn_ref, attn_out, later=True)
    for slot in (first, second, third):
        attn_all[2].complete(slot)
    copies.receive(other_squares_ref.at[other], base + 1, place.across)
    gating(1)
    feed_done(first)
    base += 2
    for n in range(rows // SPAN):
        gated = gated_ref[pl.ds(rows + n * SPAN, SPAN), :]
        branch_ref[pl.ds(n * SPAN, SPAN), :] = dot(gated, wo_ref[...]).astype(BF)
    copies.send(branch_ref, other_branch_ref, base, base, place.across)
    copies.receive(other_squares_ref.at[own], base - 2, place.across)
    gating(0)
    copies.move(other_squares_ref, scale_out, later=True)
    copies.move(gated_ref, gated_out, later=True)
    copies.move(wo_ref, wo_out, later=True)
    feed.spread(third)
    feed_done(second)

    @pl.loop(0, rows // SPAN)
    def _(i):
        at = tile(i)
        hidden_ref[at, :] = x_ref[at, :].astype(F32) + dot(gated_ref[at, :], wo_ref[...])

    copies.receive(other_branch_ref, base, place.across)

    @pl.loop(0, rows // 128)
    def _(i):
        at = pl.ds(pl.multiple_of(i * 128, 128), 128)
        hidden = hidden_ref[at, :] + other_branch_ref[at, :].astype(F32)
        hidden_ref[at, :] = hidden
        nm_ref[at, :] = norm_rows(hidden).astype(BF)

    copies.send(nm_ref.at[own], nm_ref.at[other], base + 1, base + 1, place.across)
    copies.move(hidden_ref, hidden_out, later=True)
    feed_done(third)
    copies.receive(nm_ref.at[other], base + 1, place.across)
    copies.move(nm_ref, nm_out, later=True)

    @pl.when(z < last)
    def _():
        @pl.loop(0, n_chain)
        def _(index):
            slot, seq, _ = chain_at(index)
            chain_copy(index, slot, seq).wait_send()

    copies.finish()


def forward(n_head, tokens, out_grad, wq, wk, wv, wg, wo, ffn_left, ffn_right, ffn_down, rates):
    rows, width = tokens.shape
    units = ffn_down.shape[0] // 2
    tall = 2 * rows
    buffers = [
        ((n_head, width, 4 * HEAD_DIM), BF),
        ((n_head * HEAD_DIM, width), BF),
        ((3, n_head * units, width), BF),
        ((rows, width), BF),
        ((tall, width), BF),
        ((n_head, tall, 4 * HEAD_DIM), F32),
        ((n_head, tall, 2 * HEAD_DIM), BF),
        ((n_head, tall, 2 * HEAD_DIM), BF),
        ((n_head, tall, HEAD_DIM), BF),
        ((n_head, tall, HEAD_DIM), F32),
        ((n_head, rows, HEAD_DIM), F32),
        ((n_head, rows, HEAD_DIM), F32),
        ((n_head, tall // SPAN, 2 * HEAD_DIM, HEAD_DIM), F32),
        ((n_head, 2, 2 * HEAD_DIM, HEAD_DIM), BF),
        ((n_head, 2, 2 * HEAD_DIM, HEAD_DIM), BF),
        ((tall, HEAD_DIM), F32),
        ((tall, HEAD_DIM), F32),
        ((tall, n_head * HEAD_DIM), BF),
        ((rows, width), BF),
        ((rows, width), BF),
        ((rows, width), F32),
        ((tall, width), BF),
        ((n_head, 1, 2 * HEAD_DIM), F32),
        ((tall, width), BF),
    ]
    out_of = [0, 1, 2, 4, 5, 6, 7, 8, 9, 10, 11, 12, 13, 16, 17, 20, 21, 23]
    n_sems = 4 * PER_GATHER + 4 + 1 + 1 + 2 * n_head + 2 + 2
    return pl.pallas_call(
        functools.partial(forward_kernel, n_head),
        out_shape=[jax.ShapeDtypeStruct(*buffers[i]) for i in out_of],
        in_specs=[ANY] * 10 + [IN_VMEM],
        out_specs=[ANY] * len(out_of),
        scratch_shapes=[pltpu.VMEM(*b) for b in buffers]
        + [
            pltpu.SemaphoreType.DMA((n_sems,)),
            pltpu.SemaphoreType.DMA((n_sems,)),
            pltpu.SemaphoreType.DMA((96,)),
        ],
        compiler_params=pltpu.CompilerParams(
            collective_id=0, has_side_effects=True, vmem_limit_bytes=62 << 20
        ),
        name="forward",
    )(tokens, out_grad, wq, wk, wv, wg, wo, ffn_left, ffn_right, ffn_down, rates)


class Scatter:
    def __init__(self, place, copies, view, far_x, far_y, near_x, near_y, high, base, items=None):
        self.place, self.copies, self.view, self.base = place, copies, view, base
        self.items = items
        self.far_x, self.far_y, self.near_x, self.near_y, self.high = far_x, far_y, near_x, near_y, high

    def part(self, buffer, slot):
        return buffer.at[slot] if self.items is None else buffer.at[slot, pl.ds(0, self.items(slot))]

    def begin(self, slot):
        place, at = self.place, self.base + 4 * slot
        self.copies.send(self.view(slot, 3, 0), self.part(self.far_y, slot), at, at, place.by_y)
        self.copies.send(self.view(slot, 3, 1), self.part(self.far_x, slot), at + 1, at + 1, place.by_x)

    def middle(self, slot):
        place, copies, at = self.place, self.copies, self.base + 4 * slot
        copies.receive(self.part(self.far_y, slot), at, place.by_y)
        add_to(self.view(slot, 1, 0), self.part(self.far_y, slot))
        copies.send(self.view(slot, 1, None), self.part(self.near_x, slot), at + 2, at + 2, place.by_x)
        copies.receive(self.part(self.far_x, slot), at + 1, place.by_x)
        add_to(self.view(slot, 2, 1), self.part(self.far_x, slot))
        copies.send(self.view(slot, 2, None), self.part(self.near_y, slot), at + 3, at + 3, place.by_y)

    def end(self, slot, onward=True):
        place, copies, at = self.place, self.copies, self.base + 4 * slot
        copies.receive(self.part(self.near_x, slot), at + 2, place.by_x)
        copies.receive(self.part(self.near_y, slot), at + 3, place.by_y)
        add_to(self.view(slot, 0, None), self.part(self.near_x, slot), self.part(self.near_y, slot))
        if slot and onward:
            self.go_up(slot)

    def go_up(self, slot):
        at = self.base + 4 * self.place.n_head + slot
        into = self.high.at[slot - 1]
        self.copies.send(self.view(slot, 0, None), into, at, at, self.place.above(slot))

    def total(self, into=None, slots=(1, 2, 3)):
        place = self.place
        high = [self.high.at[slot - 1] for slot in slots]
        for slot, part in zip(slots, high):
            self.copies.receive(part, self.base + 4 * place.n_head + slot, place.up)
        add_to(self.view(0, 0, None), *high, into=into)


PER_SCATTER = 20


def add_to(ref, *others, into=None):
    def add(into, *refs):
        total = refs[0][...].astype(F32)
        for other in refs[1:]:
            total += other[...].astype(F32)
        into[...] = total.astype(BF)

    refs = (ref if into is None else into, ref) + others
    if len(ref.shape) == 2:
        add(*refs)
    else:
        for i in range(ref.shape[0]):
            add(*(one.at[i] for one in refs))


def dot(left, right):
    return jnp.dot(left, right, preferred_element_type=F32)


def iota(shape, axis):
    return lax.broadcasted_iota(jnp.int32, shape, axis).astype(F32)


def decay_of(head):
    exponent = jnp.full((1, 1), -8.0 / HEADS, F32) * (head + 1).astype(F32)
    return jnp.exp2(exponent)


def middle_kernel(
    n_head,
    wf,
    nm,
    og,
    hidden,
    wo,
    pre,
    query,
    attn,
    scale,
    feed_out,
    block_out,
    hidden_grad_out,
    branch_out,
    gate_out,
    ga_out,
    late_out,
    wf_ref,
    t_ref,
    g_ref,
    far_x,
    far_y,
    near_x,
    near_y,
    early_ref,
    high_ref,
    high_first_ref,
    high_third_ref,
    nm_ref,
    og_ref,
    branch_ref,
    hidden_ref,
    mid_ref,
    send_ref,
    got_ref,
    block_ref,
    wo_ref,
    gate_ref,
    attn_ref,
    ga_ref,
    late_ref,
    scale_ref,
    sum_ref,
    other_sum_ref,
    sends,
    receives,
    locals_,
):
    rows, width = hidden.shape
    quarter = width // 4
    units = wf.shape[1] // n_head
    spans = rows // SPAN
    tiles = 2 * spans
    last = n_head - 1
    place = Place(n_head)
    z, core = place.z, place.core
    place.greet()
    copies = Copies(sends, receives, locals_)
    own, other = pl.ds(0, rows), pl.ds(rows, rows)

    order = (2, 1, 3, 0)
    load_nm = copies.move(nm, nm_ref)
    load_og = copies.move(og, og_ref)
    load_wf = {}
    for slot in order:
        at = pl.ds(slot * units, units)
        lanes = pl.ds(0, width if slot < last else width - quarter)
        load_wf[slot] = copies.move(wf.at[:, at, lanes], wf_ref.at[:, at, lanes])
    early_loads = [
        copies.move(hidden, hidden_ref),
        copies.move(wo, wo_ref),
        copies.move(scale, scale_ref),
        copies.move(attn, attn_ref),
        copies.move(pre.at[:, :, pl.ds(3 * HEAD_DIM, HEAD_DIM)], gate_ref),
    ]
    place.meet()

    def tile(i):
        return pl.ds(pl.multiple_of(i * SPAN, SPAN), SPAN)

    def dot_last(left, right):
        return lax.dot_general(left, right, (((1,), (1,)), ((), ())), preferred_element_type=F32)

    def dot_first(left, right):
        return lax.dot_general(left, right, (((0,), (0,)), ((), ())), preferred_element_type=F32)

    early_slot, down = 1, 2

    def items(slot):
        return down if slot == early_slot else 3

    def g_view(slot, q, half):
        size = units if half is None else units // 2
        start = slot * units + (half or 0) * size
        return g_ref.at[pl.ds(0, items(slot)), pl.ds(start, size), pl.ds(q * quarter, quarter)]

    def late_view(ref, q, half):
        rows_at = pl.ds(last * units + half * (units // 2), units // 2)
        return ref.at[:, rows_at, pl.ds(q * quarter, quarter)]

    base = PER_SCATTER
    late_low, late_high = late_view(wf_ref, 3, 0), late_view(wf_ref, 3, 1)
    copies.send(late_view(wf, 1, 0), late_low, base, base, place.by_y)
    copies.send(late_view(wf, 2, 1), late_high, base + 1, base + 1, place.by_x)
    feed = Scatter(place, copies, g_view, far_x, far_y, near_x, near_y, None, 0, items)
    up_base = base + 2

    def feed_products(slot):
        at = pl.ds(slot * units, units)
        load_wf[slot].wait()

        @pl.loop(0, tiles)
        def _(i):
            rows_at = tile(i)
            left = dot_last(wf_ref[0, at, :], nm_ref[rows_at, :])
            right = dot_last(wf_ref[1, at, :], nm_ref[rows_at, :])
            grad = dot_last(wf_ref[2, at, :], og_ref[rows_at, :])
            t_ref[0, at, rows_at] = (grad * right).astype(BF)
            t_ref[1, at, rows_at] = (grad * left).astype(BF)
            t_ref[2, at, rows_at] = (left * right).astype(BF)

    def feed_gradients(slot):
        at = pl.ds(slot * units, units)

        def gradient(columns, of=(0, 1, 2)):
            for m in of:
                right = og_ref if m == down else nm_ref
                g_ref[m, at, columns] = dot(t_ref[m, at, :], right[:, columns]).astype(BF)

        def gradients(n, of=(0, 1, 2)):
            @pl.loop(0, n)
            def _(q):
                gradient(pl.ds(pl.multiple_of(q * quarter, quarter), quarter), of)

        if slot == 0:
            gradients(4)
            return
        of = tuple(range(items(slot)))
        if slot == early_slot:
            gradients(4, (down,))
            copies.send(g_ref.at[down, at], early_ref, up_base, up_base, place.above(slot))
        gradient(pl.ds(3 * quarter, quarter), of)
        feed.begin(slot)
        gradients(3, of)

    load_nm.wait()
    load_og.wait()
    for slot in order[:2]:
        feed_products(slot)
        feed_gradients(slot)
    feed.middle(order[0])
    copies.receive(late_low, base, place.by_y)
    copies.receive(late_high, base + 1, place.by_x)
    feed_products(order[2])
    feed_gradients(order[2])
    feed_products(order[3])
    feed.middle(order[1])
    base += 2 + 4
    for load in early_loads:
        load.wait()

    @pl.loop(0, spans)
    def _(i):
        at = tile(spans + i)
        total = dot_first(t_ref[0, :, at], wf_ref[0]) + dot_first(t_ref[1, :, at], wf_ref[1])
        send_ref[tile(i), :] = total.astype(BF)

    copies.send(send_ref, got_ref, base, base, place.across)

    @pl.loop(0, spans)
    def _(i):
        at = tile(i)
        total = dot_first(t_ref[0, :, at], wf_ref[0]) + dot_first(t_ref[1, :, at], wf_ref[1])
        mid_ref[at, :] = total

    feed_gradients(order[3])
    feed.end(order[0], False)
    both, second_at = pl.ds(0, down), pl.ds(order[0] * units, units)
    near = pl.ds(0, quarter)
    above = place.above(order[0])
    copies.send(g_ref.at[:, second_at, near], high_ref, up_base + 1, up_base + 1, above)
    copies.receive(early_ref, up_base, place.up)
    add_to(g_ref.at[down, pl.ds(0, units)], early_ref)
    feed.begin(0)
    copies.receive(got_ref, base, place.across)

    @pl.loop(0, rows // 128)
    def _(i):
        at = pl.ds(pl.multiple_of(i * 128, 128), 128)
        grad = mid_ref[at, :] + got_ref[at, :].astype(F32)
        values = hidden_ref[at, :]
        norm = lax.rsqrt(jnp.mean(values * values, axis=-1, keepdims=True) + EPSILON)
        normed = values * norm
        mean = jnp.mean(grad * normed, axis=-1, keepdims=True)
        grad = og_ref[at, :].astype(F32) + norm * (grad - normed * mean)
        mid_ref[at, :] = grad
        branch_ref[at, :] = grad.astype(BF)

    copies.send(branch_ref.at[own], branch_ref.at[other], base + 1, base + 1, place.across)
    copies.move(mid_ref, hidden_grad_out, later=True)
    query_loads = []
    for slot in range(n_head):
        lanes = pl.ds(slot * 2 * HEAD_DIM, 2 * HEAD_DIM)
        query_loads.append(copies.move(query.at[slot], t_ref.at[0, pl.ds(0, 2 * rows), lanes]))

    def gate_back(seq):
        for n in range(spans):
            at = pl.ds(seq * rows + n * SPAN, SPAN)
            grad = dot_last(branch_ref[at, :], wo_ref[...])
            norm = scale_ref[at, :]
            total = jnp.zeros((SPAN, 1), F32)
            for slot in range(n_head):
                lanes = pl.ds(slot * HEAD_DIM, HEAD_DIM)
                part = grad[:, slot * HEAD_DIM : (slot + 1) * HEAD_DIM]
                normed = attn_ref[slot, at, :] * norm
                og_ref[at, lanes] = (part * normed).astype(BF)
                part = part * gate_ref[slot, at, :]
                gate_ref[slot, at, :] = part
                total += jnp.sum(part * normed, axis=-1, keepdims=True)
            sum_ref[at, :] = jnp.broadcast_to(total, (SPAN, HEAD_DIM))

    gate_back(0)
    base += 2
    copies.send(sum_ref.at[own], other_sum_ref.at[other], base, base, place.across)
    copies.receive(branch_ref.at[other], base - 1, place.across)
    copies.move(branch_ref, branch_out, later=True)
    gate_back(1)
    copies.send(sum_ref.at[other], other_sum_ref.at[own], base + 1, base + 1, place.across)
    copies.move(og_ref.at[:, pl.ds(0, n_head * HEAD_DIM)], gate_out, later=True)
    copies.sent(base - 2)
    feed.middle(order[2])

    @pl.loop(0, spans)
    def _(i):
        send_ref[tile(i), :] = dot_first(t_ref[2, :, tile(spans + i)], wf_ref[2]).astype(BF)

    copies.send(send_ref, got_ref, base + 2, base + 2, place.across)

    @pl.loop(0, spans)
    def _(i):
        at = tile(i)
        hidden_ref[at, :] += dot_first(t_ref[2, :, at], wf_ref[2])

    feed.end(order[1], False)
    src = g_ref.at[both, pl.ds(order[1] * units, units), near]
    copies.send(src, high_first_ref, up_base + 2, up_base + 2, place.above(order[1]))
    for load in query_loads:
        load.wait()
    copies.receive(other_sum_ref.at[other], base, place.across)
    copies.receive(other_sum_ref.at[own], base + 1, place.across)
    feed.middle(order[3])

    for slot in range(n_head):
        decay = decay_of(2 * lax.rem(z + slot, n_head) + core)
        early = jnp.exp(-decay * (iota((SPAN, HEAD_DIM), 0) + 1.0))

        @pl.loop(0, tiles)
        def _(i):
            at = tile(i)
            norm = scale_ref[at, :]
            mean = (sum_ref[at, :] + other_sum_ref[at, :]) / width
            grad = norm * (gate_ref[slot, at, :] - attn_ref[slot, at, :] * norm * mean)
            grad = grad.astype(BF)
            ga_ref[slot, at, :] = grad
            q = t_ref[0, at, pl.ds(slot * 2 * HEAD_DIM, 2 * HEAD_DIM)]
            both_terms = dot_first(
                q, jnp.concatenate(split(grad.astype(F32) * early), axis=1)
            )
            late_ref[slot, i] = both_terms[:, :HEAD_DIM] + both_terms[:, HEAD_DIM:]

        copies.move(ga_ref.at[slot], ga_out.at[slot], later=True)
        copies.move(late_ref.at[slot], late_out.at[slot], later=True)

    copies.receive(got_ref, base + 2, place.across)

    @pl.loop(0, rows // 128)
    def _(i):
        at = pl.ds(pl.multiple_of(i * 128, 128), 128)
        block_ref[at, :] = (hidden_ref[at, :] + got_ref[at, :].astype(F32)).astype(BF)

    for q in range(4):
        far = pl.ds(pl.multiple_of(place.at[q] * quarter, quarter), quarter)
        src = block_ref.at[:, pl.ds(q * quarter, quarter)]
        copies.move(src, block_out.at[:, far], later=True)
    feed.end(order[2], False)
    src = g_ref.at[:, pl.ds(order[2] * units, units), near]
    copies.send(src, high_third_ref, up_base + 3, up_base + 3, place.above(order[2]))
    copies.receive(high_ref, up_base + 1, place.up)
    copies.receive(high_first_ref, up_base + 2, place.up)
    feed.end(order[3], False)
    first_rows = pl.ds(0, units)
    add_to(g_ref.at[both, first_rows, near], high_ref.at[both], high_first_ref)
    add_to(g_ref.at[down, first_rows, near], high_ref.at[down])
    copies.receive(high_third_ref, up_base + 3, place.up)
    add_to(g_view(0, 0, None), high_third_ref)
    copies.move(g_view(0, 0, None), feed_out, later=True)
    copies.finish()


def middle(n_head, wf, nm, og, hidden, wo, pre, query, attn, scale):
    rows, width = hidden.shape
    units = wf.shape[1] // n_head
    quarter = width // 4
    tall = 2 * rows
    halves = (n_head, 3, units // 2, quarter)
    wholes = (n_head, 3, units, quarter)
    late = ((n_head, tall // SPAN, 2 * HEAD_DIM, HEAD_DIM), F32)
    buffers = [
        (wf.shape, BF),
        (wf.shape, BF),
        (wf.shape, BF),
        (halves, BF),
        (halves, BF),
        (wholes, BF),
        (wholes, BF),
        ((units, width), BF),
        (wholes[1:], BF),
        ((2, units, quarter), BF),
        (wholes[1:], BF),
        ((tall, width), BF),
        ((tall, width), BF),
        ((tall, width), BF),
        ((rows, width), F32),
        ((rows, width), F32),
        ((rows, width), BF),
        ((rows, width), BF),
        ((rows, width), BF),
        (wo.shape, BF),
        (attn.shape, F32),
        (attn.shape, F32),
        (attn.shape, BF),
        late,
        (scale.shape, F32),
        (scale.shape, F32),
        (scale.shape, F32),
    ]
    outs = [
        (wholes[1:], BF),
        ((rows, width), BF),
        ((rows, width), F32),
        ((tall, width), BF),
        ((tall, n_head * HEAD_DIM), BF),
        (attn.shape, BF),
        late,
    ]
    n_sems = PER_SCATTER + 2 + 4 + 2 + 3
    return pl.pallas_call(
        functools.partial(middle_kernel, n_head),
        out_shape=[jax.ShapeDtypeStruct(*out) for out in outs],
        in_specs=[ANY] * 9,
        out_specs=[ANY] * len(outs),
        scratch_shapes=[pltpu.VMEM(*b) for b in buffers]
        + [
            pltpu.SemaphoreType.DMA((n_sems,)),
            pltpu.SemaphoreType.DMA((n_sems,)),
            pltpu.SemaphoreType.DMA((64,)),
        ],
        compiler_params=pltpu.CompilerParams(
            collective_id=1, has_side_effects=True, vmem_limit_bytes=63 << 20
        ),
        name="middle",
    )(wf, nm, og, hidden, wo, pre, query, attn, scale)


class Share:
    def __init__(self, place, copies, view, base):
        self.place, self.copies, self.view, self.base = place, copies, view, base

    def pass_on(self, q, half, at, device):
        part = self.view(0, q, half)
        self.copies.send(part, part, self.base + at, self.base + at, device)

    def begin(self):
        self.pass_on(0, None, 0, self.place.by_x)
        self.pass_on(0, None, 1, self.place.by_y)
        self.pass_on(0, None, 4, self.place.across)

    def spread(self):
        place, copies, at = self.place, self.copies, self.base
        copies.receive(self.view(0, 1, None), at, place.by_x)
        self.pass_on(1, 0, 2, place.by_y)
        copies.receive(self.view(0, 2, None), at + 1, place.by_y)
        self.pass_on(2, 1, 3, place.by_x)
        self.pass_on(1, None, 5, place.across)
        self.pass_on(2, None, 6, place.across)

    def complete(self):
        place, copies, at = self.place, self.copies, self.base
        copies.receive(self.view(0, 3, 0), at + 2, place.by_y)
        copies.receive(self.view(0, 3, 1), at + 3, place.by_x)
        self.pass_on(3, None, 7, place.across)

    def other_side(self):
        for q in range(4):
            self.copies.receive(self.view(1, q, None), self.base + 4 + q, self.place.across)


PER_SHARE = 8


def last_kernel(
    n_head,
    late,
    feed_piece,
    nin,
    gate_pre,
    gated,
    branch,
    query,
    keys,
    values,
    grad_attn,
    carry,
    fresh,
    pre,
    cosines,
    sines,
    wa,
    hidden_grad,
    block,
    tokens,
    input_ref,
    block_ref,
    feed_ref,
    attn_ref,
    rates_both,
    ga_ref,
    a_far_x,
    a_far_y,
    a_near_x,
    a_near_y,
    a_high,
    g_far_x,
    g_far_y,
    g_near_x,
    g_near_y,
    g_high,
    late_ref,
    pending_ref,
    message_ref,
    nin_ref,
    gate_ref,
    gated_ref,
    branch_ref,
    q_ref,
    k_ref,
    v_ref,
    grad_attn_ref,
    carry_ref,
    fresh_ref,
    qk_pre_ref,
    cos_ref,
    sin_ref,
    pre_ref,
    wa_ref,
    x_ref,
    grad_ref,
    send_ref,
    got_ref,
    rates_ref,
    rates_high,
    rates_sum,
    rates_got,
    sends,
    receives,
    locals_,
):
    rows, width = tokens.shape
    quarter = width // 4
    units = feed_piece.shape[1]
    spans = rows // SPAN
    tiles = 2 * spans
    last = n_head - 1
    three = 3 * HEAD_DIM
    place = Place(n_head)
    place.greet()
    z, core = place.z, place.core
    copies = Copies(sends, receives, locals_)
    order = (2, 1, 3, 0)
    sides = (core, 1 - core)

    own_block = pl.ds(pl.multiple_of(place.plane * quarter, quarter), quarter)
    load_feed = copies.move(feed_piece, feed_ref.at[sides[0], :, :, own_block])
    load_late = copies.move(late, late_ref)
    load_first = [copies.move(nin, nin_ref), copies.move(gate_pre, gate_ref)]
    load_second = [copies.move(gated, gated_ref), copies.move(branch, branch_ref)]
    load_back = [
        copies.move(src, dst)
        for src, dst in (
            (query, q_ref),
            (keys, k_ref),
            (values, v_ref),
            (grad_attn, grad_attn_ref),
            (carry, carry_ref),
        )
    ]
    for seq in range(2):
        for slot in range(n_head):
            load_back.append(copies.move(fresh.at[slot, seq * spans], fresh_ref.at[slot, seq]))

    def slot_load(slot, turn):
        return [
            copies.move(pre.at[slot, :, pl.ds(0, 2 * HEAD_DIM)], qk_pre_ref.at[turn]),
            copies.move(cosines.at[slot], cos_ref.at[turn]),
            copies.move(sines.at[slot], sin_ref.at[turn]),
        ]

    slot_loads = [slot_load(slot, turn) for turn, slot in enumerate(order[:2])]
    late_loads = [
        copies.move(wa, wa_ref),
        copies.move(hidden_grad, grad_ref),
        copies.move(block, block_ref),
    ]
    for q in range(4):
        far = pl.ds(pl.multiple_of(place.at[q] * quarter, quarter), quarter)
        late_loads.append(copies.move(tokens.at[:, far], x_ref.at[:, pl.ds(q * quarter, quarter)]))
    place.meet()

    def tile(i):
        return pl.ds(pl.multiple_of(i * SPAN, SPAN), SPAN)

    def dot_last(left, right):
        return lax.dot_general(left, right, (((1,), (1,)), ((), ())), preferred_element_type=F32)

    def dot_first(left, right):
        return lax.dot_general(left, right, (((0,), (0,)), ((), ())), preferred_element_type=F32)

    def part(start, half, size):
        if half is None:
            return pl.ds(start, size)
        return pl.ds(start + half * (size // 2), size // 2)

    def start_of(q):
        return pl.multiple_of(place.at[q] * quarter, quarter)

    def feed_view(side, q, half):
        return feed_ref.at[sides[side], :, part(0, half, units), pl.ds(start_of(q), quarter)]

    def lanes_view(lanes, side, q, half):
        at = part(0, half, quarter)
        start = pl.multiple_of(start_of(q) + at.start, quarter // 2)
        return attn_ref.at[sides[side], pl.ds(start, at.size), lanes]

    def ga_view(lanes, slot, q, half):
        return ga_ref.at[slot, part(q * quarter, half, quarter), lanes]

    gate_lanes, rest_lanes = pl.ds(three, 2 * HEAD_DIM), pl.ds(0, three)
    weight_lanes = pl.ds(three, HEAD_DIM)
    of_gate = functools.partial(ga_view, gate_lanes)
    of_rest = functools.partial(ga_view, rest_lanes)
    gate = Scatter(place, copies, of_gate, g_far_x, g_far_y, g_near_x, g_near_y, g_high, 0)
    base = PER_SCATTER
    rest = Scatter(place, copies, of_rest, a_far_x, a_far_y, a_near_x, a_near_y, a_high, base)
    base += PER_SCATTER
    to_gate = functools.partial(lanes_view, gate_lanes)
    to_rest = functools.partial(lanes_view, rest_lanes)
    shares = []
    for view in (feed_view, to_gate, to_rest):
        shares.append(Share(place, copies, view, base))
        base += PER_SHARE
    feed_share, gate_share, rest_share = shares

    load_feed.wait()
    feed_share.begin()

    n_chain = 2 * n_head
    chain_base = base
    base += n_chain

    def chain_at(index):
        group, seq = lax.div(index, 2), lax.rem(index, 2)
        return lax.rem(group - z + n_head, n_head), seq, decay_of(2 * group + core)

    def chain_copy(index, slot, seq):
        return pltpu.make_async_remote_copy(
            src_ref=message_ref.at[slot, seq],
            dst_ref=pending_ref.at[lax.rem(slot + 1, n_head), seq],
            send_sem=sends.at[chain_base + index],
            recv_sem=receives.at[chain_base + index],
            device_id=place.down,
            device_id_type=MESH,
        )

    def hand_on(index):
        slot, seq, decay = chain_at(index)
        total = jnp.exp(-decay * rows) * pending_ref[slot, seq].astype(F32)
        for n in range(spans):
            total += jnp.exp(-decay * (n * SPAN)) * late_ref[slot, seq * spans + n]
        message_ref[slot, seq] = total.astype(BF)
        chain_copy(index, slot, seq).start()

    def take(index):
        slot, seq, _ = chain_at(index)
        copies.receive(pending_ref.at[slot, seq], chain_base + index, place.up)

    load_late.wait()

    @pl.when(z == last)
    def _():
        pending_ref[...] = jnp.zeros_like(pending_ref)
        pl.loop(0, n_chain)(hand_on)

    for load in load_first:
        load.wait()

    for load in load_second:
        load.wait()

    def gate_gradient(at):
        grads = dot_first(nin_ref[:, at], gate_ref[...]).astype(BF)
        outs = dot_first(branch_ref[:, at], gated_ref[...]).astype(BF)
        for slot in range(n_head):
            lanes = slice(slot * HEAD_DIM, (slot + 1) * HEAD_DIM)
            ga_ref[slot, at, pl.ds(three, HEAD_DIM)] = grads[:, lanes]
            ga_ref[slot, at, pl.ds(three + HEAD_DIM, HEAD_DIM)] = outs[:, lanes]

    gate_gradient(pl.ds(3 * quarter, quarter))
    for slot in order:
        gate.begin(slot)
    pl.loop(0, 3)(lambda q: gate_gradient(tile(q)))

    @pl.when(jnp.logical_and(z > 0, z < last))
    def _():
        @pl.loop(0, n_chain)
        def _(index):
            take(index)
            hand_on(index)

    for slot in order:
        gate.middle(slot)
    for load in load_back:
        load.wait()

    @pl.when(z == 0)
    def _():
        pl.loop(0, n_chain)(take)

    offsets = iota((SPAN, SPAN), 0) - iota((SPAN, SPAN), 1)

    def back_slot(slot, turn):
        decay = decay_of(2 * lax.rem(z + slot, n_head) + core)
        mask = jnp.where(offsets >= 0.0, jnp.exp(-decay * jnp.maximum(offsets, 0.0)), 0.0)
        places = iota((SPAN, 1), 0)
        early = jnp.exp(-decay * (places + 1.0))
        late_decay = jnp.exp(-decay * (SPAN - 1.0 - places))
        span_decay = jnp.exp(-decay * SPAN)
        rates_ref[slot] = jnp.zeros((8, HEAD_DIM), F32)

        @pl.loop(0, 2)
        def _(seq):
            for n in range(spans):
                at, here = tile(seq * spans + n), pl.ds(n * SPAN, SPAN)
                state = carry_ref[slot, seq].astype(F32)
                if n == 1:
                    state = span_decay * state + fresh_ref[slot, seq]
                later = pending_ref[slot, seq].astype(F32)
                if n == 0:
                    later = span_decay * later + late_ref[slot, seq * spans + 1]
                q, k, v = q_ref[slot, at, :], k_ref[slot, at, :], v_ref[slot, at, :]
                grad = grad_attn_ref[slot, at, :]
                weights = (dot_last(q, k) * mask).astype(BF)
                scores = (dot_last(grad, v) * mask).astype(BF)
                state_high, state_low = split(state)
                grad_query = dot(scores, k)
                grad_query += early * (dot_last(grad, state_high) + dot_last(grad, state_low))
                later_high, later_low = split(later)
                grad_keys = dot_first(scores, q)
                grad_keys += late_decay * (dot_last(v, later_high) + dot_last(v, later_low))
                both = dot(k, jnp.concatenate([later_high, later_low], axis=1))
                grad_values = dot_first(weights, grad)
                grad_values += late_decay * (both[:, :HEAD_DIM] + both[:, HEAD_DIM:])
                pre_ref[slot, at, pl.ds(2 * HEAD_DIM, HEAD_DIM)] = grad_values.astype(BF)
                cosine, sine = cos_ref[turn, here, :], sin_ref[turn, here, :]
                angles = jnp.zeros((SPAN, HEAD_DIM), F32)
                for i, turned in enumerate((grad_query, grad_keys)):
                    lanes = pl.ds(i * HEAD_DIM, HEAD_DIM)
                    value = qk_pre_ref[turn, at, lanes]
                    by_cos, by_sin = turned[:, :HEAD_DIM], turned[:, HEAD_DIM:]
                    sigmoid = 1.0 / (1.0 + jnp.exp(-value))
                    act = by_cos * cosine + by_sin * sine
                    angles += value * sigmoid * (by_sin * cosine - by_cos * sine)
                    act = act * sigmoid * (1.0 + value * (1.0 - sigmoid))
                    pre_ref[slot, at, lanes] = act.astype(BF)
                steps = (z * rows + n * SPAN).astype(F32) + places
                rates_ref[slot, pl.ds(0, 1), :] += jnp.sum(steps * angles, axis=0, keepdims=True)

    def rest_gradient(slot, at):
        ga_ref[slot, at, rest_lanes] = dot_first(nin_ref[:, at], pre_ref[slot]).astype(BF)

    rates_base = base
    base += n_head + 3
    for i, slot in enumerate(order):
        for load in slot_loads[i]:
            load.wait()
        back_slot(slot, i % 2)
        if i + 2 < n_head:
            slot_loads.append(slot_load(order[i + 2], i % 2))
        if slot:
            at = rates_base + slot
            copies.send(rates_ref.at[slot], rates_high.at[slot - 1], at, at, place.above(slot))
        rest_gradient(slot, pl.ds(3 * quarter, quarter))
        rest.begin(slot)
        pl.loop(0, 3)(lambda q: rest_gradient(slot, tile(q)))
    for slot in order:
        gate.end(slot)
    rest.middle(order[0])
    rest.middle(order[1])
    for load in late_loads:
        load.wait()

    def grad_in(at):
        total = dot_last(gate_ref[at, :], wa_gate())
        for slot in range(n_head):
            total += dot_last(pre_ref[slot, at, :], wa_ref[slot, :, rest_lanes])
        return total

    def wa_gate():
        return jnp.concatenate([wa_ref[slot, :, weight_lanes] for slot in range(n_head)], axis=1)

    @pl.loop(0, spans)
    def _(i):
        send_ref[tile(i), :] = grad_in(tile(spans + i)).astype(BF)

    copies.send(send_ref, got_ref, base, base, place.across)
    rest.middle(order[2])

    total = rates_ref[0]
    for slot in range(1, n_head):
        copies.receive(rates_high.at[slot - 1], rates_base + slot, place.up)
        total += rates_high[slot - 1]
    rates_sum[0] = total
    rates_base += n_head
    copies.send(rates_sum.at[0], rates_got.at[0], rates_base, rates_base, place.by_x)
    rest.middle(order[3])
    feed_share.spread()
    rest.end(order[0])
    copies.receive(rates_got.at[0], rates_base, place.by_x)
    rates_sum[1] = total + rates_got[0]
    copies.send(rates_sum.at[1], rates_got.at[1], rates_base + 1, rates_base + 1, place.by_y)
    copies.receive(got_ref, base, place.across)

    @pl.loop(0, spans)
    def _(i):
        at = tile(i)
        values = x_ref[at, :].astype(F32)
        norm = lax.rsqrt(jnp.mean(values * values, axis=-1, keepdims=True) + EPSILON)
        normed = values * norm
        grad = grad_in(at) + got_ref[at, :].astype(F32)
        mean = jnp.mean(grad * normed, axis=-1, keepdims=True)
        grad_ref[at, :] += norm * (grad - normed * mean)

    for q in range(4):
        src = grad_ref.at[:, pl.ds(q * quarter, quarter)]
        copies.move(src, input_ref.at[:, pl.ds(start_of(q), quarter)], later=True)
    gate.total(to_gate(0, 0, None))
    gate_share.begin()
    rest.end(order[1])
    copies.receive(rates_got.at[1], rates_base + 1, place.by_y)
    rates_both[sides[0]] = rates_sum[1] + rates_got[1]
    mine = rates_both.at[sides[0]]
    copies.send(mine, mine, rates_base + 2, rates_base + 2, place.across)
    feed_share.complete()
    rest.end(order[2])
    rest.end(order[3])
    rest.total(to_rest(0, 0, None))
    rest_share.begin()
    gate_share.spread()
    copies.receive(rates_both.at[sides[1]], rates_base + 2, place.across)
    feed_share.other_side()
    rest_share.spread()
    gate_share.complete()
    rest_share.complete()
    for share in shares[1:]:
        share.other_side()

    @pl.when(z > 0)
    def _():
        @pl.loop(0, n_chain)
        def _(index):
            slot, seq, _ = chain_at(index)
            chain_copy(index, slot, seq).wait_send()

    copies.finish()


def last(
    n_head,
    late,
    feed_piece,
    nin,
    gate_pre,
    gated,
    branch,
    query,
    keys,
    values,
    grad_attn,
    carry,
    fresh,
    pre,
    cosines,
    sines,
    wa,
    hidden_grad,
    block,
    tokens,
):
    rows, width = tokens.shape
    _, units, quarter = feed_piece.shape
    tall = 2 * rows

    def scatter_buffers(shape, halved):
        half = tuple(n // 2 if i == halved else n for i, n in enumerate(shape))
        return [
            ((n_head,) + half, BF),
            ((n_head,) + half, BF),
            ((n_head,) + shape, BF),
            ((n_head,) + shape, BF),
            ((n_head - 1,) + shape, BF),
        ]

    outs = [
        ((rows, width), F32),
        ((rows, width), BF),
        ((2, 3, units, width), BF),
        ((2, width, 5 * HEAD_DIM), BF),
        ((2, 8, HEAD_DIM), F32),
    ]
    chain = ((n_head, 2, 2 * HEAD_DIM, HEAD_DIM), BF)
    buffers = [
        ((n_head, width, 5 * HEAD_DIM), BF),
        *scatter_buffers((quarter, 3 * HEAD_DIM), 0),
        *scatter_buffers((quarter, 2 * HEAD_DIM), 0),
        (late.shape, F32),
        chain,
        chain,
        (nin.shape, BF),
        (gate_pre.shape, BF),
        (gated.shape, BF),
        (branch.shape, BF),
        (query.shape, BF),
        (keys.shape, BF),
        (values.shape, BF),
        (grad_attn.shape, BF),
        chain,
        (chain[0], F32),
        ((2, tall, 2 * HEAD_DIM), F32),
        ((2, rows, HEAD_DIM), F32),
        ((2, rows, HEAD_DIM), F32),
        ((n_head, tall, 3 * HEAD_DIM), BF),
        (wa.shape, BF),
        ((rows, width), BF),
        ((rows, width), F32),
        ((rows, width), BF),
        ((rows, width), BF),
        ((n_head, 8, HEAD_DIM), F32),
        ((n_head - 1, 8, HEAD_DIM), F32),
        ((2, 8, HEAD_DIM), F32),
        ((2, 8, HEAD_DIM), F32),
    ]
    n_sems = 2 * PER_SCATTER + 3 * PER_SHARE + 2 * n_head + n_head + 3 + 1
    arrays = [late, feed_piece, nin, gate_pre, gated, branch, query, keys, values, grad_attn]
    arrays += [carry, fresh, pre, cosines, sines, wa, hidden_grad, block, tokens]
    arrays = [pltpu.with_memory_space_constraint(array, pltpu.HBM) for array in arrays]
    return pl.pallas_call(
        functools.partial(last_kernel, n_head),
        out_shape=[pltpu.VMEM(*out) for out in outs],
        in_specs=[ANY] * len(arrays),
        out_specs=[IN_VMEM] * len(outs),
        scratch_shapes=[pltpu.VMEM(*b) for b in buffers]
        + [
            pltpu.SemaphoreType.DMA((n_sems,)),
            pltpu.SemaphoreType.DMA((n_sems,)),
            pltpu.SemaphoreType.DMA((64,)),
        ],
        compiler_params=pltpu.CompilerParams(
            collective_id=2, has_side_effects=True, vmem_limit_bytes=52 << 20
        ),
        name="last",
    )(*arrays)


def finish_kernel(grad, block, feed, attn, rates, *refs):
    outs, results, locals_ = refs[:11], refs[11:-1], refs[-1]
    copies = Copies(None, None, locals_)
    (block_out, grad_out, q_out, k_out, v_out, g_out, o_out, rates_out, l_out, r_out, d_out) = outs
    units = feed.shape[2]
    copies.move(grad, grad_out, later=True)
    copies.move(block, block_out, later=True)
    l_ref, r_ref, d_ref, q_ref, k_ref, v_ref, g_ref, o_ref, rates_ref = results
    for side in range(2):
        rates_ref[:, pl.ds(side * HEAD_DIM, HEAD_DIM)] = rates[side, pl.ds(0, 1), :]
    copies.move(rates_ref, rates_out, later=True)
    for i, (ref, out) in enumerate(((l_ref, l_out), (r_ref, r_out), (d_ref, d_out))):
        for side in range(2):
            at = pl.ds(side * units, units)
            ref[at, :] = feed[side, i].astype(F32)
            copies.move(ref.at[at], out.at[at], later=True)
    for i, (ref, out) in enumerate(((q_ref, q_out), (k_ref, k_out), (v_ref, v_out), (g_ref, g_out))):
        lanes = pl.ds(i * HEAD_DIM, HEAD_DIM)
        for side in range(2):
            ref[:, pl.ds(side * HEAD_DIM, HEAD_DIM)] = attn[side, :, lanes].astype(F32)
        copies.move(ref, out, later=True)
    for side in range(2):
        lanes = pl.ds(4 * HEAD_DIM, HEAD_DIM)
        o_ref[pl.ds(side * HEAD_DIM, HEAD_DIM), :] = attn[side, :, lanes].T.astype(F32)
    copies.move(o_ref, o_out, later=True)
    copies.finish()


def finish(grad, block, feed, attn, rates):
    _, _, units, width = feed.shape
    projection = ((width, 2 * HEAD_DIM), F32)
    back = ((2 * HEAD_DIM, width), F32)
    results = [((2 * units, width), F32)] * 3 + [projection] * 4 + [back]
    results.append(((1, 2 * HEAD_DIM), F32))
    outs = [(block.shape, BF), (grad.shape, F32)] + results[3:] + results[:3]
    return pl.pallas_call(
        finish_kernel,
        out_shape=[jax.ShapeDtypeStruct(*out) for out in outs],
        in_specs=[IN_VMEM] * 5,
        out_specs=[ANY] * len(outs),
        scratch_shapes=[pltpu.VMEM(*b) for b in results] + [pltpu.SemaphoreType.DMA((48,))],
        compiler_params=pltpu.CompilerParams(vmem_limit_bytes=24 << 20),
        name="finish",
    )(grad, block, feed, attn, rates)


def make(n_dp, n_head):
    def on_device(
        tokens,
        attn_query,
        attn_key,
        attn_value,
        attn_gate,
        attn_out,
        rotation_rates,
        ffn_left,
        ffn_right,
        ffn_down,
        out_grad,
    ):
        rates_in = rotation_rates.reshape(1, -1)
        (
            attn_weights,
            out_w,
            ffn_all,
            gathered_in,
            pre,
            query,
            keys,
            values,
            attn,
            cosines,
            sines,
            fresh,
            carry,
            scale_attn,
            gated,
            hidden,
            gathered_mid,
            grad_rows,
        ) = forward(
            n_head,
            tokens,
            out_grad,
            attn_query,
            attn_key,
            attn_value,
            attn_gate,
            attn_out,
            ffn_left.T,
            ffn_right.T,
            ffn_down,
            rates_in,
        )
        feed_piece, block_out, grad_hidden, branch_rows, gate_pre, grad_attn, late = middle(
            n_head,
            ffn_all,
            gathered_mid,
            grad_rows,
            hidden,
            out_w,
            pre,
            query,
            attn,
            scale_attn,
        )
        grads = last(
            n_head,
            late,
            feed_piece,
            gathered_in,
            gate_pre,
            gated,
            branch_rows,
            query,
            keys,
            values,
            grad_attn,
            carry,
            fresh,
            pre,
            cosines,
            sines,
            attn_weights,
            grad_hidden,
            block_out,
            tokens,
        )
        results = finish(*grads)
        rates_grad, left_grad, right_grad = results[7][0], results[8].T, results[9].T
        results = list(results[:7]) + [rates_grad, left_grad, right_grad, results[10]]
        if n_dp > 8:
            groups = [[i + 8 * j for j in range(n_dp // 8)] for i in range(8)]
            grads = [lax.psum(grad, "dp", axis_index_groups=groups) for grad in results[2:]]
            results = results[:2] + grads
        return tuple(results)

    return on_device


def solution(mesh):
    weights = (P(None, "head"),) * 4 + (P("head", None), P("head")) + (P(None, "head"),) * 2
    weights = weights + (P("head", None),)
    rows = P(("dp", "head"), None)
    return jax.shard_map(
        make(mesh.shape["dp"], mesh.shape["head"]),
        mesh=mesh,
        in_specs=(rows,) + weights + (rows,),
        out_specs=(rows, rows) + weights,
        check_vma=False,
    )
```

```python
import functools

import jax
import jax.numpy as jnp
from jax import lax
from jax.experimental import pallas as pl
from jax.experimental.pallas import tpu as pltpu
from jax.sharding import PartitionSpec as P

HEADS = 8
HEAD_DIM = 128
SPAN = 256
EPSILON = 1e-06
BF = jnp.bfloat16
F32 = jnp.float32


MESH = pl.DeviceIdType.MESH
ANY = pl.BlockSpec(memory_space=pl.ANY)
IN_VMEM = pl.BlockSpec(memory_space=pltpu.VMEM)


def split(value):
    high = value.astype(BF)
    return high, (value - high.astype(F32)).astype(BF)


class Place:
    def __init__(self, n_head):
        self.n_head = n_head
        dp = lax.axis_index("dp")
        self.z = lax.axis_index("head")
        self.core = lax.rem(dp, 2)
        x = lax.rem(lax.div(dp, 2), 2)
        y = lax.rem(lax.div(dp, 4), 2)
        self.plane = x + 2 * y
        self.at = [self.plane, self.plane + 1 - 2 * x, self.plane + 2 - 4 * y, 3 - self.plane]
        self.across = {"dp": dp + 1 - 2 * self.core}
        self.by_x = {"dp": dp + 2 - 4 * x}
        self.by_y = {"dp": dp + 4 - 8 * y}
        self.up = {"head": lax.rem(self.z + 1, n_head)}
        self.down = {"head": lax.rem(self.z + n_head - 1, n_head)}

    def above(self, step):
        return {"head": lax.rem(self.z + step, self.n_head)}

    def below(self, step):
        return {"head": lax.rem(self.z + self.n_head - step, self.n_head)}

    def greet(self):
        others = [self.across, self.by_x, self.by_y]
        others += [self.below(step) for step in range(1, self.n_head)]
        for other in others:
            barrier = pltpu.get_barrier_semaphore()
            pl.semaphore_signal(barrier, inc=1, device_id=other, device_id_type=MESH)

    def meet(self):
        pl.semaphore_wait(pltpu.get_barrier_semaphore(), self.n_head + 2)


class Copies:
    def __init__(self, sends, receives, locals_):
        self.sends, self.receives, self.locals = sends, receives, locals_
        self.pending = []
        self.started = {}
        self.n_local = 0

    def send(self, src, dst, out, into, device, when=None):
        copy = pltpu.make_async_remote_copy(
            src_ref=src,
            dst_ref=dst,
            send_sem=self.sends.at[out],
            recv_sem=self.receives.at[into],
            device_id=device,
            device_id_type=MESH,
        )
        if when is None:
            copy.start()
            self.pending.append(copy.wait_send)
            if isinstance(out, int):
                self.started[out] = copy.wait_send
        else:
            pl.when(when)(copy.start)
            self.pending.append(lambda: pl.when(when)(copy.wait_send))

    def receive(self, dst, into, device):
        pltpu.make_async_remote_copy(
            src_ref=dst,
            dst_ref=dst,
            send_sem=self.sends.at[0],
            recv_sem=self.receives.at[into],
            device_id=device,
            device_id_type=MESH,
        ).wait_recv()

    def move(self, src, dst, later=False):
        copy = pltpu.make_async_copy(src, dst, self.locals.at[self.n_local])
        self.n_local += 1
        copy.start()
        if later:
            self.pending.append(copy.wait)
        return copy

    def sent(self, out):
        wait = self.started.pop(out)
        self.pending.remove(wait)
        wait()

    def finish(self):
        for wait in self.pending:
            wait()


class Gather:
    def __init__(self, place, copies, view, base, late=None):
        self.place, self.copies, self.view, self.base = place, copies, view, base
        self.late = late

    def begin(self):
        place, z = self.place, self.place.z
        own = self.view(0, 0, None)
        last = place.n_head - 1
        self.copies.send(
            own, self.view(last, 0, None), self.base, self.base + last, place.up, when=z < last
        )
        self.copies.send(own, self.view(1, 0, None), self.base + 1, self.base + 1, place.down, when=z > 0)

    def arrived(self, slot, when=True):
        place, copies, z, base = self.place, self.copies, self.place.z, self.base
        last = place.n_head - 1
        if when is True:
            copies.receive(self.view(slot, 0, None), base + slot, place.up)
        else:
            pl.when(when)(lambda: copies.receive(self.view(slot, 0, None), base + slot, place.up))
        from_up = z + slot <= last
        piece = self.view(slot, 0, None)
        down = jnp.logical_and(jnp.logical_and(from_up, z > 0), when)
        up = jnp.logical_and(jnp.logical_not(from_up), z < last)
        up = jnp.logical_and(up, when)
        always = None if when is True else when
        after = jnp.minimum(slot + 1, last)
        before = jnp.maximum(slot - 1, 1)
        copies.send(piece, self.view(after, 0, None), base + 1 + slot, base + after, place.down, when=down)
        copies.send(piece, self.view(before, 0, None), base + 1 + slot, base + before, place.up, when=up)
        at = base + 4 * slot + 4
        copies.send(piece, self.view(slot, 1, None), at, at, place.by_x, when=always)
        copies.send(piece, self.view(slot, 2, None), at + 1, at + 1, place.by_y, when=always)

    def spread(self, slot):
        place, copies = self.place, self.copies
        at = self.base + 4 * slot + 4
        now = None if self.late is None else slot != self.late
        low, high = self.view(slot, 3, 0), self.view(slot, 3, 1)
        copies.receive(self.view(slot, 1, None), at, place.by_x)
        copies.send(self.view(slot, 1, 0), low, at + 2, at + 2, place.by_y, when=now)
        copies.receive(self.view(slot, 2, None), at + 1, place.by_y)
        copies.send(self.view(slot, 2, 1), high, at + 3, at + 3, place.by_x, when=now)

    def complete(self, slot):
        place, copies = self.place, self.copies
        at = self.base + 4 * slot + 4

        def receive():
            copies.receive(self.view(slot, 3, 0), at + 2, place.by_y)
            copies.receive(self.view(slot, 3, 1), at + 3, place.by_x)

        if self.late is None:
            receive()
        else:
            pl.when(slot != self.late)(receive)


PER_GATHER = 24


def forward_kernel(
    n_head,
    tokens,
    out_grad,
    wq,
    wk,
    wv,
    wg,
    wo,
    ffn_left,
    ffn_right,
    ffn_down,
    rates,
    wa_out,
    wo_out,
    wf_out,
    nin_out,
    pre_out,
    q_out,
    k_out,
    v_out,
    attn_out,
    cos_out,
    sin_out,
    fresh_out,
    carry_out,
    scale_out,
    gated_out,
    hidden_out,
    nm_out,
    og_out,
    wa_ref,
    wo_ref,
    wf_ref,
    x_ref,
    nin_ref,
    pre_ref,
    q_ref,
    k_ref,
    v_ref,
    attn_ref,
    cos_ref,
    sin_ref,
    fresh_ref,
    carry_ref,
    message_ref,
    squares_ref,
    other_squares_ref,
    gated_ref,
    branch_ref,
    other_branch_ref,
    hidden_ref,
    nm_ref,
    rates_ref,
    og_ref,
    sends,
    receives,
    locals_,
):
    rows, width = tokens.shape
    quarter = width // 4
    units = ffn_down.shape[0] // 2
    tiles = 2 * rows // SPAN
    place = Place(n_head)
    z, core = place.z, place.core
    last = n_head - 1
    place.greet()
    copies = Copies(sends, receives, locals_)

    def columns(start, size):
        return pl.ds(pl.multiple_of(start, size), size)

    def own_weights(q):
        far = columns(place.at[q] * quarter, quarter)
        near = pl.ds(q * quarter, quarter)
        loads = []
        for i, w in enumerate((wq, wk, wv, wg)):
            src = w.at[far, columns(core * HEAD_DIM, HEAD_DIM)]
            loads.append(copies.move(src, wa_ref.at[0, near, pl.ds(i * HEAD_DIM, HEAD_DIM)]))
        src = wo.at[columns(core * HEAD_DIM, HEAD_DIM), far]
        loads.append(copies.move(src, wo_ref.at[pl.ds(0, HEAD_DIM), near]))
        for i, w in enumerate((ffn_left, ffn_right, ffn_down)):
            src = w.at[pl.ds(pl.multiple_of(core * units, 16), units), far]
            loads.append(copies.move(src, wf_ref.at[i, pl.ds(0, units), near]))
        return loads

    own_loads = [own_weights(0)]
    token_loads = [
        copies.move(
            tokens.at[:, columns(place.at[q] * quarter, quarter)],
            x_ref.at[:, pl.ds(q * quarter, quarter)],
        )
        for q in range(4)
    ]
    place.meet()

    def half_rows(half, size):
        return pl.ds(0, size) if half is None else pl.ds(half * (size // 2), size // 2)

    def wa_view(part, slot, q, half):
        at = half_rows(half, quarter)
        lanes = pl.ds(part * 2 * HEAD_DIM, 2 * HEAD_DIM)
        return wa_ref.at[slot, pl.ds(q * quarter + at.start, at.size), lanes]

    def wo_view(slot, q, half):
        at = half_rows(half, HEAD_DIM)
        return wo_ref.at[
            pl.ds(pl.multiple_of(slot * HEAD_DIM + at.start, HEAD_DIM // 2), at.size),
            pl.ds(q * quarter, quarter),
        ]

    def wf_view(slot, q, half):
        at = half_rows(half, units)
        return wf_ref.at[
            :,
            pl.ds(pl.multiple_of(slot * units + at.start, 16), at.size),
            pl.ds(q * quarter, quarter),
        ]

    attn_all = [
        Gather(place, copies, functools.partial(wa_view, part), part * PER_GATHER)
        for part in range(2)
    ]
    attn_all.append(Gather(place, copies, wo_view, 2 * PER_GATHER))
    feed = Gather(place, copies, wf_view, 3 * PER_GATHER, late=last)
    base = 4 * PER_GATHER
    for loads, part in zip((own_loads[0][:2], own_loads[0][2:4], own_loads[0][4:5]), attn_all):
        for load in loads:
            load.wait()
        part.begin()
    grad_loads = [
        copies.move(
            out_grad.at[:, columns(place.at[q] * quarter, quarter)],
            og_ref.at[pl.ds(0, rows), pl.ds(q * quarter, quarter)],
        )
        for q in range(4)
    ]
    own_loads += [own_weights(q) for q in range(1, 4)]
    for step in range(1, n_head):
        copies.send(rates, rates_ref.at[step], base + step, base + step, place.below(step))
    rates_ref[0] = rates[...]

    for load in token_loads:
        load.wait()

    def norm_rows(values):
        mean = jnp.mean(values * values, axis=-1, keepdims=True)
        return values * lax.rsqrt(mean + EPSILON)

    @pl.loop(0, rows // 128)
    def _(i):
        at = pl.ds(pl.multiple_of(i * 128, 128), 128)
        nin_ref[at, :] = norm_rows(x_ref[at, :].astype(F32)).astype(BF)

    base += 4
    for load in grad_loads:
        load.wait()
    og_other = og_ref.at[pl.ds(rows, rows)]
    copies.send(og_ref.at[pl.ds(0, rows)], og_other, base, base, place.across)
    base += 1
    nin_other = nin_ref.at[pl.ds(rows, rows)]
    copies.send(nin_ref.at[pl.ds(0, rows)], nin_other, base, base, place.across)
    for q, loads in enumerate(own_loads):
        for load in loads[5:] if q == 0 else loads:
            load.wait()
    for step in range(1, n_head):
        copies.receive(rates_ref.at[step], base - 5 + step, place.up)
    copies.receive(nin_other, base, place.across)
    copies.move(nin_ref, nin_out, later=True)
    own_rows = pl.ds(0, units)
    copies.move(wf_ref.at[:, own_rows], wf_out.at[:, own_rows], later=True)
    copies.receive(og_other, base - 1, place.across)
    copies.move(og_ref, og_out, later=True)

    def decay_of(head):
        exponent = jnp.full((1, 1), -8.0 / HEADS, F32) * (head + 1).astype(F32)
        return jnp.exp2(exponent)

    def tile(i):
        return pl.ds(pl.multiple_of(i * SPAN, SPAN), SPAN)

    def iota(shape, axis):
        return lax.broadcasted_iota(jnp.int32, shape, axis).astype(F32)

    def dot(left, right):
        return jnp.dot(left, right, preferred_element_type=F32)

    def slot_compute(slot):
        head = 2 * lax.rem(z + slot, n_head) + core
        decay = decay_of(head)
        rate = rates_ref[slot, :, columns(core * HEAD_DIM, HEAD_DIM)]
        coarse = (z * rows).astype(F32) + 32.0 * iota((rows // 32, HEAD_DIM), 0)
        coarse = coarse * rate
        fine = iota((32, HEAD_DIM), 0) * rate
        cos_a, sin_a = jnp.cos(coarse), jnp.sin(coarse)
        cos_b, sin_b = jnp.cos(fine), jnp.sin(fine)
        for a in range(rows // 32):
            cos_row, sin_row = cos_a[a : a + 1], sin_a[a : a + 1]
            cos_ref[slot, pl.ds(a * 32, 32), :] = cos_row * cos_b - sin_row * sin_b
            sin_ref[slot, pl.ds(a * 32, 32), :] = sin_row * cos_b + cos_row * sin_b
        offsets = iota((SPAN, SPAN), 0) - iota((SPAN, SPAN), 1)
        mask = jnp.where(offsets >= 0.0, jnp.exp(-decay * jnp.maximum(offsets, 0.0)), 0.0)
        late = jnp.exp(-decay * (SPAN - 1.0 - iota((SPAN, HEAD_DIM), 0)))

        @pl.loop(0, tiles)
        def _(i):
            at = tile(i)
            pre = dot(nin_ref[at, :], wa_ref[slot])
            pre_ref[slot, at, :] = pre
            here = tile(lax.rem(i, rows // SPAN))
            cosines, sines = cos_ref[slot, here, :], sin_ref[slot, here, :]

            def rotate(values):
                activated = values / (1.0 + jnp.exp(-values))
                turned = jnp.concatenate([activated * cosines, activated * sines], axis=1)
                return turned.astype(BF)

            query = rotate(pre[:, :HEAD_DIM])
            keys = rotate(pre[:, HEAD_DIM : 2 * HEAD_DIM])
            value = pre[:, 2 * HEAD_DIM : 3 * HEAD_DIM].astype(BF)
            q_ref[slot, at, :] = query
            k_ref[slot, at, :] = keys
            v_ref[slot, at, :] = value
            scores = lax.dot_general(
                query, keys, (((1,), (1,)), ((), ())), preferred_element_type=F32
            )
            weights = (scores * mask).astype(BF)
            attn_ref[slot, at, :] = dot(weights, value)
            high, low = split(value.astype(F32) * late)
            both = lax.dot_general(
                keys,
                jnp.concatenate([high, low], axis=1),
                (((0,), (0,)), ((), ())),
                preferred_element_type=F32,
            )
            fresh_ref[slot, i] = both[:, :HEAD_DIM] + both[:, HEAD_DIM:]

        for ref, out in (
            (wa_ref, wa_out),
            (pre_ref, pre_out),
            (q_ref, q_out),
            (k_ref, k_out),
            (v_ref, v_out),
            (cos_ref, cos_out),
            (sin_ref, sin_out),
            (fresh_ref, fresh_out),
        ):
            copies.move(ref.at[slot], out.at[slot], later=True)

    first = 1 + 2 * lax.div(z, last)
    second = 2 + lax.rem(lax.div(z + 1, 2), 2)
    third = 6 - first - second

    for part in attn_all:
        part.arrived(first)
    slot_compute(0)
    for part in attn_all:
        part.arrived(second)
    for part in attn_all:
        part.spread(first)
    for part in attn_all:
        part.arrived(third)
    feed.begin()
    for part in attn_all:
        part.spread(second)
    for part in attn_all[:2]:
        part.complete(first)
    slot_compute(first)
    for part in attn_all:
        part.spread(third)
    feed.arrived(first)
    for part in attn_all[:2]:
        part.complete(second)
    slot_compute(second)
    inner = jnp.logical_and(z > 0, z < last)
    feed.arrived(second, inner)
    for part in attn_all[:2]:
        part.complete(third)
    slot_compute(third)
    base += 1
    chain_base = base
    n_chain = 2 * n_head

    def chain_at(index):
        group, seq = lax.div(index, 2), lax.rem(index, 2)
        return lax.rem(group - z + n_head, n_head), seq, decay_of(2 * group + core)

    def chain_copy(index, slot, seq):
        after = lax.rem(slot + n_head - 1, n_head)
        return pltpu.make_async_remote_copy(
            src_ref=message_ref.at[slot, seq],
            dst_ref=carry_ref.at[after, seq],
            send_sem=sends.at[chain_base + index],
            recv_sem=receives.at[chain_base + index],
            device_id=place.up,
            device_id_type=MESH,
        )

    def hand_on(index, slot, seq, decay):
        total = jnp.exp(-decay * rows) * carry_ref[slot, seq].astype(F32)
        for n in range(rows // SPAN):
            left = rows - (n + 1) * SPAN
            total += jnp.exp(-decay * left) * fresh_ref[slot, seq * (rows // SPAN) + n]
        message_ref[slot, seq] = total.astype(BF)
        chain_copy(index, slot, seq).start()

    @pl.when(z == 0)
    def _():
        @pl.loop(0, n_chain)
        def _(index):
            slot, seq, decay = chain_at(index)
            carry_ref[slot, seq] = jnp.zeros(carry_ref.shape[2:], BF)
            hand_on(index, slot, seq, decay)

    feed.arrived(second, jnp.logical_not(inner))
    feed.spread(first)
    feed.arrived(third)

    @pl.when(z > 0)
    def _():
        @pl.loop(0, n_chain)
        def _(index):
            slot, seq, decay = chain_at(index)
            copies.receive(carry_ref.at[slot, seq], chain_base + index, place.down)
            pl.when(z < last)(lambda: hand_on(index, slot, seq, decay))

    copies.move(carry_ref, carry_out, later=True)
    feed.spread(second)

    def feed_done(slot):
        feed.complete(slot)
        at = pl.ds(pl.multiple_of(slot * units, 16), units)
        copies.move(wf_ref.at[:, at], wf_out.at[:, at], later=True)

    def apply(seq):
        mine = pl.ds(seq * rows, rows)
        squares_ref[mine, :] = jnp.zeros((rows, HEAD_DIM), F32)

        @pl.loop(0, n_head)
        def _(slot):
            decay = decay_of(2 * lax.rem(z + slot, n_head) + core)
            early = jnp.exp(-decay * (iota((SPAN, HEAD_DIM), 0) + 1.0))
            state = carry_ref[slot, seq].astype(F32)
            for n in range(rows // SPAN):
                i = seq * (rows // SPAN) + n
                at = pl.ds(i * SPAN, SPAN)
                both = dot(q_ref[slot, at, :], jnp.concatenate(split(state), axis=1))
                attn = attn_ref[slot, at, :]
                attn += early * (both[:, :HEAD_DIM] + both[:, HEAD_DIM:])
                attn_ref[slot, at, :] = attn
                squares_ref[at, :] += jnp.sum(attn * attn, axis=-1, keepdims=True)
                if n + 1 < rows // SPAN:
                    state = jnp.exp(-decay * SPAN) * state + fresh_ref[slot, i]

    def gating(seq):
        for n in range(rows // SPAN):
            at = pl.ds(seq * rows + n * SPAN, SPAN)
            total = squares_ref[at, :] + other_squares_ref[at, :]
            scale = lax.rsqrt(total / width + EPSILON)
            other_squares_ref[at, :] = scale
            for slot in range(n_head):
                gate = pre_ref[slot, at, pl.ds(3 * HEAD_DIM, HEAD_DIM)]
                gated = (attn_ref[slot, at, :] * scale * gate).astype(BF)
                gated_ref[at, pl.ds(slot * HEAD_DIM, HEAD_DIM)] = gated

    base += n_chain
    own, other = pl.ds(0, rows), pl.ds(rows, rows)
    apply(1)
    copies.send(squares_ref.at[other], other_squares_ref.at[own], base, base, place.across)
    apply(0)
    copies.send(squares_ref.at[own], other_squares_ref.at[other], base + 1, base + 1, place.across)
    copies.move(attn_ref, attn_out, later=True)
    for slot in (first, second, third):
        attn_all[2].complete(slot)
    copies.receive(other_squares_ref.at[other], base + 1, place.across)
    gating(1)
    feed_done(first)
    base += 2
    for n in range(rows // SPAN):
        gated = gated_ref[pl.ds(rows + n * SPAN, SPAN), :]
        branch_ref[pl.ds(n * SPAN, SPAN), :] = dot(gated, wo_ref[...]).astype(BF)
    copies.send(branch_ref, other_branch_ref, base, base, place.across)
    copies.receive(other_squares_ref.at[own], base - 2, place.across)
    gating(0)
    copies.move(other_squares_ref, scale_out, later=True)
    copies.move(gated_ref, gated_out, later=True)
    copies.move(wo_ref, wo_out, later=True)
    feed.spread(third)
    feed_done(second)

    @pl.loop(0, rows // SPAN)
    def _(i):
        at = tile(i)
        hidden_ref[at, :] = x_ref[at, :].astype(F32) + dot(gated_ref[at, :], wo_ref[...])

    copies.receive(other_branch_ref, base, place.across)

    @pl.loop(0, rows // 128)
    def _(i):
        at = pl.ds(pl.multiple_of(i * 128, 128), 128)
        hidden = hidden_ref[at, :] + other_branch_ref[at, :].astype(F32)
        hidden_ref[at, :] = hidden
        nm_ref[at, :] = norm_rows(hidden).astype(BF)

    copies.send(nm_ref.at[own], nm_ref.at[other], base + 1, base + 1, place.across)
    copies.move(hidden_ref, hidden_out, later=True)
    feed_done(third)
    copies.receive(nm_ref.at[other], base + 1, place.across)
    copies.move(nm_ref, nm_out, later=True)

    @pl.when(z < last)
    def _():
        @pl.loop(0, n_chain)
        def _(index):
            slot, seq, _ = chain_at(index)
            chain_copy(index, slot, seq).wait_send()

    copies.finish()


def forward(n_head, tokens, out_grad, wq, wk, wv, wg, wo, ffn_left, ffn_right, ffn_down, rates):
    rows, width = tokens.shape
    units = ffn_down.shape[0] // 2
    tall = 2 * rows
    buffers = [
        ((n_head, width, 4 * HEAD_DIM), BF),
        ((n_head * HEAD_DIM, width), BF),
        ((3, n_head * units, width), BF),
        ((rows, width), BF),
        ((tall, width), BF),
        ((n_head, tall, 4 * HEAD_DIM), F32),
        ((n_head, tall, 2 * HEAD_DIM), BF),
        ((n_head, tall, 2 * HEAD_DIM), BF),
        ((n_head, tall, HEAD_DIM), BF),
        ((n_head, tall, HEAD_DIM), F32),
        ((n_head, rows, HEAD_DIM), F32),
        ((n_head, rows, HEAD_DIM), F32),
        ((n_head, tall // SPAN, 2 * HEAD_DIM, HEAD_DIM), F32),
        ((n_head, 2, 2 * HEAD_DIM, HEAD_DIM), BF),
        ((n_head, 2, 2 * HEAD_DIM, HEAD_DIM), BF),
        ((tall, HEAD_DIM), F32),
        ((tall, HEAD_DIM), F32),
        ((tall, n_head * HEAD_DIM), BF),
        ((rows, width), BF),
        ((rows, width), BF),
        ((rows, width), F32),
        ((tall, width), BF),
        ((n_head, 1, 2 * HEAD_DIM), F32),
        ((tall, width), BF),
    ]
    out_of = [0, 1, 2, 4, 5, 6, 7, 8, 9, 10, 11, 12, 13, 16, 17, 20, 21, 23]
    n_sems = 4 * PER_GATHER + 4 + 1 + 1 + 2 * n_head + 2 + 2
    return pl.pallas_call(
        functools.partial(forward_kernel, n_head),
        out_shape=[jax.ShapeDtypeStruct(*buffers[i]) for i in out_of],
        in_specs=[ANY] * 10 + [IN_VMEM],
        out_specs=[ANY] * len(out_of),
        scratch_shapes=[pltpu.VMEM(*b) for b in buffers]
        + [
            pltpu.SemaphoreType.DMA((n_sems,)),
            pltpu.SemaphoreType.DMA((n_sems,)),
            pltpu.SemaphoreType.DMA((96,)),
        ],
        compiler_params=pltpu.CompilerParams(
            collective_id=0, has_side_effects=True, vmem_limit_bytes=62 << 20
        ),
        name="forward",
    )(tokens, out_grad, wq, wk, wv, wg, wo, ffn_left, ffn_right, ffn_down, rates)


class Scatter:
    def __init__(self, place, copies, view, far_x, far_y, near_x, near_y, high, base, items=None):
        self.place, self.copies, self.view, self.base = place, copies, view, base
        self.items = items
        self.far_x, self.far_y, self.near_x, self.near_y, self.high = far_x, far_y, near_x, near_y, high

    def part(self, buffer, slot):
        return buffer.at[slot] if self.items is None else buffer.at[slot, pl.ds(0, self.items(slot))]

    def begin(self, slot):
        place, at = self.place, self.base + 4 * slot
        self.copies.send(self.view(slot, 3, 0), self.part(self.far_y, slot), at, at, place.by_y)
        self.copies.send(self.view(slot, 3, 1), self.part(self.far_x, slot), at + 1, at + 1, place.by_x)

    def middle(self, slot):
        place, copies, at = self.place, self.copies, self.base + 4 * slot
        copies.receive(self.part(self.far_y, slot), at, place.by_y)
        add_to(self.view(slot, 1, 0), self.part(self.far_y, slot))
        copies.send(self.view(slot, 1, None), self.part(self.near_x, slot), at + 2, at + 2, place.by_x)
        copies.receive(self.part(self.far_x, slot), at + 1, place.by_x)
        add_to(self.view(slot, 2, 1), self.part(self.far_x, slot))
        copies.send(self.view(slot, 2, None), self.part(self.near_y, slot), at + 3, at + 3, place.by_y)

    def end(self, slot, onward=True):
        place, copies, at = self.place, self.copies, self.base + 4 * slot
        copies.receive(self.part(self.near_x, slot), at + 2, place.by_x)
        copies.receive(self.part(self.near_y, slot), at + 3, place.by_y)
        add_to(self.view(slot, 0, None), self.part(self.near_x, slot), self.part(self.near_y, slot))
        if slot and onward:
            self.go_up(slot)

    def go_up(self, slot):
        at = self.base + 4 * self.place.n_head + slot
        into = self.high.at[slot - 1]
        self.copies.send(self.view(slot, 0, None), into, at, at, self.place.above(slot))

    def total(self, into=None, slots=(1, 2, 3)):
        place = self.place
        high = [self.high.at[slot - 1] for slot in slots]
        for slot, part in zip(slots, high):
            self.copies.receive(part, self.base + 4 * place.n_head + slot, place.up)
        add_to(self.view(0, 0, None), *high, into=into)


PER_SCATTER = 20


def add_to(ref, *others, into=None):
    def add(into, *refs):
        total = refs[0][...].astype(F32)
        for other in refs[1:]:
            total += other[...].astype(F32)
        into[...] = total.astype(BF)

    refs = (ref if into is None else into, ref) + others
    if len(ref.shape) == 2:
        add(*refs)
    else:
        for i in range(ref.shape[0]):
            add(*(one.at[i] for one in refs))


def dot(left, right):
    return jnp.dot(left, right, preferred_element_type=F32)


def iota(shape, axis):
    return lax.broadcasted_iota(jnp.int32, shape, axis).astype(F32)


def decay_of(head):
    exponent = jnp.full((1, 1), -8.0 / HEADS, F32) * (head + 1).astype(F32)
    return jnp.exp2(exponent)


def middle_kernel(
    n_head,
    wf,
    nm,
    og,
    hidden,
    wo,
    pre,
    query,
    attn,
    scale,
    feed_out,
    block_out,
    hidden_grad_out,
    branch_out,
    gate_out,
    ga_out,
    late_out,
    wf_ref,
    t_ref,
    g_ref,
    far_x,
    far_y,
    near_x,
    near_y,
    early_ref,
    high_ref,
    high_first_ref,
    high_third_ref,
    nm_ref,
    og_ref,
    branch_ref,
    hidden_ref,
    mid_ref,
    send_ref,
    got_ref,
    block_ref,
    wo_ref,
    gate_ref,
    attn_ref,
    ga_ref,
    late_ref,
    scale_ref,
    sum_ref,
    other_sum_ref,
    sends,
    receives,
    locals_,
):
    rows, width = hidden.shape
    quarter = width // 4
    units = wf.shape[1] // n_head
    spans = rows // SPAN
    tiles = 2 * spans
    last = n_head - 1
    place = Place(n_head)
    z, core = place.z, place.core
    place.greet()
    copies = Copies(sends, receives, locals_)
    own, other = pl.ds(0, rows), pl.ds(rows, rows)

    order = (2, 1, 3, 0)
    load_nm = copies.move(nm, nm_ref)
    load_og = copies.move(og, og_ref)
    load_wf = {}
    for slot in order:
        at = pl.ds(slot * units, units)
        lanes = pl.ds(0, width if slot < last else width - quarter)
        load_wf[slot] = copies.move(wf.at[:, at, lanes], wf_ref.at[:, at, lanes])
    early_loads = [
        copies.move(hidden, hidden_ref),
        copies.move(wo, wo_ref),
        copies.move(scale, scale_ref),
        copies.move(attn, attn_ref),
        copies.move(pre.at[:, :, pl.ds(3 * HEAD_DIM, HEAD_DIM)], gate_ref),
    ]
    place.meet()

    def tile(i):
        return pl.ds(pl.multiple_of(i * SPAN, SPAN), SPAN)

    def dot_last(left, right):
        return lax.dot_general(left, right, (((1,), (1,)), ((), ())), preferred_element_type=F32)

    def dot_first(left, right):
        return lax.dot_general(left, right, (((0,), (0,)), ((), ())), preferred_element_type=F32)

    early_slot, down = 1, 2

    def items(slot):
        return down if slot == early_slot else 3

    def g_view(slot, q, half):
        size = units if half is None else units // 2
        start = slot * units + (half or 0) * size
        return g_ref.at[pl.ds(0, items(slot)), pl.ds(start, size), pl.ds(q * quarter, quarter)]

    def late_view(ref, q, half):
        rows_at = pl.ds(last * units + half * (units // 2), units // 2)
        return ref.at[:, rows_at, pl.ds(q * quarter, quarter)]

    base = PER_SCATTER
    late_low, late_high = late_view(wf_ref, 3, 0), late_view(wf_ref, 3, 1)
    copies.send(late_view(wf, 1, 0), late_low, base, base, place.by_y)
    copies.send(late_view(wf, 2, 1), late_high, base + 1, base + 1, place.by_x)
    feed = Scatter(place, copies, g_view, far_x, far_y, near_x, near_y, None, 0, items)
    up_base = base + 2

    def feed_products(slot):
        at = pl.ds(slot * units, units)
        load_wf[slot].wait()

        @pl.loop(0, tiles)
        def _(i):
            rows_at = tile(i)
            left = dot_last(wf_ref[0, at, :], nm_ref[rows_at, :])
            right = dot_last(wf_ref[1, at, :], nm_ref[rows_at, :])
            grad = dot_last(wf_ref[2, at, :], og_ref[rows_at, :])
            t_ref[0, at, rows_at] = (grad * right).astype(BF)
            t_ref[1, at, rows_at] = (grad * left).astype(BF)
            t_ref[2, at, rows_at] = (left * right).astype(BF)

    def feed_gradients(slot):
        at = pl.ds(slot * units, units)

        def gradient(columns, of=(0, 1, 2)):
            for m in of:
                right = og_ref if m == down else nm_ref
                g_ref[m, at, columns] = dot(t_ref[m, at, :], right[:, columns]).astype(BF)

        def gradients(n, of=(0, 1, 2)):
            @pl.loop(0, n)
            def _(q):
                gradient(pl.ds(pl.multiple_of(q * quarter, quarter), quarter), of)

        if slot == 0:
            gradients(4)
            return
        of = tuple(range(items(slot)))
        if slot == early_slot:
            gradients(4, (down,))
            copies.send(g_ref.at[down, at], early_ref, up_base, up_base, place.above(slot))
        gradient(pl.ds(3 * quarter, quarter), of)
        feed.begin(slot)
        gradients(3, of)

    load_nm.wait()
    load_og.wait()
    for slot in order[:2]:
        feed_products(slot)
        feed_gradients(slot)
    feed.middle(order[0])
    copies.receive(late_low, base, place.by_y)
    copies.receive(late_high, base + 1, place.by_x)
    feed_products(order[2])
    feed_gradients(order[2])
    feed_products(order[3])
    feed.middle(order[1])
    base += 2 + 4
    for load in early_loads:
        load.wait()

    @pl.loop(0, spans)
    def _(i):
        at = tile(spans + i)
        total = dot_first(t_ref[0, :, at], wf_ref[0]) + dot_first(t_ref[1, :, at], wf_ref[1])
        send_ref[tile(i), :] = total.astype(BF)

    copies.send(send_ref, got_ref, base, base, place.across)

    @pl.loop(0, spans)
    def _(i):
        at = tile(i)
        total = dot_first(t_ref[0, :, at], wf_ref[0]) + dot_first(t_ref[1, :, at], wf_ref[1])
        mid_ref[at, :] = total

    feed.end(order[0], False)
    both, second_at = pl.ds(0, down), pl.ds(order[0] * units, units)
    near = pl.ds(0, quarter)
    above = place.above(order[0])
    copies.send(g_ref.at[:, second_at, near], high_ref, up_base + 1, up_base + 1, above)
    copies.receive(got_ref, base, place.across)

    @pl.loop(0, rows // 128)
    def _(i):
        at = pl.ds(pl.multiple_of(i * 128, 128), 128)
        grad = mid_ref[at, :] + got_ref[at, :].astype(F32)
        values = hidden_ref[at, :]
        norm = lax.rsqrt(jnp.mean(values * values, axis=-1, keepdims=True) + EPSILON)
        normed = values * norm
        mean = jnp.mean(grad * normed, axis=-1, keepdims=True)
        grad = og_ref[at, :].astype(F32) + norm * (grad - normed * mean)
        mid_ref[at, :] = grad
        branch_ref[at, :] = grad.astype(BF)

    copies.send(branch_ref.at[own], branch_ref.at[other], base + 1, base + 1, place.across)
    copies.move(mid_ref, hidden_grad_out, later=True)
    feed_gradients(order[3])
    copies.receive(early_ref, up_base, place.up)
    add_to(g_ref.at[down, pl.ds(0, units)], early_ref)
    feed.begin(0)
    query_loads = []
    for slot in range(n_head):
        lanes = pl.ds(slot * 2 * HEAD_DIM, 2 * HEAD_DIM)
        query_loads.append(copies.move(query.at[slot], t_ref.at[0, pl.ds(0, 2 * rows), lanes]))

    def gate_back(seq):
        for n in range(spans):
            at = pl.ds(seq * rows + n * SPAN, SPAN)
            grad = dot_last(branch_ref[at, :], wo_ref[...])
            norm = scale_ref[at, :]
            total = jnp.zeros((SPAN, 1), F32)
            for slot in range(n_head):
                lanes = pl.ds(slot * HEAD_DIM, HEAD_DIM)
                part = grad[:, slot * HEAD_DIM : (slot + 1) * HEAD_DIM]
                normed = attn_ref[slot, at, :] * norm
                og_ref[at, lanes] = (part * normed).astype(BF)
                part = part * gate_ref[slot, at, :]
                gate_ref[slot, at, :] = part
                total += jnp.sum(part * normed, axis=-1, keepdims=True)
            sum_ref[at, :] = jnp.broadcast_to(total, (SPAN, HEAD_DIM))

    gate_back(0)
    base += 2
    copies.send(sum_ref.at[own], other_sum_ref.at[other], base, base, place.across)
    copies.receive(branch_ref.at[other], base - 1, place.across)
    copies.move(branch_ref, branch_out, later=True)
    gate_back(1)
    copies.send(sum_ref.at[other], other_sum_ref.at[own], base + 1, base + 1, place.across)
    copies.move(og_ref.at[:, pl.ds(0, n_head * HEAD_DIM)], gate_out, later=True)
    copies.sent(base - 2)
    feed.middle(order[2])

    @pl.loop(0, spans)
    def _(i):
        send_ref[tile(i), :] = dot_first(t_ref[2, :, tile(spans + i)], wf_ref[2]).astype(BF)

    copies.send(send_ref, got_ref, base + 2, base + 2, place.across)

    @pl.loop(0, spans)
    def _(i):
        at = tile(i)
        hidden_ref[at, :] += dot_first(t_ref[2, :, at], wf_ref[2])

    feed.end(order[1], False)
    src = g_ref.at[both, pl.ds(order[1] * units, units), near]
    copies.send(src, high_first_ref, up_base + 2, up_base + 2, place.above(order[1]))
    for load in query_loads:
        load.wait()
    copies.receive(other_sum_ref.at[other], base, place.across)
    copies.receive(other_sum_ref.at[own], base + 1, place.across)

    for slot in range(n_head):
        decay = decay_of(2 * lax.rem(z + slot, n_head) + core)
        early = jnp.exp(-decay * (iota((SPAN, HEAD_DIM), 0) + 1.0))

        @pl.loop(0, tiles)
        def _(i):
            at = tile(i)
            norm = scale_ref[at, :]
            mean = (sum_ref[at, :] + other_sum_ref[at, :]) / width
            grad = norm * (gate_ref[slot, at, :] - attn_ref[slot, at, :] * norm * mean)
            grad = grad.astype(BF)
            ga_ref[slot, at, :] = grad
            q = t_ref[0, at, pl.ds(slot * 2 * HEAD_DIM, 2 * HEAD_DIM)]
            both_terms = dot_first(
                q, jnp.concatenate(split(grad.astype(F32) * early), axis=1)
            )
            late_ref[slot, i] = both_terms[:, :HEAD_DIM] + both_terms[:, HEAD_DIM:]

        copies.move(ga_ref.at[slot], ga_out.at[slot], later=True)
        copies.move(late_ref.at[slot], late_out.at[slot], later=True)

    feed.middle(order[3])
    copies.receive(got_ref, base + 2, place.across)

    @pl.loop(0, rows // 128)
    def _(i):
        at = pl.ds(pl.multiple_of(i * 128, 128), 128)
        block_ref[at, :] = (hidden_ref[at, :] + got_ref[at, :].astype(F32)).astype(BF)

    for q in range(4):
        far = pl.ds(pl.multiple_of(place.at[q] * quarter, quarter), quarter)
        src = block_ref.at[:, pl.ds(q * quarter, quarter)]
        copies.move(src, block_out.at[:, far], later=True)
    feed.end(order[2], False)
    src = g_ref.at[:, pl.ds(order[2] * units, units), near]
    copies.send(src, high_third_ref, up_base + 3, up_base + 3, place.above(order[2]))
    copies.receive(high_ref, up_base + 1, place.up)
    copies.receive(high_first_ref, up_base + 2, place.up)
    feed.end(order[3], False)
    first_rows = pl.ds(0, units)
    add_to(g_ref.at[both, first_rows, near], high_ref.at[both], high_first_ref)
    add_to(g_ref.at[down, first_rows, near], high_ref.at[down])
    copies.receive(high_third_ref, up_base + 3, place.up)
    add_to(g_view(0, 0, None), high_third_ref)
    copies.move(g_view(0, 0, None), feed_out, later=True)
    copies.finish()


def middle(n_head, wf, nm, og, hidden, wo, pre, query, attn, scale):
    rows, width = hidden.shape
    units = wf.shape[1] // n_head
    quarter = width // 4
    tall = 2 * rows
    halves = (n_head, 3, units // 2, quarter)
    wholes = (n_head, 3, units, quarter)
    late = ((n_head, tall // SPAN, 2 * HEAD_DIM, HEAD_DIM), F32)
    buffers = [
        (wf.shape, BF),
        (wf.shape, BF),
        (wf.shape, BF),
        (halves, BF),
        (halves, BF),
        (wholes, BF),
        (wholes, BF),
        ((units, width), BF),
        (wholes[1:], BF),
        ((2, units, quarter), BF),
        (wholes[1:], BF),
        ((tall, width), BF),
        ((tall, width), BF),
        ((tall, width), BF),
        ((rows, width), F32),
        ((rows, width), F32),
        ((rows, width), BF),
        ((rows, width), BF),
        ((rows, width), BF),
        (wo.shape, BF),
        (attn.shape, F32),
        (attn.shape, F32),
        (attn.shape, BF),
        late,
        (scale.shape, F32),
        (scale.shape, F32),
        (scale.shape, F32),
    ]
    outs = [
        (wholes[1:], BF),
        ((rows, width), BF),
        ((rows, width), F32),
        ((tall, width), BF),
        ((tall, n_head * HEAD_DIM), BF),
        (attn.shape, BF),
        late,
    ]
    n_sems = PER_SCATTER + 2 + 4 + 2 + 3
    return pl.pallas_call(
        functools.partial(middle_kernel, n_head),
        out_shape=[jax.ShapeDtypeStruct(*out) for out in outs],
        in_specs=[ANY] * 9,
        out_specs=[ANY] * len(outs),
        scratch_shapes=[pltpu.VMEM(*b) for b in buffers]
        + [
            pltpu.SemaphoreType.DMA((n_sems,)),
            pltpu.SemaphoreType.DMA((n_sems,)),
            pltpu.SemaphoreType.DMA((64,)),
        ],
        compiler_params=pltpu.CompilerParams(
            collective_id=1, has_side_effects=True, vmem_limit_bytes=63 << 20
        ),
        name="middle",
    )(wf, nm, og, hidden, wo, pre, query, attn, scale)


class Share:
    def __init__(self, place, copies, view, base):
        self.place, self.copies, self.view, self.base = place, copies, view, base

    def pass_on(self, q, half, at, device):
        part = self.view(0, q, half)
        self.copies.send(part, part, self.base + at, self.base + at, device)

    def begin(self):
        self.pass_on(0, None, 0, self.place.by_x)
        self.pass_on(0, None, 1, self.place.by_y)
        self.pass_on(0, None, 4, self.place.across)

    def spread(self):
        place, copies, at = self.place, self.copies, self.base
        copies.receive(self.view(0, 1, None), at, place.by_x)
        self.pass_on(1, 0, 2, place.by_y)
        copies.receive(self.view(0, 2, None), at + 1, place.by_y)
        self.pass_on(2, 1, 3, place.by_x)
        self.pass_on(1, None, 5, place.across)
        self.pass_on(2, None, 6, place.across)

    def complete(self):
        place, copies, at = self.place, self.copies, self.base
        copies.receive(self.view(0, 3, 0), at + 2, place.by_y)
        copies.receive(self.view(0, 3, 1), at + 3, place.by_x)
        self.pass_on(3, None, 7, place.across)

    def other_side(self):
        for q in range(4):
            self.copies.receive(self.view(1, q, None), self.base + 4 + q, self.place.across)


PER_SHARE = 8


def last_kernel(
    n_head,
    late,
    feed_piece,
    nin,
    gate_pre,
    gated,
    branch,
    query,
    keys,
    values,
    grad_attn,
    carry,
    fresh,
    pre,
    cosines,
    sines,
    wa,
    hidden_grad,
    block,
    tokens,
    input_ref,
    block_ref,
    feed_ref,
    attn_ref,
    rates_both,
    ga_ref,
    a_far_x,
    a_far_y,
    a_near_x,
    a_near_y,
    a_high,
    g_far_x,
    g_far_y,
    g_near_x,
    g_near_y,
    g_high,
    late_ref,
    pending_ref,
    message_ref,
    nin_ref,
    gate_ref,
    gated_ref,
    branch_ref,
    q_ref,
    k_ref,
    v_ref,
    grad_attn_ref,
    carry_ref,
    fresh_ref,
    qk_pre_ref,
    cos_ref,
    sin_ref,
    pre_ref,
    wa_ref,
    x_ref,
    grad_ref,
    send_ref,
    got_ref,
    rates_ref,
    rates_high,
    rates_sum,
    rates_got,
    sends,
    receives,
    locals_,
):
    rows, width = tokens.shape
    quarter = width // 4
    units = feed_piece.shape[1]
    spans = rows // SPAN
    tiles = 2 * spans
    last = n_head - 1
    three = 3 * HEAD_DIM
    place = Place(n_head)
    place.greet()
    z, core = place.z, place.core
    copies = Copies(sends, receives, locals_)
    order = (2, 1, 3, 0)
    sides = (core, 1 - core)

    own_block = pl.ds(pl.multiple_of(place.plane * quarter, quarter), quarter)
    load_feed = copies.move(feed_piece, feed_ref.at[sides[0], :, :, own_block])
    load_late = copies.move(late, late_ref)
    load_first = [copies.move(nin, nin_ref), copies.move(gate_pre, gate_ref)]
    load_second = [copies.move(gated, gated_ref), copies.move(branch, branch_ref)]
    load_back = [
        copies.move(src, dst)
        for src, dst in (
            (query, q_ref),
            (keys, k_ref),
            (values, v_ref),
            (grad_attn, grad_attn_ref),
            (carry, carry_ref),
        )
    ]
    for seq in range(2):
        for slot in range(n_head):
            load_back.append(copies.move(fresh.at[slot, seq * spans], fresh_ref.at[slot, seq]))

    def slot_load(slot, turn):
        return [
            copies.move(pre.at[slot, :, pl.ds(0, 2 * HEAD_DIM)], qk_pre_ref.at[turn]),
            copies.move(cosines.at[slot], cos_ref.at[turn]),
            copies.move(sines.at[slot], sin_ref.at[turn]),
        ]

    slot_loads = [slot_load(slot, turn) for turn, slot in enumerate(order[:2])]
    late_loads = [
        copies.move(wa, wa_ref),
        copies.move(hidden_grad, grad_ref),
        copies.move(block, block_ref),
    ]
    for q in range(4):
        far = pl.ds(pl.multiple_of(place.at[q] * quarter, quarter), quarter)
        late_loads.append(copies.move(tokens.at[:, far], x_ref.at[:, pl.ds(q * quarter, quarter)]))
    place.meet()

    def tile(i):
        return pl.ds(pl.multiple_of(i * SPAN, SPAN), SPAN)

    def dot_last(left, right):
        return lax.dot_general(left, right, (((1,), (1,)), ((), ())), preferred_element_type=F32)

    def dot_first(left, right):
        return lax.dot_general(left, right, (((0,), (0,)), ((), ())), preferred_element_type=F32)

    def part(start, half, size):
        if half is None:
            return pl.ds(start, size)
        return pl.ds(start + half * (size // 2), size // 2)

    def start_of(q):
        return pl.multiple_of(place.at[q] * quarter, quarter)

    def feed_view(side, q, half):
        return feed_ref.at[sides[side], :, part(0, half, units), pl.ds(start_of(q), quarter)]

    def lanes_view(lanes, side, q, half):
        at = part(0, half, quarter)
        start = pl.multiple_of(start_of(q) + at.start, quarter // 2)
        return attn_ref.at[sides[side], pl.ds(start, at.size), lanes]

    def ga_view(lanes, slot, q, half):
        return ga_ref.at[slot, part(q * quarter, half, quarter), lanes]

    gate_lanes, rest_lanes = pl.ds(three, 2 * HEAD_DIM), pl.ds(0, three)
    weight_lanes = pl.ds(three, HEAD_DIM)
    of_gate = functools.partial(ga_view, gate_lanes)
    of_rest = functools.partial(ga_view, rest_lanes)
    gate = Scatter(place, copies, of_gate, g_far_x, g_far_y, g_near_x, g_near_y, g_high, 0)
    base = PER_SCATTER
    rest = Scatter(place, copies, of_rest, a_far_x, a_far_y, a_near_x, a_near_y, a_high, base)
    base += PER_SCATTER
    to_gate = functools.partial(lanes_view, gate_lanes)
    to_rest = functools.partial(lanes_view, rest_lanes)
    shares = []
    for view in (feed_view, to_gate, to_rest):
        shares.append(Share(place, copies, view, base))
        base += PER_SHARE
    feed_share, gate_share, rest_share = shares

    load_feed.wait()
    feed_share.begin()

    n_chain = 2 * n_head
    chain_base = base
    base += n_chain

    def chain_at(index):
        group, seq = lax.div(index, 2), lax.rem(index, 2)
        return lax.rem(group - z + n_head, n_head), seq, decay_of(2 * group + core)

    def chain_copy(index, slot, seq):
        return pltpu.make_async_remote_copy(
            src_ref=message_ref.at[slot, seq],
            dst_ref=pending_ref.at[lax.rem(slot + 1, n_head), seq],
            send_sem=sends.at[chain_base + index],
            recv_sem=receives.at[chain_base + index],
            device_id=place.down,
            device_id_type=MESH,
        )

    def hand_on(index):
        slot, seq, decay = chain_at(index)
        total = jnp.exp(-decay * rows) * pending_ref[slot, seq].astype(F32)
        for n in range(spans):
            total += jnp.exp(-decay * (n * SPAN)) * late_ref[slot, seq * spans + n]
        message_ref[slot, seq] = total.astype(BF)
        chain_copy(index, slot, seq).start()

    def take(index):
        slot, seq, _ = chain_at(index)
        copies.receive(pending_ref.at[slot, seq], chain_base + index, place.up)

    load_late.wait()

    @pl.when(z == last)
    def _():
        pending_ref[...] = jnp.zeros_like(pending_ref)
        pl.loop(0, n_chain)(hand_on)

    for load in load_first:
        load.wait()

    for load in load_second:
        load.wait()

    def gate_gradient(at):
        grads = dot_first(nin_ref[:, at], gate_ref[...]).astype(BF)
        outs = dot_first(branch_ref[:, at], gated_ref[...]).astype(BF)
        for slot in range(n_head):
            lanes = slice(slot * HEAD_DIM, (slot + 1) * HEAD_DIM)
            ga_ref[slot, at, pl.ds(three, HEAD_DIM)] = grads[:, lanes]
            ga_ref[slot, at, pl.ds(three + HEAD_DIM, HEAD_DIM)] = outs[:, lanes]

    gate_gradient(pl.ds(3 * quarter, quarter))
    for slot in order:
        gate.begin(slot)
    pl.loop(0, 3)(lambda q: gate_gradient(tile(q)))

    @pl.when(jnp.logical_and(z > 0, z < last))
    def _():
        @pl.loop(0, n_chain)
        def _(index):
            take(index)
            hand_on(index)

    for slot in order:
        gate.middle(slot)
    for load in load_back:
        load.wait()

    @pl.when(z == 0)
    def _():
        pl.loop(0, n_chain)(take)

    offsets = iota((SPAN, SPAN), 0) - iota((SPAN, SPAN), 1)

    def back_slot(slot, turn):
        decay = decay_of(2 * lax.rem(z + slot, n_head) + core)
        mask = jnp.where(offsets >= 0.0, jnp.exp(-decay * jnp.maximum(offsets, 0.0)), 0.0)
        places = iota((SPAN, 1), 0)
        early = jnp.exp(-decay * (places + 1.0))
        late_decay = jnp.exp(-decay * (SPAN - 1.0 - places))
        span_decay = jnp.exp(-decay * SPAN)
        rates_ref[slot] = jnp.zeros((8, HEAD_DIM), F32)

        @pl.loop(0, 2)
        def _(seq):
            for n in range(spans):
                at, here = tile(seq * spans + n), pl.ds(n * SPAN, SPAN)
                state = carry_ref[slot, seq].astype(F32)
                if n == 1:
                    state = span_decay * state + fresh_ref[slot, seq]
                later = pending_ref[slot, seq].astype(F32)
                if n == 0:
                    later = span_decay * later + late_ref[slot, seq * spans + 1]
                q, k, v = q_ref[slot, at, :], k_ref[slot, at, :], v_ref[slot, at, :]
                grad = grad_attn_ref[slot, at, :]
                weights = (dot_last(q, k) * mask).astype(BF)
                scores = (dot_last(grad, v) * mask).astype(BF)
                state_high, state_low = split(state)
                grad_query = dot(scores, k)
                grad_query += early * (dot_last(grad, state_high) + dot_last(grad, state_low))
                later_high, later_low = split(later)
                grad_keys = dot_first(scores, q)
                grad_keys += late_decay * (dot_last(v, later_high) + dot_last(v, later_low))
                both = dot(k, jnp.concatenate([later_high, later_low], axis=1))
                grad_values = dot_first(weights, grad)
                grad_values += late_decay * (both[:, :HEAD_DIM] + both[:, HEAD_DIM:])
                pre_ref[slot, at, pl.ds(2 * HEAD_DIM, HEAD_DIM)] = grad_values.astype(BF)
                cosine, sine = cos_ref[turn, here, :], sin_ref[turn, here, :]
                angles = jnp.zeros((SPAN, HEAD_DIM), F32)
                for i, turned in enumerate((grad_query, grad_keys)):
                    lanes = pl.ds(i * HEAD_DIM, HEAD_DIM)
                    value = qk_pre_ref[turn, at, lanes]
                    by_cos, by_sin = turned[:, :HEAD_DIM], turned[:, HEAD_DIM:]
                    sigmoid = 1.0 / (1.0 + jnp.exp(-value))
                    act = by_cos * cosine + by_sin * sine
                    angles += value * sigmoid * (by_sin * cosine - by_cos * sine)
                    act = act * sigmoid * (1.0 + value * (1.0 - sigmoid))
                    pre_ref[slot, at, lanes] = act.astype(BF)
                steps = (z * rows + n * SPAN).astype(F32) + places
                rates_ref[slot, pl.ds(0, 1), :] += jnp.sum(steps * angles, axis=0, keepdims=True)

    def rest_gradient(slot, at):
        ga_ref[slot, at, rest_lanes] = dot_first(nin_ref[:, at], pre_ref[slot]).astype(BF)

    rates_base = base
    base += n_head + 3
    for i, slot in enumerate(order):
        for load in slot_loads[i]:
            load.wait()
        back_slot(slot, i % 2)
        if i + 2 < n_head:
            slot_loads.append(slot_load(order[i + 2], i % 2))
        if slot:
            at = rates_base + slot
            copies.send(rates_ref.at[slot], rates_high.at[slot - 1], at, at, place.above(slot))
        rest_gradient(slot, pl.ds(3 * quarter, quarter))
        rest.begin(slot)
        pl.loop(0, 3)(lambda q: rest_gradient(slot, tile(q)))
    for slot in order:
        gate.end(slot)
    rest.middle(order[0])
    rest.middle(order[1])
    for load in late_loads:
        load.wait()

    def grad_in(at):
        total = dot_last(gate_ref[at, :], wa_gate())
        for slot in range(n_head):
            total += dot_last(pre_ref[slot, at, :], wa_ref[slot, :, rest_lanes])
        return total

    def wa_gate():
        return jnp.concatenate([wa_ref[slot, :, weight_lanes] for slot in range(n_head)], axis=1)

    @pl.loop(0, spans)
    def _(i):
        send_ref[tile(i), :] = grad_in(tile(spans + i)).astype(BF)

    copies.send(send_ref, got_ref, base, base, place.across)
    rest.middle(order[2])

    total = rates_ref[0]
    for slot in range(1, n_head):
        copies.receive(rates_high.at[slot - 1], rates_base + slot, place.up)
        total += rates_high[slot - 1]
    rates_sum[0] = total
    rates_base += n_head
    copies.send(rates_sum.at[0], rates_got.at[0], rates_base, rates_base, place.by_x)
    rest.middle(order[3])
    feed_share.spread()
    rest.end(order[0])
    copies.receive(rates_got.at[0], rates_base, place.by_x)
    rates_sum[1] = total + rates_got[0]
    copies.send(rates_sum.at[1], rates_got.at[1], rates_base + 1, rates_base + 1, place.by_y)
    copies.receive(got_ref, base, place.across)

    @pl.loop(0, spans)
    def _(i):
        at = tile(i)
        values = x_ref[at, :].astype(F32)
        norm = lax.rsqrt(jnp.mean(values * values, axis=-1, keepdims=True) + EPSILON)
        normed = values * norm
        grad = grad_in(at) + got_ref[at, :].astype(F32)
        mean = jnp.mean(grad * normed, axis=-1, keepdims=True)
        grad_ref[at, :] += norm * (grad - normed * mean)

    for q in range(4):
        src = grad_ref.at[:, pl.ds(q * quarter, quarter)]
        copies.move(src, input_ref.at[:, pl.ds(start_of(q), quarter)], later=True)
    gate.total(to_gate(0, 0, None))
    gate_share.begin()
    rest.end(order[1])
    copies.receive(rates_got.at[1], rates_base + 1, place.by_y)
    rates_both[sides[0]] = rates_sum[1] + rates_got[1]
    mine = rates_both.at[sides[0]]
    copies.send(mine, mine, rates_base + 2, rates_base + 2, place.across)
    feed_share.complete()
    rest.end(order[2])
    rest.end(order[3])
    rest.total(to_rest(0, 0, None))
    rest_share.begin()
    gate_share.spread()
    copies.receive(rates_both.at[sides[1]], rates_base + 2, place.across)
    feed_share.other_side()
    rest_share.spread()
    gate_share.complete()
    rest_share.complete()
    for share in shares[1:]:
        share.other_side()

    @pl.when(z > 0)
    def _():
        @pl.loop(0, n_chain)
        def _(index):
            slot, seq, _ = chain_at(index)
            chain_copy(index, slot, seq).wait_send()

    copies.finish()


def last(
    n_head,
    late,
    feed_piece,
    nin,
    gate_pre,
    gated,
    branch,
    query,
    keys,
    values,
    grad_attn,
    carry,
    fresh,
    pre,
    cosines,
    sines,
    wa,
    hidden_grad,
    block,
    tokens,
):
    rows, width = tokens.shape
    _, units, quarter = feed_piece.shape
    tall = 2 * rows

    def scatter_buffers(shape, halved):
        half = tuple(n // 2 if i == halved else n for i, n in enumerate(shape))
        return [
            ((n_head,) + half, BF),
            ((n_head,) + half, BF),
            ((n_head,) + shape, BF),
            ((n_head,) + shape, BF),
            ((n_head - 1,) + shape, BF),
        ]

    outs = [
        ((rows, width), F32),
        ((rows, width), BF),
        ((2, 3, units, width), BF),
        ((2, width, 5 * HEAD_DIM), BF),
        ((2, 8, HEAD_DIM), F32),
    ]
    chain = ((n_head, 2, 2 * HEAD_DIM, HEAD_DIM), BF)
    buffers = [
        ((n_head, width, 5 * HEAD_DIM), BF),
        *scatter_buffers((quarter, 3 * HEAD_DIM), 0),
        *scatter_buffers((quarter, 2 * HEAD_DIM), 0),
        (late.shape, F32),
        chain,
        chain,
        (nin.shape, BF),
        (gate_pre.shape, BF),
        (gated.shape, BF),
        (branch.shape, BF),
        (query.shape, BF),
        (keys.shape, BF),
        (values.shape, BF),
        (grad_attn.shape, BF),
        chain,
        (chain[0], F32),
        ((2, tall, 2 * HEAD_DIM), F32),
        ((2, rows, HEAD_DIM), F32),
        ((2, rows, HEAD_DIM), F32),
        ((n_head, tall, 3 * HEAD_DIM), BF),
        (wa.shape, BF),
        ((rows, width), BF),
        ((rows, width), F32),
        ((rows, width), BF),
        ((rows, width), BF),
        ((n_head, 8, HEAD_DIM), F32),
        ((n_head - 1, 8, HEAD_DIM), F32),
        ((2, 8, HEAD_DIM), F32),
        ((2, 8, HEAD_DIM), F32),
    ]
    n_sems = 2 * PER_SCATTER + 3 * PER_SHARE + 2 * n_head + n_head + 3 + 1
    arrays = [late, feed_piece, nin, gate_pre, gated, branch, query, keys, values, grad_attn]
    arrays += [carry, fresh, pre, cosines, sines, wa, hidden_grad, block, tokens]
    arrays = [pltpu.with_memory_space_constraint(array, pltpu.HBM) for array in arrays]
    return pl.pallas_call(
        functools.partial(last_kernel, n_head),
        out_shape=[pltpu.VMEM(*out) for out in outs],
        in_specs=[ANY] * len(arrays),
        out_specs=[IN_VMEM] * len(outs),
        scratch_shapes=[pltpu.VMEM(*b) for b in buffers]
        + [
            pltpu.SemaphoreType.DMA((n_sems,)),
            pltpu.SemaphoreType.DMA((n_sems,)),
            pltpu.SemaphoreType.DMA((64,)),
        ],
        compiler_params=pltpu.CompilerParams(
            collective_id=2, has_side_effects=True, vmem_limit_bytes=52 << 20
        ),
        name="last",
    )(*arrays)


def finish_kernel(grad, block, feed, attn, rates, *refs):
    outs, results, locals_ = refs[:11], refs[11:-1], refs[-1]
    copies = Copies(None, None, locals_)
    (block_out, grad_out, q_out, k_out, v_out, g_out, o_out, rates_out, l_out, r_out, d_out) = outs
    units = feed.shape[2]
    copies.move(grad, grad_out, later=True)
    copies.move(block, block_out, later=True)
    l_ref, r_ref, d_ref, q_ref, k_ref, v_ref, g_ref, o_ref, rates_ref = results
    for side in range(2):
        rates_ref[:, pl.ds(side * HEAD_DIM, HEAD_DIM)] = rates[side, pl.ds(0, 1), :]
    copies.move(rates_ref, rates_out, later=True)
    for i, (ref, out) in enumerate(((l_ref, l_out), (r_ref, r_out), (d_ref, d_out))):
        for side in range(2):
            at = pl.ds(side * units, units)
            ref[at, :] = feed[side, i].astype(F32)
            copies.move(ref.at[at], out.at[at], later=True)
    for i, (ref, out) in enumerate(((q_ref, q_out), (k_ref, k_out), (v_ref, v_out), (g_ref, g_out))):
        lanes = pl.ds(i * HEAD_DIM, HEAD_DIM)
        for side in range(2):
            ref[:, pl.ds(side * HEAD_DIM, HEAD_DIM)] = attn[side, :, lanes].astype(F32)
        copies.move(ref, out, later=True)
    for side in range(2):
        lanes = pl.ds(4 * HEAD_DIM, HEAD_DIM)
        o_ref[pl.ds(side * HEAD_DIM, HEAD_DIM), :] = attn[side, :, lanes].T.astype(F32)
    copies.move(o_ref, o_out, later=True)
    copies.finish()


def finish(grad, block, feed, attn, rates):
    _, _, units, width = feed.shape
    projection = ((width, 2 * HEAD_DIM), F32)
    back = ((2 * HEAD_DIM, width), F32)
    results = [((2 * units, width), F32)] * 3 + [projection] * 4 + [back]
    results.append(((1, 2 * HEAD_DIM), F32))
    outs = [(block.shape, BF), (grad.shape, F32)] + results[3:] + results[:3]
    return pl.pallas_call(
        finish_kernel,
        out_shape=[jax.ShapeDtypeStruct(*out) for out in outs],
        in_specs=[IN_VMEM] * 5,
        out_specs=[ANY] * len(outs),
        scratch_shapes=[pltpu.VMEM(*b) for b in results] + [pltpu.SemaphoreType.DMA((48,))],
        compiler_params=pltpu.CompilerParams(vmem_limit_bytes=24 << 20),
        name="finish",
    )(grad, block, feed, attn, rates)


def make(n_dp, n_head):
    def on_device(
        tokens,
        attn_query,
        attn_key,
        attn_value,
        attn_gate,
        attn_out,
        rotation_rates,
        ffn_left,
        ffn_right,
        ffn_down,
        out_grad,
    ):
        rates_in = rotation_rates.reshape(1, -1)
        (
            attn_weights,
            out_w,
            ffn_all,
            gathered_in,
            pre,
            query,
            keys,
            values,
            attn,
            cosines,
            sines,
            fresh,
            carry,
            scale_attn,
            gated,
            hidden,
            gathered_mid,
            grad_rows,
        ) = forward(
            n_head,
            tokens,
            out_grad,
            attn_query,
            attn_key,
            attn_value,
            attn_gate,
            attn_out,
            ffn_left.T,
            ffn_right.T,
            ffn_down,
            rates_in,
        )
        feed_piece, block_out, grad_hidden, branch_rows, gate_pre, grad_attn, late = middle(
            n_head,
            ffn_all,
            gathered_mid,
            grad_rows,
            hidden,
            out_w,
            pre,
            query,
            attn,
            scale_attn,
        )
        grads = last(
            n_head,
            late,
            feed_piece,
            gathered_in,
            gate_pre,
            gated,
            branch_rows,
            query,
            keys,
            values,
            grad_attn,
            carry,
            fresh,
            pre,
            cosines,
            sines,
            attn_weights,
            grad_hidden,
            block_out,
            tokens,
        )
        results = finish(*grads)
        rates_grad, left_grad, right_grad = results[7][0], results[8].T, results[9].T
        results = list(results[:7]) + [rates_grad, left_grad, right_grad, results[10]]
        if n_dp > 8:
            groups = [[i + 8 * j for j in range(n_dp // 8)] for i in range(8)]
            grads = [lax.psum(grad, "dp", axis_index_groups=groups) for grad in results[2:]]
            results = results[:2] + grads
        return tuple(results)

    return on_device


def solution(mesh):
    weights = (P(None, "head"),) * 4 + (P("head", None), P("head")) + (P(None, "head"),) * 2
    weights = weights + (P("head", None),)
    rows = P(("dp", "head"), None)
    return jax.shard_map(
        make(mesh.shape["dp"], mesh.shape["head"]),
        mesh=mesh,
        in_specs=(rows,) + weights + (rows,),
        out_specs=(rows, rows) + weights,
        check_vma=False,
    )
```

```python
import functools

import jax
import jax.numpy as jnp
from jax import lax
from jax.experimental import pallas as pl
from jax.experimental.pallas import tpu as pltpu
from jax.sharding import PartitionSpec as P

HEADS = 8
HEAD_DIM = 128
SPAN = 256
EPSILON = 1e-06
BF = jnp.bfloat16
F32 = jnp.float32


MESH = pl.DeviceIdType.MESH
ANY = pl.BlockSpec(memory_space=pl.ANY)
IN_VMEM = pl.BlockSpec(memory_space=pltpu.VMEM)


def split(value):
    high = value.astype(BF)
    return high, (value - high.astype(F32)).astype(BF)


class Place:
    def __init__(self, n_head):
        self.n_head = n_head
        dp = lax.axis_index("dp")
        self.z = lax.axis_index("head")
        self.core = lax.rem(dp, 2)
        x = lax.rem(lax.div(dp, 2), 2)
        y = lax.rem(lax.div(dp, 4), 2)
        self.plane = x + 2 * y
        self.at = [self.plane, self.plane + 1 - 2 * x, self.plane + 2 - 4 * y, 3 - self.plane]
        self.across = {"dp": dp + 1 - 2 * self.core}
        self.by_x = {"dp": dp + 2 - 4 * x}
        self.by_y = {"dp": dp + 4 - 8 * y}
        self.up = {"head": lax.rem(self.z + 1, n_head)}
        self.down = {"head": lax.rem(self.z + n_head - 1, n_head)}

    def above(self, step):
        return {"head": lax.rem(self.z + step, self.n_head)}

    def below(self, step):
        return {"head": lax.rem(self.z + self.n_head - step, self.n_head)}

    def greet(self):
        others = [self.across, self.by_x, self.by_y]
        others += [self.below(step) for step in range(1, self.n_head)]
        for other in others:
            barrier = pltpu.get_barrier_semaphore()
            pl.semaphore_signal(barrier, inc=1, device_id=other, device_id_type=MESH)

    def meet(self):
        pl.semaphore_wait(pltpu.get_barrier_semaphore(), self.n_head + 2)


class Copies:
    def __init__(self, sends, receives, locals_):
        self.sends, self.receives, self.locals = sends, receives, locals_
        self.pending = []
        self.started = {}
        self.n_local = 0

    def send(self, src, dst, out, into, device, when=None):
        copy = pltpu.make_async_remote_copy(
            src_ref=src,
            dst_ref=dst,
            send_sem=self.sends.at[out],
            recv_sem=self.receives.at[into],
            device_id=device,
            device_id_type=MESH,
        )
        if when is None:
            copy.start()
            self.pending.append(copy.wait_send)
            if isinstance(out, int):
                self.started[out] = copy.wait_send
        else:
            pl.when(when)(copy.start)
            self.pending.append(lambda: pl.when(when)(copy.wait_send))

    def receive(self, dst, into, device):
        pltpu.make_async_remote_copy(
            src_ref=dst,
            dst_ref=dst,
            send_sem=self.sends.at[0],
            recv_sem=self.receives.at[into],
            device_id=device,
            device_id_type=MESH,
        ).wait_recv()

    def move(self, src, dst, later=False):
        copy = pltpu.make_async_copy(src, dst, self.locals.at[self.n_local])
        self.n_local += 1
        copy.start()
        if later:
            self.pending.append(copy.wait)
        return copy

    def sent(self, out):
        wait = self.started.pop(out)
        self.pending.remove(wait)
        wait()

    def finish(self):
        for wait in self.pending:
            wait()


class Gather:
    def __init__(self, place, copies, view, base, late=None):
        self.place, self.copies, self.view, self.base = place, copies, view, base
        self.late = late

    def begin(self):
        place, z = self.place, self.place.z
        own = self.view(0, 0, None)
        last = place.n_head - 1
        self.copies.send(
            own, self.view(last, 0, None), self.base, self.base + last, place.up, when=z < last
        )
        self.copies.send(own, self.view(1, 0, None), self.base + 1, self.base + 1, place.down, when=z > 0)

    def arrived(self, slot, when=True):
        place, copies, z, base = self.place, self.copies, self.place.z, self.base
        last = place.n_head - 1
        if when is True:
            copies.receive(self.view(slot, 0, None), base + slot, place.up)
        else:
            pl.when(when)(lambda: copies.receive(self.view(slot, 0, None), base + slot, place.up))
        from_up = z + slot <= last
        piece = self.view(slot, 0, None)
        down = jnp.logical_and(jnp.logical_and(from_up, z > 0), when)
        up = jnp.logical_and(jnp.logical_not(from_up), z < last)
        up = jnp.logical_and(up, when)
        always = None if when is True else when
        after = jnp.minimum(slot + 1, last)
        before = jnp.maximum(slot - 1, 1)
        copies.send(piece, self.view(after, 0, None), base + 1 + slot, base + after, place.down, when=down)
        copies.send(piece, self.view(before, 0, None), base + 1 + slot, base + before, place.up, when=up)
        at = base + 4 * slot + 4
        copies.send(piece, self.view(slot, 1, None), at, at, place.by_x, when=always)
        copies.send(piece, self.view(slot, 2, None), at + 1, at + 1, place.by_y, when=always)

    def spread(self, slot):
        place, copies = self.place, self.copies
        at = self.base + 4 * slot + 4
        now = None if self.late is None else slot != self.late
        low, high = self.view(slot, 3, 0), self.view(slot, 3, 1)
        copies.receive(self.view(slot, 1, None), at, place.by_x)
        copies.send(self.view(slot, 1, 0), low, at + 2, at + 2, place.by_y, when=now)
        copies.receive(self.view(slot, 2, None), at + 1, place.by_y)
        copies.send(self.view(slot, 2, 1), high, at + 3, at + 3, place.by_x, when=now)

    def complete(self, slot):
        place, copies = self.place, self.copies
        at = self.base + 4 * slot + 4

        def receive():
            copies.receive(self.view(slot, 3, 0), at + 2, place.by_y)
            copies.receive(self.view(slot, 3, 1), at + 3, place.by_x)

        if self.late is None:
            receive()
        else:
            pl.when(slot != self.late)(receive)


PER_GATHER = 24


def forward_kernel(
    n_head,
    tokens,
    out_grad,
    wq,
    wk,
    wv,
    wg,
    wo,
    ffn_left,
    ffn_right,
    ffn_down,
    rates,
    wa_out,
    wo_out,
    wf_out,
    nin_out,
    pre_out,
    q_out,
    k_out,
    v_out,
    attn_out,
    cos_out,
    sin_out,
    fresh_out,
    carry_out,
    scale_out,
    gated_out,
    hidden_out,
    nm_out,
    og_out,
    wa_ref,
    wo_ref,
    wf_ref,
    x_ref,
    nin_ref,
    pre_ref,
    q_ref,
    k_ref,
    v_ref,
    attn_ref,
    cos_ref,
    sin_ref,
    fresh_ref,
    carry_ref,
    message_ref,
    squares_ref,
    other_squares_ref,
    gated_ref,
    branch_ref,
    other_branch_ref,
    hidden_ref,
    nm_ref,
    rates_ref,
    og_ref,
    sends,
    receives,
    locals_,
):
    rows, width = tokens.shape
    quarter = width // 4
    units = ffn_down.shape[0] // 2
    tiles = 2 * rows // SPAN
    place = Place(n_head)
    z, core = place.z, place.core
    last = n_head - 1
    place.greet()
    copies = Copies(sends, receives, locals_)

    def columns(start, size):
        return pl.ds(pl.multiple_of(start, size), size)

    def own_weights(q):
        far = columns(place.at[q] * quarter, quarter)
        near = pl.ds(q * quarter, quarter)
        loads = []
        for i, w in enumerate((wq, wk, wv, wg)):
            src = w.at[far, columns(core * HEAD_DIM, HEAD_DIM)]
            loads.append(copies.move(src, wa_ref.at[0, near, pl.ds(i * HEAD_DIM, HEAD_DIM)]))
        src = wo.at[columns(core * HEAD_DIM, HEAD_DIM), far]
        loads.append(copies.move(src, wo_ref.at[pl.ds(0, HEAD_DIM), near]))
        for i, w in enumerate((ffn_left, ffn_right, ffn_down)):
            src = w.at[pl.ds(pl.multiple_of(core * units, 16), units), far]
            loads.append(copies.move(src, wf_ref.at[i, pl.ds(0, units), near]))
        return loads

    own_loads = [own_weights(0)]
    token_loads = [
        copies.move(
            tokens.at[:, columns(place.at[q] * quarter, quarter)],
            x_ref.at[:, pl.ds(q * quarter, quarter)],
        )
        for q in range(4)
    ]
    place.meet()

    def half_rows(half, size):
        return pl.ds(0, size) if half is None else pl.ds(half * (size // 2), size // 2)

    def wa_view(part, slot, q, half):
        at = half_rows(half, quarter)
        lanes = pl.ds(part * 2 * HEAD_DIM, 2 * HEAD_DIM)
        return wa_ref.at[slot, pl.ds(q * quarter + at.start, at.size), lanes]

    def wo_view(slot, q, half):
        at = half_rows(half, HEAD_DIM)
        return wo_ref.at[
            pl.ds(pl.multiple_of(slot * HEAD_DIM + at.start, HEAD_DIM // 2), at.size),
            pl.ds(q * quarter, quarter),
        ]

    def wf_view(slot, q, half):
        at = half_rows(half, units)
        return wf_ref.at[
            :,
            pl.ds(pl.multiple_of(slot * units + at.start, 16), at.size),
            pl.ds(q * quarter, quarter),
        ]

    attn_all = [
        Gather(place, copies, functools.partial(wa_view, part), part * PER_GATHER)
        for part in range(2)
    ]
    attn_all.append(Gather(place, copies, wo_view, 2 * PER_GATHER))
    feed = Gather(place, copies, wf_view, 3 * PER_GATHER, late=last)
    base = 4 * PER_GATHER
    for loads, part in zip((own_loads[0][:2], own_loads[0][2:4], own_loads[0][4:5]), attn_all):
        for load in loads:
            load.wait()
        part.begin()
    grad_loads = [
        copies.move(
            out_grad.at[:, columns(place.at[q] * quarter, quarter)],
            og_ref.at[pl.ds(0, rows), pl.ds(q * quarter, quarter)],
        )
        for q in range(4)
    ]
    own_loads += [own_weights(q) for q in range(1, 4)]
    for step in range(1, n_head):
        copies.send(rates, rates_ref.at[step], base + step, base + step, place.below(step))
    rates_ref[0] = rates[...]

    for load in token_loads:
        load.wait()

    def norm_rows(values):
        mean = jnp.mean(values * values, axis=-1, keepdims=True)
        return values * lax.rsqrt(mean + EPSILON)

    @pl.loop(0, rows // 128)
    def _(i):
        at = pl.ds(pl.multiple_of(i * 128, 128), 128)
        nin_ref[at, :] = norm_rows(x_ref[at, :].astype(F32)).astype(BF)

    base += 4
    for load in grad_loads:
        load.wait()
    og_other = og_ref.at[pl.ds(rows, rows)]
    copies.send(og_ref.at[pl.ds(0, rows)], og_other, base, base, place.across)
    base += 1
    nin_other = nin_ref.at[pl.ds(rows, rows)]
    copies.send(nin_ref.at[pl.ds(0, rows)], nin_other, base, base, place.across)
    for q, loads in enumerate(own_loads):
        for load in loads[5:] if q == 0 else loads:
            load.wait()
    for step in range(1, n_head):
        copies.receive(rates_ref.at[step], base - 5 + step, place.up)
    copies.receive(nin_other, base, place.across)
    copies.move(nin_ref, nin_out, later=True)
    own_rows = pl.ds(0, units)
    copies.move(wf_ref.at[:, own_rows], wf_out.at[:, own_rows], later=True)
    copies.receive(og_other, base - 1, place.across)
    copies.move(og_ref, og_out, later=True)

    def decay_of(head):
        exponent = jnp.full((1, 1), -8.0 / HEADS, F32) * (head + 1).astype(F32)
        return jnp.exp2(exponent)

    def tile(i):
        return pl.ds(pl.multiple_of(i * SPAN, SPAN), SPAN)

    def iota(shape, axis):
        return lax.broadcasted_iota(jnp.int32, shape, axis).astype(F32)

    def dot(left, right):
        return jnp.dot(left, right, preferred_element_type=F32)

    def slot_compute(slot):
        head = 2 * lax.rem(z + slot, n_head) + core
        decay = decay_of(head)
        rate = rates_ref[slot, :, columns(core * HEAD_DIM, HEAD_DIM)]
        coarse = (z * rows).astype(F32) + 32.0 * iota((rows // 32, HEAD_DIM), 0)
        coarse = coarse * rate
        fine = iota((32, HEAD_DIM), 0) * rate
        cos_a, sin_a = jnp.cos(coarse), jnp.sin(coarse)
        cos_b, sin_b = jnp.cos(fine), jnp.sin(fine)
        for a in range(rows // 32):
            cos_row, sin_row = cos_a[a : a + 1], sin_a[a : a + 1]
            cos_ref[slot, pl.ds(a * 32, 32), :] = cos_row * cos_b - sin_row * sin_b
            sin_ref[slot, pl.ds(a * 32, 32), :] = sin_row * cos_b + cos_row * sin_b
        offsets = iota((SPAN, SPAN), 0) - iota((SPAN, SPAN), 1)
        mask = jnp.where(offsets >= 0.0, jnp.exp(-decay * jnp.maximum(offsets, 0.0)), 0.0)
        late = jnp.exp(-decay * (SPAN - 1.0 - iota((SPAN, HEAD_DIM), 0)))

        @pl.loop(0, tiles)
        def _(i):
            at = tile(i)
            pre = dot(nin_ref[at, :], wa_ref[slot])
            pre_ref[slot, at, :] = pre
            here = tile(lax.rem(i, rows // SPAN))
            cosines, sines = cos_ref[slot, here, :], sin_ref[slot, here, :]

            def rotate(values):
                activated = values / (1.0 + jnp.exp(-values))
                turned = jnp.concatenate([activated * cosines, activated * sines], axis=1)
                return turned.astype(BF)

            query = rotate(pre[:, :HEAD_DIM])
            keys = rotate(pre[:, HEAD_DIM : 2 * HEAD_DIM])
            value = pre[:, 2 * HEAD_DIM : 3 * HEAD_DIM].astype(BF)
            q_ref[slot, at, :] = query
            k_ref[slot, at, :] = keys
            v_ref[slot, at, :] = value
            scores = lax.dot_general(
                query, keys, (((1,), (1,)), ((), ())), preferred_element_type=F32
            )
            weights = (scores * mask).astype(BF)
            attn_ref[slot, at, :] = dot(weights, value)
            high, low = split(value.astype(F32) * late)
            both = lax.dot_general(
                keys,
                jnp.concatenate([high, low], axis=1),
                (((0,), (0,)), ((), ())),
                preferred_element_type=F32,
            )
            fresh_ref[slot, i] = both[:, :HEAD_DIM] + both[:, HEAD_DIM:]

        for ref, out in (
            (wa_ref, wa_out),
            (pre_ref, pre_out),
            (q_ref, q_out),
            (k_ref, k_out),
            (v_ref, v_out),
            (cos_ref, cos_out),
            (sin_ref, sin_out),
            (fresh_ref, fresh_out),
        ):
            copies.move(ref.at[slot], out.at[slot], later=True)

    first = 1 + 2 * lax.div(z, last)
    second = 2 + lax.rem(lax.div(z + 1, 2), 2)
    third = 6 - first - second

    for part in attn_all:
        part.arrived(first)
    slot_compute(0)
    for part in attn_all:
        part.arrived(second)
    for part in attn_all:
        part.spread(first)
    for part in attn_all:
        part.arrived(third)
    feed.begin()
    for part in attn_all:
        part.spread(second)
    for part in attn_all[:2]:
        part.complete(first)
    slot_compute(first)
    for part in attn_all:
        part.spread(third)
    feed.arrived(first)
    for part in attn_all[:2]:
        part.complete(second)
    slot_compute(second)
    inner = jnp.logical_and(z > 0, z < last)
    feed.arrived(second, inner)
    for part in attn_all[:2]:
        part.complete(third)
    slot_compute(third)
    base += 1
    chain_base = base
    n_chain = 2 * n_head

    def chain_at(index):
        group, seq = lax.div(index, 2), lax.rem(index, 2)
        return lax.rem(group - z + n_head, n_head), seq, decay_of(2 * group + core)

    def chain_copy(index, slot, seq):
        after = lax.rem(slot + n_head - 1, n_head)
        return pltpu.make_async_remote_copy(
            src_ref=message_ref.at[slot, seq],
            dst_ref=carry_ref.at[after, seq],
            send_sem=sends.at[chain_base + index],
            recv_sem=receives.at[chain_base + index],
            device_id=place.up,
            device_id_type=MESH,
        )

    def hand_on(index, slot, seq, decay):
        total = jnp.exp(-decay * rows) * carry_ref[slot, seq].astype(F32)
        for n in range(rows // SPAN):
            left = rows - (n + 1) * SPAN
            total += jnp.exp(-decay * left) * fresh_ref[slot, seq * (rows // SPAN) + n]
        message_ref[slot, seq] = total.astype(BF)
        chain_copy(index, slot, seq).start()

    @pl.when(z == 0)
    def _():
        @pl.loop(0, n_chain)
        def _(index):
            slot, seq, decay = chain_at(index)
            carry_ref[slot, seq] = jnp.zeros(carry_ref.shape[2:], BF)
            hand_on(index, slot, seq, decay)

    feed.arrived(second, jnp.logical_not(inner))
    feed.spread(first)
    feed.arrived(third)

    @pl.when(z > 0)
    def _():
        @pl.loop(0, n_chain)
        def _(index):
            slot, seq, decay = chain_at(index)
            copies.receive(carry_ref.at[slot, seq], chain_base + index, place.down)
            pl.when(z < last)(lambda: hand_on(index, slot, seq, decay))

    copies.move(carry_ref, carry_out, later=True)
    feed.spread(second)

    def feed_done(slot):
        feed.complete(slot)
        at = pl.ds(pl.multiple_of(slot * units, 16), units)
        copies.move(wf_ref.at[:, at], wf_out.at[:, at], later=True)

    def apply(seq):
        mine = pl.ds(seq * rows, rows)
        squares_ref[mine, :] = jnp.zeros((rows, HEAD_DIM), F32)

        @pl.loop(0, n_head)
        def _(slot):
            decay = decay_of(2 * lax.rem(z + slot, n_head) + core)
            early = jnp.exp(-decay * (iota((SPAN, HEAD_DIM), 0) + 1.0))
            state = carry_ref[slot, seq].astype(F32)
            for n in range(rows // SPAN):
                i = seq * (rows // SPAN) + n
                at = pl.ds(i * SPAN, SPAN)
                both = dot(q_ref[slot, at, :], jnp.concatenate(split(state), axis=1))
                attn = attn_ref[slot, at, :]
                attn += early * (both[:, :HEAD_DIM] + both[:, HEAD_DIM:])
                attn_ref[slot, at, :] = attn
                squares_ref[at, :] += jnp.sum(attn * attn, axis=-1, keepdims=True)
                if n + 1 < rows // SPAN:
                    state = jnp.exp(-decay * SPAN) * state + fresh_ref[slot, i]

    def gating(seq):
        for n in range(rows // SPAN):
            at = pl.ds(seq * rows + n * SPAN, SPAN)
            total = squares_ref[at, :] + other_squares_ref[at, :]
            scale = lax.rsqrt(total / width + EPSILON)
            other_squares_ref[at, :] = scale
            for slot in range(n_head):
                gate = pre_ref[slot, at, pl.ds(3 * HEAD_DIM, HEAD_DIM)]
                gated = (attn_ref[slot, at, :] * scale * gate).astype(BF)
                gated_ref[at, pl.ds(slot * HEAD_DIM, HEAD_DIM)] = gated

    base += n_chain
    own, other = pl.ds(0, rows), pl.ds(rows, rows)
    apply(1)
    copies.send(squares_ref.at[other], other_squares_ref.at[own], base, base, place.across)
    apply(0)
    copies.send(squares_ref.at[own], other_squares_ref.at[other], base + 1, base + 1, place.across)
    copies.move(attn_ref, attn_out, later=True)
    for slot in (first, second, third):
        attn_all[2].complete(slot)
    copies.receive(other_squares_ref.at[other], base + 1, place.across)
    gating(1)
    feed_done(first)
    base += 2
    for n in range(rows // SPAN):
        gated = gated_ref[pl.ds(rows + n * SPAN, SPAN), :]
        branch_ref[pl.ds(n * SPAN, SPAN), :] = dot(gated, wo_ref[...]).astype(BF)
    copies.send(branch_ref, other_branch_ref, base, base, place.across)
    copies.receive(other_squares_ref.at[own], base - 2, place.across)
    gating(0)
    copies.move(other_squares_ref, scale_out, later=True)
    copies.move(gated_ref, gated_out, later=True)
    copies.move(wo_ref, wo_out, later=True)
    feed.spread(third)
    feed_done(second)

    @pl.loop(0, rows // SPAN)
    def _(i):
        at = tile(i)
        hidden_ref[at, :] = x_ref[at, :].astype(F32) + dot(gated_ref[at, :], wo_ref[...])

    copies.receive(other_branch_ref, base, place.across)

    @pl.loop(0, rows // 128)
    def _(i):
        at = pl.ds(pl.multiple_of(i * 128, 128), 128)
        hidden = hidden_ref[at, :] + other_branch_ref[at, :].astype(F32)
        hidden_ref[at, :] = hidden
        nm_ref[at, :] = norm_rows(hidden).astype(BF)

    copies.send(nm_ref.at[own], nm_ref.at[other], base + 1, base + 1, place.across)
    copies.move(hidden_ref, hidden_out, later=True)
    feed_done(third)
    copies.receive(nm_ref.at[other], base + 1, place.across)
    copies.move(nm_ref, nm_out, later=True)

    @pl.when(z < last)
    def _():
        @pl.loop(0, n_chain)
        def _(index):
            slot, seq, _ = chain_at(index)
            chain_copy(index, slot, seq).wait_send()

    copies.finish()


def forward(n_head, tokens, out_grad, wq, wk, wv, wg, wo, ffn_left, ffn_right, ffn_down, rates):
    rows, width = tokens.shape
    units = ffn_down.shape[0] // 2
    tall = 2 * rows
    buffers = [
        ((n_head, width, 4 * HEAD_DIM), BF),
        ((n_head * HEAD_DIM, width), BF),
        ((3, n_head * units, width), BF),
        ((rows, width), BF),
        ((tall, width), BF),
        ((n_head, tall, 4 * HEAD_DIM), F32),
        ((n_head, tall, 2 * HEAD_DIM), BF),
        ((n_head, tall, 2 * HEAD_DIM), BF),
        ((n_head, tall, HEAD_DIM), BF),
        ((n_head, tall, HEAD_DIM), F32),
        ((n_head, rows, HEAD_DIM), F32),
        ((n_head, rows, HEAD_DIM), F32),
        ((n_head, tall // SPAN, 2 * HEAD_DIM, HEAD_DIM), F32),
        ((n_head, 2, 2 * HEAD_DIM, HEAD_DIM), BF),
        ((n_head, 2, 2 * HEAD_DIM, HEAD_DIM), BF),
        ((tall, HEAD_DIM), F32),
        ((tall, HEAD_DIM), F32),
        ((tall, n_head * HEAD_DIM), BF),
        ((rows, width), BF),
        ((rows, width), BF),
        ((rows, width), F32),
        ((tall, width), BF),
        ((n_head, 1, 2 * HEAD_DIM), F32),
        ((tall, width), BF),
    ]
    out_of = [0, 1, 2, 4, 5, 6, 7, 8, 9, 10, 11, 12, 13, 16, 17, 20, 21, 23]
    n_sems = 4 * PER_GATHER + 4 + 1 + 1 + 2 * n_head + 2 + 2
    return pl.pallas_call(
        functools.partial(forward_kernel, n_head),
        out_shape=[jax.ShapeDtypeStruct(*buffers[i]) for i in out_of],
        in_specs=[ANY] * 10 + [IN_VMEM],
        out_specs=[ANY] * len(out_of),
        scratch_shapes=[pltpu.VMEM(*b) for b in buffers]
        + [
            pltpu.SemaphoreType.DMA((n_sems,)),
            pltpu.SemaphoreType.DMA((n_sems,)),
            pltpu.SemaphoreType.DMA((96,)),
        ],
        compiler_params=pltpu.CompilerParams(
            collective_id=0, has_side_effects=True, vmem_limit_bytes=62 << 20
        ),
        name="forward",
    )(tokens, out_grad, wq, wk, wv, wg, wo, ffn_left, ffn_right, ffn_down, rates)


class Scatter:
    def __init__(self, place, copies, view, far_x, far_y, near_x, near_y, high, base, items=None):
        self.place, self.copies, self.view, self.base = place, copies, view, base
        self.items = items
        self.far_x, self.far_y, self.near_x, self.near_y, self.high = far_x, far_y, near_x, near_y, high

    def part(self, buffer, slot):
        return buffer.at[slot] if self.items is None else buffer.at[slot, pl.ds(0, self.items(slot))]

    def begin(self, slot):
        place, at = self.place, self.base + 4 * slot
        self.copies.send(self.view(slot, 3, 0), self.part(self.far_y, slot), at, at, place.by_y)
        self.copies.send(self.view(slot, 3, 1), self.part(self.far_x, slot), at + 1, at + 1, place.by_x)

    def middle(self, slot):
        place, copies, at = self.place, self.copies, self.base + 4 * slot
        copies.receive(self.part(self.far_y, slot), at, place.by_y)
        add_to(self.view(slot, 1, 0), self.part(self.far_y, slot))
        copies.send(self.view(slot, 1, None), self.part(self.near_x, slot), at + 2, at + 2, place.by_x)
        copies.receive(self.part(self.far_x, slot), at + 1, place.by_x)
        add_to(self.view(slot, 2, 1), self.part(self.far_x, slot))
        copies.send(self.view(slot, 2, None), self.part(self.near_y, slot), at + 3, at + 3, place.by_y)

    def end(self, slot, onward=True):
        place, copies, at = self.place, self.copies, self.base + 4 * slot
        copies.receive(self.part(self.near_x, slot), at + 2, place.by_x)
        copies.receive(self.part(self.near_y, slot), at + 3, place.by_y)
        add_to(self.view(slot, 0, None), self.part(self.near_x, slot), self.part(self.near_y, slot))
        if slot and onward:
            self.go_up(slot)

    def go_up(self, slot):
        at = self.base + 4 * self.place.n_head + slot
        into = self.high.at[slot - 1]
        self.copies.send(self.view(slot, 0, None), into, at, at, self.place.above(slot))

    def total(self, into=None, slots=(1, 2, 3)):
        place = self.place
        high = [self.high.at[slot - 1] for slot in slots]
        for slot, part in zip(slots, high):
            self.copies.receive(part, self.base + 4 * place.n_head + slot, place.up)
        add_to(self.view(0, 0, None), *high, into=into)


PER_SCATTER = 20


def add_to(ref, *others, into=None):
    def add(into, *refs):
        total = refs[0][...].astype(F32)
        for other in refs[1:]:
            total += other[...].astype(F32)
        into[...] = total.astype(BF)

    refs = (ref if into is None else into, ref) + others
    if len(ref.shape) == 2:
        add(*refs)
    else:
        for i in range(ref.shape[0]):
            add(*(one.at[i] for one in refs))


def dot(left, right):
    return jnp.dot(left, right, preferred_element_type=F32)


def iota(shape, axis):
    return lax.broadcasted_iota(jnp.int32, shape, axis).astype(F32)


def decay_of(head):
    exponent = jnp.full((1, 1), -8.0 / HEADS, F32) * (head + 1).astype(F32)
    return jnp.exp2(exponent)


def middle_kernel(
    n_head,
    wf,
    nm,
    og,
    hidden,
    wo,
    pre,
    query,
    attn,
    scale,
    feed_out,
    block_out,
    hidden_grad_out,
    branch_out,
    gate_out,
    ga_out,
    late_out,
    wf_ref,
    t_ref,
    g_ref,
    far_x,
    far_y,
    near_x,
    near_y,
    early_ref,
    high_ref,
    high_first_ref,
    high_third_ref,
    nm_ref,
    og_ref,
    branch_ref,
    hidden_ref,
    mid_ref,
    send_ref,
    got_ref,
    block_ref,
    wo_ref,
    gate_ref,
    attn_ref,
    ga_ref,
    late_ref,
    scale_ref,
    sum_ref,
    other_sum_ref,
    sends,
    receives,
    locals_,
):
    rows, width = hidden.shape
    quarter = width // 4
    units = wf.shape[1] // n_head
    spans = rows // SPAN
    tiles = 2 * spans
    last = n_head - 1
    place = Place(n_head)
    z, core = place.z, place.core
    place.greet()
    copies = Copies(sends, receives, locals_)
    own, other = pl.ds(0, rows), pl.ds(rows, rows)

    order = (2, 1, 3, 0)
    load_nm = copies.move(nm, nm_ref)
    load_og = copies.move(og, og_ref)
    load_wf = {}
    for slot in order:
        at = pl.ds(slot * units, units)
        lanes = pl.ds(0, width if slot < last else width - quarter)
        load_wf[slot] = copies.move(wf.at[:, at, lanes], wf_ref.at[:, at, lanes])
    early_loads = [
        copies.move(hidden, hidden_ref),
        copies.move(wo, wo_ref),
        copies.move(scale, scale_ref),
        copies.move(attn, attn_ref),
        copies.move(pre.at[:, :, pl.ds(3 * HEAD_DIM, HEAD_DIM)], gate_ref),
    ]
    place.meet()

    def tile(i):
        return pl.ds(pl.multiple_of(i * SPAN, SPAN), SPAN)

    def dot_last(left, right):
        return lax.dot_general(left, right, (((1,), (1,)), ((), ())), preferred_element_type=F32)

    def dot_first(left, right):
        return lax.dot_general(left, right, (((0,), (0,)), ((), ())), preferred_element_type=F32)

    early_slot, down = 1, 2

    def items(slot):
        return down if slot == early_slot else 3

    def g_view(slot, q, half):
        size = units if half is None else units // 2
        start = slot * units + (half or 0) * size
        return g_ref.at[pl.ds(0, items(slot)), pl.ds(start, size), pl.ds(q * quarter, quarter)]

    def late_view(ref, q, half):
        rows_at = pl.ds(last * units + half * (units // 2), units // 2)
        return ref.at[:, rows_at, pl.ds(q * quarter, quarter)]

    base = PER_SCATTER
    late_low, late_high = late_view(wf_ref, 3, 0), late_view(wf_ref, 3, 1)
    copies.send(late_view(wf, 1, 0), late_low, base, base, place.by_y)
    copies.send(late_view(wf, 2, 1), late_high, base + 1, base + 1, place.by_x)
    feed = Scatter(place, copies, g_view, far_x, far_y, near_x, near_y, None, 0, items)
    up_base = base + 2

    def feed_products(slot):
        at = pl.ds(slot * units, units)
        load_wf[slot].wait()

        @pl.loop(0, tiles)
        def _(i):
            rows_at = tile(i)
            left = dot_last(wf_ref[0, at, :], nm_ref[rows_at, :])
            right = dot_last(wf_ref[1, at, :], nm_ref[rows_at, :])
            grad = dot_last(wf_ref[2, at, :], og_ref[rows_at, :])
            t_ref[0, at, rows_at] = (grad * right).astype(BF)
            t_ref[1, at, rows_at] = (grad * left).astype(BF)
            t_ref[2, at, rows_at] = (left * right).astype(BF)

    def feed_gradients(slot):
        at = pl.ds(slot * units, units)

        def gradient(columns, of=(0, 1, 2)):
            for m in of:
                right = og_ref if m == down else nm_ref
                g_ref[m, at, columns] = dot(t_ref[m, at, :], right[:, columns]).astype(BF)

        def gradients(n, of=(0, 1, 2)):
            @pl.loop(0, n)
            def _(q):
                gradient(pl.ds(pl.multiple_of(q * quarter, quarter), quarter), of)

        if slot == 0:
            gradients(4)
            return
        of = tuple(range(items(slot)))
        if slot == early_slot:
            gradients(4, (down,))
            copies.send(g_ref.at[down, at], early_ref, up_base, up_base, place.above(slot))
        gradient(pl.ds(3 * quarter, quarter), of)
        feed.begin(slot)
        gradients(3, of)

    load_nm.wait()
    load_og.wait()
    for slot in order[:2]:
        feed_products(slot)
        feed_gradients(slot)
    feed.middle(order[0])
    copies.receive(late_low, base, place.by_y)
    copies.receive(late_high, base + 1, place.by_x)
    feed_products(order[2])
    feed_gradients(order[2])
    feed_products(order[3])
    feed.middle(order[1])
    base += 2 + 4
    for load in early_loads:
        load.wait()

    @pl.loop(0, spans)
    def _(i):
        at = tile(spans + i)
        total = dot_first(t_ref[0, :, at], wf_ref[0]) + dot_first(t_ref[1, :, at], wf_ref[1])
        send_ref[tile(i), :] = total.astype(BF)

    copies.send(send_ref, got_ref, base, base, place.across)

    @pl.loop(0, spans)
    def _(i):
        at = tile(i)
        total = dot_first(t_ref[0, :, at], wf_ref[0]) + dot_first(t_ref[1, :, at], wf_ref[1])
        mid_ref[at, :] = total

    feed.end(order[0], False)
    both, second_at = pl.ds(0, down), pl.ds(order[0] * units, units)
    near = pl.ds(0, quarter)
    above = place.above(order[0])
    copies.send(g_ref.at[:, second_at, near], high_ref, up_base + 1, up_base + 1, above)
    copies.receive(got_ref, base, place.across)

    @pl.loop(0, rows // 128)
    def _(i):
        at = pl.ds(pl.multiple_of(i * 128, 128), 128)
        grad = mid_ref[at, :] + got_ref[at, :].astype(F32)
        values = hidden_ref[at, :]
        norm = lax.rsqrt(jnp.mean(values * values, axis=-1, keepdims=True) + EPSILON)
        normed = values * norm
        mean = jnp.mean(grad * normed, axis=-1, keepdims=True)
        grad = og_ref[at, :].astype(F32) + norm * (grad - normed * mean)
        mid_ref[at, :] = grad
        branch_ref[at, :] = grad.astype(BF)

    copies.send(branch_ref.at[own], branch_ref.at[other], base + 1, base + 1, place.across)
    copies.move(mid_ref, hidden_grad_out, later=True)
    feed_gradients(order[3])
    copies.receive(early_ref, up_base, place.up)
    add_to(g_ref.at[down, pl.ds(0, units)], early_ref)
    feed.begin(0)
    query_loads = []
    for slot in range(n_head):
        lanes = pl.ds(slot * 2 * HEAD_DIM, 2 * HEAD_DIM)
        query_loads.append(copies.move(query.at[slot], t_ref.at[0, pl.ds(0, 2 * rows), lanes]))

    def gate_back(seq):
        for n in range(spans):
            at = pl.ds(seq * rows + n * SPAN, SPAN)
            grad = dot_last(branch_ref[at, :], wo_ref[...])
            norm = scale_ref[at, :]
            total = jnp.zeros((SPAN, 1), F32)
            for slot in range(n_head):
                lanes = pl.ds(slot * HEAD_DIM, HEAD_DIM)
                part = grad[:, slot * HEAD_DIM : (slot + 1) * HEAD_DIM]
                normed = attn_ref[slot, at, :] * norm
                og_ref[at, lanes] = (part * normed).astype(BF)
                part = part * gate_ref[slot, at, :]
                gate_ref[slot, at, :] = part
                total += jnp.sum(part * normed, axis=-1, keepdims=True)
            sum_ref[at, :] = jnp.broadcast_to(total, (SPAN, HEAD_DIM))

    gate_back(0)
    base += 2
    copies.send(sum_ref.at[own], other_sum_ref.at[other], base, base, place.across)
    copies.receive(branch_ref.at[other], base - 1, place.across)
    copies.move(branch_ref, branch_out, later=True)
    gate_back(1)
    copies.send(sum_ref.at[other], other_sum_ref.at[own], base + 1, base + 1, place.across)
    copies.move(og_ref.at[:, pl.ds(0, n_head * HEAD_DIM)], gate_out, later=True)
    copies.sent(base - 2)
    feed.middle(order[2])

    @pl.loop(0, spans)
    def _(i):
        send_ref[tile(i), :] = dot_first(t_ref[2, :, tile(spans + i)], wf_ref[2]).astype(BF)

    copies.send(send_ref, got_ref, base + 2, base + 2, place.across)

    @pl.loop(0, spans)
    def _(i):
        at = tile(i)
        hidden_ref[at, :] += dot_first(t_ref[2, :, at], wf_ref[2])

    feed.end(order[1], False)
    src = g_ref.at[both, pl.ds(order[1] * units, units), near]
    copies.send(src, high_first_ref, up_base + 2, up_base + 2, place.above(order[1]))
    for load in query_loads:
        load.wait()
    copies.receive(other_sum_ref.at[other], base, place.across)
    copies.receive(other_sum_ref.at[own], base + 1, place.across)

    for slot in range(n_head):
        decay = decay_of(2 * lax.rem(z + slot, n_head) + core)
        early = jnp.exp(-decay * (iota((SPAN, HEAD_DIM), 0) + 1.0))

        @pl.loop(0, tiles)
        def _(i):
            at = tile(i)
            norm = scale_ref[at, :]
            mean = (sum_ref[at, :] + other_sum_ref[at, :]) / width
            grad = norm * (gate_ref[slot, at, :] - attn_ref[slot, at, :] * norm * mean)
            grad = grad.astype(BF)
            ga_ref[slot, at, :] = grad
            q = t_ref[0, at, pl.ds(slot * 2 * HEAD_DIM, 2 * HEAD_DIM)]
            both_terms = dot_first(
                q, jnp.concatenate(split(grad.astype(F32) * early), axis=1)
            )
            late_ref[slot, i] = both_terms[:, :HEAD_DIM] + both_terms[:, HEAD_DIM:]

        copies.move(ga_ref.at[slot], ga_out.at[slot], later=True)
        copies.move(late_ref.at[slot], late_out.at[slot], later=True)

    feed.middle(order[3])
    copies.receive(got_ref, base + 2, place.across)

    @pl.loop(0, rows // 128)
    def _(i):
        at = pl.ds(pl.multiple_of(i * 128, 128), 128)
        block_ref[at, :] = (hidden_ref[at, :] + got_ref[at, :].astype(F32)).astype(BF)

    for q in range(4):
        far = pl.ds(pl.multiple_of(place.at[q] * quarter, quarter), quarter)
        src = block_ref.at[:, pl.ds(q * quarter, quarter)]
        copies.move(src, block_out.at[:, far], later=True)
    feed.end(order[2], False)
    src = g_ref.at[:, pl.ds(order[2] * units, units), near]
    copies.send(src, high_third_ref, up_base + 3, up_base + 3, place.above(order[2]))
    copies.receive(high_ref, up_base + 1, place.up)
    copies.receive(high_first_ref, up_base + 2, place.up)
    feed.end(order[3], False)
    first_rows = pl.ds(0, units)
    add_to(g_ref.at[both, first_rows, near], high_ref.at[both], high_first_ref)
    add_to(g_ref.at[down, first_rows, near], high_ref.at[down])
    copies.receive(high_third_ref, up_base + 3, place.up)
    add_to(g_view(0, 0, None), high_third_ref)
    copies.move(g_view(0, 0, None), feed_out, later=True)
    copies.finish()


def middle(n_head, wf, nm, og, hidden, wo, pre, query, attn, scale):
    rows, width = hidden.shape
    units = wf.shape[1] // n_head
    quarter = width // 4
    tall = 2 * rows
    halves = (n_head, 3, units // 2, quarter)
    wholes = (n_head, 3, units, quarter)
    late = ((n_head, tall // SPAN, 2 * HEAD_DIM, HEAD_DIM), F32)
    buffers = [
        (wf.shape, BF),
        (wf.shape, BF),
        (wf.shape, BF),
        (halves, BF),
        (halves, BF),
        (wholes, BF),
        (wholes, BF),
        ((units, width), BF),
        (wholes[1:], BF),
        ((2, units, quarter), BF),
        (wholes[1:], BF),
        ((tall, width), BF),
        ((tall, width), BF),
        ((tall, width), BF),
        ((rows, width), F32),
        ((rows, width), F32),
        ((rows, width), BF),
        ((rows, width), BF),
        ((rows, width), BF),
        (wo.shape, BF),
        (attn.shape, F32),
        (attn.shape, F32),
        (attn.shape, BF),
        late,
        (scale.shape, F32),
        (scale.shape, F32),
        (scale.shape, F32),
    ]
    outs = [
        (wholes[1:], BF),
        ((rows, width), BF),
        ((rows, width), F32),
        ((tall, width), BF),
        ((tall, n_head * HEAD_DIM), BF),
        (attn.shape, BF),
        late,
    ]
    n_sems = PER_SCATTER + 2 + 4 + 2 + 3
    return pl.pallas_call(
        functools.partial(middle_kernel, n_head),
        out_shape=[jax.ShapeDtypeStruct(*out) for out in outs],
        in_specs=[ANY] * 9,
        out_specs=[ANY] * len(outs),
        scratch_shapes=[pltpu.VMEM(*b) for b in buffers]
        + [
            pltpu.SemaphoreType.DMA((n_sems,)),
            pltpu.SemaphoreType.DMA((n_sems,)),
            pltpu.SemaphoreType.DMA((64,)),
        ],
        compiler_params=pltpu.CompilerParams(
            collective_id=1, has_side_effects=True, vmem_limit_bytes=63 << 20
        ),
        name="middle",
    )(wf, nm, og, hidden, wo, pre, query, attn, scale)


class Share:
    def __init__(self, place, copies, view, base):
        self.place, self.copies, self.view, self.base = place, copies, view, base

    def pass_on(self, q, half, at, device):
        part = self.view(0, q, half)
        self.copies.send(part, part, self.base + at, self.base + at, device)

    def begin(self):
        self.pass_on(0, None, 0, self.place.by_x)
        self.pass_on(0, None, 1, self.place.by_y)
        self.pass_on(0, None, 4, self.place.across)

    def spread(self):
        place, copies, at = self.place, self.copies, self.base
        copies.receive(self.view(0, 1, None), at, place.by_x)
        self.pass_on(1, 0, 2, place.by_y)
        copies.receive(self.view(0, 2, None), at + 1, place.by_y)
        self.pass_on(2, 1, 3, place.by_x)
        self.pass_on(1, None, 5, place.across)
        self.pass_on(2, None, 6, place.across)

    def complete(self):
        place, copies, at = self.place, self.copies, self.base
        copies.receive(self.view(0, 3, 0), at + 2, place.by_y)
        copies.receive(self.view(0, 3, 1), at + 3, place.by_x)
        self.pass_on(3, None, 7, place.across)

    def other_side(self):
        for q in range(4):
            self.copies.receive(self.view(1, q, None), self.base + 4 + q, self.place.across)


PER_SHARE = 8


def last_kernel(
    n_head,
    late,
    feed_piece,
    nin,
    gate_pre,
    gated,
    branch,
    query,
    keys,
    values,
    grad_attn,
    carry,
    fresh,
    pre,
    cosines,
    sines,
    wa,
    hidden_grad,
    block,
    tokens,
    input_ref,
    block_ref,
    feed_ref,
    attn_ref,
    rates_both,
    ga_ref,
    a_far_x,
    a_far_y,
    a_near_x,
    a_near_y,
    a_high,
    g_far_x,
    g_far_y,
    g_near_x,
    g_near_y,
    g_high,
    late_ref,
    pending_ref,
    message_ref,
    nin_ref,
    gate_ref,
    gated_ref,
    branch_ref,
    q_ref,
    k_ref,
    v_ref,
    grad_attn_ref,
    carry_ref,
    fresh_ref,
    qk_pre_ref,
    cos_ref,
    sin_ref,
    pre_ref,
    wa_ref,
    x_ref,
    grad_ref,
    send_ref,
    got_ref,
    rates_ref,
    rates_high,
    rates_sum,
    rates_got,
    sends,
    receives,
    locals_,
):
    rows, width = tokens.shape
    quarter = width // 4
    units = feed_piece.shape[1]
    spans = rows // SPAN
    tiles = 2 * spans
    last = n_head - 1
    three = 3 * HEAD_DIM
    place = Place(n_head)
    place.greet()
    z, core = place.z, place.core
    copies = Copies(sends, receives, locals_)
    order = (2, 1, 3, 0)
    sides = (core, 1 - core)

    own_block = pl.ds(pl.multiple_of(place.plane * quarter, quarter), quarter)
    load_feed = copies.move(feed_piece, feed_ref.at[sides[0], :, :, own_block])
    load_late = copies.move(late, late_ref)
    load_first = [copies.move(nin, nin_ref), copies.move(gate_pre, gate_ref)]
    load_second = [copies.move(gated, gated_ref), copies.move(branch, branch_ref)]
    load_back = [
        copies.move(src, dst)
        for src, dst in (
            (query, q_ref),
            (keys, k_ref),
            (values, v_ref),
            (grad_attn, grad_attn_ref),
            (carry, carry_ref),
        )
    ]
    for seq in range(2):
        for slot in range(n_head):
            load_back.append(copies.move(fresh.at[slot, seq * spans], fresh_ref.at[slot, seq]))

    def slot_load(slot, turn):
        return [
            copies.move(pre.at[slot, :, pl.ds(0, 2 * HEAD_DIM)], qk_pre_ref.at[turn]),
            copies.move(cosines.at[slot], cos_ref.at[turn]),
            copies.move(sines.at[slot], sin_ref.at[turn]),
        ]

    slot_loads = [slot_load(slot, turn) for turn, slot in enumerate(order[:2])]
    late_loads = [
        copies.move(wa, wa_ref),
        copies.move(hidden_grad, grad_ref),
        copies.move(block, block_ref),
    ]
    for q in range(4):
        far = pl.ds(pl.multiple_of(place.at[q] * quarter, quarter), quarter)
        late_loads.append(copies.move(tokens.at[:, far], x_ref.at[:, pl.ds(q * quarter, quarter)]))
    place.meet()

    def tile(i):
        return pl.ds(pl.multiple_of(i * SPAN, SPAN), SPAN)

    def dot_last(left, right):
        return lax.dot_general(left, right, (((1,), (1,)), ((), ())), preferred_element_type=F32)

    def dot_first(left, right):
        return lax.dot_general(left, right, (((0,), (0,)), ((), ())), preferred_element_type=F32)

    def part(start, half, size):
        if half is None:
            return pl.ds(start, size)
        return pl.ds(start + half * (size // 2), size // 2)

    def start_of(q):
        return pl.multiple_of(place.at[q] * quarter, quarter)

    def feed_view(side, q, half):
        return feed_ref.at[sides[side], :, part(0, half, units), pl.ds(start_of(q), quarter)]

    def lanes_view(lanes, side, q, half):
        at = part(0, half, quarter)
        start = pl.multiple_of(start_of(q) + at.start, quarter // 2)
        return attn_ref.at[sides[side], pl.ds(start, at.size), lanes]

    def ga_view(lanes, slot, q, half):
        return ga_ref.at[slot, part(q * quarter, half, quarter), lanes]

    gate_lanes, rest_lanes = pl.ds(three, 2 * HEAD_DIM), pl.ds(0, three)
    weight_lanes = pl.ds(three, HEAD_DIM)
    of_gate = functools.partial(ga_view, gate_lanes)
    of_rest = functools.partial(ga_view, rest_lanes)
    gate = Scatter(place, copies, of_gate, g_far_x, g_far_y, g_near_x, g_near_y, g_high, 0)
    base = PER_SCATTER
    rest = Scatter(place, copies, of_rest, a_far_x, a_far_y, a_near_x, a_near_y, a_high, base)
    base += PER_SCATTER
    to_gate = functools.partial(lanes_view, gate_lanes)
    to_rest = functools.partial(lanes_view, rest_lanes)
    shares = []
    for view in (feed_view, to_gate, to_rest):
        shares.append(Share(place, copies, view, base))
        base += PER_SHARE
    feed_share, gate_share, rest_share = shares

    load_feed.wait()
    feed_share.begin()

    n_chain = 2 * n_head
    chain_base = base
    base += n_chain

    def chain_at(index):
        group, seq = lax.div(index, 2), lax.rem(index, 2)
        return lax.rem(group - z + n_head, n_head), seq, decay_of(2 * group + core)

    def chain_copy(index, slot, seq):
        return pltpu.make_async_remote_copy(
            src_ref=message_ref.at[slot, seq],
            dst_ref=pending_ref.at[lax.rem(slot + 1, n_head), seq],
            send_sem=sends.at[chain_base + index],
            recv_sem=receives.at[chain_base + index],
            device_id=place.down,
            device_id_type=MESH,
        )

    def hand_on(index):
        slot, seq, decay = chain_at(index)
        total = jnp.exp(-decay * rows) * pending_ref[slot, seq].astype(F32)
        for n in range(spans):
            total += jnp.exp(-decay * (n * SPAN)) * late_ref[slot, seq * spans + n]
        message_ref[slot, seq] = total.astype(BF)
        chain_copy(index, slot, seq).start()

    def take(index):
        slot, seq, _ = chain_at(index)
        copies.receive(pending_ref.at[slot, seq], chain_base + index, place.up)

    load_late.wait()

    @pl.when(z == last)
    def _():
        pending_ref[...] = jnp.zeros_like(pending_ref)
        pl.loop(0, n_chain)(hand_on)

    for load in load_first:
        load.wait()

    for load in load_second:
        load.wait()

    def gate_gradient(at):
        grads = dot_first(nin_ref[:, at], gate_ref[...]).astype(BF)
        outs = dot_first(branch_ref[:, at], gated_ref[...]).astype(BF)
        for slot in range(n_head):
            lanes = slice(slot * HEAD_DIM, (slot + 1) * HEAD_DIM)
            ga_ref[slot, at, pl.ds(three, HEAD_DIM)] = grads[:, lanes]
            ga_ref[slot, at, pl.ds(three + HEAD_DIM, HEAD_DIM)] = outs[:, lanes]

    gate_gradient(pl.ds(3 * quarter, quarter))
    for slot in order:
        gate.begin(slot)
    pl.loop(0, 3)(lambda q: gate_gradient(tile(q)))

    @pl.when(jnp.logical_and(z > 0, z < last))
    def _():
        @pl.loop(0, n_chain)
        def _(index):
            take(index)
            hand_on(index)

    for slot in order:
        gate.middle(slot)
    for load in load_back:
        load.wait()

    @pl.when(z == 0)
    def _():
        pl.loop(0, n_chain)(take)

    offsets = iota((SPAN, SPAN), 0) - iota((SPAN, SPAN), 1)

    def back_slot(slot, turn):
        decay = decay_of(2 * lax.rem(z + slot, n_head) + core)
        mask = jnp.where(offsets >= 0.0, jnp.exp(-decay * jnp.maximum(offsets, 0.0)), 0.0)
        places = iota((SPAN, 1), 0)
        early = jnp.exp(-decay * (places + 1.0))
        late_decay = jnp.exp(-decay * (SPAN - 1.0 - places))
        span_decay = jnp.exp(-decay * SPAN)
        rates_ref[slot] = jnp.zeros((8, HEAD_DIM), F32)

        @pl.loop(0, 2)
        def _(seq):
            for n in range(spans):
                at, here = tile(seq * spans + n), pl.ds(n * SPAN, SPAN)
                state = carry_ref[slot, seq].astype(F32)
                if n == 1:
                    state = span_decay * state + fresh_ref[slot, seq]
                later = pending_ref[slot, seq].astype(F32)
                if n == 0:
                    later = span_decay * later + late_ref[slot, seq * spans + 1]
                q, k, v = q_ref[slot, at, :], k_ref[slot, at, :], v_ref[slot, at, :]
                grad = grad_attn_ref[slot, at, :]
                weights = (dot_last(q, k) * mask).astype(BF)
                scores = (dot_last(grad, v) * mask).astype(BF)
                state_high, state_low = split(state)
                grad_query = dot(scores, k)
                grad_query += early * (dot_last(grad, state_high) + dot_last(grad, state_low))
                later_high, later_low = split(later)
                grad_keys = dot_first(scores, q)
                grad_keys += late_decay * (dot_last(v, later_high) + dot_last(v, later_low))
                both = dot(k, jnp.concatenate([later_high, later_low], axis=1))
                grad_values = dot_first(weights, grad)
                grad_values += late_decay * (both[:, :HEAD_DIM] + both[:, HEAD_DIM:])
                pre_ref[slot, at, pl.ds(2 * HEAD_DIM, HEAD_DIM)] = grad_values.astype(BF)
                cosine, sine = cos_ref[turn, here, :], sin_ref[turn, here, :]
                angles = jnp.zeros((SPAN, HEAD_DIM), F32)
                for i, turned in enumerate((grad_query, grad_keys)):
                    lanes = pl.ds(i * HEAD_DIM, HEAD_DIM)
                    value = qk_pre_ref[turn, at, lanes]
                    by_cos, by_sin = turned[:, :HEAD_DIM], turned[:, HEAD_DIM:]
                    sigmoid = 1.0 / (1.0 + jnp.exp(-value))
                    act = by_cos * cosine + by_sin * sine
                    angles += value * sigmoid * (by_sin * cosine - by_cos * sine)
                    act = act * sigmoid * (1.0 + value * (1.0 - sigmoid))
                    pre_ref[slot, at, lanes] = act.astype(BF)
                steps = (z * rows + n * SPAN).astype(F32) + places
                rates_ref[slot, pl.ds(0, 1), :] += jnp.sum(steps * angles, axis=0, keepdims=True)

    def rest_gradient(slot, at):
        ga_ref[slot, at, rest_lanes] = dot_first(nin_ref[:, at], pre_ref[slot]).astype(BF)

    rates_base = base
    base += n_head + 3
    for i, slot in enumerate(order):
        for load in slot_loads[i]:
            load.wait()
        back_slot(slot, i % 2)
        if i + 2 < n_head:
            slot_loads.append(slot_load(order[i + 2], i % 2))
        if slot:
            at = rates_base + slot
            copies.send(rates_ref.at[slot], rates_high.at[slot - 1], at, at, place.above(slot))
        rest_gradient(slot, pl.ds(3 * quarter, quarter))
        rest.begin(slot)
        pl.loop(0, 3)(lambda q: rest_gradient(slot, tile(q)))
    total = rates_ref[0]
    for slot in range(1, n_head):
        copies.receive(rates_high.at[slot - 1], rates_base + slot, place.up)
        total += rates_high[slot - 1]
    rates_sum[0] = total
    rates_base += n_head
    copies.send(rates_sum.at[0], rates_got.at[0], rates_base, rates_base, place.by_x)
    for slot in order:
        gate.end(slot)
    copies.receive(rates_got.at[0], rates_base, place.by_x)
    rates_sum[1] = total + rates_got[0]
    copies.send(rates_sum.at[1], rates_got.at[1], rates_base + 1, rates_base + 1, place.by_y)
    rest.middle(order[0])
    rest.middle(order[1])
    for load in late_loads:
        load.wait()

    def grad_in(at):
        total = dot_last(gate_ref[at, :], wa_gate())
        for slot in range(n_head):
            total += dot_last(pre_ref[slot, at, :], wa_ref[slot, :, rest_lanes])
        return total

    def wa_gate():
        return jnp.concatenate([wa_ref[slot, :, weight_lanes] for slot in range(n_head)], axis=1)

    @pl.loop(0, spans)
    def _(i):
        send_ref[tile(i), :] = grad_in(tile(spans + i)).astype(BF)

    copies.send(send_ref, got_ref, base, base, place.across)
    rest.middle(order[2])

    rest.middle(order[3])
    feed_share.spread()
    rest.end(order[0])
    copies.receive(got_ref, base, place.across)

    @pl.loop(0, spans)
    def _(i):
        at = tile(i)
        values = x_ref[at, :].astype(F32)
        norm = lax.rsqrt(jnp.mean(values * values, axis=-1, keepdims=True) + EPSILON)
        normed = values * norm
        grad = grad_in(at) + got_ref[at, :].astype(F32)
        mean = jnp.mean(grad * normed, axis=-1, keepdims=True)
        grad_ref[at, :] += norm * (grad - normed * mean)

    for q in range(4):
        src = grad_ref.at[:, pl.ds(q * quarter, quarter)]
        copies.move(src, input_ref.at[:, pl.ds(start_of(q), quarter)], later=True)
    gate.total(to_gate(0, 0, None))
    gate_share.begin()
    rest.end(order[1])
    rest.end(order[2])
    rest.end(order[3])
    rest.total(to_rest(0, 0, None))
    rest_share.begin()
    copies.receive(rates_got.at[1], rates_base + 1, place.by_y)
    rates_both[sides[0]] = rates_sum[1] + rates_got[1]
    mine = rates_both.at[sides[0]]
    copies.send(mine, mine, rates_base + 2, rates_base + 2, place.across)
    feed_share.complete()
    gate_share.spread()
    copies.receive(rates_both.at[sides[1]], rates_base + 2, place.across)
    feed_share.other_side()
    rest_share.spread()
    gate_share.complete()
    rest_share.complete()
    for share in shares[1:]:
        share.other_side()

    @pl.when(z > 0)
    def _():
        @pl.loop(0, n_chain)
        def _(index):
            slot, seq, _ = chain_at(index)
            chain_copy(index, slot, seq).wait_send()

    copies.finish()


def last(
    n_head,
    late,
    feed_piece,
    nin,
    gate_pre,
    gated,
    branch,
    query,
    keys,
    values,
    grad_attn,
    carry,
    fresh,
    pre,
    cosines,
    sines,
    wa,
    hidden_grad,
    block,
    tokens,
):
    rows, width = tokens.shape
    _, units, quarter = feed_piece.shape
    tall = 2 * rows

    def scatter_buffers(shape, halved):
        half = tuple(n // 2 if i == halved else n for i, n in enumerate(shape))
        return [
            ((n_head,) + half, BF),
            ((n_head,) + half, BF),
            ((n_head,) + shape, BF),
            ((n_head,) + shape, BF),
            ((n_head - 1,) + shape, BF),
        ]

    outs = [
        ((rows, width), F32),
        ((rows, width), BF),
        ((2, 3, units, width), BF),
        ((2, width, 5 * HEAD_DIM), BF),
        ((2, 8, HEAD_DIM), F32),
    ]
    chain = ((n_head, 2, 2 * HEAD_DIM, HEAD_DIM), BF)
    buffers = [
        ((n_head, width, 5 * HEAD_DIM), BF),
        *scatter_buffers((quarter, 3 * HEAD_DIM), 0),
        *scatter_buffers((quarter, 2 * HEAD_DIM), 0),
        (late.shape, F32),
        chain,
        chain,
        (nin.shape, BF),
        (gate_pre.shape, BF),
        (gated.shape, BF),
        (branch.shape, BF),
        (query.shape, BF),
        (keys.shape, BF),
        (values.shape, BF),
        (grad_attn.shape, BF),
        chain,
        (chain[0], F32),
        ((2, tall, 2 * HEAD_DIM), F32),
        ((2, rows, HEAD_DIM), F32),
        ((2, rows, HEAD_DIM), F32),
        ((n_head, tall, 3 * HEAD_DIM), BF),
        (wa.shape, BF),
        ((rows, width), BF),
        ((rows, width), F32),
        ((rows, width), BF),
        ((rows, width), BF),
        ((n_head, 8, HEAD_DIM), F32),
        ((n_head - 1, 8, HEAD_DIM), F32),
        ((2, 8, HEAD_DIM), F32),
        ((2, 8, HEAD_DIM), F32),
    ]
    n_sems = 2 * PER_SCATTER + 3 * PER_SHARE + 2 * n_head + n_head + 3 + 1
    arrays = [late, feed_piece, nin, gate_pre, gated, branch, query, keys, values, grad_attn]
    arrays += [carry, fresh, pre, cosines, sines, wa, hidden_grad, block, tokens]
    arrays = [pltpu.with_memory_space_constraint(array, pltpu.HBM) for array in arrays]
    return pl.pallas_call(
        functools.partial(last_kernel, n_head),
        out_shape=[pltpu.VMEM(*out) for out in outs],
        in_specs=[ANY] * len(arrays),
        out_specs=[IN_VMEM] * len(outs),
        scratch_shapes=[pltpu.VMEM(*b) for b in buffers]
        + [
            pltpu.SemaphoreType.DMA((n_sems,)),
            pltpu.SemaphoreType.DMA((n_sems,)),
            pltpu.SemaphoreType.DMA((64,)),
        ],
        compiler_params=pltpu.CompilerParams(
            collective_id=2, has_side_effects=True, vmem_limit_bytes=52 << 20
        ),
        name="last",
    )(*arrays)


def finish_kernel(grad, block, feed, attn, rates, *refs):
    outs, results, locals_ = refs[:11], refs[11:-1], refs[-1]
    copies = Copies(None, None, locals_)
    (block_out, grad_out, q_out, k_out, v_out, g_out, o_out, rates_out, l_out, r_out, d_out) = outs
    units = feed.shape[2]
    copies.move(grad, grad_out, later=True)
    copies.move(block, block_out, later=True)
    l_ref, r_ref, d_ref, q_ref, k_ref, v_ref, g_ref, o_ref, rates_ref = results
    for side in range(2):
        rates_ref[:, pl.ds(side * HEAD_DIM, HEAD_DIM)] = rates[side, pl.ds(0, 1), :]
    copies.move(rates_ref, rates_out, later=True)
    for i, (ref, out) in enumerate(((l_ref, l_out), (r_ref, r_out), (d_ref, d_out))):
        for side in range(2):
            at = pl.ds(side * units, units)
            ref[at, :] = feed[side, i].astype(F32)
            copies.move(ref.at[at], out.at[at], later=True)
    for i, (ref, out) in enumerate(((q_ref, q_out), (k_ref, k_out), (v_ref, v_out), (g_ref, g_out))):
        lanes = pl.ds(i * HEAD_DIM, HEAD_DIM)
        for side in range(2):
            ref[:, pl.ds(side * HEAD_DIM, HEAD_DIM)] = attn[side, :, lanes].astype(F32)
        copies.move(ref, out, later=True)
    for side in range(2):
        lanes = pl.ds(4 * HEAD_DIM, HEAD_DIM)
        o_ref[pl.ds(side * HEAD_DIM, HEAD_DIM), :] = attn[side, :, lanes].T.astype(F32)
    copies.move(o_ref, o_out, later=True)
    copies.finish()


def finish(grad, block, feed, attn, rates):
    _, _, units, width = feed.shape
    projection = ((width, 2 * HEAD_DIM), F32)
    back = ((2 * HEAD_DIM, width), F32)
    results = [((2 * units, width), F32)] * 3 + [projection] * 4 + [back]
    results.append(((1, 2 * HEAD_DIM), F32))
    outs = [(block.shape, BF), (grad.shape, F32)] + results[3:] + results[:3]
    return pl.pallas_call(
        finish_kernel,
        out_shape=[jax.ShapeDtypeStruct(*out) for out in outs],
        in_specs=[IN_VMEM] * 5,
        out_specs=[ANY] * len(outs),
        scratch_shapes=[pltpu.VMEM(*b) for b in results] + [pltpu.SemaphoreType.DMA((48,))],
        compiler_params=pltpu.CompilerParams(vmem_limit_bytes=24 << 20),
        name="finish",
    )(grad, block, feed, attn, rates)


def make(n_dp, n_head):
    def on_device(
        tokens,
        attn_query,
        attn_key,
        attn_value,
        attn_gate,
        attn_out,
        rotation_rates,
        ffn_left,
        ffn_right,
        ffn_down,
        out_grad,
    ):
        rates_in = rotation_rates.reshape(1, -1)
        (
            attn_weights,
            out_w,
            ffn_all,
            gathered_in,
            pre,
            query,
            keys,
            values,
            attn,
            cosines,
            sines,
            fresh,
            carry,
            scale_attn,
            gated,
            hidden,
            gathered_mid,
            grad_rows,
        ) = forward(
            n_head,
            tokens,
            out_grad,
            attn_query,
            attn_key,
            attn_value,
            attn_gate,
            attn_out,
            ffn_left.T,
            ffn_right.T,
            ffn_down,
            rates_in,
        )
        feed_piece, block_out, grad_hidden, branch_rows, gate_pre, grad_attn, late = middle(
            n_head,
            ffn_all,
            gathered_mid,
            grad_rows,
            hidden,
            out_w,
            pre,
            query,
            attn,
            scale_attn,
        )
        grads = last(
            n_head,
            late,
            feed_piece,
            gathered_in,
            gate_pre,
            gated,
            branch_rows,
            query,
            keys,
            values,
            grad_attn,
            carry,
            fresh,
            pre,
            cosines,
            sines,
            attn_weights,
            grad_hidden,
            block_out,
            tokens,
        )
        results = finish(*grads)
        rates_grad, left_grad, right_grad = results[7][0], results[8].T, results[9].T
        results = list(results[:7]) + [rates_grad, left_grad, right_grad, results[10]]
        if n_dp > 8:
            groups = [[i + 8 * j for j in range(n_dp // 8)] for i in range(8)]
            grads = [lax.psum(grad, "dp", axis_index_groups=groups) for grad in results[2:]]
            results = results[:2] + grads
        return tuple(results)

    return on_device


def solution(mesh):
    weights = (P(None, "head"),) * 4 + (P("head", None), P("head")) + (P(None, "head"),) * 2
    weights = weights + (P("head", None),)
    rows = P(("dp", "head"), None)
    return jax.shard_map(
        make(mesh.shape["dp"], mesh.shape["head"]),
        mesh=mesh,
        in_specs=(rows,) + weights + (rows,),
        out_specs=(rows, rows) + weights,
        check_vma=False,
    )
```

```python
import functools

import jax
import jax.numpy as jnp
from jax import lax
from jax.experimental import pallas as pl
from jax.experimental.pallas import tpu as pltpu
from jax.sharding import PartitionSpec as P

HEADS = 8
HEAD_DIM = 128
SPAN = 256
EPSILON = 1e-06
BF = jnp.bfloat16
F32 = jnp.float32


MESH = pl.DeviceIdType.MESH
ANY = pl.BlockSpec(memory_space=pl.ANY)
IN_VMEM = pl.BlockSpec(memory_space=pltpu.VMEM)


def split(value):
    high = value.astype(BF)
    return high, (value - high.astype(F32)).astype(BF)


class Place:
    def __init__(self, n_head):
        self.n_head = n_head
        dp = lax.axis_index("dp")
        self.z = lax.axis_index("head")
        self.core = lax.rem(dp, 2)
        x = lax.rem(lax.div(dp, 2), 2)
        y = lax.rem(lax.div(dp, 4), 2)
        self.plane = x + 2 * y
        self.at = [self.plane, self.plane + 1 - 2 * x, self.plane + 2 - 4 * y, 3 - self.plane]
        self.across = {"dp": dp + 1 - 2 * self.core}
        self.by_x = {"dp": dp + 2 - 4 * x}
        self.by_y = {"dp": dp + 4 - 8 * y}
        self.up = {"head": lax.rem(self.z + 1, n_head)}
        self.down = {"head": lax.rem(self.z + n_head - 1, n_head)}

    def above(self, step):
        return {"head": lax.rem(self.z + step, self.n_head)}

    def below(self, step):
        return {"head": lax.rem(self.z + self.n_head - step, self.n_head)}

    def greet(self):
        others = [self.across, self.by_x, self.by_y]
        others += [self.below(step) for step in range(1, self.n_head)]
        for other in others:
            barrier = pltpu.get_barrier_semaphore()
            pl.semaphore_signal(barrier, inc=1, device_id=other, device_id_type=MESH)

    def meet(self):
        pl.semaphore_wait(pltpu.get_barrier_semaphore(), self.n_head + 2)


class Copies:
    def __init__(self, sends, receives, locals_):
        self.sends, self.receives, self.locals = sends, receives, locals_
        self.pending = []
        self.started = {}
        self.n_local = 0

    def send(self, src, dst, out, into, device, when=None):
        copy = pltpu.make_async_remote_copy(
            src_ref=src,
            dst_ref=dst,
            send_sem=self.sends.at[out],
            recv_sem=self.receives.at[into],
            device_id=device,
            device_id_type=MESH,
        )
        if when is None:
            copy.start()
            self.pending.append(copy.wait_send)
            if isinstance(out, int):
                self.started[out] = copy.wait_send
        else:
            pl.when(when)(copy.start)
            self.pending.append(lambda: pl.when(when)(copy.wait_send))

    def receive(self, dst, into, device):
        pltpu.make_async_remote_copy(
            src_ref=dst,
            dst_ref=dst,
            send_sem=self.sends.at[0],
            recv_sem=self.receives.at[into],
            device_id=device,
            device_id_type=MESH,
        ).wait_recv()

    def move(self, src, dst, later=False):
        copy = pltpu.make_async_copy(src, dst, self.locals.at[self.n_local])
        self.n_local += 1
        copy.start()
        if later:
            self.pending.append(copy.wait)
        return copy

    def sent(self, out):
        wait = self.started.pop(out)
        self.pending.remove(wait)
        wait()

    def finish(self):
        for wait in self.pending:
            wait()


class Gather:
    def __init__(self, place, copies, view, base, late=None):
        self.place, self.copies, self.view, self.base = place, copies, view, base
        self.late = late

    def begin(self):
        place, z = self.place, self.place.z
        own = self.view(0, 0, None)
        last = place.n_head - 1
        self.copies.send(
            own, self.view(last, 0, None), self.base, self.base + last, place.up, when=z < last
        )
        self.copies.send(own, self.view(1, 0, None), self.base + 1, self.base + 1, place.down, when=z > 0)

    def arrived(self, slot, when=True):
        place, copies, z, base = self.place, self.copies, self.place.z, self.base
        last = place.n_head - 1
        if when is True:
            copies.receive(self.view(slot, 0, None), base + slot, place.up)
        else:
            pl.when(when)(lambda: copies.receive(self.view(slot, 0, None), base + slot, place.up))
        from_up = z + slot <= last
        piece = self.view(slot, 0, None)
        down = jnp.logical_and(jnp.logical_and(from_up, z > 0), when)
        up = jnp.logical_and(jnp.logical_not(from_up), z < last)
        up = jnp.logical_and(up, when)
        always = None if when is True else when
        after = jnp.minimum(slot + 1, last)
        before = jnp.maximum(slot - 1, 1)
        copies.send(piece, self.view(after, 0, None), base + 1 + slot, base + after, place.down, when=down)
        copies.send(piece, self.view(before, 0, None), base + 1 + slot, base + before, place.up, when=up)
        at = base + 4 * slot + 4
        copies.send(piece, self.view(slot, 1, None), at, at, place.by_x, when=always)
        copies.send(piece, self.view(slot, 2, None), at + 1, at + 1, place.by_y, when=always)

    def spread(self, slot):
        place, copies = self.place, self.copies
        at = self.base + 4 * slot + 4
        now = None if self.late is None else slot != self.late
        low, high = self.view(slot, 3, 0), self.view(slot, 3, 1)
        copies.receive(self.view(slot, 1, None), at, place.by_x)
        copies.send(self.view(slot, 1, 0), low, at + 2, at + 2, place.by_y, when=now)
        copies.receive(self.view(slot, 2, None), at + 1, place.by_y)
        copies.send(self.view(slot, 2, 1), high, at + 3, at + 3, place.by_x, when=now)

    def complete(self, slot):
        place, copies = self.place, self.copies
        at = self.base + 4 * slot + 4

        def receive():
            copies.receive(self.view(slot, 3, 0), at + 2, place.by_y)
            copies.receive(self.view(slot, 3, 1), at + 3, place.by_x)

        if self.late is None:
            receive()
        else:
            pl.when(slot != self.late)(receive)


PER_GATHER = 24


def forward_kernel(
    n_head,
    tokens,
    out_grad,
    wq,
    wk,
    wv,
    wg,
    wo,
    ffn_left,
    ffn_right,
    ffn_down,
    rates,
    wa_out,
    wo_out,
    wf_out,
    nin_out,
    pre_out,
    q_out,
    k_out,
    v_out,
    attn_out,
    cos_out,
    sin_out,
    fresh_out,
    carry_out,
    scale_out,
    gated_out,
    hidden_out,
    nm_out,
    og_out,
    wa_ref,
    wo_ref,
    wf_ref,
    x_ref,
    nin_ref,
    pre_ref,
    q_ref,
    k_ref,
    v_ref,
    attn_ref,
    cos_ref,
    sin_ref,
    fresh_ref,
    carry_ref,
    message_ref,
    squares_ref,
    other_squares_ref,
    gated_ref,
    branch_ref,
    other_branch_ref,
    hidden_ref,
    nm_ref,
    rates_ref,
    og_ref,
    sends,
    receives,
    locals_,
):
    rows, width = tokens.shape
    quarter = width // 4
    units = ffn_down.shape[0] // 2
    tiles = 2 * rows // SPAN
    place = Place(n_head)
    z, core = place.z, place.core
    last = n_head - 1
    place.greet()
    copies = Copies(sends, receives, locals_)

    def columns(start, size):
        return pl.ds(pl.multiple_of(start, size), size)

    def own_weights(q):
        far = columns(place.at[q] * quarter, quarter)
        near = pl.ds(q * quarter, quarter)
        loads = []
        for i, w in enumerate((wq, wk, wv, wg)):
            src = w.at[far, columns(core * HEAD_DIM, HEAD_DIM)]
            loads.append(copies.move(src, wa_ref.at[0, near, pl.ds(i * HEAD_DIM, HEAD_DIM)]))
        src = wo.at[columns(core * HEAD_DIM, HEAD_DIM), far]
        loads.append(copies.move(src, wo_ref.at[pl.ds(0, HEAD_DIM), near]))
        for i, w in enumerate((ffn_left, ffn_right, ffn_down)):
            src = w.at[pl.ds(pl.multiple_of(core * units, 16), units), far]
            loads.append(copies.move(src, wf_ref.at[i, pl.ds(0, units), near]))
        return loads

    own_loads = [own_weights(0)]
    token_loads = [
        copies.move(
            tokens.at[:, columns(place.at[q] * quarter, quarter)],
            x_ref.at[:, pl.ds(q * quarter, quarter)],
        )
        for q in range(4)
    ]
    place.meet()

    def half_rows(half, size):
        return pl.ds(0, size) if half is None else pl.ds(half * (size // 2), size // 2)

    def wa_view(part, slot, q, half):
        at = half_rows(half, quarter)
        lanes = pl.ds(part * 2 * HEAD_DIM, 2 * HEAD_DIM)
        return wa_ref.at[slot, pl.ds(q * quarter + at.start, at.size), lanes]

    def wo_view(slot, q, half):
        at = half_rows(half, HEAD_DIM)
        return wo_ref.at[
            pl.ds(pl.multiple_of(slot * HEAD_DIM + at.start, HEAD_DIM // 2), at.size),
            pl.ds(q * quarter, quarter),
        ]

    def wf_view(slot, q, half):
        at = half_rows(half, units)
        return wf_ref.at[
            :,
            pl.ds(pl.multiple_of(slot * units + at.start, 16), at.size),
            pl.ds(q * quarter, quarter),
        ]

    attn_all = [
        Gather(place, copies, functools.partial(wa_view, part), part * PER_GATHER)
        for part in range(2)
    ]
    attn_all.append(Gather(place, copies, wo_view, 2 * PER_GATHER))
    feed = Gather(place, copies, wf_view, 3 * PER_GATHER, late=last)
    base = 4 * PER_GATHER
    for step in range(1, n_head):
        copies.send(rates, rates_ref.at[step], base + step, base + step, place.below(step))
    for loads, part in zip((own_loads[0][:2], own_loads[0][2:4], own_loads[0][4:5]), attn_all):
        for load in loads:
            load.wait()
        part.begin()
    grad_loads = [
        copies.move(
            out_grad.at[:, columns(place.at[q] * quarter, quarter)],
            og_ref.at[pl.ds(0, rows), pl.ds(q * quarter, quarter)],
        )
        for q in range(4)
    ]
    own_loads += [own_weights(q) for q in range(1, 4)]
    rates_ref[0] = rates[...]

    for load in token_loads:
        load.wait()

    def norm_rows(values):
        mean = jnp.mean(values * values, axis=-1, keepdims=True)
        return values * lax.rsqrt(mean + EPSILON)

    @pl.loop(0, rows // 128)
    def _(i):
        at = pl.ds(pl.multiple_of(i * 128, 128), 128)
        nin_ref[at, :] = norm_rows(x_ref[at, :].astype(F32)).astype(BF)

    base += 5
    nin_other = nin_ref.at[pl.ds(rows, rows)]
    copies.send(nin_ref.at[pl.ds(0, rows)], nin_other, base, base, place.across)
    inner = jnp.logical_and(z > 0, z < last)
    first = 1 + 2 * lax.div(z, last)
    second = 2 + lax.rem(lax.div(z + 1, 2), 2)
    third = 6 - first - second
    for part in attn_all:
        part.arrived(first)
        part.arrived(second, inner)
    for load in grad_loads:
        load.wait()
    og_other = og_ref.at[pl.ds(rows, rows)]
    og_base = base - 1
    copies.send(og_ref.at[pl.ds(0, rows)], og_other, og_base, og_base, place.across)
    for q, loads in enumerate(own_loads):
        for load in loads[5:] if q == 0 else loads:
            load.wait()
    for step in range(1, n_head):
        copies.receive(rates_ref.at[step], base - 5 + step, place.up)
    copies.receive(nin_other, base, place.across)
    copies.move(nin_ref, nin_out, later=True)
    own_rows = pl.ds(0, units)
    copies.move(wf_ref.at[:, own_rows], wf_out.at[:, own_rows], later=True)

    def decay_of(head):
        exponent = jnp.full((1, 1), -8.0 / HEADS, F32) * (head + 1).astype(F32)
        return jnp.exp2(exponent)

    def tile(i):
        return pl.ds(pl.multiple_of(i * SPAN, SPAN), SPAN)

    def iota(shape, axis):
        return lax.broadcasted_iota(jnp.int32, shape, axis).astype(F32)

    def dot(left, right):
        return jnp.dot(left, right, preferred_element_type=F32)

    def slot_compute(slot):
        head = 2 * lax.rem(z + slot, n_head) + core
        decay = decay_of(head)
        rate = rates_ref[slot, :, columns(core * HEAD_DIM, HEAD_DIM)]
        coarse = (z * rows).astype(F32) + 32.0 * iota((rows // 32, HEAD_DIM), 0)
        coarse = coarse * rate
        fine = iota((32, HEAD_DIM), 0) * rate
        cos_a, sin_a = jnp.cos(coarse), jnp.sin(coarse)
        cos_b, sin_b = jnp.cos(fine), jnp.sin(fine)
        for a in range(rows // 32):
            cos_row, sin_row = cos_a[a : a + 1], sin_a[a : a + 1]
            cos_ref[slot, pl.ds(a * 32, 32), :] = cos_row * cos_b - sin_row * sin_b
            sin_ref[slot, pl.ds(a * 32, 32), :] = sin_row * cos_b + cos_row * sin_b
        offsets = iota((SPAN, SPAN), 0) - iota((SPAN, SPAN), 1)
        mask = jnp.where(offsets >= 0.0, jnp.exp(-decay * jnp.maximum(offsets, 0.0)), 0.0)
        late = jnp.exp(-decay * (SPAN - 1.0 - iota((SPAN, HEAD_DIM), 0)))

        @pl.loop(0, tiles)
        def _(i):
            at = tile(i)
            pre = dot(nin_ref[at, :], wa_ref[slot])
            pre_ref[slot, at, :] = pre
            here = tile(lax.rem(i, rows // SPAN))
            cosines, sines = cos_ref[slot, here, :], sin_ref[slot, here, :]

            def rotate(values):
                activated = values / (1.0 + jnp.exp(-values))
                turned = jnp.concatenate([activated * cosines, activated * sines], axis=1)
                return turned.astype(BF)

            query = rotate(pre[:, :HEAD_DIM])
            keys = rotate(pre[:, HEAD_DIM : 2 * HEAD_DIM])
            value = pre[:, 2 * HEAD_DIM : 3 * HEAD_DIM].astype(BF)
            q_ref[slot, at, :] = query
            k_ref[slot, at, :] = keys
            v_ref[slot, at, :] = value
            scores = lax.dot_general(
                query, keys, (((1,), (1,)), ((), ())), preferred_element_type=F32
            )
            weights = (scores * mask).astype(BF)
            attn_ref[slot, at, :] = dot(weights, value)
            high, low = split(value.astype(F32) * late)
            both = lax.dot_general(
                keys,
                jnp.concatenate([high, low], axis=1),
                (((0,), (0,)), ((), ())),
                preferred_element_type=F32,
            )
            fresh_ref[slot, i] = both[:, :HEAD_DIM] + both[:, HEAD_DIM:]

        for ref, out in (
            (wa_ref, wa_out),
            (pre_ref, pre_out),
            (q_ref, q_out),
            (k_ref, k_out),
            (v_ref, v_out),
            (cos_ref, cos_out),
            (sin_ref, sin_out),
            (fresh_ref, fresh_out),
        ):
            copies.move(ref.at[slot], out.at[slot], later=True)

    slot_compute(0)
    for part in attn_all:
        part.arrived(second, jnp.logical_not(inner))
    for part in attn_all:
        part.spread(first)
    for part in attn_all:
        part.arrived(third)
    feed.begin()
    for part in attn_all:
        part.spread(second)
    for part in attn_all[:2]:
        part.complete(first)
    slot_compute(first)
    for part in attn_all:
        part.spread(third)
    feed.arrived(first)
    for part in attn_all[:2]:
        part.complete(second)
    slot_compute(second)
    feed.arrived(second, inner)
    for part in attn_all[:2]:
        part.complete(third)
    slot_compute(third)
    base += 1
    chain_base = base
    n_chain = 2 * n_head

    def chain_at(index):
        group, seq = lax.div(index, 2), lax.rem(index, 2)
        return lax.rem(group - z + n_head, n_head), seq, decay_of(2 * group + core)

    def chain_copy(index, slot, seq):
        after = lax.rem(slot + n_head - 1, n_head)
        return pltpu.make_async_remote_copy(
            src_ref=message_ref.at[slot, seq],
            dst_ref=carry_ref.at[after, seq],
            send_sem=sends.at[chain_base + index],
            recv_sem=receives.at[chain_base + index],
            device_id=place.up,
            device_id_type=MESH,
        )

    def hand_on(index, slot, seq, decay):
        total = jnp.exp(-decay * rows) * carry_ref[slot, seq].astype(F32)
        for n in range(rows // SPAN):
            left = rows - (n + 1) * SPAN
            total += jnp.exp(-decay * left) * fresh_ref[slot, seq * (rows // SPAN) + n]
        message_ref[slot, seq] = total.astype(BF)
        chain_copy(index, slot, seq).start()

    @pl.when(z == 0)
    def _():
        @pl.loop(0, n_chain)
        def _(index):
            slot, seq, decay = chain_at(index)
            carry_ref[slot, seq] = jnp.zeros(carry_ref.shape[2:], BF)
            hand_on(index, slot, seq, decay)

    feed.arrived(second, jnp.logical_not(inner))
    feed.spread(first)
    feed.arrived(third)

    @pl.when(z > 0)
    def _():
        @pl.loop(0, n_chain)
        def _(index):
            slot, seq, decay = chain_at(index)
            copies.receive(carry_ref.at[slot, seq], chain_base + index, place.down)
            pl.when(z < last)(lambda: hand_on(index, slot, seq, decay))

    copies.move(carry_ref, carry_out, later=True)
    copies.receive(og_other, og_base, place.across)
    copies.move(og_ref, og_out, later=True)
    feed.spread(second)

    def feed_done(slot):
        feed.complete(slot)
        at = pl.ds(pl.multiple_of(slot * units, 16), units)
        copies.move(wf_ref.at[:, at], wf_out.at[:, at], later=True)

    def apply(seq):
        mine = pl.ds(seq * rows, rows)
        squares_ref[mine, :] = jnp.zeros((rows, HEAD_DIM), F32)

        @pl.loop(0, n_head)
        def _(slot):
            decay = decay_of(2 * lax.rem(z + slot, n_head) + core)
            early = jnp.exp(-decay * (iota((SPAN, HEAD_DIM), 0) + 1.0))
            state = carry_ref[slot, seq].astype(F32)
            for n in range(rows // SPAN):
                i = seq * (rows // SPAN) + n
                at = pl.ds(i * SPAN, SPAN)
                both = dot(q_ref[slot, at, :], jnp.concatenate(split(state), axis=1))
                attn = attn_ref[slot, at, :]
                attn += early * (both[:, :HEAD_DIM] + both[:, HEAD_DIM:])
                attn_ref[slot, at, :] = attn
                squares_ref[at, :] += jnp.sum(attn * attn, axis=-1, keepdims=True)
                if n + 1 < rows // SPAN:
                    state = jnp.exp(-decay * SPAN) * state + fresh_ref[slot, i]

    def gating(seq):
        for n in range(rows // SPAN):
            at = pl.ds(seq * rows + n * SPAN, SPAN)
            total = squares_ref[at, :] + other_squares_ref[at, :]
            scale = lax.rsqrt(total / width + EPSILON)
            other_squares_ref[at, :] = scale
            for slot in range(n_head):
                gate = pre_ref[slot, at, pl.ds(3 * HEAD_DIM, HEAD_DIM)]
                gated = (attn_ref[slot, at, :] * scale * gate).astype(BF)
                gated_ref[at, pl.ds(slot * HEAD_DIM, HEAD_DIM)] = gated

    base += n_chain
    own, other = pl.ds(0, rows), pl.ds(rows, rows)
    apply(1)
    copies.send(squares_ref.at[other], other_squares_ref.at[own], base, base, place.across)
    apply(0)
    copies.send(squares_ref.at[own], other_squares_ref.at[other], base + 1, base + 1, place.across)
    copies.move(attn_ref, attn_out, later=True)
    for slot in (first, second, third):
        attn_all[2].complete(slot)
    copies.receive(other_squares_ref.at[other], base + 1, place.across)
    gating(1)
    feed_done(first)
    base += 2
    for n in range(rows // SPAN):
        gated = gated_ref[pl.ds(rows + n * SPAN, SPAN), :]
        branch_ref[pl.ds(n * SPAN, SPAN), :] = dot(gated, wo_ref[...]).astype(BF)
    copies.send(branch_ref, other_branch_ref, base, base, place.across)
    copies.receive(other_squares_ref.at[own], base - 2, place.across)
    gating(0)
    copies.move(other_squares_ref, scale_out, later=True)
    copies.move(gated_ref, gated_out, later=True)
    copies.move(wo_ref, wo_out, later=True)
    feed.spread(third)
    feed_done(second)

    @pl.loop(0, rows // SPAN)
    def _(i):
        at = tile(i)
        hidden_ref[at, :] = x_ref[at, :].astype(F32) + dot(gated_ref[at, :], wo_ref[...])

    copies.receive(other_branch_ref, base, place.across)

    @pl.loop(0, rows // 128)
    def _(i):
        at = pl.ds(pl.multiple_of(i * 128, 128), 128)
        hidden = hidden_ref[at, :] + other_branch_ref[at, :].astype(F32)
        hidden_ref[at, :] = hidden
        nm_ref[at, :] = norm_rows(hidden).astype(BF)

    copies.send(nm_ref.at[own], nm_ref.at[other], base + 1, base + 1, place.across)
    copies.move(hidden_ref, hidden_out, later=True)
    feed_done(third)
    copies.receive(nm_ref.at[other], base + 1, place.across)
    copies.move(nm_ref, nm_out, later=True)

    @pl.when(z < last)
    def _():
        @pl.loop(0, n_chain)
        def _(index):
            slot, seq, _ = chain_at(index)
            chain_copy(index, slot, seq).wait_send()

    copies.finish()


def forward(n_head, tokens, out_grad, wq, wk, wv, wg, wo, ffn_left, ffn_right, ffn_down, rates):
    rows, width = tokens.shape
    units = ffn_down.shape[0] // 2
    tall = 2 * rows
    buffers = [
        ((n_head, width, 4 * HEAD_DIM), BF),
        ((n_head * HEAD_DIM, width), BF),
        ((3, n_head * units, width), BF),
        ((rows, width), BF),
        ((tall, width), BF),
        ((n_head, tall, 4 * HEAD_DIM), F32),
        ((n_head, tall, 2 * HEAD_DIM), BF),
        ((n_head, tall, 2 * HEAD_DIM), BF),
        ((n_head, tall, HEAD_DIM), BF),
        ((n_head, tall, HEAD_DIM), F32),
        ((n_head, rows, HEAD_DIM), F32),
        ((n_head, rows, HEAD_DIM), F32),
        ((n_head, tall // SPAN, 2 * HEAD_DIM, HEAD_DIM), F32),
        ((n_head, 2, 2 * HEAD_DIM, HEAD_DIM), BF),
        ((n_head, 2, 2 * HEAD_DIM, HEAD_DIM), BF),
        ((tall, HEAD_DIM), F32),
        ((tall, HEAD_DIM), F32),
        ((tall, n_head * HEAD_DIM), BF),
        ((rows, width), BF),
        ((rows, width), BF),
        ((rows, width), F32),
        ((tall, width), BF),
        ((n_head, 1, 2 * HEAD_DIM), F32),
        ((tall, width), BF),
    ]
    out_of = [0, 1, 2, 4, 5, 6, 7, 8, 9, 10, 11, 12, 13, 16, 17, 20, 21, 23]
    n_sems = 4 * PER_GATHER + 4 + 1 + 1 + 2 * n_head + 2 + 2
    return pl.pallas_call(
        functools.partial(forward_kernel, n_head),
        out_shape=[jax.ShapeDtypeStruct(*buffers[i]) for i in out_of],
        in_specs=[ANY] * 10 + [IN_VMEM],
        out_specs=[ANY] * len(out_of),
        scratch_shapes=[pltpu.VMEM(*b) for b in buffers]
        + [
            pltpu.SemaphoreType.DMA((n_sems,)),
            pltpu.SemaphoreType.DMA((n_sems,)),
            pltpu.SemaphoreType.DMA((96,)),
        ],
        compiler_params=pltpu.CompilerParams(
            collective_id=0, has_side_effects=True, vmem_limit_bytes=62 << 20
        ),
        name="forward",
    )(tokens, out_grad, wq, wk, wv, wg, wo, ffn_left, ffn_right, ffn_down, rates)


class Scatter:
    def __init__(self, place, copies, view, far_x, far_y, near_x, near_y, high, base, items=None):
        self.place, self.copies, self.view, self.base = place, copies, view, base
        self.items = items
        self.far_x, self.far_y, self.near_x, self.near_y, self.high = far_x, far_y, near_x, near_y, high

    def part(self, buffer, slot):
        return buffer.at[slot] if self.items is None else buffer.at[slot, pl.ds(0, self.items(slot))]

    def begin(self, slot):
        place, at = self.place, self.base + 4 * slot
        self.copies.send(self.view(slot, 3, 0), self.part(self.far_y, slot), at, at, place.by_y)
        self.copies.send(self.view(slot, 3, 1), self.part(self.far_x, slot), at + 1, at + 1, place.by_x)

    def middle(self, slot):
        place, copies, at = self.place, self.copies, self.base + 4 * slot
        copies.receive(self.part(self.far_y, slot), at, place.by_y)
        add_to(self.view(slot, 1, 0), self.part(self.far_y, slot))
        copies.send(self.view(slot, 1, None), self.part(self.near_x, slot), at + 2, at + 2, place.by_x)
        copies.receive(self.part(self.far_x, slot), at + 1, place.by_x)
        add_to(self.view(slot, 2, 1), self.part(self.far_x, slot))
        copies.send(self.view(slot, 2, None), self.part(self.near_y, slot), at + 3, at + 3, place.by_y)

    def end(self, slot, onward=True):
        place, copies, at = self.place, self.copies, self.base + 4 * slot
        copies.receive(self.part(self.near_x, slot), at + 2, place.by_x)
        copies.receive(self.part(self.near_y, slot), at + 3, place.by_y)
        add_to(self.view(slot, 0, None), self.part(self.near_x, slot), self.part(self.near_y, slot))
        if slot and onward:
            self.go_up(slot)

    def go_up(self, slot):
        at = self.base + 4 * self.place.n_head + slot
        into = self.high.at[slot - 1]
        self.copies.send(self.view(slot, 0, None), into, at, at, self.place.above(slot))

    def total(self, into=None, slots=(1, 2, 3)):
        place = self.place
        high = [self.high.at[slot - 1] for slot in slots]
        for slot, part in zip(slots, high):
            self.copies.receive(part, self.base + 4 * place.n_head + slot, place.up)
        add_to(self.view(0, 0, None), *high, into=into)


PER_SCATTER = 20


def add_to(ref, *others, into=None):
    def add(into, *refs):
        total = refs[0][...].astype(F32)
        for other in refs[1:]:
            total += other[...].astype(F32)
        into[...] = total.astype(BF)

    refs = (ref if into is None else into, ref) + others
    if len(ref.shape) == 2:
        add(*refs)
    else:
        for i in range(ref.shape[0]):
            add(*(one.at[i] for one in refs))


def dot(left, right):
    return jnp.dot(left, right, preferred_element_type=F32)


def iota(shape, axis):
    return lax.broadcasted_iota(jnp.int32, shape, axis).astype(F32)


def decay_of(head):
    exponent = jnp.full((1, 1), -8.0 / HEADS, F32) * (head + 1).astype(F32)
    return jnp.exp2(exponent)


def middle_kernel(
    n_head,
    wf,
    nm,
    og,
    hidden,
    wo,
    pre,
    query,
    attn,
    scale,
    feed_out,
    block_out,
    hidden_grad_out,
    branch_out,
    gate_out,
    ga_out,
    late_out,
    wf_ref,
    t_ref,
    g_ref,
    far_x,
    far_y,
    near_x,
    near_y,
    early_ref,
    high_ref,
    high_first_ref,
    high_third_ref,
    nm_ref,
    og_ref,
    branch_ref,
    hidden_ref,
    mid_ref,
    send_ref,
    got_ref,
    block_ref,
    wo_ref,
    gate_ref,
    attn_ref,
    ga_ref,
    late_ref,
    scale_ref,
    sum_ref,
    other_sum_ref,
    sends,
    receives,
    locals_,
):
    rows, width = hidden.shape
    quarter = width // 4
    units = wf.shape[1] // n_head
    spans = rows // SPAN
    tiles = 2 * spans
    last = n_head - 1
    place = Place(n_head)
    z, core = place.z, place.core
    place.greet()
    copies = Copies(sends, receives, locals_)
    own, other = pl.ds(0, rows), pl.ds(rows, rows)

    order = (2, 1, 3, 0)
    load_nm = copies.move(nm, nm_ref)
    load_og = copies.move(og, og_ref)
    load_wf = {}
    for slot in order:
        at = pl.ds(slot * units, units)
        lanes = pl.ds(0, width if slot < last else width - quarter)
        load_wf[slot] = copies.move(wf.at[:, at, lanes], wf_ref.at[:, at, lanes])
    early_loads = [
        copies.move(hidden, hidden_ref),
        copies.move(wo, wo_ref),
        copies.move(scale, scale_ref),
        copies.move(attn, attn_ref),
        copies.move(pre.at[:, :, pl.ds(3 * HEAD_DIM, HEAD_DIM)], gate_ref),
    ]
    place.meet()

    def tile(i):
        return pl.ds(pl.multiple_of(i * SPAN, SPAN), SPAN)

    def dot_last(left, right):
        return lax.dot_general(left, right, (((1,), (1,)), ((), ())), preferred_element_type=F32)

    def dot_first(left, right):
        return lax.dot_general(left, right, (((0,), (0,)), ((), ())), preferred_element_type=F32)

    early_slot, down = 1, 2

    def items(slot):
        return down if slot == early_slot else 3

    def g_view(slot, q, half):
        size = units if half is None else units // 2
        start = slot * units + (half or 0) * size
        return g_ref.at[pl.ds(0, items(slot)), pl.ds(start, size), pl.ds(q * quarter, quarter)]

    def late_view(ref, q, half):
        rows_at = pl.ds(last * units + half * (units // 2), units // 2)
        return ref.at[:, rows_at, pl.ds(q * quarter, quarter)]

    base = PER_SCATTER
    late_low, late_high = late_view(wf_ref, 3, 0), late_view(wf_ref, 3, 1)
    copies.send(late_view(wf, 1, 0), late_low, base, base, place.by_y)
    copies.send(late_view(wf, 2, 1), late_high, base + 1, base + 1, place.by_x)
    feed = Scatter(place, copies, g_view, far_x, far_y, near_x, near_y, None, 0, items)
    up_base = base + 2

    def feed_products(slot):
        at = pl.ds(slot * units, units)
        load_wf[slot].wait()

        @pl.loop(0, tiles)
        def _(i):
            rows_at = tile(i)
            left = dot_last(wf_ref[0, at, :], nm_ref[rows_at, :])
            right = dot_last(wf_ref[1, at, :], nm_ref[rows_at, :])
            grad = dot_last(wf_ref[2, at, :], og_ref[rows_at, :])
            t_ref[0, at, rows_at] = (grad * right).astype(BF)
            t_ref[1, at, rows_at] = (grad * left).astype(BF)
            t_ref[2, at, rows_at] = (left * right).astype(BF)

    def feed_gradients(slot):
        at = pl.ds(slot * units, units)

        def gradient(columns, of=(0, 1, 2)):
            for m in of:
                right = og_ref if m == down else nm_ref
                g_ref[m, at, columns] = dot(t_ref[m, at, :], right[:, columns]).astype(BF)

        def gradients(n, of=(0, 1, 2)):
            @pl.loop(0, n)
            def _(q):
                gradient(pl.ds(pl.multiple_of(q * quarter, quarter), quarter), of)

        if slot == 0:
            gradients(4)
            return
        of = tuple(range(items(slot)))
        if slot == early_slot:
            gradients(4, (down,))
            copies.send(g_ref.at[down, at], early_ref, up_base, up_base, place.above(slot))
        gradient(pl.ds(3 * quarter, quarter), of)
        feed.begin(slot)
        gradients(3, of)

    load_nm.wait()
    load_og.wait()
    for slot in order[:2]:
        feed_products(slot)
        feed_gradients(slot)
    feed.middle(order[0])
    copies.receive(late_low, base, place.by_y)
    copies.receive(late_high, base + 1, place.by_x)
    feed_products(order[2])
    feed_gradients(order[2])
    feed_products(order[3])
    feed.middle(order[1])
    base += 2 + 4
    for load in early_loads:
        load.wait()

    @pl.loop(0, spans)
    def _(i):
        at = tile(spans + i)
        total = dot_first(t_ref[0, :, at], wf_ref[0]) + dot_first(t_ref[1, :, at], wf_ref[1])
        send_ref[tile(i), :] = total.astype(BF)

    copies.send(send_ref, got_ref, base, base, place.across)

    @pl.loop(0, spans)
    def _(i):
        at = tile(i)
        total = dot_first(t_ref[0, :, at], wf_ref[0]) + dot_first(t_ref[1, :, at], wf_ref[1])
        mid_ref[at, :] = total

    feed.end(order[0], False)
    both, second_at = pl.ds(0, down), pl.ds(order[0] * units, units)
    near = pl.ds(0, quarter)
    above = place.above(order[0])
    copies.send(g_ref.at[:, second_at, near], high_ref, up_base + 1, up_base + 1, above)
    copies.receive(got_ref, base, place.across)

    @pl.loop(0, rows // 128)
    def _(i):
        at = pl.ds(pl.multiple_of(i * 128, 128), 128)
        grad = mid_ref[at, :] + got_ref[at, :].astype(F32)
        values = hidden_ref[at, :]
        norm = lax.rsqrt(jnp.mean(values * values, axis=-1, keepdims=True) + EPSILON)
        normed = values * norm
        mean = jnp.mean(grad * normed, axis=-1, keepdims=True)
        grad = og_ref[at, :].astype(F32) + norm * (grad - normed * mean)
        mid_ref[at, :] = grad
        branch_ref[at, :] = grad.astype(BF)

    copies.send(branch_ref.at[own], branch_ref.at[other], base + 1, base + 1, place.across)
    copies.move(mid_ref, hidden_grad_out, later=True)
    feed_gradients(order[3])
    copies.receive(early_ref, up_base, place.up)
    add_to(g_ref.at[down, pl.ds(0, units)], early_ref)
    feed.begin(0)
    query_loads = []
    for slot in range(n_head):
        lanes = pl.ds(slot * 2 * HEAD_DIM, 2 * HEAD_DIM)
        query_loads.append(copies.move(query.at[slot], t_ref.at[0, pl.ds(0, 2 * rows), lanes]))

    def gate_back(seq):
        for n in range(spans):
            at = pl.ds(seq * rows + n * SPAN, SPAN)
            grad = dot_last(branch_ref[at, :], wo_ref[...])
            norm = scale_ref[at, :]
            total = jnp.zeros((SPAN, 1), F32)
            for slot in range(n_head):
                lanes = pl.ds(slot * HEAD_DIM, HEAD_DIM)
                part = grad[:, slot * HEAD_DIM : (slot + 1) * HEAD_DIM]
                normed = attn_ref[slot, at, :] * norm
                og_ref[at, lanes] = (part * normed).astype(BF)
                part = part * gate_ref[slot, at, :]
                gate_ref[slot, at, :] = part
                total += jnp.sum(part * normed, axis=-1, keepdims=True)
            sum_ref[at, :] = jnp.broadcast_to(total, (SPAN, HEAD_DIM))

    gate_back(0)
    base += 2
    copies.send(sum_ref.at[own], other_sum_ref.at[other], base, base, place.across)
    copies.receive(branch_ref.at[other], base - 1, place.across)
    copies.move(branch_ref, branch_out, later=True)
    gate_back(1)
    copies.send(sum_ref.at[other], other_sum_ref.at[own], base + 1, base + 1, place.across)
    copies.move(og_ref.at[:, pl.ds(0, n_head * HEAD_DIM)], gate_out, later=True)
    copies.sent(base - 2)
    feed.middle(order[2])

    @pl.loop(0, spans)
    def _(i):
        send_ref[tile(i), :] = dot_first(t_ref[2, :, tile(spans + i)], wf_ref[2]).astype(BF)

    copies.send(send_ref, got_ref, base + 2, base + 2, place.across)

    @pl.loop(0, spans)
    def _(i):
        at = tile(i)
        hidden_ref[at, :] += dot_first(t_ref[2, :, at], wf_ref[2])

    feed.end(order[1], False)
    src = g_ref.at[both, pl.ds(order[1] * units, units), near]
    copies.send(src, high_first_ref, up_base + 2, up_base + 2, place.above(order[1]))
    for load in query_loads:
        load.wait()
    copies.receive(other_sum_ref.at[other], base, place.across)
    copies.receive(other_sum_ref.at[own], base + 1, place.across)

    for slot in range(n_head):
        decay = decay_of(2 * lax.rem(z + slot, n_head) + core)
        early = jnp.exp(-decay * (iota((SPAN, HEAD_DIM), 0) + 1.0))

        @pl.loop(0, tiles)
        def _(i):
            at = tile(i)
            norm = scale_ref[at, :]
            mean = (sum_ref[at, :] + other_sum_ref[at, :]) / width
            grad = norm * (gate_ref[slot, at, :] - attn_ref[slot, at, :] * norm * mean)
            grad = grad.astype(BF)
            ga_ref[slot, at, :] = grad
            q = t_ref[0, at, pl.ds(slot * 2 * HEAD_DIM, 2 * HEAD_DIM)]
            both_terms = dot_first(
                q, jnp.concatenate(split(grad.astype(F32) * early), axis=1)
            )
            late_ref[slot, i] = both_terms[:, :HEAD_DIM] + both_terms[:, HEAD_DIM:]

        copies.move(ga_ref.at[slot], ga_out.at[slot], later=True)
        copies.move(late_ref.at[slot], late_out.at[slot], later=True)

    feed.middle(order[3])
    copies.receive(got_ref, base + 2, place.across)

    @pl.loop(0, rows // 128)
    def _(i):
        at = pl.ds(pl.multiple_of(i * 128, 128), 128)
        block_ref[at, :] = (hidden_ref[at, :] + got_ref[at, :].astype(F32)).astype(BF)

    for q in range(4):
        far = pl.ds(pl.multiple_of(place.at[q] * quarter, quarter), quarter)
        src = block_ref.at[:, pl.ds(q * quarter, quarter)]
        copies.move(src, block_out.at[:, far], later=True)
    feed.end(order[2], False)
    src = g_ref.at[:, pl.ds(order[2] * units, units), near]
    copies.send(src, high_third_ref, up_base + 3, up_base + 3, place.above(order[2]))
    copies.receive(high_ref, up_base + 1, place.up)
    copies.receive(high_first_ref, up_base + 2, place.up)
    feed.end(order[3], False)
    first_rows = pl.ds(0, units)
    add_to(g_ref.at[both, first_rows, near], high_ref.at[both], high_first_ref)
    add_to(g_ref.at[down, first_rows, near], high_ref.at[down])
    copies.receive(high_third_ref, up_base + 3, place.up)
    add_to(g_view(0, 0, None), high_third_ref)
    copies.move(g_view(0, 0, None), feed_out, later=True)
    copies.finish()


def middle(n_head, wf, nm, og, hidden, wo, pre, query, attn, scale):
    rows, width = hidden.shape
    units = wf.shape[1] // n_head
    quarter = width // 4
    tall = 2 * rows
    halves = (n_head, 3, units // 2, quarter)
    wholes = (n_head, 3, units, quarter)
    late = ((n_head, tall // SPAN, 2 * HEAD_DIM, HEAD_DIM), F32)
    buffers = [
        (wf.shape, BF),
        (wf.shape, BF),
        (wf.shape, BF),
        (halves, BF),
        (halves, BF),
        (wholes, BF),
        (wholes, BF),
        ((units, width), BF),
        (wholes[1:], BF),
        ((2, units, quarter), BF),
        (wholes[1:], BF),
        ((tall, width), BF),
        ((tall, width), BF),
        ((tall, width), BF),
        ((rows, width), F32),
        ((rows, width), F32),
        ((rows, width), BF),
        ((rows, width), BF),
        ((rows, width), BF),
        (wo.shape, BF),
        (attn.shape, F32),
        (attn.shape, F32),
        (attn.shape, BF),
        late,
        (scale.shape, F32),
        (scale.shape, F32),
        (scale.shape, F32),
    ]
    outs = [
        (wholes[1:], BF),
        ((rows, width), BF),
        ((rows, width), F32),
        ((tall, width), BF),
        ((tall, n_head * HEAD_DIM), BF),
        (attn.shape, BF),
        late,
    ]
    n_sems = PER_SCATTER + 2 + 4 + 2 + 3
    return pl.pallas_call(
        functools.partial(middle_kernel, n_head),
        out_shape=[jax.ShapeDtypeStruct(*out) for out in outs],
        in_specs=[ANY] * 9,
        out_specs=[ANY] * len(outs),
        scratch_shapes=[pltpu.VMEM(*b) for b in buffers]
        + [
            pltpu.SemaphoreType.DMA((n_sems,)),
            pltpu.SemaphoreType.DMA((n_sems,)),
            pltpu.SemaphoreType.DMA((64,)),
        ],
        compiler_params=pltpu.CompilerParams(
            collective_id=1, has_side_effects=True, vmem_limit_bytes=63 << 20
        ),
        name="middle",
    )(wf, nm, og, hidden, wo, pre, query, attn, scale)


class Share:
    def __init__(self, place, copies, view, base):
        self.place, self.copies, self.view, self.base = place, copies, view, base

    def pass_on(self, q, half, at, device):
        part = self.view(0, q, half)
        self.copies.send(part, part, self.base + at, self.base + at, device)

    def begin(self):
        self.pass_on(0, None, 0, self.place.by_x)
        self.pass_on(0, None, 1, self.place.by_y)
        self.pass_on(0, None, 4, self.place.across)

    def spread(self):
        place, copies, at = self.place, self.copies, self.base
        copies.receive(self.view(0, 1, None), at, place.by_x)
        self.pass_on(1, 0, 2, place.by_y)
        copies.receive(self.view(0, 2, None), at + 1, place.by_y)
        self.pass_on(2, 1, 3, place.by_x)
        self.pass_on(1, None, 5, place.across)
        self.pass_on(2, None, 6, place.across)

    def complete(self):
        place, copies, at = self.place, self.copies, self.base
        copies.receive(self.view(0, 3, 0), at + 2, place.by_y)
        copies.receive(self.view(0, 3, 1), at + 3, place.by_x)
        self.pass_on(3, None, 7, place.across)

    def other_side(self):
        for q in range(4):
            self.copies.receive(self.view(1, q, None), self.base + 4 + q, self.place.across)


PER_SHARE = 8


def last_kernel(
    n_head,
    late,
    feed_piece,
    nin,
    gate_pre,
    gated,
    branch,
    query,
    keys,
    values,
    grad_attn,
    carry,
    fresh,
    pre,
    cosines,
    sines,
    wa,
    hidden_grad,
    block,
    tokens,
    input_ref,
    block_ref,
    feed_ref,
    attn_ref,
    rates_both,
    ga_ref,
    a_far_x,
    a_far_y,
    a_near_x,
    a_near_y,
    a_high,
    g_far_x,
    g_far_y,
    g_near_x,
    g_near_y,
    g_high,
    late_ref,
    pending_ref,
    message_ref,
    nin_ref,
    gate_ref,
    gated_ref,
    branch_ref,
    q_ref,
    k_ref,
    v_ref,
    grad_attn_ref,
    carry_ref,
    fresh_ref,
    qk_pre_ref,
    cos_ref,
    sin_ref,
    pre_ref,
    wa_ref,
    x_ref,
    grad_ref,
    send_ref,
    got_ref,
    rates_ref,
    rates_high,
    rates_sum,
    rates_got,
    sends,
    receives,
    locals_,
):
    rows, width = tokens.shape
    quarter = width // 4
    units = feed_piece.shape[1]
    spans = rows // SPAN
    tiles = 2 * spans
    last = n_head - 1
    three = 3 * HEAD_DIM
    place = Place(n_head)
    place.greet()
    z, core = place.z, place.core
    copies = Copies(sends, receives, locals_)
    order = (2, 1, 3, 0)
    sides = (core, 1 - core)

    own_block = pl.ds(pl.multiple_of(place.plane * quarter, quarter), quarter)
    load_feed = copies.move(feed_piece, feed_ref.at[sides[0], :, :, own_block])
    load_late = copies.move(late, late_ref)
    load_first = [copies.move(nin, nin_ref), copies.move(gate_pre, gate_ref)]
    load_second = [copies.move(gated, gated_ref), copies.move(branch, branch_ref)]
    load_back = [
        copies.move(src, dst)
        for src, dst in (
            (query, q_ref),
            (keys, k_ref),
            (values, v_ref),
            (grad_attn, grad_attn_ref),
            (carry, carry_ref),
        )
    ]
    for seq in range(2):
        for slot in range(n_head):
            load_back.append(copies.move(fresh.at[slot, seq * spans], fresh_ref.at[slot, seq]))

    def slot_load(slot, turn):
        return [
            copies.move(pre.at[slot, :, pl.ds(0, 2 * HEAD_DIM)], qk_pre_ref.at[turn]),
            copies.move(cosines.at[slot], cos_ref.at[turn]),
            copies.move(sines.at[slot], sin_ref.at[turn]),
        ]

    slot_loads = [slot_load(slot, turn) for turn, slot in enumerate(order[:2])]
    late_loads = [
        copies.move(wa, wa_ref),
        copies.move(hidden_grad, grad_ref),
        copies.move(block, block_ref),
    ]
    for q in range(4):
        far = pl.ds(pl.multiple_of(place.at[q] * quarter, quarter), quarter)
        late_loads.append(copies.move(tokens.at[:, far], x_ref.at[:, pl.ds(q * quarter, quarter)]))
    place.meet()

    def tile(i):
        return pl.ds(pl.multiple_of(i * SPAN, SPAN), SPAN)

    def dot_last(left, right):
        return lax.dot_general(left, right, (((1,), (1,)), ((), ())), preferred_element_type=F32)

    def dot_first(left, right):
        return lax.dot_general(left, right, (((0,), (0,)), ((), ())), preferred_element_type=F32)

    def part(start, half, size):
        if half is None:
            return pl.ds(start, size)
        return pl.ds(start + half * (size // 2), size // 2)

    def start_of(q):
        return pl.multiple_of(place.at[q] * quarter, quarter)

    def feed_view(side, q, half):
        return feed_ref.at[sides[side], :, part(0, half, units), pl.ds(start_of(q), quarter)]

    def lanes_view(lanes, side, q, half):
        at = part(0, half, quarter)
        start = pl.multiple_of(start_of(q) + at.start, quarter // 2)
        return attn_ref.at[sides[side], pl.ds(start, at.size), lanes]

    def ga_view(lanes, slot, q, half):
        return ga_ref.at[slot, part(q * quarter, half, quarter), lanes]

    gate_lanes, rest_lanes = pl.ds(three, 2 * HEAD_DIM), pl.ds(0, three)
    weight_lanes = pl.ds(three, HEAD_DIM)
    of_gate = functools.partial(ga_view, gate_lanes)
    of_rest = functools.partial(ga_view, rest_lanes)
    gate = Scatter(place, copies, of_gate, g_far_x, g_far_y, g_near_x, g_near_y, g_high, 0)
    base = PER_SCATTER
    rest = Scatter(place, copies, of_rest, a_far_x, a_far_y, a_near_x, a_near_y, a_high, base)
    base += PER_SCATTER
    to_gate = functools.partial(lanes_view, gate_lanes)
    to_rest = functools.partial(lanes_view, rest_lanes)
    shares = []
    for view in (feed_view, to_gate, to_rest):
        shares.append(Share(place, copies, view, base))
        base += PER_SHARE
    feed_share, gate_share, rest_share = shares

    load_feed.wait()
    feed_share.begin()

    n_chain = 2 * n_head
    chain_base = base
    base += n_chain

    def chain_at(index):
        group, seq = lax.div(index, 2), lax.rem(index, 2)
        return lax.rem(group - z + n_head, n_head), seq, decay_of(2 * group + core)

    def chain_copy(index, slot, seq):
        return pltpu.make_async_remote_copy(
            src_ref=message_ref.at[slot, seq],
            dst_ref=pending_ref.at[lax.rem(slot + 1, n_head), seq],
            send_sem=sends.at[chain_base + index],
            recv_sem=receives.at[chain_base + index],
            device_id=place.down,
            device_id_type=MESH,
        )

    def hand_on(index):
        slot, seq, decay = chain_at(index)
        total = jnp.exp(-decay * rows) * pending_ref[slot, seq].astype(F32)
        for n in range(spans):
            total += jnp.exp(-decay * (n * SPAN)) * late_ref[slot, seq * spans + n]
        message_ref[slot, seq] = total.astype(BF)
        chain_copy(index, slot, seq).start()

    def take(index):
        slot, seq, _ = chain_at(index)
        copies.receive(pending_ref.at[slot, seq], chain_base + index, place.up)

    load_late.wait()

    @pl.when(z == last)
    def _():
        pending_ref[...] = jnp.zeros_like(pending_ref)
        pl.loop(0, n_chain)(hand_on)

    for load in load_first:
        load.wait()

    for load in load_second:
        load.wait()

    def gate_gradient(at):
        grads = dot_first(nin_ref[:, at], gate_ref[...]).astype(BF)
        outs = dot_first(branch_ref[:, at], gated_ref[...]).astype(BF)
        for slot in range(n_head):
            lanes = slice(slot * HEAD_DIM, (slot + 1) * HEAD_DIM)
            ga_ref[slot, at, pl.ds(three, HEAD_DIM)] = grads[:, lanes]
            ga_ref[slot, at, pl.ds(three + HEAD_DIM, HEAD_DIM)] = outs[:, lanes]

    gate_gradient(pl.ds(3 * quarter, quarter))
    for slot in order:
        gate.begin(slot)
    pl.loop(0, 3)(lambda q: gate_gradient(tile(q)))

    @pl.when(jnp.logical_and(z > 0, z < last))
    def _():
        @pl.loop(0, n_chain)
        def _(index):
            take(index)
            hand_on(index)

    for slot in order:
        gate.middle(slot)
    for load in load_back:
        load.wait()

    @pl.when(z == 0)
    def _():
        pl.loop(0, n_chain)(take)

    offsets = iota((SPAN, SPAN), 0) - iota((SPAN, SPAN), 1)

    def back_slot(slot, turn):
        decay = decay_of(2 * lax.rem(z + slot, n_head) + core)
        mask = jnp.where(offsets >= 0.0, jnp.exp(-decay * jnp.maximum(offsets, 0.0)), 0.0)
        places = iota((SPAN, 1), 0)
        early = jnp.exp(-decay * (places + 1.0))
        late_decay = jnp.exp(-decay * (SPAN - 1.0 - places))
        span_decay = jnp.exp(-decay * SPAN)
        rates_ref[slot] = jnp.zeros((8, HEAD_DIM), F32)

        @pl.loop(0, 2)
        def _(seq):
            for n in range(spans):
                at, here = tile(seq * spans + n), pl.ds(n * SPAN, SPAN)
                state = carry_ref[slot, seq].astype(F32)
                if n == 1:
                    state = span_decay * state + fresh_ref[slot, seq]
                later = pending_ref[slot, seq].astype(F32)
                if n == 0:
                    later = span_decay * later + late_ref[slot, seq * spans + 1]
                q, k, v = q_ref[slot, at, :], k_ref[slot, at, :], v_ref[slot, at, :]
                grad = grad_attn_ref[slot, at, :]
                weights = (dot_last(q, k) * mask).astype(BF)
                scores = (dot_last(grad, v) * mask).astype(BF)
                state_high, state_low = split(state)
                grad_query = dot(scores, k)
                grad_query += early * (dot_last(grad, state_high) + dot_last(grad, state_low))
                later_high, later_low = split(later)
                grad_keys = dot_first(scores, q)
                grad_keys += late_decay * (dot_last(v, later_high) + dot_last(v, later_low))
                both = dot(k, jnp.concatenate([later_high, later_low], axis=1))
                grad_values = dot_first(weights, grad)
                grad_values += late_decay * (both[:, :HEAD_DIM] + both[:, HEAD_DIM:])
                pre_ref[slot, at, pl.ds(2 * HEAD_DIM, HEAD_DIM)] = grad_values.astype(BF)
                cosine, sine = cos_ref[turn, here, :], sin_ref[turn, here, :]
                angles = jnp.zeros((SPAN, HEAD_DIM), F32)
                for i, turned in enumerate((grad_query, grad_keys)):
                    lanes = pl.ds(i * HEAD_DIM, HEAD_DIM)
                    value = qk_pre_ref[turn, at, lanes]
                    by_cos, by_sin = turned[:, :HEAD_DIM], turned[:, HEAD_DIM:]
                    sigmoid = 1.0 / (1.0 + jnp.exp(-value))
                    act = by_cos * cosine + by_sin * sine
                    angles += value * sigmoid * (by_sin * cosine - by_cos * sine)
                    act = act * sigmoid * (1.0 + value * (1.0 - sigmoid))
                    pre_ref[slot, at, lanes] = act.astype(BF)
                steps = (z * rows + n * SPAN).astype(F32) + places
                rates_ref[slot, pl.ds(0, 1), :] += jnp.sum(steps * angles, axis=0, keepdims=True)

    def rest_gradient(slot, at):
        ga_ref[slot, at, rest_lanes] = dot_first(nin_ref[:, at], pre_ref[slot]).astype(BF)

    rates_base = base
    base += n_head + 3
    for i, slot in enumerate(order):
        for load in slot_loads[i]:
            load.wait()
        back_slot(slot, i % 2)
        if i + 2 < n_head:
            slot_loads.append(slot_load(order[i + 2], i % 2))
        if slot:
            at = rates_base + slot
            copies.send(rates_ref.at[slot], rates_high.at[slot - 1], at, at, place.above(slot))
        rest_gradient(slot, pl.ds(3 * quarter, quarter))
        rest.begin(slot)
        pl.loop(0, 3)(lambda q: rest_gradient(slot, tile(q)))
    total = rates_ref[0]
    for slot in range(1, n_head):
        copies.receive(rates_high.at[slot - 1], rates_base + slot, place.up)
        total += rates_high[slot - 1]
    rates_sum[0] = total
    rates_base += n_head
    copies.send(rates_sum.at[0], rates_got.at[0], rates_base, rates_base, place.by_x)
    for slot in order:
        gate.end(slot)
    copies.receive(rates_got.at[0], rates_base, place.by_x)
    rates_sum[1] = total + rates_got[0]
    copies.send(rates_sum.at[1], rates_got.at[1], rates_base + 1, rates_base + 1, place.by_y)
    rest.middle(order[0])
    rest.middle(order[1])
    for load in late_loads:
        load.wait()

    def grad_in(at):
        total = dot_last(gate_ref[at, :], wa_gate())
        for slot in range(n_head):
            total += dot_last(pre_ref[slot, at, :], wa_ref[slot, :, rest_lanes])
        return total

    def wa_gate():
        return jnp.concatenate([wa_ref[slot, :, weight_lanes] for slot in range(n_head)], axis=1)

    @pl.loop(0, spans)
    def _(i):
        send_ref[tile(i), :] = grad_in(tile(spans + i)).astype(BF)

    copies.send(send_ref, got_ref, base, base, place.across)
    rest.middle(order[2])

    rest.middle(order[3])
    feed_share.spread()
    rest.end(order[0])
    copies.receive(got_ref, base, place.across)

    @pl.loop(0, spans)
    def _(i):
        at = tile(i)
        values = x_ref[at, :].astype(F32)
        norm = lax.rsqrt(jnp.mean(values * values, axis=-1, keepdims=True) + EPSILON)
        normed = values * norm
        grad = grad_in(at) + got_ref[at, :].astype(F32)
        mean = jnp.mean(grad * normed, axis=-1, keepdims=True)
        grad_ref[at, :] += norm * (grad - normed * mean)

    for q in range(4):
        src = grad_ref.at[:, pl.ds(q * quarter, quarter)]
        copies.move(src, input_ref.at[:, pl.ds(start_of(q), quarter)], later=True)
    gate.total(to_gate(0, 0, None))
    gate_share.begin()
    rest.end(order[1])
    rest.end(order[2])
    rest.end(order[3])
    rest.total(to_rest(0, 0, None))
    rest_share.begin()
    copies.receive(rates_got.at[1], rates_base + 1, place.by_y)
    rates_both[sides[0]] = rates_sum[1] + rates_got[1]
    mine = rates_both.at[sides[0]]
    copies.send(mine, mine, rates_base + 2, rates_base + 2, place.across)
    feed_share.complete()
    gate_share.spread()
    copies.receive(rates_both.at[sides[1]], rates_base + 2, place.across)
    feed_share.other_side()
    rest_share.spread()
    gate_share.complete()
    rest_share.complete()
    for share in shares[1:]:
        share.other_side()

    @pl.when(z > 0)
    def _():
        @pl.loop(0, n_chain)
        def _(index):
            slot, seq, _ = chain_at(index)
            chain_copy(index, slot, seq).wait_send()

    copies.finish()


def last(
    n_head,
    late,
    feed_piece,
    nin,
    gate_pre,
    gated,
    branch,
    query,
    keys,
    values,
    grad_attn,
    carry,
    fresh,
    pre,
    cosines,
    sines,
    wa,
    hidden_grad,
    block,
    tokens,
):
    rows, width = tokens.shape
    _, units, quarter = feed_piece.shape
    tall = 2 * rows

    def scatter_buffers(shape, halved):
        half = tuple(n // 2 if i == halved else n for i, n in enumerate(shape))
        return [
            ((n_head,) + half, BF),
            ((n_head,) + half, BF),
            ((n_head,) + shape, BF),
            ((n_head,) + shape, BF),
            ((n_head - 1,) + shape, BF),
        ]

    outs = [
        ((rows, width), F32),
        ((rows, width), BF),
        ((2, 3, units, width), BF),
        ((2, width, 5 * HEAD_DIM), BF),
        ((2, 8, HEAD_DIM), F32),
    ]
    chain = ((n_head, 2, 2 * HEAD_DIM, HEAD_DIM), BF)
    buffers = [
        ((n_head, width, 5 * HEAD_DIM), BF),
        *scatter_buffers((quarter, 3 * HEAD_DIM), 0),
        *scatter_buffers((quarter, 2 * HEAD_DIM), 0),
        (late.shape, F32),
        chain,
        chain,
        (nin.shape, BF),
        (gate_pre.shape, BF),
        (gated.shape, BF),
        (branch.shape, BF),
        (query.shape, BF),
        (keys.shape, BF),
        (values.shape, BF),
        (grad_attn.shape, BF),
        chain,
        (chain[0], F32),
        ((2, tall, 2 * HEAD_DIM), F32),
        ((2, rows, HEAD_DIM), F32),
        ((2, rows, HEAD_DIM), F32),
        ((n_head, tall, 3 * HEAD_DIM), BF),
        (wa.shape, BF),
        ((rows, width), BF),
        ((rows, width), F32),
        ((rows, width), BF),
        ((rows, width), BF),
        ((n_head, 8, HEAD_DIM), F32),
        ((n_head - 1, 8, HEAD_DIM), F32),
        ((2, 8, HEAD_DIM), F32),
        ((2, 8, HEAD_DIM), F32),
    ]
    n_sems = 2 * PER_SCATTER + 3 * PER_SHARE + 2 * n_head + n_head + 3 + 1
    arrays = [late, feed_piece, nin, gate_pre, gated, branch, query, keys, values, grad_attn]
    arrays += [carry, fresh, pre, cosines, sines, wa, hidden_grad, block, tokens]
    arrays = [pltpu.with_memory_space_constraint(array, pltpu.HBM) for array in arrays]
    return pl.pallas_call(
        functools.partial(last_kernel, n_head),
        out_shape=[pltpu.VMEM(*out) for out in outs],
        in_specs=[ANY] * len(arrays),
        out_specs=[IN_VMEM] * len(outs),
        scratch_shapes=[pltpu.VMEM(*b) for b in buffers]
        + [
            pltpu.SemaphoreType.DMA((n_sems,)),
            pltpu.SemaphoreType.DMA((n_sems,)),
            pltpu.SemaphoreType.DMA((64,)),
        ],
        compiler_params=pltpu.CompilerParams(
            collective_id=2, has_side_effects=True, vmem_limit_bytes=52 << 20
        ),
        name="last",
    )(*arrays)


def finish_kernel(grad, block, feed, attn, rates, *refs):
    outs, results, locals_ = refs[:11], refs[11:-1], refs[-1]
    copies = Copies(None, None, locals_)
    (block_out, grad_out, q_out, k_out, v_out, g_out, o_out, rates_out, l_out, r_out, d_out) = outs
    units = feed.shape[2]
    copies.move(grad, grad_out, later=True)
    copies.move(block, block_out, later=True)
    l_ref, r_ref, d_ref, q_ref, k_ref, v_ref, g_ref, o_ref, rates_ref = results
    for side in range(2):
        rates_ref[:, pl.ds(side * HEAD_DIM, HEAD_DIM)] = rates[side, pl.ds(0, 1), :]
    copies.move(rates_ref, rates_out, later=True)
    for i, (ref, out) in enumerate(((l_ref, l_out), (r_ref, r_out), (d_ref, d_out))):
        for side in range(2):
            at = pl.ds(side * units, units)
            ref[at, :] = feed[side, i].astype(F32)
            copies.move(ref.at[at], out.at[at], later=True)
    for i, (ref, out) in enumerate(((q_ref, q_out), (k_ref, k_out), (v_ref, v_out), (g_ref, g_out))):
        lanes = pl.ds(i * HEAD_DIM, HEAD_DIM)
        for side in range(2):
            ref[:, pl.ds(side * HEAD_DIM, HEAD_DIM)] = attn[side, :, lanes].astype(F32)
        copies.move(ref, out, later=True)
    for side in range(2):
        lanes = pl.ds(4 * HEAD_DIM, HEAD_DIM)
        o_ref[pl.ds(side * HEAD_DIM, HEAD_DIM), :] = attn[side, :, lanes].T.astype(F32)
    copies.move(o_ref, o_out, later=True)
    copies.finish()


def finish(grad, block, feed, attn, rates):
    _, _, units, width = feed.shape
    projection = ((width, 2 * HEAD_DIM), F32)
    back = ((2 * HEAD_DIM, width), F32)
    results = [((2 * units, width), F32)] * 3 + [projection] * 4 + [back]
    results.append(((1, 2 * HEAD_DIM), F32))
    outs = [(block.shape, BF), (grad.shape, F32)] + results[3:] + results[:3]
    return pl.pallas_call(
        finish_kernel,
        out_shape=[jax.ShapeDtypeStruct(*out) for out in outs],
        in_specs=[IN_VMEM] * 5,
        out_specs=[ANY] * len(outs),
        scratch_shapes=[pltpu.VMEM(*b) for b in results] + [pltpu.SemaphoreType.DMA((48,))],
        compiler_params=pltpu.CompilerParams(vmem_limit_bytes=24 << 20),
        name="finish",
    )(grad, block, feed, attn, rates)


def make(n_dp, n_head):
    def on_device(
        tokens,
        attn_query,
        attn_key,
        attn_value,
        attn_gate,
        attn_out,
        rotation_rates,
        ffn_left,
        ffn_right,
        ffn_down,
        out_grad,
    ):
        rates_in = rotation_rates.reshape(1, -1)
        (
            attn_weights,
            out_w,
            ffn_all,
            gathered_in,
            pre,
            query,
            keys,
            values,
            attn,
            cosines,
            sines,
            fresh,
            carry,
            scale_attn,
            gated,
            hidden,
            gathered_mid,
            grad_rows,
        ) = forward(
            n_head,
            tokens,
            out_grad,
            attn_query,
            attn_key,
            attn_value,
            attn_gate,
            attn_out,
            ffn_left.T,
            ffn_right.T,
            ffn_down,
            rates_in,
        )
        feed_piece, block_out, grad_hidden, branch_rows, gate_pre, grad_attn, late = middle(
            n_head,
            ffn_all,
            gathered_mid,
            grad_rows,
            hidden,
            out_w,
            pre,
            query,
            attn,
            scale_attn,
        )
        grads = last(
            n_head,
            late,
            feed_piece,
            gathered_in,
            gate_pre,
            gated,
            branch_rows,
            query,
            keys,
            values,
            grad_attn,
            carry,
            fresh,
            pre,
            cosines,
            sines,
            attn_weights,
            grad_hidden,
            block_out,
            tokens,
        )
        results = finish(*grads)
        rates_grad, left_grad, right_grad = results[7][0], results[8].T, results[9].T
        results = list(results[:7]) + [rates_grad, left_grad, right_grad, results[10]]
        if n_dp > 8:
            groups = [[i + 8 * j for j in range(n_dp // 8)] for i in range(8)]
            grads = [lax.psum(grad, "dp", axis_index_groups=groups) for grad in results[2:]]
            results = results[:2] + grads
        return tuple(results)

    return on_device


def solution(mesh):
    weights = (P(None, "head"),) * 4 + (P("head", None), P("head")) + (P(None, "head"),) * 2
    weights = weights + (P("head", None),)
    rows = P(("dp", "head"), None)
    return jax.shard_map(
        make(mesh.shape["dp"], mesh.shape["head"]),
        mesh=mesh,
        in_specs=(rows,) + weights + (rows,),
        out_specs=(rows, rows) + weights,
        check_vma=False,
    )
```

```python
import functools

import jax
import jax.numpy as jnp
from jax import lax
from jax.experimental import pallas as pl
from jax.experimental.pallas import tpu as pltpu
from jax.sharding import PartitionSpec as P

HEADS = 8
HEAD_DIM = 128
SPAN = 256
EPSILON = 1e-06
BF = jnp.bfloat16
F32 = jnp.float32


MESH = pl.DeviceIdType.MESH
ANY = pl.BlockSpec(memory_space=pl.ANY)
IN_VMEM = pl.BlockSpec(memory_space=pltpu.VMEM)


def split(value):
    high = value.astype(BF)
    return high, (value - high.astype(F32)).astype(BF)


class Place:
    def __init__(self, n_head):
        self.n_head = n_head
        dp = lax.axis_index("dp")
        self.z = lax.axis_index("head")
        self.core = lax.rem(dp, 2)
        x = lax.rem(lax.div(dp, 2), 2)
        y = lax.rem(lax.div(dp, 4), 2)
        self.plane = x + 2 * y
        self.at = [self.plane, self.plane + 1 - 2 * x, self.plane + 2 - 4 * y, 3 - self.plane]
        self.across = {"dp": dp + 1 - 2 * self.core}
        self.by_x = {"dp": dp + 2 - 4 * x}
        self.by_y = {"dp": dp + 4 - 8 * y}
        self.up = {"head": lax.rem(self.z + 1, n_head)}
        self.down = {"head": lax.rem(self.z + n_head - 1, n_head)}

    def above(self, step):
        return {"head": lax.rem(self.z + step, self.n_head)}

    def below(self, step):
        return {"head": lax.rem(self.z + self.n_head - step, self.n_head)}

    def greet(self):
        others = [self.across, self.by_x, self.by_y]
        others += [self.below(step) for step in range(1, self.n_head)]
        for other in others:
            barrier = pltpu.get_barrier_semaphore()
            pl.semaphore_signal(barrier, inc=1, device_id=other, device_id_type=MESH)

    def meet(self):
        pl.semaphore_wait(pltpu.get_barrier_semaphore(), self.n_head + 2)


class Copies:
    def __init__(self, sends, receives, locals_):
        self.sends, self.receives, self.locals = sends, receives, locals_
        self.pending = []
        self.started = {}
        self.n_local = 0

    def send(self, src, dst, out, into, device, when=None):
        copy = pltpu.make_async_remote_copy(
            src_ref=src,
            dst_ref=dst,
            send_sem=self.sends.at[out],
            recv_sem=self.receives.at[into],
            device_id=device,
            device_id_type=MESH,
        )
        if when is None:
            copy.start()
            self.pending.append(copy.wait_send)
            if isinstance(out, int):
                self.started[out] = copy.wait_send
        else:
            pl.when(when)(copy.start)
            self.pending.append(lambda: pl.when(when)(copy.wait_send))

    def receive(self, dst, into, device):
        pltpu.make_async_remote_copy(
            src_ref=dst,
            dst_ref=dst,
            send_sem=self.sends.at[0],
            recv_sem=self.receives.at[into],
            device_id=device,
            device_id_type=MESH,
        ).wait_recv()

    def move(self, src, dst, later=False):
        copy = pltpu.make_async_copy(src, dst, self.locals.at[self.n_local])
        self.n_local += 1
        copy.start()
        if later:
            self.pending.append(copy.wait)
        return copy

    def sent(self, out):
        wait = self.started.pop(out)
        self.pending.remove(wait)
        wait()

    def finish(self):
        for wait in self.pending:
            wait()


class Gather:
    def __init__(self, place, copies, view, base, late=None):
        self.place, self.copies, self.view, self.base = place, copies, view, base
        self.late = late

    def begin(self):
        place, z = self.place, self.place.z
        own = self.view(0, 0, None)
        last = place.n_head - 1
        self.copies.send(
            own, self.view(last, 0, None), self.base, self.base + last, place.up, when=z < last
        )
        self.copies.send(own, self.view(1, 0, None), self.base + 1, self.base + 1, place.down, when=z > 0)

    def arrived(self, slot, when=True):
        place, copies, z, base = self.place, self.copies, self.place.z, self.base
        last = place.n_head - 1
        if when is True:
            copies.receive(self.view(slot, 0, None), base + slot, place.up)
        else:
            pl.when(when)(lambda: copies.receive(self.view(slot, 0, None), base + slot, place.up))
        from_up = z + slot <= last
        piece = self.view(slot, 0, None)
        down = jnp.logical_and(jnp.logical_and(from_up, z > 0), when)
        up = jnp.logical_and(jnp.logical_not(from_up), z < last)
        up = jnp.logical_and(up, when)
        always = None if when is True else when
        after = jnp.minimum(slot + 1, last)
        before = jnp.maximum(slot - 1, 1)
        copies.send(piece, self.view(after, 0, None), base + 1 + slot, base + after, place.down, when=down)
        copies.send(piece, self.view(before, 0, None), base + 1 + slot, base + before, place.up, when=up)
        at = base + 4 * slot + 4
        copies.send(piece, self.view(slot, 1, None), at, at, place.by_x, when=always)
        copies.send(piece, self.view(slot, 2, None), at + 1, at + 1, place.by_y, when=always)

    def spread(self, slot):
        place, copies = self.place, self.copies
        at = self.base + 4 * slot + 4
        now = None if self.late is None else slot != self.late
        low, high = self.view(slot, 3, 0), self.view(slot, 3, 1)
        copies.receive(self.view(slot, 1, None), at, place.by_x)
        copies.send(self.view(slot, 1, 0), low, at + 2, at + 2, place.by_y, when=now)
        copies.receive(self.view(slot, 2, None), at + 1, place.by_y)
        copies.send(self.view(slot, 2, 1), high, at + 3, at + 3, place.by_x, when=now)

    def complete(self, slot):
        place, copies = self.place, self.copies
        at = self.base + 4 * slot + 4

        def receive():
            copies.receive(self.view(slot, 3, 0), at + 2, place.by_y)
            copies.receive(self.view(slot, 3, 1), at + 3, place.by_x)

        if self.late is None:
            receive()
        else:
            pl.when(slot != self.late)(receive)


PER_GATHER = 24


def forward_kernel(
    n_head,
    tokens,
    out_grad,
    wq,
    wk,
    wv,
    wg,
    wo,
    ffn_left,
    ffn_right,
    ffn_down,
    rates,
    wa_out,
    wo_out,
    wf_out,
    nin_out,
    pre_out,
    q_out,
    k_out,
    v_out,
    attn_out,
    cos_out,
    sin_out,
    fresh_out,
    carry_out,
    scale_out,
    gated_out,
    hidden_out,
    nm_out,
    og_out,
    wa_ref,
    wo_ref,
    wf_ref,
    x_ref,
    nin_ref,
    pre_ref,
    q_ref,
    k_ref,
    v_ref,
    attn_ref,
    cos_ref,
    sin_ref,
    fresh_ref,
    carry_ref,
    message_ref,
    squares_ref,
    other_squares_ref,
    gated_ref,
    branch_ref,
    other_branch_ref,
    hidden_ref,
    nm_ref,
    rates_ref,
    og_ref,
    sends,
    receives,
    locals_,
):
    rows, width = tokens.shape
    quarter = width // 4
    units = ffn_down.shape[0] // 2
    tiles = 2 * rows // SPAN
    place = Place(n_head)
    z, core = place.z, place.core
    last = n_head - 1
    place.greet()
    copies = Copies(sends, receives, locals_)

    def columns(start, size):
        return pl.ds(pl.multiple_of(start, size), size)

    def own_weights(q):
        far = columns(place.at[q] * quarter, quarter)
        near = pl.ds(q * quarter, quarter)
        loads = []
        for i, w in enumerate((wq, wk, wv, wg)):
            src = w.at[far, columns(core * HEAD_DIM, HEAD_DIM)]
            loads.append(copies.move(src, wa_ref.at[0, near, pl.ds(i * HEAD_DIM, HEAD_DIM)]))
        src = wo.at[columns(core * HEAD_DIM, HEAD_DIM), far]
        loads.append(copies.move(src, wo_ref.at[pl.ds(0, HEAD_DIM), near]))
        for i, w in enumerate((ffn_left, ffn_right, ffn_down)):
            src = w.at[pl.ds(pl.multiple_of(core * units, 16), units), far]
            loads.append(copies.move(src, wf_ref.at[i, pl.ds(0, units), near]))
        return loads

    own_loads = [own_weights(0)]
    token_loads = [
        copies.move(
            tokens.at[:, columns(place.at[q] * quarter, quarter)],
            x_ref.at[:, pl.ds(q * quarter, quarter)],
        )
        for q in range(4)
    ]
    place.meet()

    def half_rows(half, size):
        return pl.ds(0, size) if half is None else pl.ds(half * (size // 2), size // 2)

    def wa_view(part, slot, q, half):
        at = half_rows(half, quarter)
        lanes = pl.ds(part * 2 * HEAD_DIM, 2 * HEAD_DIM)
        return wa_ref.at[slot, pl.ds(q * quarter + at.start, at.size), lanes]

    def wo_view(slot, q, half):
        at = half_rows(half, HEAD_DIM)
        return wo_ref.at[
            pl.ds(pl.multiple_of(slot * HEAD_DIM + at.start, HEAD_DIM // 2), at.size),
            pl.ds(q * quarter, quarter),
        ]

    def wf_view(slot, q, half):
        at = half_rows(half, units)
        return wf_ref.at[
            :,
            pl.ds(pl.multiple_of(slot * units + at.start, 16), at.size),
            pl.ds(q * quarter, quarter),
        ]

    attn_all = [
        Gather(place, copies, functools.partial(wa_view, part), part * PER_GATHER)
        for part in range(2)
    ]
    attn_all.append(Gather(place, copies, wo_view, 2 * PER_GATHER))
    feed = Gather(place, copies, wf_view, 3 * PER_GATHER, late=last)
    base = 4 * PER_GATHER
    for step in range(1, n_head):
        copies.send(rates, rates_ref.at[step], base + step, base + step, place.below(step))
    for loads, part in zip((own_loads[0][:2], own_loads[0][2:4], own_loads[0][4:5]), attn_all):
        for load in loads:
            load.wait()
        part.begin()
    grad_loads = [
        copies.move(
            out_grad.at[:, columns(place.at[q] * quarter, quarter)],
            og_ref.at[pl.ds(0, rows), pl.ds(q * quarter, quarter)],
        )
        for q in range(4)
    ]
    own_loads += [own_weights(q) for q in range(1, 4)]
    rates_ref[0] = rates[...]

    for load in token_loads:
        load.wait()

    def norm_rows(values):
        mean = jnp.mean(values * values, axis=-1, keepdims=True)
        return values * lax.rsqrt(mean + EPSILON)

    @pl.loop(0, rows // 128)
    def _(i):
        at = pl.ds(pl.multiple_of(i * 128, 128), 128)
        nin_ref[at, :] = norm_rows(x_ref[at, :].astype(F32)).astype(BF)

    base += 5
    nin_other = nin_ref.at[pl.ds(rows, rows)]
    copies.send(nin_ref.at[pl.ds(0, rows)], nin_other, base, base, place.across)
    inner = jnp.logical_and(z > 0, z < last)
    first = 1 + 2 * lax.div(z, last)
    second = 2 + lax.rem(lax.div(z + 1, 2), 2)
    third = 6 - first - second
    for part in attn_all:
        part.arrived(first)
        part.arrived(second, inner)
    for load in grad_loads:
        load.wait()
    og_other = og_ref.at[pl.ds(rows, rows)]
    og_base = base - 1
    copies.send(og_ref.at[pl.ds(0, rows)], og_other, og_base, og_base, place.across)
    for q, loads in enumerate(own_loads):
        for load in loads[5:] if q == 0 else loads:
            load.wait()
    for step in range(1, n_head):
        copies.receive(rates_ref.at[step], base - 5 + step, place.up)
    copies.receive(nin_other, base, place.across)
    copies.move(nin_ref, nin_out, later=True)
    own_rows = pl.ds(0, units)
    copies.move(wf_ref.at[:, own_rows], wf_out.at[:, own_rows], later=True)

    def decay_of(head):
        exponent = jnp.full((1, 1), -8.0 / HEADS, F32) * (head + 1).astype(F32)
        return jnp.exp2(exponent)

    def tile(i):
        return pl.ds(pl.multiple_of(i * SPAN, SPAN), SPAN)

    def iota(shape, axis):
        return lax.broadcasted_iota(jnp.int32, shape, axis).astype(F32)

    def dot(left, right):
        return jnp.dot(left, right, preferred_element_type=F32)

    def slot_compute(slot):
        head = 2 * lax.rem(z + slot, n_head) + core
        decay = decay_of(head)
        rate = rates_ref[slot, :, columns(core * HEAD_DIM, HEAD_DIM)]
        coarse = (z * rows).astype(F32) + 32.0 * iota((rows // 32, HEAD_DIM), 0)
        coarse = coarse * rate
        fine = iota((32, HEAD_DIM), 0) * rate
        cos_a, sin_a = jnp.cos(coarse), jnp.sin(coarse)
        cos_b, sin_b = jnp.cos(fine), jnp.sin(fine)
        for a in range(rows // 32):
            cos_row, sin_row = cos_a[a : a + 1], sin_a[a : a + 1]
            cos_ref[slot, pl.ds(a * 32, 32), :] = cos_row * cos_b - sin_row * sin_b
            sin_ref[slot, pl.ds(a * 32, 32), :] = sin_row * cos_b + cos_row * sin_b
        offsets = iota((SPAN, SPAN), 0) - iota((SPAN, SPAN), 1)
        mask = jnp.where(offsets >= 0.0, jnp.exp(-decay * jnp.maximum(offsets, 0.0)), 0.0)
        late = jnp.exp(-decay * (SPAN - 1.0 - iota((SPAN, HEAD_DIM), 0)))

        @pl.loop(0, tiles)
        def _(i):
            at = tile(i)
            pre = dot(nin_ref[at, :], wa_ref[slot])
            pre_ref[slot, at, :] = pre
            here = tile(lax.rem(i, rows // SPAN))
            cosines, sines = cos_ref[slot, here, :], sin_ref[slot, here, :]

            def rotate(values):
                activated = values / (1.0 + jnp.exp(-values))
                turned = jnp.concatenate([activated * cosines, activated * sines], axis=1)
                return turned.astype(BF)

            query = rotate(pre[:, :HEAD_DIM])
            keys = rotate(pre[:, HEAD_DIM : 2 * HEAD_DIM])
            value = pre[:, 2 * HEAD_DIM : 3 * HEAD_DIM].astype(BF)
            q_ref[slot, at, :] = query
            k_ref[slot, at, :] = keys
            v_ref[slot, at, :] = value
            scores = lax.dot_general(
                query, keys, (((1,), (1,)), ((), ())), preferred_element_type=F32
            )
            weights = (scores * mask).astype(BF)
            attn_ref[slot, at, :] = dot(weights, value)
            high, low = split(value.astype(F32) * late)
            both = lax.dot_general(
                keys,
                jnp.concatenate([high, low], axis=1),
                (((0,), (0,)), ((), ())),
                preferred_element_type=F32,
            )
            fresh_ref[slot, i] = both[:, :HEAD_DIM] + both[:, HEAD_DIM:]

        for ref, out in (
            (wa_ref, wa_out),
            (pre_ref, pre_out),
            (q_ref, q_out),
            (k_ref, k_out),
            (v_ref, v_out),
            (cos_ref, cos_out),
            (sin_ref, sin_out),
            (fresh_ref, fresh_out),
        ):
            copies.move(ref.at[slot], out.at[slot], later=True)

    slot_compute(0)
    for part in attn_all:
        part.arrived(second, jnp.logical_not(inner))
    for part in attn_all:
        part.spread(first)
    for part in attn_all:
        part.arrived(third)
    feed.begin()
    for part in attn_all:
        part.spread(second)
    for part in attn_all[:2]:
        part.complete(first)
    slot_compute(first)
    for part in attn_all:
        part.spread(third)
    feed.arrived(first)
    for part in attn_all[:2]:
        part.complete(second)
    slot_compute(second)
    feed.arrived(second, inner)
    for part in attn_all[:2]:
        part.complete(third)
    slot_compute(third)
    base += 1
    chain_base = base
    n_chain = 2 * n_head

    def chain_at(index):
        group, seq = lax.div(index, 2), lax.rem(index, 2)
        return lax.rem(group - z + n_head, n_head), seq, decay_of(2 * group + core)

    def chain_copy(index, slot, seq):
        after = lax.rem(slot + n_head - 1, n_head)
        return pltpu.make_async_remote_copy(
            src_ref=message_ref.at[slot, seq],
            dst_ref=carry_ref.at[after, seq],
            send_sem=sends.at[chain_base + index],
            recv_sem=receives.at[chain_base + index],
            device_id=place.up,
            device_id_type=MESH,
        )

    def hand_on(index, slot, seq, decay):
        total = jnp.exp(-decay * rows) * carry_ref[slot, seq].astype(F32)
        for n in range(rows // SPAN):
            left = rows - (n + 1) * SPAN
            total += jnp.exp(-decay * left) * fresh_ref[slot, seq * (rows // SPAN) + n]
        message_ref[slot, seq] = total.astype(BF)
        chain_copy(index, slot, seq).start()

    @pl.when(z == 0)
    def _():
        @pl.loop(0, n_chain)
        def _(index):
            slot, seq, decay = chain_at(index)
            carry_ref[slot, seq] = jnp.zeros(carry_ref.shape[2:], BF)
            hand_on(index, slot, seq, decay)

    feed.arrived(second, jnp.logical_not(inner))
    feed.spread(first)
    feed.arrived(third)

    @pl.when(z > 0)
    def _():
        @pl.loop(0, n_chain)
        def _(index):
            slot, seq, decay = chain_at(index)
            copies.receive(carry_ref.at[slot, seq], chain_base + index, place.down)
            pl.when(z < last)(lambda: hand_on(index, slot, seq, decay))

    copies.move(carry_ref, carry_out, later=True)
    copies.receive(og_other, og_base, place.across)
    copies.move(og_ref, og_out, later=True)
    feed.spread(second)

    def feed_done(slot):
        at = pl.ds(pl.multiple_of(slot * units, 16), units)
        near, far = pl.ds(0, 3 * quarter), pl.ds(3 * quarter, quarter)
        copies.move(wf_ref.at[:, at, near], wf_out.at[:, at, near], later=True)
        feed.complete(slot)
        copies.move(wf_ref.at[:, at, far], wf_out.at[:, at, far], later=True)

    def apply(seq):
        mine = pl.ds(seq * rows, rows)
        squares_ref[mine, :] = jnp.zeros((rows, HEAD_DIM), F32)

        @pl.loop(0, n_head)
        def _(slot):
            decay = decay_of(2 * lax.rem(z + slot, n_head) + core)
            early = jnp.exp(-decay * (iota((SPAN, HEAD_DIM), 0) + 1.0))
            state = carry_ref[slot, seq].astype(F32)
            for n in range(rows // SPAN):
                i = seq * (rows // SPAN) + n
                at = pl.ds(i * SPAN, SPAN)
                both = dot(q_ref[slot, at, :], jnp.concatenate(split(state), axis=1))
                attn = attn_ref[slot, at, :]
                attn += early * (both[:, :HEAD_DIM] + both[:, HEAD_DIM:])
                attn_ref[slot, at, :] = attn
                squares_ref[at, :] += jnp.sum(attn * attn, axis=-1, keepdims=True)
                if n + 1 < rows // SPAN:
                    state = jnp.exp(-decay * SPAN) * state + fresh_ref[slot, i]

    def gating(seq):
        for n in range(rows // SPAN):
            at = pl.ds(seq * rows + n * SPAN, SPAN)
            total = squares_ref[at, :] + other_squares_ref[at, :]
            scale = lax.rsqrt(total / width + EPSILON)
            other_squares_ref[at, :] = scale
            for slot in range(n_head):
                gate = pre_ref[slot, at, pl.ds(3 * HEAD_DIM, HEAD_DIM)]
                gated = (attn_ref[slot, at, :] * scale * gate).astype(BF)
                gated_ref[at, pl.ds(slot * HEAD_DIM, HEAD_DIM)] = gated

    base += n_chain
    own, other = pl.ds(0, rows), pl.ds(rows, rows)
    apply(1)
    copies.send(squares_ref.at[other], other_squares_ref.at[own], base, base, place.across)
    apply(0)
    copies.send(squares_ref.at[own], other_squares_ref.at[other], base + 1, base + 1, place.across)
    copies.move(attn_ref, attn_out, later=True)
    for slot in (first, second, third):
        attn_all[2].complete(slot)
    copies.receive(other_squares_ref.at[other], base + 1, place.across)
    gating(1)
    feed_done(first)
    base += 2
    for n in range(rows // SPAN):
        gated = gated_ref[pl.ds(rows + n * SPAN, SPAN), :]
        branch_ref[pl.ds(n * SPAN, SPAN), :] = dot(gated, wo_ref[...]).astype(BF)
    copies.send(branch_ref, other_branch_ref, base, base, place.across)
    copies.receive(other_squares_ref.at[own], base - 2, place.across)
    gating(0)
    copies.move(other_squares_ref, scale_out, later=True)
    copies.move(gated_ref, gated_out, later=True)
    copies.move(wo_ref, wo_out, later=True)
    feed.spread(third)
    feed_done(second)

    @pl.loop(0, rows // SPAN)
    def _(i):
        at = tile(i)
        hidden_ref[at, :] = x_ref[at, :].astype(F32) + dot(gated_ref[at, :], wo_ref[...])

    copies.receive(other_branch_ref, base, place.across)

    @pl.loop(0, rows // 128)
    def _(i):
        at = pl.ds(pl.multiple_of(i * 128, 128), 128)
        hidden = hidden_ref[at, :] + other_branch_ref[at, :].astype(F32)
        hidden_ref[at, :] = hidden
        nm_ref[at, :] = norm_rows(hidden).astype(BF)

    copies.send(nm_ref.at[own], nm_ref.at[other], base + 1, base + 1, place.across)
    copies.move(hidden_ref, hidden_out, later=True)
    feed_done(third)
    copies.receive(nm_ref.at[other], base + 1, place.across)
    copies.move(nm_ref, nm_out, later=True)

    @pl.when(z < last)
    def _():
        @pl.loop(0, n_chain)
        def _(index):
            slot, seq, _ = chain_at(index)
            chain_copy(index, slot, seq).wait_send()

    copies.finish()


def forward(n_head, tokens, out_grad, wq, wk, wv, wg, wo, ffn_left, ffn_right, ffn_down, rates):
    rows, width = tokens.shape
    units = ffn_down.shape[0] // 2
    tall = 2 * rows
    buffers = [
        ((n_head, width, 4 * HEAD_DIM), BF),
        ((n_head * HEAD_DIM, width), BF),
        ((3, n_head * units, width), BF),
        ((rows, width), BF),
        ((tall, width), BF),
        ((n_head, tall, 4 * HEAD_DIM), F32),
        ((n_head, tall, 2 * HEAD_DIM), BF),
        ((n_head, tall, 2 * HEAD_DIM), BF),
        ((n_head, tall, HEAD_DIM), BF),
        ((n_head, tall, HEAD_DIM), F32),
        ((n_head, rows, HEAD_DIM), F32),
        ((n_head, rows, HEAD_DIM), F32),
        ((n_head, tall // SPAN, 2 * HEAD_DIM, HEAD_DIM), F32),
        ((n_head, 2, 2 * HEAD_DIM, HEAD_DIM), BF),
        ((n_head, 2, 2 * HEAD_DIM, HEAD_DIM), BF),
        ((tall, HEAD_DIM), F32),
        ((tall, HEAD_DIM), F32),
        ((tall, n_head * HEAD_DIM), BF),
        ((rows, width), BF),
        ((rows, width), BF),
        ((rows, width), F32),
        ((tall, width), BF),
        ((n_head, 1, 2 * HEAD_DIM), F32),
        ((tall, width), BF),
    ]
    out_of = [0, 1, 2, 4, 5, 6, 7, 8, 9, 10, 11, 12, 13, 16, 17, 20, 21, 23]
    n_sems = 4 * PER_GATHER + 4 + 1 + 1 + 2 * n_head + 2 + 2
    return pl.pallas_call(
        functools.partial(forward_kernel, n_head),
        out_shape=[jax.ShapeDtypeStruct(*buffers[i]) for i in out_of],
        in_specs=[ANY] * 10 + [IN_VMEM],
        out_specs=[ANY] * len(out_of),
        scratch_shapes=[pltpu.VMEM(*b) for b in buffers]
        + [
            pltpu.SemaphoreType.DMA((n_sems,)),
            pltpu.SemaphoreType.DMA((n_sems,)),
            pltpu.SemaphoreType.DMA((112,)),
        ],
        compiler_params=pltpu.CompilerParams(
            collective_id=0, has_side_effects=True, vmem_limit_bytes=62 << 20
        ),
        name="forward",
    )(tokens, out_grad, wq, wk, wv, wg, wo, ffn_left, ffn_right, ffn_down, rates)


class Scatter:
    def __init__(self, place, copies, view, far_x, far_y, near_x, near_y, high, base, items=None):
        self.place, self.copies, self.view, self.base = place, copies, view, base
        self.items = items
        self.far_x, self.far_y, self.near_x, self.near_y, self.high = far_x, far_y, near_x, near_y, high

    def part(self, buffer, slot):
        return buffer.at[slot] if self.items is None else buffer.at[slot, pl.ds(0, self.items(slot))]

    def begin(self, slot):
        place, at = self.place, self.base + 4 * slot
        self.copies.send(self.view(slot, 3, 0), self.part(self.far_y, slot), at, at, place.by_y)
        self.copies.send(self.view(slot, 3, 1), self.part(self.far_x, slot), at + 1, at + 1, place.by_x)

    def middle(self, slot):
        place, copies, at = self.place, self.copies, self.base + 4 * slot
        copies.receive(self.part(self.far_y, slot), at, place.by_y)
        add_to(self.view(slot, 1, 0), self.part(self.far_y, slot))
        copies.send(self.view(slot, 1, None), self.part(self.near_x, slot), at + 2, at + 2, place.by_x)
        copies.receive(self.part(self.far_x, slot), at + 1, place.by_x)
        add_to(self.view(slot, 2, 1), self.part(self.far_x, slot))
        copies.send(self.view(slot, 2, None), self.part(self.near_y, slot), at + 3, at + 3, place.by_y)

    def end(self, slot, onward=True):
        place, copies, at = self.place, self.copies, self.base + 4 * slot
        copies.receive(self.part(self.near_x, slot), at + 2, place.by_x)
        copies.receive(self.part(self.near_y, slot), at + 3, place.by_y)
        add_to(self.view(slot, 0, None), self.part(self.near_x, slot), self.part(self.near_y, slot))
        if slot and onward:
            self.go_up(slot)

    def go_up(self, slot):
        at = self.base + 4 * self.place.n_head + slot
        into = self.high.at[slot - 1]
        self.copies.send(self.view(slot, 0, None), into, at, at, self.place.above(slot))

    def total(self, into=None, slots=(1, 2, 3)):
        place = self.place
        high = [self.high.at[slot - 1] for slot in slots]
        for slot, part in zip(slots, high):
            self.copies.receive(part, self.base + 4 * place.n_head + slot, place.up)
        add_to(self.view(0, 0, None), *high, into=into)


PER_SCATTER = 20


def add_to(ref, *others, into=None):
    def add(into, *refs):
        total = refs[0][...].astype(F32)
        for other in refs[1:]:
            total += other[...].astype(F32)
        into[...] = total.astype(BF)

    refs = (ref if into is None else into, ref) + others
    if len(ref.shape) == 2:
        add(*refs)
    else:
        for i in range(ref.shape[0]):
            add(*(one.at[i] for one in refs))


def dot(left, right):
    return jnp.dot(left, right, preferred_element_type=F32)


def iota(shape, axis):
    return lax.broadcasted_iota(jnp.int32, shape, axis).astype(F32)


def decay_of(head):
    exponent = jnp.full((1, 1), -8.0 / HEADS, F32) * (head + 1).astype(F32)
    return jnp.exp2(exponent)


def middle_kernel(
    n_head,
    wf,
    nm,
    og,
    hidden,
    wo,
    pre,
    query,
    attn,
    scale,
    feed_out,
    block_out,
    hidden_grad_out,
    branch_out,
    gate_out,
    ga_out,
    late_out,
    wf_ref,
    t_ref,
    g_ref,
    far_x,
    far_y,
    near_x,
    near_y,
    early_ref,
    high_ref,
    high_first_ref,
    high_third_ref,
    nm_ref,
    og_ref,
    branch_ref,
    hidden_ref,
    mid_ref,
    send_ref,
    got_ref,
    block_ref,
    wo_ref,
    gate_ref,
    attn_ref,
    ga_ref,
    late_ref,
    scale_ref,
    sum_ref,
    other_sum_ref,
    sends,
    receives,
    locals_,
):
    rows, width = hidden.shape
    quarter = width // 4
    units = wf.shape[1] // n_head
    spans = rows // SPAN
    tiles = 2 * spans
    last = n_head - 1
    place = Place(n_head)
    z, core = place.z, place.core
    place.greet()
    copies = Copies(sends, receives, locals_)
    own, other = pl.ds(0, rows), pl.ds(rows, rows)

    order = (2, 1, 3, 0)
    load_nm = copies.move(nm, nm_ref)
    load_og = copies.move(og, og_ref)
    load_wf = {}
    for slot in order:
        at = pl.ds(slot * units, units)
        lanes = pl.ds(0, width if slot < last else width - quarter)
        load_wf[slot] = copies.move(wf.at[:, at, lanes], wf_ref.at[:, at, lanes])
    early_loads = [
        copies.move(hidden, hidden_ref),
        copies.move(wo, wo_ref),
        copies.move(scale, scale_ref),
        copies.move(attn, attn_ref),
        copies.move(pre.at[:, :, pl.ds(3 * HEAD_DIM, HEAD_DIM)], gate_ref),
    ]
    place.meet()

    def tile(i):
        return pl.ds(pl.multiple_of(i * SPAN, SPAN), SPAN)

    def dot_last(left, right):
        return lax.dot_general(left, right, (((1,), (1,)), ((), ())), preferred_element_type=F32)

    def dot_first(left, right):
        return lax.dot_general(left, right, (((0,), (0,)), ((), ())), preferred_element_type=F32)

    early_slot, down = 1, 2

    def items(slot):
        return down if slot == early_slot else 3

    def g_view(slot, q, half):
        size = units if half is None else units // 2
        start = slot * units + (half or 0) * size
        return g_ref.at[pl.ds(0, items(slot)), pl.ds(start, size), pl.ds(q * quarter, quarter)]

    def late_view(ref, q, half):
        rows_at = pl.ds(last * units + half * (units // 2), units // 2)
        return ref.at[:, rows_at, pl.ds(q * quarter, quarter)]

    base = PER_SCATTER
    late_low, late_high = late_view(wf_ref, 3, 0), late_view(wf_ref, 3, 1)
    copies.send(late_view(wf, 1, 0), late_low, base, base, place.by_y)
    copies.send(late_view(wf, 2, 1), late_high, base + 1, base + 1, place.by_x)
    feed = Scatter(place, copies, g_view, far_x, far_y, near_x, near_y, None, 0, items)
    up_base = base + 2

    def feed_products(slot):
        at = pl.ds(slot * units, units)
        load_wf[slot].wait()

        @pl.loop(0, tiles)
        def _(i):
            rows_at = tile(i)
            left = dot_last(wf_ref[0, at, :], nm_ref[rows_at, :])
            right = dot_last(wf_ref[1, at, :], nm_ref[rows_at, :])
            grad = dot_last(wf_ref[2, at, :], og_ref[rows_at, :])
            t_ref[0, at, rows_at] = (grad * right).astype(BF)
            t_ref[1, at, rows_at] = (grad * left).astype(BF)
            t_ref[2, at, rows_at] = (left * right).astype(BF)

    def feed_gradients(slot):
        at = pl.ds(slot * units, units)

        def gradient(columns, of=(0, 1, 2)):
            for m in of:
                right = og_ref if m == down else nm_ref
                g_ref[m, at, columns] = dot(t_ref[m, at, :], right[:, columns]).astype(BF)

        def gradients(n, of=(0, 1, 2)):
            @pl.loop(0, n)
            def _(q):
                gradient(pl.ds(pl.multiple_of(q * quarter, quarter), quarter), of)

        if slot == 0:
            gradients(4)
            return
        of = tuple(range(items(slot)))
        if slot == early_slot:
            gradients(4, (down,))
            copies.send(g_ref.at[down, at], early_ref, up_base, up_base, place.above(slot))
        gradient(pl.ds(3 * quarter, quarter), of)
        feed.begin(slot)
        gradients(3, of)

    load_nm.wait()
    load_og.wait()
    for slot in order[:2]:
        feed_products(slot)
        feed_gradients(slot)
    feed.middle(order[0])
    copies.receive(late_low, base, place.by_y)
    copies.receive(late_high, base + 1, place.by_x)
    feed_products(order[2])
    feed_gradients(order[2])
    feed_products(order[3])
    feed.middle(order[1])
    base += 2 + 4
    for load in early_loads:
        load.wait()

    @pl.loop(0, spans)
    def _(i):
        at = tile(spans + i)
        total = dot_first(t_ref[0, :, at], wf_ref[0]) + dot_first(t_ref[1, :, at], wf_ref[1])
        send_ref[tile(i), :] = total.astype(BF)

    copies.send(send_ref, got_ref, base, base, place.across)

    @pl.loop(0, spans)
    def _(i):
        at = tile(i)
        total = dot_first(t_ref[0, :, at], wf_ref[0]) + dot_first(t_ref[1, :, at], wf_ref[1])
        mid_ref[at, :] = total

    feed.end(order[0], False)
    both, second_at = pl.ds(0, down), pl.ds(order[0] * units, units)
    near = pl.ds(0, quarter)
    above = place.above(order[0])
    copies.send(g_ref.at[:, second_at, near], high_ref, up_base + 1, up_base + 1, above)
    copies.receive(got_ref, base, place.across)

    @pl.loop(0, rows // 128)
    def _(i):
        at = pl.ds(pl.multiple_of(i * 128, 128), 128)
        grad = mid_ref[at, :] + got_ref[at, :].astype(F32)
        values = hidden_ref[at, :]
        norm = lax.rsqrt(jnp.mean(values * values, axis=-1, keepdims=True) + EPSILON)
        normed = values * norm
        mean = jnp.mean(grad * normed, axis=-1, keepdims=True)
        grad = og_ref[at, :].astype(F32) + norm * (grad - normed * mean)
        mid_ref[at, :] = grad
        branch_ref[at, :] = grad.astype(BF)

    copies.send(branch_ref.at[own], branch_ref.at[other], base + 1, base + 1, place.across)
    copies.move(mid_ref, hidden_grad_out, later=True)
    feed_gradients(order[3])
    copies.receive(early_ref, up_base, place.up)
    add_to(g_ref.at[down, pl.ds(0, units)], early_ref)
    feed.begin(0)
    query_loads = []
    for slot in range(n_head):
        lanes = pl.ds(slot * 2 * HEAD_DIM, 2 * HEAD_DIM)
        query_loads.append(copies.move(query.at[slot], t_ref.at[0, pl.ds(0, 2 * rows), lanes]))

    def gate_back(seq):
        for n in range(spans):
            at = pl.ds(seq * rows + n * SPAN, SPAN)
            grad = dot_last(branch_ref[at, :], wo_ref[...])
            norm = scale_ref[at, :]
            total = jnp.zeros((SPAN, 1), F32)
            for slot in range(n_head):
                lanes = pl.ds(slot * HEAD_DIM, HEAD_DIM)
                part = grad[:, slot * HEAD_DIM : (slot + 1) * HEAD_DIM]
                normed = attn_ref[slot, at, :] * norm
                og_ref[at, lanes] = (part * normed).astype(BF)
                part = part * gate_ref[slot, at, :]
                gate_ref[slot, at, :] = part
                total += jnp.sum(part * normed, axis=-1, keepdims=True)
            sum_ref[at, :] = jnp.broadcast_to(total, (SPAN, HEAD_DIM))

    gate_back(0)
    base += 2
    copies.send(sum_ref.at[own], other_sum_ref.at[other], base, base, place.across)
    copies.receive(branch_ref.at[other], base - 1, place.across)
    copies.move(branch_ref, branch_out, later=True)
    gate_back(1)
    copies.send(sum_ref.at[other], other_sum_ref.at[own], base + 1, base + 1, place.across)
    copies.move(og_ref.at[:, pl.ds(0, n_head * HEAD_DIM)], gate_out, later=True)
    copies.sent(base - 2)
    feed.middle(order[2])

    @pl.loop(0, spans)
    def _(i):
        send_ref[tile(i), :] = dot_first(t_ref[2, :, tile(spans + i)], wf_ref[2]).astype(BF)

    copies.send(send_ref, got_ref, base + 2, base + 2, place.across)

    @pl.loop(0, spans)
    def _(i):
        at = tile(i)
        hidden_ref[at, :] += dot_first(t_ref[2, :, at], wf_ref[2])

    feed.end(order[1], False)
    src = g_ref.at[both, pl.ds(order[1] * units, units), near]
    copies.send(src, high_first_ref, up_base + 2, up_base + 2, place.above(order[1]))
    for load in query_loads:
        load.wait()
    copies.receive(other_sum_ref.at[other], base, place.across)
    copies.receive(other_sum_ref.at[own], base + 1, place.across)

    for slot in range(n_head):
        decay = decay_of(2 * lax.rem(z + slot, n_head) + core)
        early = jnp.exp(-decay * (iota((SPAN, HEAD_DIM), 0) + 1.0))

        @pl.loop(0, tiles)
        def _(i):
            at = tile(i)
            norm = scale_ref[at, :]
            mean = (sum_ref[at, :] + other_sum_ref[at, :]) / width
            grad = norm * (gate_ref[slot, at, :] - attn_ref[slot, at, :] * norm * mean)
            grad = grad.astype(BF)
            ga_ref[slot, at, :] = grad
            q = t_ref[0, at, pl.ds(slot * 2 * HEAD_DIM, 2 * HEAD_DIM)]
            both_terms = dot_first(
                q, jnp.concatenate(split(grad.astype(F32) * early), axis=1)
            )
            late_ref[slot, i] = both_terms[:, :HEAD_DIM] + both_terms[:, HEAD_DIM:]

        copies.move(ga_ref.at[slot], ga_out.at[slot], later=True)
        copies.move(late_ref.at[slot], late_out.at[slot], later=True)

    feed.middle(order[3])
    copies.receive(got_ref, base + 2, place.across)

    @pl.loop(0, rows // 128)
    def _(i):
        at = pl.ds(pl.multiple_of(i * 128, 128), 128)
        block_ref[at, :] = (hidden_ref[at, :] + got_ref[at, :].astype(F32)).astype(BF)

    for q in range(4):
        far = pl.ds(pl.multiple_of(place.at[q] * quarter, quarter), quarter)
        src = block_ref.at[:, pl.ds(q * quarter, quarter)]
        copies.move(src, block_out.at[:, far], later=True)
    feed.end(order[2], False)
    src = g_ref.at[:, pl.ds(order[2] * units, units), near]
    copies.send(src, high_third_ref, up_base + 3, up_base + 3, place.above(order[2]))
    copies.receive(high_ref, up_base + 1, place.up)
    copies.receive(high_first_ref, up_base + 2, place.up)
    feed.end(order[3], False)
    first_rows = pl.ds(0, units)
    add_to(g_ref.at[both, first_rows, near], high_ref.at[both], high_first_ref)
    add_to(g_ref.at[down, first_rows, near], high_ref.at[down])
    copies.receive(high_third_ref, up_base + 3, place.up)
    add_to(g_view(0, 0, None), high_third_ref)
    copies.move(g_view(0, 0, None), feed_out, later=True)
    copies.finish()


def middle(n_head, wf, nm, og, hidden, wo, pre, query, attn, scale):
    rows, width = hidden.shape
    units = wf.shape[1] // n_head
    quarter = width // 4
    tall = 2 * rows
    halves = (n_head, 3, units // 2, quarter)
    wholes = (n_head, 3, units, quarter)
    late = ((n_head, tall // SPAN, 2 * HEAD_DIM, HEAD_DIM), F32)
    buffers = [
        (wf.shape, BF),
        (wf.shape, BF),
        (wf.shape, BF),
        (halves, BF),
        (halves, BF),
        (wholes, BF),
        (wholes, BF),
        ((units, width), BF),
        (wholes[1:], BF),
        ((2, units, quarter), BF),
        (wholes[1:], BF),
        ((tall, width), BF),
        ((tall, width), BF),
        ((tall, width), BF),
        ((rows, width), F32),
        ((rows, width), F32),
        ((rows, width), BF),
        ((rows, width), BF),
        ((rows, width), BF),
        (wo.shape, BF),
        (attn.shape, F32),
        (attn.shape, F32),
        (attn.shape, BF),
        late,
        (scale.shape, F32),
        (scale.shape, F32),
        (scale.shape, F32),
    ]
    outs = [
        (wholes[1:], BF),
        ((rows, width), BF),
        ((rows, width), F32),
        ((tall, width), BF),
        ((tall, n_head * HEAD_DIM), BF),
        (attn.shape, BF),
        late,
    ]
    n_sems = PER_SCATTER + 2 + 4 + 2 + 3
    return pl.pallas_call(
        functools.partial(middle_kernel, n_head),
        out_shape=[jax.ShapeDtypeStruct(*out) for out in outs],
        in_specs=[ANY] * 9,
        out_specs=[ANY] * len(outs),
        scratch_shapes=[pltpu.VMEM(*b) for b in buffers]
        + [
            pltpu.SemaphoreType.DMA((n_sems,)),
            pltpu.SemaphoreType.DMA((n_sems,)),
            pltpu.SemaphoreType.DMA((64,)),
        ],
        compiler_params=pltpu.CompilerParams(
            collective_id=1, has_side_effects=True, vmem_limit_bytes=63 << 20
        ),
        name="middle",
    )(wf, nm, og, hidden, wo, pre, query, attn, scale)


class Share:
    def __init__(self, place, copies, view, base):
        self.place, self.copies, self.view, self.base = place, copies, view, base

    def pass_on(self, q, half, at, device):
        part = self.view(0, q, half)
        self.copies.send(part, part, self.base + at, self.base + at, device)

    def begin(self):
        self.pass_on(0, None, 0, self.place.by_x)
        self.pass_on(0, None, 1, self.place.by_y)
        self.pass_on(0, None, 4, self.place.across)

    def spread(self):
        place, copies, at = self.place, self.copies, self.base
        copies.receive(self.view(0, 1, None), at, place.by_x)
        self.pass_on(1, 0, 2, place.by_y)
        copies.receive(self.view(0, 2, None), at + 1, place.by_y)
        self.pass_on(2, 1, 3, place.by_x)
        self.pass_on(1, None, 5, place.across)
        self.pass_on(2, None, 6, place.across)

    def complete(self):
        place, copies, at = self.place, self.copies, self.base
        copies.receive(self.view(0, 3, 0), at + 2, place.by_y)
        copies.receive(self.view(0, 3, 1), at + 3, place.by_x)
        self.pass_on(3, None, 7, place.across)

    def other_side(self):
        for q in range(4):
            self.copies.receive(self.view(1, q, None), self.base + 4 + q, self.place.across)


PER_SHARE = 8


def last_kernel(
    n_head,
    late,
    feed_piece,
    nin,
    gate_pre,
    gated,
    branch,
    query,
    keys,
    values,
    grad_attn,
    carry,
    fresh,
    pre,
    cosines,
    sines,
    wa,
    hidden_grad,
    block,
    tokens,
    input_ref,
    block_ref,
    feed_ref,
    attn_ref,
    rates_both,
    ga_ref,
    a_far_x,
    a_far_y,
    a_near_x,
    a_near_y,
    a_high,
    g_far_x,
    g_far_y,
    g_near_x,
    g_near_y,
    g_high,
    late_ref,
    pending_ref,
    message_ref,
    nin_ref,
    gate_ref,
    gated_ref,
    branch_ref,
    q_ref,
    k_ref,
    v_ref,
    grad_attn_ref,
    carry_ref,
    fresh_ref,
    qk_pre_ref,
    cos_ref,
    sin_ref,
    pre_ref,
    wa_ref,
    x_ref,
    grad_ref,
    send_ref,
    got_ref,
    rates_ref,
    rates_high,
    rates_sum,
    rates_got,
    sends,
    receives,
    locals_,
):
    rows, width = tokens.shape
    quarter = width // 4
    units = feed_piece.shape[1]
    spans = rows // SPAN
    tiles = 2 * spans
    last = n_head - 1
    three = 3 * HEAD_DIM
    place = Place(n_head)
    place.greet()
    z, core = place.z, place.core
    copies = Copies(sends, receives, locals_)
    order = (2, 1, 3, 0)
    sides = (core, 1 - core)

    own_block = pl.ds(pl.multiple_of(place.plane * quarter, quarter), quarter)
    load_feed = copies.move(feed_piece, feed_ref.at[sides[0], :, :, own_block])
    load_late = copies.move(late, late_ref)
    load_first = [copies.move(nin, nin_ref), copies.move(gate_pre, gate_ref)]
    load_second = [copies.move(gated, gated_ref), copies.move(branch, branch_ref)]
    load_back = [
        copies.move(src, dst)
        for src, dst in (
            (query, q_ref),
            (keys, k_ref),
            (values, v_ref),
            (grad_attn, grad_attn_ref),
            (carry, carry_ref),
        )
    ]
    for seq in range(2):
        for slot in range(n_head):
            load_back.append(copies.move(fresh.at[slot, seq * spans], fresh_ref.at[slot, seq]))

    def slot_load(slot, turn):
        return [
            copies.move(pre.at[slot, :, pl.ds(0, 2 * HEAD_DIM)], qk_pre_ref.at[turn]),
            copies.move(cosines.at[slot], cos_ref.at[turn]),
            copies.move(sines.at[slot], sin_ref.at[turn]),
        ]

    slot_loads = [slot_load(slot, turn) for turn, slot in enumerate(order[:2])]
    late_loads = [
        copies.move(wa, wa_ref),
        copies.move(hidden_grad, grad_ref),
        copies.move(block, block_ref),
    ]
    for q in range(4):
        far = pl.ds(pl.multiple_of(place.at[q] * quarter, quarter), quarter)
        late_loads.append(copies.move(tokens.at[:, far], x_ref.at[:, pl.ds(q * quarter, quarter)]))
    place.meet()

    def tile(i):
        return pl.ds(pl.multiple_of(i * SPAN, SPAN), SPAN)

    def dot_last(left, right):
        return lax.dot_general(left, right, (((1,), (1,)), ((), ())), preferred_element_type=F32)

    def dot_first(left, right):
        return lax.dot_general(left, right, (((0,), (0,)), ((), ())), preferred_element_type=F32)

    def part(start, half, size):
        if half is None:
            return pl.ds(start, size)
        return pl.ds(start + half * (size // 2), size // 2)

    def start_of(q):
        return pl.multiple_of(place.at[q] * quarter, quarter)

    def feed_view(side, q, half):
        return feed_ref.at[sides[side], :, part(0, half, units), pl.ds(start_of(q), quarter)]

    def lanes_view(lanes, side, q, half):
        at = part(0, half, quarter)
        start = pl.multiple_of(start_of(q) + at.start, quarter // 2)
        return attn_ref.at[sides[side], pl.ds(start, at.size), lanes]

    def ga_view(lanes, slot, q, half):
        return ga_ref.at[slot, part(q * quarter, half, quarter), lanes]

    gate_lanes, rest_lanes = pl.ds(three, 2 * HEAD_DIM), pl.ds(0, three)
    weight_lanes = pl.ds(three, HEAD_DIM)
    of_gate = functools.partial(ga_view, gate_lanes)
    of_rest = functools.partial(ga_view, rest_lanes)
    gate = Scatter(place, copies, of_gate, g_far_x, g_far_y, g_near_x, g_near_y, g_high, 0)
    base = PER_SCATTER
    rest = Scatter(place, copies, of_rest, a_far_x, a_far_y, a_near_x, a_near_y, a_high, base)
    base += PER_SCATTER
    to_gate = functools.partial(lanes_view, gate_lanes)
    to_rest = functools.partial(lanes_view, rest_lanes)
    shares = []
    for view in (feed_view, to_gate, to_rest):
        shares.append(Share(place, copies, view, base))
        base += PER_SHARE
    feed_share, gate_share, rest_share = shares

    load_feed.wait()
    feed_share.begin()

    n_chain = 2 * n_head
    chain_base = base
    base += n_chain

    def chain_at(index):
        group, seq = lax.div(index, 2), lax.rem(index, 2)
        return lax.rem(group - z + n_head, n_head), seq, decay_of(2 * group + core)

    def chain_copy(index, slot, seq):
        return pltpu.make_async_remote_copy(
            src_ref=message_ref.at[slot, seq],
            dst_ref=pending_ref.at[lax.rem(slot + 1, n_head), seq],
            send_sem=sends.at[chain_base + index],
            recv_sem=receives.at[chain_base + index],
            device_id=place.down,
            device_id_type=MESH,
        )

    def hand_on(index):
        slot, seq, decay = chain_at(index)
        total = jnp.exp(-decay * rows) * pending_ref[slot, seq].astype(F32)
        for n in range(spans):
            total += jnp.exp(-decay * (n * SPAN)) * late_ref[slot, seq * spans + n]
        message_ref[slot, seq] = total.astype(BF)
        chain_copy(index, slot, seq).start()

    def take(index):
        slot, seq, _ = chain_at(index)
        copies.receive(pending_ref.at[slot, seq], chain_base + index, place.up)

    load_late.wait()

    @pl.when(z == last)
    def _():
        pending_ref[...] = jnp.zeros_like(pending_ref)
        pl.loop(0, n_chain)(hand_on)

    for load in load_first:
        load.wait()

    for load in load_second:
        load.wait()

    def gate_gradient(at):
        grads = dot_first(nin_ref[:, at], gate_ref[...]).astype(BF)
        outs = dot_first(branch_ref[:, at], gated_ref[...]).astype(BF)
        for slot in range(n_head):
            lanes = slice(slot * HEAD_DIM, (slot + 1) * HEAD_DIM)
            ga_ref[slot, at, pl.ds(three, HEAD_DIM)] = grads[:, lanes]
            ga_ref[slot, at, pl.ds(three + HEAD_DIM, HEAD_DIM)] = outs[:, lanes]

    gate_gradient(pl.ds(3 * quarter, quarter))
    for slot in order:
        gate.begin(slot)
    pl.loop(0, 3)(lambda q: gate_gradient(tile(q)))

    @pl.when(jnp.logical_and(z > 0, z < last))
    def _():
        @pl.loop(0, n_chain)
        def _(index):
            take(index)
            hand_on(index)

    for slot in order:
        gate.middle(slot)
    for load in load_back:
        load.wait()

    @pl.when(z == 0)
    def _():
        pl.loop(0, n_chain)(take)

    offsets = iota((SPAN, SPAN), 0) - iota((SPAN, SPAN), 1)

    def back_slot(slot, turn):
        decay = decay_of(2 * lax.rem(z + slot, n_head) + core)
        mask = jnp.where(offsets >= 0.0, jnp.exp(-decay * jnp.maximum(offsets, 0.0)), 0.0)
        places = iota((SPAN, 1), 0)
        early = jnp.exp(-decay * (places + 1.0))
        late_decay = jnp.exp(-decay * (SPAN - 1.0 - places))
        span_decay = jnp.exp(-decay * SPAN)
        rates_ref[slot] = jnp.zeros((8, HEAD_DIM), F32)

        @pl.loop(0, 2)
        def _(seq):
            for n in range(spans):
                at, here = tile(seq * spans + n), pl.ds(n * SPAN, SPAN)
                state = carry_ref[slot, seq].astype(F32)
                if n == 1:
                    state = span_decay * state + fresh_ref[slot, seq]
                later = pending_ref[slot, seq].astype(F32)
                if n == 0:
                    later = span_decay * later + late_ref[slot, seq * spans + 1]
                q, k, v = q_ref[slot, at, :], k_ref[slot, at, :], v_ref[slot, at, :]
                grad = grad_attn_ref[slot, at, :]
                weights = (dot_last(q, k) * mask).astype(BF)
                scores = (dot_last(grad, v) * mask).astype(BF)
                state_high, state_low = split(state)
                grad_query = dot(scores, k)
                grad_query += early * (dot_last(grad, state_high) + dot_last(grad, state_low))
                later_high, later_low = split(later)
                grad_keys = dot_first(scores, q)
                grad_keys += late_decay * (dot_last(v, later_high) + dot_last(v, later_low))
                both = dot(k, jnp.concatenate([later_high, later_low], axis=1))
                grad_values = dot_first(weights, grad)
                grad_values += late_decay * (both[:, :HEAD_DIM] + both[:, HEAD_DIM:])
                pre_ref[slot, at, pl.ds(2 * HEAD_DIM, HEAD_DIM)] = grad_values.astype(BF)
                cosine, sine = cos_ref[turn, here, :], sin_ref[turn, here, :]
                angles = jnp.zeros((SPAN, HEAD_DIM), F32)
                for i, turned in enumerate((grad_query, grad_keys)):
                    lanes = pl.ds(i * HEAD_DIM, HEAD_DIM)
                    value = qk_pre_ref[turn, at, lanes]
                    by_cos, by_sin = turned[:, :HEAD_DIM], turned[:, HEAD_DIM:]
                    sigmoid = 1.0 / (1.0 + jnp.exp(-value))
                    act = by_cos * cosine + by_sin * sine
                    angles += value * sigmoid * (by_sin * cosine - by_cos * sine)
                    act = act * sigmoid * (1.0 + value * (1.0 - sigmoid))
                    pre_ref[slot, at, lanes] = act.astype(BF)
                steps = (z * rows + n * SPAN).astype(F32) + places
                rates_ref[slot, pl.ds(0, 1), :] += jnp.sum(steps * angles, axis=0, keepdims=True)

    def rest_gradient(slot, at):
        ga_ref[slot, at, rest_lanes] = dot_first(nin_ref[:, at], pre_ref[slot]).astype(BF)

    rates_base = base
    base += n_head + 3
    for i, slot in enumerate(order):
        for load in slot_loads[i]:
            load.wait()
        back_slot(slot, i % 2)
        if i + 2 < n_head:
            slot_loads.append(slot_load(order[i + 2], i % 2))
        if slot:
            at = rates_base + slot
            copies.send(rates_ref.at[slot], rates_high.at[slot - 1], at, at, place.above(slot))
        rest_gradient(slot, pl.ds(3 * quarter, quarter))
        rest.begin(slot)
        pl.loop(0, 3)(lambda q: rest_gradient(slot, tile(q)))
    total = rates_ref[0]
    for slot in range(1, n_head):
        copies.receive(rates_high.at[slot - 1], rates_base + slot, place.up)
        total += rates_high[slot - 1]
    rates_sum[0] = total
    rates_base += n_head
    copies.send(rates_sum.at[0], rates_got.at[0], rates_base, rates_base, place.by_x)
    for slot in order:
        gate.end(slot)
    copies.receive(rates_got.at[0], rates_base, place.by_x)
    rates_sum[1] = total + rates_got[0]
    copies.send(rates_sum.at[1], rates_got.at[1], rates_base + 1, rates_base + 1, place.by_y)
    rest.middle(order[0])
    rest.middle(order[1])
    for load in late_loads:
        load.wait()

    def grad_in(at):
        total = dot_last(gate_ref[at, :], wa_gate())
        for slot in range(n_head):
            total += dot_last(pre_ref[slot, at, :], wa_ref[slot, :, rest_lanes])
        return total

    def wa_gate():
        return jnp.concatenate([wa_ref[slot, :, weight_lanes] for slot in range(n_head)], axis=1)

    @pl.loop(0, spans)
    def _(i):
        send_ref[tile(i), :] = grad_in(tile(spans + i)).astype(BF)

    copies.send(send_ref, got_ref, base, base, place.across)
    rest.middle(order[2])

    rest.middle(order[3])
    feed_share.spread()
    rest.end(order[0])
    copies.receive(got_ref, base, place.across)
    rest.end(order[1])

    @pl.loop(0, spans)
    def _(i):
        at = tile(i)
        values = x_ref[at, :].astype(F32)
        norm = lax.rsqrt(jnp.mean(values * values, axis=-1, keepdims=True) + EPSILON)
        normed = values * norm
        grad = grad_in(at) + got_ref[at, :].astype(F32)
        mean = jnp.mean(grad * normed, axis=-1, keepdims=True)
        grad_ref[at, :] += norm * (grad - normed * mean)

    for q in range(4):
        src = grad_ref.at[:, pl.ds(q * quarter, quarter)]
        copies.move(src, input_ref.at[:, pl.ds(start_of(q), quarter)], later=True)
    gate.total(to_gate(0, 0, None))
    gate_share.begin()
    rest.end(order[2])
    rest.end(order[3])
    rest.total(to_rest(0, 0, None))
    rest_share.begin()
    copies.receive(rates_got.at[1], rates_base + 1, place.by_y)
    rates_both[sides[0]] = rates_sum[1] + rates_got[1]
    mine = rates_both.at[sides[0]]
    copies.send(mine, mine, rates_base + 2, rates_base + 2, place.across)
    feed_share.complete()
    gate_share.spread()
    copies.receive(rates_both.at[sides[1]], rates_base + 2, place.across)
    feed_share.other_side()
    rest_share.spread()
    gate_share.complete()
    rest_share.complete()
    for share in shares[1:]:
        share.other_side()

    @pl.when(z > 0)
    def _():
        @pl.loop(0, n_chain)
        def _(index):
            slot, seq, _ = chain_at(index)
            chain_copy(index, slot, seq).wait_send()

    copies.finish()


def last(
    n_head,
    late,
    feed_piece,
    nin,
    gate_pre,
    gated,
    branch,
    query,
    keys,
    values,
    grad_attn,
    carry,
    fresh,
    pre,
    cosines,
    sines,
    wa,
    hidden_grad,
    block,
    tokens,
):
    rows, width = tokens.shape
    _, units, quarter = feed_piece.shape
    tall = 2 * rows

    def scatter_buffers(shape, halved):
        half = tuple(n // 2 if i == halved else n for i, n in enumerate(shape))
        return [
            ((n_head,) + half, BF),
            ((n_head,) + half, BF),
            ((n_head,) + shape, BF),
            ((n_head,) + shape, BF),
            ((n_head - 1,) + shape, BF),
        ]

    outs = [
        ((rows, width), F32),
        ((rows, width), BF),
        ((2, 3, units, width), BF),
        ((2, width, 5 * HEAD_DIM), BF),
        ((2, 8, HEAD_DIM), F32),
    ]
    chain = ((n_head, 2, 2 * HEAD_DIM, HEAD_DIM), BF)
    buffers = [
        ((n_head, width, 5 * HEAD_DIM), BF),
        *scatter_buffers((quarter, 3 * HEAD_DIM), 0),
        *scatter_buffers((quarter, 2 * HEAD_DIM), 0),
        (late.shape, F32),
        chain,
        chain,
        (nin.shape, BF),
        (gate_pre.shape, BF),
        (gated.shape, BF),
        (branch.shape, BF),
        (query.shape, BF),
        (keys.shape, BF),
        (values.shape, BF),
        (grad_attn.shape, BF),
        chain,
        (chain[0], F32),
        ((2, tall, 2 * HEAD_DIM), F32),
        ((2, rows, HEAD_DIM), F32),
        ((2, rows, HEAD_DIM), F32),
        ((n_head, tall, 3 * HEAD_DIM), BF),
        (wa.shape, BF),
        ((rows, width), BF),
        ((rows, width), F32),
        ((rows, width), BF),
        ((rows, width), BF),
        ((n_head, 8, HEAD_DIM), F32),
        ((n_head - 1, 8, HEAD_DIM), F32),
        ((2, 8, HEAD_DIM), F32),
        ((2, 8, HEAD_DIM), F32),
    ]
    n_sems = 2 * PER_SCATTER + 3 * PER_SHARE + 2 * n_head + n_head + 3 + 1
    arrays = [late, feed_piece, nin, gate_pre, gated, branch, query, keys, values, grad_attn]
    arrays += [carry, fresh, pre, cosines, sines, wa, hidden_grad, block, tokens]
    arrays = [pltpu.with_memory_space_constraint(array, pltpu.HBM) for array in arrays]
    return pl.pallas_call(
        functools.partial(last_kernel, n_head),
        out_shape=[pltpu.VMEM(*out) for out in outs],
        in_specs=[ANY] * len(arrays),
        out_specs=[IN_VMEM] * len(outs),
        scratch_shapes=[pltpu.VMEM(*b) for b in buffers]
        + [
            pltpu.SemaphoreType.DMA((n_sems,)),
            pltpu.SemaphoreType.DMA((n_sems,)),
            pltpu.SemaphoreType.DMA((64,)),
        ],
        compiler_params=pltpu.CompilerParams(
            collective_id=2, has_side_effects=True, vmem_limit_bytes=52 << 20
        ),
        name="last",
    )(*arrays)


def finish_kernel(grad, block, feed, attn, rates, *refs):
    outs, results, locals_ = refs[:11], refs[11:-1], refs[-1]
    copies = Copies(None, None, locals_)
    (block_out, grad_out, q_out, k_out, v_out, g_out, o_out, rates_out, l_out, r_out, d_out) = outs
    units = feed.shape[2]
    copies.move(grad, grad_out, later=True)
    copies.move(block, block_out, later=True)
    l_ref, r_ref, d_ref, q_ref, k_ref, v_ref, g_ref, o_ref, rates_ref = results
    for side in range(2):
        rates_ref[:, pl.ds(side * HEAD_DIM, HEAD_DIM)] = rates[side, pl.ds(0, 1), :]
    copies.move(rates_ref, rates_out, later=True)
    for i, (ref, out) in enumerate(((l_ref, l_out), (r_ref, r_out), (d_ref, d_out))):
        for side in range(2):
            at = pl.ds(side * units, units)
            ref[at, :] = feed[side, i].astype(F32)
            copies.move(ref.at[at], out.at[at], later=True)
    for i, (ref, out) in enumerate(((q_ref, q_out), (k_ref, k_out), (v_ref, v_out), (g_ref, g_out))):
        lanes = pl.ds(i * HEAD_DIM, HEAD_DIM)
        for side in range(2):
            ref[:, pl.ds(side * HEAD_DIM, HEAD_DIM)] = attn[side, :, lanes].astype(F32)
        copies.move(ref, out, later=True)
    for side in range(2):
        lanes = pl.ds(4 * HEAD_DIM, HEAD_DIM)
        o_ref[pl.ds(side * HEAD_DIM, HEAD_DIM), :] = attn[side, :, lanes].T.astype(F32)
    copies.move(o_ref, o_out, later=True)
    copies.finish()


def finish(grad, block, feed, attn, rates):
    _, _, units, width = feed.shape
    projection = ((width, 2 * HEAD_DIM), F32)
    back = ((2 * HEAD_DIM, width), F32)
    results = [((2 * units, width), F32)] * 3 + [projection] * 4 + [back]
    results.append(((1, 2 * HEAD_DIM), F32))
    outs = [(block.shape, BF), (grad.shape, F32)] + results[3:] + results[:3]
    return pl.pallas_call(
        finish_kernel,
        out_shape=[jax.ShapeDtypeStruct(*out) for out in outs],
        in_specs=[IN_VMEM] * 5,
        out_specs=[ANY] * len(outs),
        scratch_shapes=[pltpu.VMEM(*b) for b in results] + [pltpu.SemaphoreType.DMA((48,))],
        compiler_params=pltpu.CompilerParams(vmem_limit_bytes=24 << 20),
        name="finish",
    )(grad, block, feed, attn, rates)


def make(n_dp, n_head):
    def on_device(
        tokens,
        attn_query,
        attn_key,
        attn_value,
        attn_gate,
        attn_out,
        rotation_rates,
        ffn_left,
        ffn_right,
        ffn_down,
        out_grad,
    ):
        rates_in = rotation_rates.reshape(1, -1)
        (
            attn_weights,
            out_w,
            ffn_all,
            gathered_in,
            pre,
            query,
            keys,
            values,
            attn,
            cosines,
            sines,
            fresh,
            carry,
            scale_attn,
            gated,
            hidden,
            gathered_mid,
            grad_rows,
        ) = forward(
            n_head,
            tokens,
            out_grad,
            attn_query,
            attn_key,
            attn_value,
            attn_gate,
            attn_out,
            ffn_left.T,
            ffn_right.T,
            ffn_down,
            rates_in,
        )
        feed_piece, block_out, grad_hidden, branch_rows, gate_pre, grad_attn, late = middle(
            n_head,
            ffn_all,
            gathered_mid,
            grad_rows,
            hidden,
            out_w,
            pre,
            query,
            attn,
            scale_attn,
        )
        grads = last(
            n_head,
            late,
            feed_piece,
            gathered_in,
            gate_pre,
            gated,
            branch_rows,
            query,
            keys,
            values,
            grad_attn,
            carry,
            fresh,
            pre,
            cosines,
            sines,
            attn_weights,
            grad_hidden,
            block_out,
            tokens,
        )
        results = finish(*grads)
        rates_grad, left_grad, right_grad = results[7][0], results[8].T, results[9].T
        results = list(results[:7]) + [rates_grad, left_grad, right_grad, results[10]]
        if n_dp > 8:
            groups = [[i + 8 * j for j in range(n_dp // 8)] for i in range(8)]
            grads = [lax.psum(grad, "dp", axis_index_groups=groups) for grad in results[2:]]
            results = results[:2] + grads
        return tuple(results)

    return on_device


def solution(mesh):
    weights = (P(None, "head"),) * 4 + (P("head", None), P("head")) + (P(None, "head"),) * 2
    weights = weights + (P("head", None),)
    rows = P(("dp", "head"), None)
    return jax.shard_map(
        make(mesh.shape["dp"], mesh.shape["head"]),
        mesh=mesh,
        in_specs=(rows,) + weights + (rows,),
        out_specs=(rows, rows) + weights,
        check_vma=False,
    )
```
